32 devices in a mesh: img: 16 (over z, y, x), seq: 2 (over core).
Axes of the slice: x: 2, y: 2, z: 4, core: 2. Of those that a mesh axis runs over, the one named last changes fastest.
Arguments:
- pixels: bfloat16 [256, 49, 3072], P(('img', 'seq')), may hold values from -6 to 6
- keep_mask: int32 [256, 49], P(('img', 'seq')), may hold values from 0 to 1, as said below
- partner_index: int32 [256], P(('img', 'seq')), may hold values from 0 to 255, each once
- partner_emb: bfloat16 [256, 768], P(('img', 'seq')), may hold values from -0.796875 to 0.796875
- masters: float32 [512, 32, 1024], P('img', 'seq'), may hold values from -0.1875 to 0.1875
- first_moment_slots: float32 [512, 32, 1024], P('img', 'seq'), may hold values from -0.0009822747 to 0.0009822747
- second_moment_slots: float32 [512, 32, 1024], P('img', 'seq'), may hold values from 6.030397e-08 to 2.4121587e-07
- slot_unit_index: int32 [512], replicated, may hold values from 0 to 511, as said below
- small_params: float32 [66, 1024], replicated
- small_first: float32 [66, 1024], replicated, may hold values from -0.0019645493 to 0.0019645493
- small_second: float32 [66, 1024], replicated, may hold values from 6.030397e-08 to 9.648635e-07
- step_count: int32 [], replicated, may hold values from 2 to 20
Outputs:
- new_masters: float32 [512, 32, 1024], P('img', 'seq')
- new_first: float32 [512, 32, 1024], P('img', 'seq')
- new_second: float32 [512, 32, 1024], P('img', 'seq')
- new_small: float32 [66, 1024], replicated
- new_small_first: float32 [66, 1024], replicated
- new_small_second: float32 [66, 1024], replicated
- loss: float32 [], replicated
- grad_norm: float32 [], replicated
The draws below stay inside these ranges and needn't reach their ends.
Inputs may be any that keep to these rules, and one draw needn't show every extreme that they name: `keep_mask`: each image keeps at least half of its 49 patches, rounded up; some image keeps all and some keeps exactly that least. `slot_unit_index`: a permutation of the slots; values of 504 or more mark slots that hold no unit; the slot of value u differs from u by at most 2. `partner_index`: a permutation of the images.
All inputs are finite; a program needn't handle non-finite values.
Results may differ from the reference program's by a relative error of at most 0.015.
Values may be sent and summed in bfloat16 or wider, within the bound.
No kernel may reach another device: no remote copies, remote signals or barrier semaphores. Data moves between devices by JAX's collectives and lax.ppermute only.
A program may use at most 384 MiB of HBM per device.

```python
import math
import jax
import jax.numpy as jnp
from jax import lax

MODEL_WIDTH = 1024
HEADS = 16
HEAD_DIM = 64
FF = 4096
PIX = 3072
PATCHES = 49
PROJ = 768
TOKS = 50
IMAGES = 256
ROWS_PER_UNIT = 32
UNIT_COUNT = 504
SLOT_COUNT = 512
SMALL = 66
PARAMETER_COUNT = 16582656


def draw_keep_mask(key, part):
    count_key, order_key = jax.random.split(key)
    least = (PATCHES + 1) // 2
    counts = jax.random.randint(count_key, (IMAGES,), least, PATCHES + 1)
    counts = counts.at[0].set(PATCHES).at[1].set(least)
    row_keys = jax.random.split(order_key, IMAGES)

    def row_order(row_key):
        return jax.random.permutation(row_key, PATCHES)
    ranking = jax.vmap(row_order)(row_keys)
    return (ranking < counts[:, None]).astype(jnp.int32)


def draw_slot_unit_index(key, part):
    jitter = jax.random.randint(jax.random.fold_in(key, 7), (SLOT_COUNT,), 0, 12)
    units = jnp.arange(SLOT_COUNT, dtype=jnp.int32)
    scores = (4 * units + jitter) * SLOT_COUNT + units
    return jnp.argsort(scores, stable=True).astype(jnp.int32)


def draw_small_params(key, part):
    values = 0.2 * jax.random.normal(key, (SMALL, MODEL_WIDTH), jnp.float32)
    base = 1 + TOKS
    tail = base + 8 + FF // MODEL_WIDTH
    row_ids = jnp.arange(SMALL)[:, None]
    is_gain = (row_ids == base + 1) | (row_ids == base + 6) | (row_ids == tail + 1)
    return jnp.where(is_gain, values + 1.0, values)


def steps_of(own_key, shape, pieces, low, top_value):
    def one(axis_at, parts):
        draws = jax.random.uniform(jax.random.fold_in(jax.random.fold_in(own_key, 6), axis_at), (parts,), jnp.float32, low / len(pieces), top_value / len(pieces))
        return jnp.repeat(jnp.exp(draws), shape[axis_at] // parts).reshape((-1,) + (1,) * (len(shape) - axis_at - 1))

    factor_of = one(*pieces[0])
    for cut in pieces[1:]:
        factor_of = factor_of * one(*cut)
    return factor_of


def scatter_about(rng, shape, scale, bound, pieces=(), held_as=jnp.bfloat16):
    drawn = jax.random.normal(rng, shape, jnp.float32) * scale
    if len(pieces) > 0:
        drawn = steps_of(rng, shape, pieces, -0.22, 0.18) * drawn
    return jnp.clip(drawn, min=-bound, max=bound).astype(held_as)


def setup_inputs(seed: int = 0) -> dict:
    key_of = jax.random.split(jax.random.key(seed), 13)
    return {
        "pixels": scatter_about(key_of[0], (IMAGES, PATCHES, PIX), 1.0, 6.0, ((0, 32),)),
        "keep_mask": draw_keep_mask(jax.random.fold_in(key_of[12], 71), 0),
        "partner_index": jax.random.permutation(key_of[2], IMAGES).astype(jnp.int32),
        "partner_emb": scatter_about(key_of[3], (IMAGES, PROJ), 0.14, 0.796875, ((0, 32),)),
        "masters": scatter_about(key_of[4], (SLOT_COUNT, ROWS_PER_UNIT, MODEL_WIDTH), MODEL_WIDTH ** -0.5, 0.1875, ((0, 16), (1, 2)), jnp.float32),
        "first_moment_slots": scatter_about(key_of[5], (SLOT_COUNT, ROWS_PER_UNIT, MODEL_WIDTH), (1.0 / PARAMETER_COUNT ** 0.5), 0.0009822747, ((0, 16), (1, 2)), jnp.float32),
        "second_moment_slots": jnp.clip(jnp.exp(math.log(2.412158721654123e-07) - 1.3862944 * jax.random.uniform(key_of[6], (SLOT_COUNT, ROWS_PER_UNIT, MODEL_WIDTH), jnp.float32) ** steps_of(key_of[6], (SLOT_COUNT, ROWS_PER_UNIT, MODEL_WIDTH), ((0, 16), (1, 2)), -0.2, 0.2)), 6.030396804135307e-08, 2.412158721654123e-07),
        "slot_unit_index": draw_slot_unit_index(jax.random.fold_in(key_of[12], 71), 0),
        "small_params": draw_small_params(jax.random.fold_in(key_of[12], 71), 0),
        "small_first": scatter_about(key_of[9], (SMALL, MODEL_WIDTH), (2.0 / PARAMETER_COUNT ** 0.5), 0.0019645493, (), jnp.float32),
        "small_second": jnp.clip(jnp.exp(jax.random.uniform(key_of[10], (SMALL, MODEL_WIDTH), jnp.float32, math.log(6.030396804135307e-08), math.log(9.648634886616492e-07))), 6.030396804135307e-08, 9.648634886616492e-07),
        "step_count": jax.random.randint(key_of[11], (), 2, 21).astype(jnp.int32),
    }


EPS_NORM = 1e-06
SOFTMAX_SCALE = 0.07
LEARN_RATE = 0.03
BETA_ONE = 0.5
BETA_TWO = 0.5
DECAY_RATE = 0.05
ADAM_EPS = 1e-08
MASKED = -1000000000.0
EXACT_ARITHMETIC = lax.Precision.HIGHEST

@jax.custom_vjp
def low(v):
    return lax.optimization_barrier(v.astype(jnp.bfloat16)).astype(jnp.float32)

@jax.custom_vjp
def low_back(v):
    return v

def low_keep(v):
    return (low(v), None)

def low_pass(kept, grad):
    return (grad,)

def back_keep(v):
    return (v, None)

def back_low(kept, grad):
    return (low(grad),)
low.defvjp(low_keep, low_pass)
low_back.defvjp(back_keep, back_low)

def layer_norm(values, gain, shift):
    center = values - lax.optimization_barrier(jnp.mean(values, axis=-1, keepdims=True))
    spread = lax.optimization_barrier(jnp.mean(center * center, axis=-1, keepdims=True))
    return center * lax.rsqrt(spread + EPS_NORM) * gain + shift

def small_parts(small):
    base = 1 + TOKS
    tail = base + 8 + FF // MODEL_WIDTH
    return (small[0], small[1:base], small[base], small[base + 1], small[base + 2], small[base + 3], small[base + 4], small[base + 5], small[base + 6], small[base + 7], small[base + 8:tail].reshape(FF), small[tail], small[tail + 1], small[tail + 2])

def table_parts(flat):
    offset = PIX
    embed_w = flat[:offset]
    qkv_w = flat[offset:offset + 3 * MODEL_WIDTH].reshape(3, MODEL_WIDTH, MODEL_WIDTH)
    offset = offset + 3 * MODEL_WIDTH
    output_w = flat[offset:offset + MODEL_WIDTH]
    offset = offset + MODEL_WIDTH
    fc_in_w = flat[offset:offset + FF]
    offset = offset + FF
    fc_out_w = flat[offset:offset + FF]
    offset = offset + FF
    proj_w = flat[offset:offset + PROJ]
    return (embed_w, qkv_w[0], qkv_w[1:], output_w, fc_in_w, fc_out_w, proj_w)

def block_loss(table, small, pixel_block, keep_block, partner_block, paired_view_entries):
    flat = low(table).reshape(UNIT_COUNT * ROWS_PER_UNIT, MODEL_WIDTH)
    embed_w, query_w, keyval_w, output_w, fc_in_w, fc_out_w, proj_w = table_parts(flat)
    class_row, pos_rows, patch_bias, gain_one, shift_one, query_bias, value_bias, out_bias, gain_two, shift_two, fc_in_bias, fc_out_bias, gain_end, shift_end = small_parts(small)
    count = pixel_block.shape[0]
    embedded = low_back(jnp.einsum('bnp,pd->bnd', pixel_block, embed_w, precision=EXACT_ARITHMETIC))
    patch_state = embedded + patch_bias + pos_rows[1:]
    class_state = class_row + pos_rows[0]
    tokens = jnp.concatenate([jnp.broadcast_to(class_state, (count, 1, MODEL_WIDTH)), patch_state], axis=1)
    hidden = low(layer_norm(tokens, gain_one, shift_one))
    value_add = jnp.stack([jnp.zeros_like(value_bias), value_bias])
    keyval = jnp.einsum('btd,cde->btce', hidden, keyval_w, precision=EXACT_ARITHMETIC) + value_add
    keyval = low_back(low(keyval))
    query = jnp.einsum('bd,de->be', hidden[:, 0], query_w, precision=EXACT_ARITHMETIC) + query_bias
    query = low_back(low(query * HEAD_DIM ** (-0.5))).reshape(count, HEADS, HEAD_DIM)
    keys = keyval[:, :, 0].reshape(count, TOKS, HEADS, HEAD_DIM)
    values = keyval[:, :, 1].reshape(count, TOKS, HEADS, HEAD_DIM)
    scores = low_back(jnp.einsum('bhd,bthd->bht', query, keys, precision=EXACT_ARITHMETIC))
    valid = jnp.concatenate([jnp.ones((count, 1), jnp.int32), keep_block], axis=1) > 0
    scores = jnp.where(valid[:, None, :], scores, MASKED)
    weights = jax.nn.softmax(scores, axis=-1)
    attended = jnp.einsum('bht,bthd->bhd', low(weights), values, precision=EXACT_ARITHMETIC)
    attended = low_back(low(attended)).reshape(count, MODEL_WIDTH)
    resid = class_state + low_back(jnp.einsum('be,ed->bd', attended, output_w, precision=EXACT_ARITHMETIC)) + out_bias
    hidden_two = low(layer_norm(resid, gain_two, shift_two))
    preact = low_back(jnp.einsum('bd,fd->bf', hidden_two, fc_in_w, precision=EXACT_ARITHMETIC) + fc_in_bias)
    active = low(jax.nn.gelu(preact, approximate=False))
    state = resid + low_back(jnp.einsum('bf,fd->bd', active, fc_out_w, precision=EXACT_ARITHMETIC)) + fc_out_bias
    final = low(layer_norm(state, gain_end, shift_end))
    projected = low_back(jnp.einsum('bd,pd->bp', final, proj_w, precision=EXACT_ARITHMETIC))
    device_position = low(projected * lax.rsqrt(lax.optimization_barrier(jnp.sum(projected * projected, axis=-1, keepdims=True)) + EPS_NORM))
    cosine_score_matrix = low_back(jnp.einsum('xl,zl->xz', device_position, paired_view_entries, precision=EXACT_ARITHMETIC)) / SOFTMAX_SCALE
    total = jax.nn.logsumexp(cosine_score_matrix, axis=-1)
    target = jnp.take_along_axis(cosine_score_matrix, partner_block[:, None], axis=1)[:, 0]
    return jnp.sum(total - target) / paired_view_entries.shape[0]

def adamw(weight, grad, first, second, step):
    first_new = BETA_ONE * first + (1.0 - BETA_ONE) * grad
    second_new = BETA_TWO * second + (1.0 - BETA_TWO) * grad * grad
    first_hat = first_new / (1.0 - jnp.power(BETA_ONE, step))
    second_hat = second_new / (1.0 - jnp.power(BETA_TWO, step))
    weight_new = weight - LEARN_RATE * (first_hat / (jnp.sqrt(second_hat) + ADAM_EPS) + DECAY_RATE * weight)
    return (weight_new, first_new, second_new)

def reference(pixels, keep_mask, partner_index, partner_emb, masters, first_moment_slots, second_moment_slots, slot_unit_index, small_params, small_first, small_second, step_count):
    unit_slot_index = jnp.zeros((SLOT_COUNT,), jnp.int32).at[slot_unit_index].set(jnp.arange(SLOT_COUNT, dtype=jnp.int32))
    table = masters[unit_slot_index[:UNIT_COUNT]]
    paired_view_entries = partner_emb.astype(jnp.float32)
    blocks = IMAGES // 64
    pixel_blocks = pixels.reshape(blocks, 64, PATCHES, PIX)
    keep_blocks = keep_mask.reshape(blocks, 64, PATCHES)
    partner_blocks = partner_index.reshape(blocks, 64)

    def one_block(carry, inputs):
        pixel_block, keep_block, partner_block = inputs

        def loss_of(tab, sml):
            return block_loss(tab, sml, pixel_block.astype(jnp.float32), keep_block, partner_block, paired_view_entries)
        value, pullback = jax.vjp(loss_of, table, small_params)
        grad_table, grad_small = pullback(jnp.ones((), value.dtype))
        return ((carry[0] + grad_table, carry[1] + grad_small, carry[2] + value), None)
    start = (jnp.zeros_like(table), jnp.zeros_like(small_params), jnp.zeros((), table.dtype))
    (grad_table, grad_small, loss), _ = lax.scan(one_block, start, (pixel_blocks, keep_blocks, partner_blocks))
    slot_grads = jnp.take(grad_table, slot_unit_index, axis=0, mode='fill', fill_value=0.0)
    grad_norm = jnp.sqrt(jnp.sum(slot_grads * slot_grads) + jnp.sum(grad_small * grad_small))
    factor = 1.0 / jnp.maximum(grad_norm, 1.0)
    step_value = step_count.astype(masters.dtype)
    new_masters, new_first, new_second = adamw(masters, slot_grads * factor, first_moment_slots, second_moment_slots, step_value)
    new_small, new_small_first, new_small_second = adamw(small_params, grad_small * factor, small_first, small_second, step_value)
    return (new_masters, new_first, new_second, new_small, new_small_first, new_small_second, loss, grad_norm)
```

```python
import functools

import jax
import jax.numpy as jnp
from jax import lax
from jax.experimental import pallas as pl
from jax.experimental.pallas import tpu as pltpu
from jax.sharding import PartitionSpec as P

WIDTH = 1024
HEADS = 16
HEAD_DIM = 64
FF = 4096
PIX = 3072
PROJ = 768
TOKS = 50
PATCHES = TOKS - 1
ROWS_PER_UNIT = 32
UNIT_COUNT = 504
JITTER = 2

EPS_NORM = 1e-06
SOFTMAX_SCALE = 0.07
LEARN_RATE = 0.03
BETA_ONE = 0.5
BETA_TWO = 0.5
DECAY_RATE = 0.05
ADAM_EPS = 1e-08
MASKED = -1000000000.0
SCALE = HEAD_DIM ** (-0.5)

F32 = jnp.float32
BF = jnp.bfloat16
ROW_BASE = 1 + TOKS
ROW_TAIL = ROW_BASE + 8 + FF // WIDTH
SLOT = 64


def low(values):
    return values.astype(BF)


def dot(a, b, dims=((1,), (0,)), precision=None):
    return lax.dot_general(a, b, (dims, ((), ())), precision=precision, preferred_element_type=F32)


NN = ((1,), (0,))
NT = ((1,), (1,))
TN = ((0,), (0,))


def layer_norm(values, gain, shift):
    center = values - jnp.mean(values, axis=-1, keepdims=True)
    spread = jnp.mean(center * center, axis=-1, keepdims=True)
    return center * lax.rsqrt(spread + EPS_NORM) * gain + shift


def normalize(values):
    return values * lax.rsqrt(jnp.sum(values * values, axis=-1, keepdims=True) + EPS_NORM)


def exact_gelu(values):
    return jax.nn.gelu(values, approximate=False)


def small_parts(small):
    base, tail = ROW_BASE, ROW_TAIL
    return (
        small[0],
        small[1:base],
        small[base],
        small[base + 1],
        small[base + 2],
        small[base + 3],
        small[base + 4],
        small[base + 5],
        small[base + 6],
        small[base + 7],
        small[base + 8 : tail].reshape(FF),
        small[tail],
        small[tail + 1],
        small[tail + 2],
    )


def adamw(weight, grad, first, second, step):
    first_new = BETA_ONE * first + (1.0 - BETA_ONE) * grad
    second_new = BETA_TWO * second + (1.0 - BETA_TWO) * grad * grad
    first_hat = first_new / (1.0 - jnp.power(BETA_ONE, step))
    second_hat = second_new / (1.0 - jnp.power(BETA_TWO, step))
    weight_new = weight - LEARN_RATE * (
        first_hat / (jnp.sqrt(second_hat) + ADAM_EPS) + DECAY_RATE * weight
    )
    return (weight_new, first_new, second_new)


def with_halo(values, chips):
    before = lax.ppermute(values[-JITTER:], "img", [(i, i + 1) for i in range(chips - 1)])
    after = lax.ppermute(values[:JITTER], "img", [(i + 1, i) for i in range(chips - 1)])
    return jnp.concatenate([before, values, after], axis=0)


def slots_near(slot_unit_index, img, slots):
    padded = jnp.pad(slot_unit_index, (JITTER, JITTER), constant_values=-1)
    return lax.dynamic_slice(padded, (img * slots,), (slots + 2 * JITTER,))


def pick(ext, matches, slots):
    out = jnp.zeros((slots,) + ext.shape[1:], ext.dtype)
    for shift in range(2 * JITTER + 1):
        out = jnp.where(matches[shift][:, None, None], ext[shift : shift + slots], out)
    return out


def to_units(values, near, img, chips):
    slots = values.shape[0]
    ids = img * slots + jnp.arange(slots, dtype=jnp.int32)
    matches = [near[s : s + slots] == ids for s in range(2 * JITTER + 1)]
    return pick(with_halo(values, chips), matches, slots)


def to_slots(values, near, img, chips):
    slots = values.shape[0]
    here = near[JITTER : JITTER + slots]
    ids = img * slots + jnp.arange(slots, dtype=jnp.int32)
    matches = [
        (here == ids + (s - JITTER)) & (here < UNIT_COUNT) for s in range(2 * JITTER + 1)
    ]
    return pick(with_halo(values, chips), matches, slots)


def shuffle_matrix():
    source = lax.broadcasted_iota(jnp.int32, (256, 256), 0)
    target = lax.broadcasted_iota(jnp.int32, (256, 256), 1)
    moved = ((source // 16) % 2) * 128 + (source // 32) * 16 + source % 16
    return (moved == target).astype(F32).astype(BF)


def full_spec():
    return pl.BlockSpec(memory_space=pltpu.VMEM)


def smem_spec():
    return pl.BlockSpec(memory_space=pltpu.SMEM)


def prep_kernel(pix_ref, shuffle_ref, out_ref):
    shuffle = shuffle_ref[...]
    for block in range(PIX // 256):
        moved = dot(pix_ref[0, :, 256 * block : 256 * block + 256], shuffle).astype(BF)
        out_ref[0, 0, :, 128 * block : 128 * block + 128] = moved[:, :128]
        out_ref[1, 0, :, 128 * block : 128 * block + 128] = moved[:, 128:]


def prep(padded, shuffle):
    images = padded.shape[0]
    return pl.pallas_call(
        prep_kernel,
        grid=(images,),
        in_specs=[
            pl.BlockSpec((1, SLOT, PIX), lambda i: (i, 0, 0)),
            pl.BlockSpec((256, 256), lambda i: (0, 0)),
        ],
        out_specs=pl.BlockSpec((2, 1, SLOT, PIX // 2), lambda i: (0, i, 0, 0)),
        out_shape=jax.ShapeDtypeStruct((2, images, SLOT, PIX // 2), BF),
        compiler_params=pltpu.CompilerParams(vmem_limit_bytes=24 * 2**20),
        cost_estimate=pl.CostEstimate(flops=8 * 10**8, bytes_accessed=6 * 2**20, transcendentals=0),
        name="prep",
    )(padded, shuffle)


def head_mask(rows):
    lane = lax.broadcasted_iota(jnp.int32, (rows, WIDTH), 1) // HEAD_DIM
    row = lax.broadcasted_iota(jnp.int32, (rows, WIDTH), 0) % HEADS
    return lane == row


def forward_kernel(pieces, images, where_ref, pix_ref, *refs):
    count = len(pieces)
    own, peer = refs[:count], refs[count : 2 * count]
    add_ref, rows_ref, qk_ref, valid_ref, shuffle_ref = refs[2 * count : 2 * count + 5]
    hid_ref, xhat_ref, rstd_ref, p_ref, pooled_ref, mass_ref, wv_ref, o_ref = refs[
        2 * count + 5 : 2 * count + 13
    ]
    acc_ref, pool_ref = refs[2 * count + 13 :]
    col, core = where_ref[0], where_ref[1]
    acc_ref[...] = add_ref[...]
    for flip, group in ((0, own), (1, peer)):
        half = core ^ flip
        for (source, first, rows), ref in zip(pieces, group):
            block = col ^ source

            @pl.when(block < 3)
            def _():
                lanes = pl.ds(pl.multiple_of(block * 512 + first, 128), rows)
                acc_ref[...] += dot(pix_ref[half, :, lanes], ref[...])

            @pl.when(block == 3)
            def _():
                wv_ref[half, first : first + rows] = ref[...]

    gain, shift, value_bias = rows_ref[0:1], rows_ref[1:2], rows_ref[2:3]
    valid = valid_ref[...] > 0
    qk = qk_ref[...]
    for i in range(images):
        part = slice(SLOT * i, SLOT * (i + 1))
        x = acc_ref[part]
        center = x - jnp.mean(x, axis=-1, keepdims=True)
        rstd = lax.rsqrt(jnp.mean(center * center, axis=-1, keepdims=True) + EPS_NORM)
        xhat = center * rstd
        hid = low(xhat * gain + shift)
        xhat_ref[part] = xhat
        rstd_ref[part] = jnp.broadcast_to(rstd, (SLOT, 128))
        hid_ref[part] = hid
        scores = jnp.where(valid[part], dot(hid, qk, NT), MASKED)
        e = jnp.exp(scores - jnp.max(scores, axis=0, keepdims=True))
        p = e / jnp.sum(e, axis=0, keepdims=True)
        p_ref[part] = p
        pb = low(p)
        pool_ref[HEADS * i : HEADS * (i + 1)] = low(dot(pb, hid, TN))
        mass_ref[HEADS * i : HEADS * (i + 1)] = dot(pb, jnp.ones((SLOT, 128), BF), TN)
    shuffle = shuffle_ref[...]
    for block in range(WIDTH // 256):
        moved = low(dot(pool_ref[:, 256 * block : 256 * block + 256], shuffle))
        pooled_ref[0, :, 128 * block : 128 * block + 128] = moved[:, :128]
        pooled_ref[1, :, 128 * block : 128 * block + 128] = moved[:, 128:]
    rows = images * HEADS
    mixed = dot(pooled_ref[0], wv_ref[0]) + dot(pooled_ref[1], wv_ref[1])
    mixed = mixed + mass_ref[:, 0:1] * value_bias
    mixed = jnp.where(head_mask(rows), mixed, 0.0)
    joined = low(jnp.sum(mixed.reshape(images, HEADS, WIDTH), axis=1))
    for block in range(WIDTH // 256):
        moved = low(dot(joined[:, 256 * block : 256 * block + 256], shuffle))
        o_ref[0, :, 128 * block : 128 * block + 128] = moved[:, :128]
        o_ref[1, :, 128 * block : 128 * block + 128] = moved[:, 128:]


def forward_call(pieces, images, where, pix, own, peer, add, rows, qk, valid, shuffle):
    tokens = images * SLOT
    n_in = 1 + 2 * len(pieces) + 5
    return pl.pallas_call(
        functools.partial(forward_kernel, pieces, images),
        in_specs=[smem_spec()] + [full_spec()] * n_in,
        out_specs=[full_spec()] * 8,
        out_shape=[
            jax.ShapeDtypeStruct((tokens, WIDTH), BF),
            jax.ShapeDtypeStruct((tokens, WIDTH), F32),
            jax.ShapeDtypeStruct((tokens, 128), F32),
            jax.ShapeDtypeStruct((tokens, HEADS), F32),
            jax.ShapeDtypeStruct((2, images * HEADS, WIDTH // 2), BF),
            jax.ShapeDtypeStruct((images * HEADS, 128), F32),
            jax.ShapeDtypeStruct((2, WIDTH // 2, WIDTH), BF),
            jax.ShapeDtypeStruct((2, images, WIDTH // 2), BF),
        ],
        scratch_shapes=[
            pltpu.VMEM((tokens, WIDTH), F32),
            pltpu.VMEM((images * HEADS, WIDTH), BF),
        ],
        compiler_params=pltpu.CompilerParams(vmem_limit_bytes=48 * 2**20),
        cost_estimate=pl.CostEstimate(flops=4 * 10**9, bytes_accessed=18 * 2**20, transcendentals=0),
        name="forward",
    )(where, pix, *own, *peer, add, rows, qk, valid, shuffle)


def backward_kernel(
    images, do_ref, wv_ref, hid_ref, xhat_ref, rstd_ref, p_ref, mass_ref, qk_ref, rows_ref,
    shuffle_ref, de_ref, pos_ref, vec_ref, pull_ref, dom_ref, da_ref,
):
    rows = images * HEADS
    gain, value_bias = rows_ref[0:1], rows_ref[2:3]
    spread = jnp.broadcast_to(do_ref[...].reshape(images, 1, WIDTH).astype(F32), (images, HEADS, WIDTH))
    wide = jnp.where(head_mask(rows), spread.reshape(rows, WIDTH), 0.0)
    dom_ref[...] = low(wide)
    vec_ref[...] = jnp.zeros_like(vec_ref)
    vec_ref[2:3] = jnp.sum(wide * mass_ref[:, 0:1], axis=0, keepdims=True)
    first = low(dot(dom_ref[...], wv_ref[0], NT))
    second = low(dot(dom_ref[...], wv_ref[1], NT))
    shuffle = shuffle_ref[...]
    for block in range(WIDTH // 256):
        both = jnp.concatenate(
            [first[:, 128 * block : 128 * block + 128], second[:, 128 * block : 128 * block + 128]],
            axis=1,
        )
        da_ref[:, 256 * block : 256 * block + 256] = low(dot(both, shuffle, NT))
    qk = qk_ref[...]
    bias_rows = low(jnp.broadcast_to(value_bias, (8, WIDTH)))
    real = lax.broadcasted_iota(jnp.int32, (SLOT, WIDTH), 0) < PATCHES
    for i in range(images):
        part = slice(SLOT * i, SLOT * (i + 1))
        mine = slice(HEADS * i, HEADS * (i + 1))
        hid, p, da = hid_ref[part], p_ref[part], da_ref[mine]
        dp = dot(hid, da, NT) + dot(bias_rows, dom_ref[mine], NT)[0:1]
        ds = low(p * (dp - jnp.sum(p * dp, axis=0, keepdims=True)))
        dh = dot(low(p), da) + dot(ds, qk)
        pull = dot(ds, hid, TN)
        xhat, rstd = xhat_ref[part], rstd_ref[part, 0:1]
        gy = dh * gain
        dx = rstd * (
            gy
            - jnp.mean(gy, axis=-1, keepdims=True)
            - xhat * jnp.mean(gy * xhat, axis=-1, keepdims=True)
        )
        de_ref[part] = low(jnp.where(real, dx, 0.0))
        vec_ref[0:1] += jnp.sum(dh * xhat, axis=0, keepdims=True)
        vec_ref[1:2] += jnp.sum(dh, axis=0, keepdims=True)
        if i == 0:
            pos_ref[...] = dx
            pull_ref[...] = pull
        else:
            pos_ref[...] += dx
            pull_ref[...] += pull


def backward_call(images, do, wv, hid, xhat, rstd, p, mass, qk, rows, shuffle):
    tokens = images * SLOT
    return pl.pallas_call(
        functools.partial(backward_kernel, images),
        in_specs=[full_spec()] * 10,
        out_specs=[full_spec()] * 4,
        out_shape=[
            jax.ShapeDtypeStruct((tokens, WIDTH), BF),
            jax.ShapeDtypeStruct((SLOT, WIDTH), F32),
            jax.ShapeDtypeStruct((8, WIDTH), F32),
            jax.ShapeDtypeStruct((HEADS, WIDTH), F32),
        ],
        scratch_shapes=[
            pltpu.VMEM((images * HEADS, WIDTH), BF),
            pltpu.VMEM((images * HEADS, WIDTH), BF),
        ],
        compiler_params=pltpu.CompilerParams(vmem_limit_bytes=40 * 2**20),
        cost_estimate=pl.CostEstimate(flops=10**9, bytes_accessed=8 * 2**20, transcendentals=0),
        name="backward",
    )(do, wv, hid, xhat, rstd, p, mass, qk, rows, shuffle)


def embed_grad_kernel(
    images, where_ref, pix_ref, pixp_ref, de_ref, dep_ref, pooled_ref, pooledp_ref, do_ref,
    dop_ref, own_ref, x_ref, y_ref, d_ref,
):
    col = where_ref[0]
    rows = images * HEADS
    for source, out_ref in ((3, d_ref), (1, x_ref), (2, y_ref), (0, own_ref)):
        block = col ^ source

        @pl.when(block < 3)
        def _():
            lanes = pl.ds(pl.multiple_of(block * 512, 128), 512)
            total = dot(pix_ref[:, lanes], de_ref[...], TN) + dot(pixp_ref[:, lanes], dep_ref[...], TN)
            out_ref[...] = total.astype(out_ref.dtype)

        @pl.when(block == 3)
        def _():
            total = None
            for pooled, do in ((pooled_ref, do_ref), (pooledp_ref, dop_ref)):
                spread = jnp.broadcast_to(
                    do[...].reshape(images, 1, WIDTH).astype(F32), (images, HEADS, WIDTH)
                )
                wide = low(jnp.where(head_mask(rows), spread.reshape(rows, WIDTH), 0.0))
                term = dot(pooled[...], wide, TN)
                total = term if total is None else total + term
            out_ref[...] = total.astype(out_ref.dtype)


def embed_grad_call(images, where, pix, pixp, de, dep, pooled, pooledp, do, dop):
    return pl.pallas_call(
        functools.partial(embed_grad_kernel, images),
        in_specs=[smem_spec()] + [full_spec()] * 8,
        out_specs=[full_spec()] * 4,
        out_shape=[
            jax.ShapeDtypeStruct((512, WIDTH), F32),
            jax.ShapeDtypeStruct((512, WIDTH), BF),
            jax.ShapeDtypeStruct((512, WIDTH), BF),
            jax.ShapeDtypeStruct((512, WIDTH), BF),
        ],
        compiler_params=pltpu.CompilerParams(vmem_limit_bytes=40 * 2**20),
        cost_estimate=pl.CostEstimate(flops=4 * 10**9, bytes_accessed=12 * 2**20, transcendentals=0),
        name="embed_grad",
    )(where, pix, pixp, de, dep, pooled, pooledp, do, dop)


CHIPS = 16
FLIP_X = [(i, i ^ 1) for i in range(CHIPS)]
FLIP_Y = [(i, i ^ 2) for i in range(CHIPS)]
FLIP_CORE = [(0, 1), (1, 0)]
CHUNKS = 2


def hop(values, pairs):
    return lax.ppermute(values, "img", pairs)


def swap(values):
    return lax.ppermute(values, "seq", FLIP_CORE)


def among(img, chips):
    hit = img == chips[0]
    for chip in chips[1:]:
        hit = hit | (img == chip)
    return hit


def spread_blocks(base, img, sources, rounds):
    got = []
    for pairs, sent in rounds:
        got.append(hop(base if sent < 0 else got[sent], pairs))
    total = jnp.where(among(img, sources), base, jnp.zeros_like(base))
    for part in got:
        total = total + part
    return total


def plane_gather(block):
    half = block.shape[0] // 2
    by_x, by_y = hop(block, FLIP_X), hop(block, FLIP_Y)
    first, second = hop(by_y[:half], FLIP_X), hop(by_x[half:], FLIP_Y)
    return [block, by_x, by_y, first, second]


def everywhere(values):
    sent = jnp.broadcast_to(values[None], (CHIPS,) + values.shape)
    got = lax.all_to_all(sent, "img", 0, 0, tiled=True)
    got = got.reshape((CHIPS * values.shape[0],) + values.shape[1:])
    return jnp.concatenate([got, swap(got)], axis=0)


def back_home(partial, images, sources):
    half = partial.shape[0] // 2
    mine = partial[:half] + swap(partial[half:])
    sent = low(mine).reshape(CHIPS, images, partial.shape[-1])
    got = lax.all_to_all(sent, "img", 0, 0, tiled=True)
    return jnp.sum(got[sources[0] : sources[-1] + 1].astype(F32), axis=0)


def from_all(values):
    sent = jnp.broadcast_to(values[None], (2 * CHIPS,) + values.shape)
    return lax.all_to_all(sent, ("img", "seq"), 0, 0, tiled=True)


def natural(values):
    lead = values.shape[:-2]
    units = values.shape[-1] // 16
    split = values.reshape(lead + (2, units, 16))
    return jnp.swapaxes(split, -3, -2).reshape(lead + (units * 32,))


def halves(values):
    lead = values.shape[:-1]
    units = values.shape[-1] // 32
    return jnp.swapaxes(values.reshape(lead + (units, 2, 16)), -3, -2).reshape(
        lead + (2, units * 16)
    )


FF_CHIPS = (7, 8, 9, 10)
T1_SOURCES = (0, 1, 2, 7)
T1_ROUNDS = [
    ([(0, 4), (1, 5), (2, 6), (7, 11)], -1),
    ([(4, 8), (5, 9), (6, 10), (11, 15)], 0),
    ([(8, 12), (9, 13), (10, 14)], 1),
    ([(7, 3)], -1),
]
T2_SOURCES = (4, 1, 6, 15)
T2_ROUNDS = [
    ([(4, 8), (1, 5), (6, 10), (15, 11)], -1),
    ([(8, 12), (5, 9), (10, 14), (11, 7)], 0),
    ([(9, 13), (7, 3)], 1),
    ([(4, 0), (6, 2)], -1),
]


def per_device_16(
    pixels, keep_mask, partner_index, partner_emb, masters, first_moment_slots,
    second_moment_slots, slot_unit_index, small_params, small_first, small_second, step_count,
):
    img, core = lax.axis_index("img"), lax.axis_index("seq")
    col = img % 4
    images = pixels.shape[0]
    total_images = images * 2 * CHIPS
    slots = masters.shape[0]
    where = jnp.stack([col, core]).astype(jnp.int32)
    shuffle = shuffle_matrix()
    (
        class_row, pos_rows, patch_bias, gain_one, shift_one, query_bias, value_bias, out_bias,
        gain_two, shift_two, fc_in_bias, fc_out_bias, gain_end, shift_end,
    ) = small_parts(small_params)
    class_state = class_row + pos_rows[0]

    near = slots_near(slot_unit_index, img, slots)
    own_w = to_units(low(masters), near, img, CHIPS).reshape(512, WIDTH)

    step = 512 // CHUNKS
    pieces, own_pieces = [], []
    for chunk in range(CHUNKS):
        part = own_w[step * chunk : step * (chunk + 1)]
        base = jnp.where(img == 7, hop(part, [(5, 7)]), part)
        block = spread_blocks(base, img, T1_SOURCES, T1_ROUNDS)
        got = plane_gather(block)
        first = step * chunk
        pieces += [
            (0, first, step), (1, first, step), (2, first, step),
            (3, first, step // 2), (3, first + step // 2, step // 2),
        ]
        own_pieces += got
    peer_pieces = [swap(piece) for piece in own_pieces]

    base = jnp.where(img == 1, hop(own_w, [(3, 1)]), own_w)
    got = plane_gather(spread_blocks(base, img, T2_SOURCES, T2_ROUNDS))
    table = jnp.zeros((4, 512, WIDTH), BF)
    table = lax.dynamic_update_slice(table, got[0][None], (col, 0, 0))
    table = lax.dynamic_update_slice(table, got[1][None], (col ^ 1, 0, 0))
    table = lax.dynamic_update_slice(table, got[2][None], (col ^ 2, 0, 0))
    table = lax.dynamic_update_slice(table, got[3][None], (col ^ 3, 0, 0))
    table = lax.dynamic_update_slice(table, got[4][None], (col ^ 3, 256, 0))
    table_peer = swap(table)

    def both(block, rows=512):
        mine, theirs = table[block, :rows], table_peer[block, :rows]
        return jnp.where(core == 0, mine, theirs), jnp.where(core == 0, theirs, mine)

    w_two = hop(own_w, [(11, 7), (12, 8), (13, 9), (14, 10)])

    class_hidden = low(layer_norm(class_state, gain_one, shift_one))
    class_halves = halves(class_hidden)
    class_half = jnp.where(core == 0, class_halves[0], class_halves[1])
    query_parts = from_all(dot(class_half[None], own_w))
    query = low((query_parts[6, 0] + query_parts[7, 0] + query_bias) * SCALE)
    mask16 = head_mask(HEADS)
    query_heads = jnp.where(mask16, query[None], jnp.zeros((), BF))
    pulled = from_all(low(dot(query_heads, own_w, NT)))
    qk = natural(jnp.stack([pulled[8], pulled[9]], axis=1))

    padded = jnp.pad(pixels, ((0, 0), (0, SLOT - PATCHES), (0, 0)))
    pix = prep(padded, shuffle).reshape(2, images * SLOT, PIX // 2)
    pix_own = jnp.where(core == 0, pix[0], pix[1])
    pix_peer = swap(jnp.where(core == 0, pix[1], pix[0]))

    add_image = jnp.concatenate(
        [
            pos_rows[1:] + patch_bias,
            class_state[None],
            jnp.zeros((SLOT - TOKS, WIDTH), F32),
        ],
        axis=0,
    )
    add = jnp.tile(add_image, (images, 1))
    valid = jnp.concatenate(
        [
            keep_mask,
            jnp.ones((images, 1), jnp.int32),
            jnp.zeros((images, SLOT - TOKS), jnp.int32),
        ],
        axis=1,
    ).reshape(images * SLOT, 1)
    rows = jnp.stack([gain_one, shift_one, value_bias] + [jnp.zeros_like(gain_one)] * 5)
    hid, xhat, rstd, p, pooled, mass, wv, attended = forward_call(
        pieces, images, where, pix, own_pieces, peer_pieces, add, rows, qk, valid, shuffle
    )

    wo = both(2)
    resid = class_state + dot(attended[0], wo[0]) + dot(attended[1], wo[1]) + out_bias
    hidden_two = low(layer_norm(resid, gain_two, shift_two))
    hidden_all = everywhere(hidden_two)
    ff_block = jnp.clip(img - FF_CHIPS[0], 0, 3)
    is_ff = among(img, FF_CHIPS)
    bias_part = lax.dynamic_slice(
        fc_in_bias.reshape(4, 32, 2, 16), (ff_block, 0, core, 0), (1, 32, 1, 16)
    ).reshape(512)
    preact = dot(hidden_all, own_w, NT) + bias_part
    active = low(exact_gelu(preact))
    state = resid + back_home(dot(active, w_two), images, FF_CHIPS) + fc_out_bias
    final = low(layer_norm(state, gain_end, shift_end))
    proj = both(3, PROJ // 2)
    projected = jnp.concatenate([dot(final, proj[0], NT), dot(final, proj[1], NT)], axis=1)

    partners = everywhere(halves(partner_emb).reshape(images, PROJ))
    unit = low(normalize(projected))
    logits = dot(unit, partners, NT) / SOFTMAX_SCALE
    ids = jnp.arange(CHIPS, dtype=jnp.int32)[None, :, None] * (2 * images)
    ids = ids + (core ^ jnp.arange(2, dtype=jnp.int32))[:, None, None] * images
    ids = (ids + jnp.arange(images, dtype=jnp.int32)[None, None, :]).reshape(1, total_images)
    onehot = (ids == partner_index[:, None]).astype(F32)
    total = jax.nn.logsumexp(logits, axis=-1)
    target = jnp.sum(logits * onehot, axis=-1)
    loss_part = jnp.sum(total - target) / total_images
    d_logits = (jax.nn.softmax(logits, axis=-1) - onehot) / total_images
    d_unit = dot(low(d_logits / SOFTMAX_SCALE), partners)
    d_projected = low(jax.vjp(normalize, projected)[1](d_unit)[0])
    d_final = dot(d_projected[:, : PROJ // 2], proj[0]) + dot(d_projected[:, PROJ // 2 :], proj[1])
    d_state, d_gain_end, d_shift_end = jax.vjp(layer_norm, state, gain_end, shift_end)[1](d_final)
    d_state_low = low(d_state)
    d_state_all = everywhere(d_state_low)
    d_active = dot(d_state_all, w_two, NT)
    d_preact = low(jax.vjp(exact_gelu, preact)[1](d_active)[0])
    d_preact = jnp.where(is_ff, d_preact, jnp.zeros((), BF))
    d_hidden_two = back_home(dot(d_preact, own_w), images, FF_CHIPS)
    d_norm, d_gain_two, d_shift_two = jax.vjp(layer_norm, resid, gain_two, shift_two)[1](
        d_hidden_two
    )
    d_resid = d_state + d_norm
    d_resid_low = low(d_resid)
    d_attended = low(
        natural(jnp.stack([dot(d_resid_low, wo[0], NT), dot(d_resid_low, wo[1], NT)], axis=1))
    )

    d_embed, d_pos, d_vec, pull = backward_call(
        images, d_attended, wv, hid, xhat, rstd, p, mass, qk, rows, shuffle
    )
    pooled_own = jnp.where(core == 0, pooled[0], pooled[1])
    pooled_peer = swap(jnp.where(core == 0, pooled[1], pooled[0]))
    grad_own, grad_x, grad_y, grad_d = embed_grad_call(
        images, where, pix_own, pix_peer, d_embed, swap(d_embed), pooled_own, pooled_peer,
        d_attended, swap(d_attended),
    )
    reduced = []
    for chunk in range(CHUNKS):
        first, middle, last = step * chunk, step * chunk + step // 2, step * (chunk + 1)
        to_y = hop(grad_d[first:middle], FLIP_X)
        to_x = hop(grad_d[middle:last], FLIP_Y)
        send_y = jnp.concatenate(
            [low(grad_y[first:middle].astype(F32) + to_y.astype(F32)), grad_y[middle:last]], axis=0
        )
        send_x = jnp.concatenate(
            [grad_x[first:middle], low(grad_x[middle:last].astype(F32) + to_x.astype(F32))], axis=0
        )
        got_x, got_y = hop(send_x, FLIP_X), hop(send_y, FLIP_Y)
        acc = grad_own[first:last] + got_x.astype(F32) + got_y.astype(F32)
        got = hop(low(acc), [(12, 8), (13, 9), (14, 10), (15, 11), (3, 7)])
        acc = acc + got.astype(F32)
        got = hop(low(acc), [(8, 4), (9, 5), (10, 6), (11, 7)])
        acc = acc + got.astype(F32)
        got = hop(low(acc), [(4, 0), (5, 1), (6, 2), (7, 5)]).astype(F32)
        reduced.append(jnp.where(img == 5, got, acc + got))
    reduced = jnp.concatenate(reduced, axis=0)

    wk, wq = both(0), both(1)
    pull_halves = low(halves(pull))
    d_query = jnp.where(mask16, dot(pull_halves[:, 0], wk[0]) + dot(pull_halves[:, 1], wk[1]), 0.0)
    d_query = jnp.sum(d_query, axis=0, keepdims=True) * SCALE
    d_query_low = low(d_query)
    d_class_hidden = natural(
        jnp.stack([dot(d_query_low, wq[0], NT), dot(d_query_low, wq[1], NT)], axis=1)
    )
    d_class, d_gain_cls, d_shift_cls = jax.vjp(layer_norm, class_state[None], gain_one, shift_one)[
        1
    ](d_class_hidden)
    d_resid_sum = jnp.sum(d_resid, axis=0)
    d_class = d_class[0] + d_pos[PATCHES] + d_resid_sum
    bias_sum = jnp.sum(d_preact.astype(F32), axis=0).reshape(1, 32, 1, 16)
    d_fc_in_bias = lax.dynamic_update_slice(
        jnp.zeros((4, 32, 2, 16), F32), bias_sum, (ff_block, 0, core, 0)
    ).reshape(FF // WIDTH, WIDTH)
    small_local = jnp.concatenate(
        [
            d_class[None],
            d_class[None],
            d_pos[:PATCHES],
            jnp.sum(d_pos[:PATCHES], axis=0, keepdims=True),
            (d_vec[0] + d_gain_cls)[None],
            (d_vec[1] + d_shift_cls)[None],
            d_query,
            d_vec[2:3],
            d_resid_sum[None],
            d_gain_two[None],
            d_shift_two[None],
            d_fc_in_bias,
            jnp.sum(d_state, axis=0, keepdims=True),
            d_gain_end[None],
            d_shift_end[None],
            pull,
            jnp.broadcast_to(loss_part, (1, WIDTH)),
            jnp.zeros((13, WIDTH), F32),
        ],
        axis=0,
    )
    shares = lax.all_to_all(small_local.reshape(32, 3, WIDTH), ("img", "seq"), 0, 0, tiled=True)
    small_total = from_all(jnp.sum(shares, axis=0)).reshape(96, WIDTH)
    small_grad, pull_total, loss = small_total[:66], small_total[66:82], small_total[82, 0]

    extra = jnp.concatenate(
        [attended[0], attended[1], d_resid_low, d_projected, final], axis=1
    )
    extra, d_embed = lax.optimization_barrier((extra, d_embed))
    extra = everywhere(extra)
    att_half = jnp.where(core == 0, extra[:, :512], extra[:, 512:1024])
    proj_half = jnp.where(core == 0, extra[:, 2048 : 2048 + 384], extra[:, 2048 + 384 : 2816])
    proj_half = jnp.pad(proj_half, ((0, 0), (0, 128)))
    left = jnp.where(img == 6, att_half, jnp.where(img == 15, proj_half, d_preact))
    right = jnp.where(
        img == 6, extra[:, 1024:2048], jnp.where(img == 15, extra[:, 2816:], hidden_all)
    )
    formed = dot(left, right, TN)
    from_ff = hop(
        low(dot(active, d_state_all, TN)), [(7, 11), (8, 12), (9, 13), (10, 14)]
    ).astype(F32)
    pull_half = halves(pull_total)
    pull_half = jnp.where(core == 0, pull_half[:, 0], pull_half[:, 1])
    key_grad = dot(pull_half, query_heads.astype(F32), TN, precision=lax.Precision.HIGHEST)
    query_grad = class_half.astype(F32)[:, None] * small_total[54][None, :]
    own_grad = jnp.where(among(img, (0, 1, 2, 5)), reduced, formed)
    own_grad = jnp.where(among(img, (11, 12, 13, 14)), from_ff, own_grad)
    own_grad = jnp.where(img == 3, query_grad, jnp.where(img == 4, key_grad, own_grad))

    squares = jnp.broadcast_to(jnp.sum(own_grad * own_grad), (1, 128))
    owner_total = jnp.sum(from_all(squares)[:, 0, 0])
    grad_norm = jnp.sqrt(owner_total + jnp.sum(small_grad * small_grad))
    factor = 1.0 / jnp.maximum(grad_norm, 1.0)
    slot_grad = to_slots(own_grad.reshape(slots, 16, WIDTH), near, img, CHIPS)
    step_value = step_count.astype(F32)
    new_masters, new_first, new_second = adamw(
        masters, slot_grad * factor, first_moment_slots, second_moment_slots, step_value
    )
    new_small, new_small_first, new_small_second = adamw(
        small_params, small_grad * factor, small_first, small_second, step_value
    )
    return (
        new_masters, new_first, new_second, new_small, new_small_first, new_small_second,
        loss, grad_norm,
    )


def per_device_any(
    pixels, keep_mask, partner_index, partner_emb, masters, first_moment_slots,
    second_moment_slots, slot_unit_index, small_params, small_first, small_second, step_count,
):
    chips, seq = lax.axis_size("img"), lax.axis_size("seq")
    img = lax.axis_index("img")
    images = pixels.shape[0]
    slots, part = masters.shape[0], masters.shape[1]
    near = slots_near(slot_unit_index, img, slots)
    own_w = to_units(low(masters), near, img, chips)
    gathered = lax.all_gather(own_w, ("img", "seq"), axis=0, tiled=False)
    flat = gathered.reshape(chips, seq, slots, part, WIDTH).transpose(0, 2, 1, 3, 4)
    flat = flat.reshape(chips * slots * ROWS_PER_UNIT, WIDTH)
    bounds = [0, PIX, WIDTH, WIDTH, WIDTH, WIDTH, FF, FF, PROJ]
    parts, offset = [], 0
    for size in bounds[1:]:
        parts.append(flat[offset : offset + size])
        offset += size
    embed_w, query_w, key_w, value_w, output_w, fc_in_w, fc_out_w, proj_w = parts
    (
        class_row, pos_rows, patch_bias, gain_one, shift_one, query_bias, value_bias, out_bias,
        gain_two, shift_two, fc_in_bias, fc_out_bias, gain_end, shift_end,
    ) = small_parts(small_params)
    class_state = class_row + pos_rows[0]
    embedded = jnp.einsum("itp,pd->itd", pixels, embed_w, preferred_element_type=F32)
    tokens = jnp.concatenate(
        [
            jnp.broadcast_to(class_state, (images, 1, WIDTH)),
            embedded + patch_bias + pos_rows[1:],
        ],
        axis=1,
    )
    hidden = low(layer_norm(tokens, gain_one, shift_one))
    class_hidden = hidden[0, 0]
    mask16 = head_mask(HEADS)
    query = low((dot(class_hidden[None], query_w)[0] + query_bias) * SCALE)
    query_heads = jnp.where(mask16, query[None], jnp.zeros((), BF))
    qk = low(dot(query_heads, key_w, NT))
    scores = jnp.einsum("hd,itd->iht", qk, hidden, preferred_element_type=F32)
    keep = jnp.concatenate([jnp.ones((images, 1), jnp.int32), keep_mask], axis=1)
    scores = jnp.where(keep[:, None, :] > 0, scores, MASKED)
    weights = jax.nn.softmax(scores, axis=-1)
    weights_low = low(weights)
    pooled = low(jnp.einsum("iht,itd->ihd", weights_low, hidden, preferred_element_type=F32))
    mass = jnp.sum(weights_low.astype(F32), axis=-1)
    mixed = dot(pooled.reshape(-1, WIDTH), value_w).reshape(images, HEADS, WIDTH)
    mixed = mixed + mass[:, :, None] * value_bias
    attended = low(jnp.sum(jnp.where(mask16, mixed, 0.0), axis=1))
    resid = class_state + dot(attended, output_w) + out_bias
    hidden_two = low(layer_norm(resid, gain_two, shift_two))
    preact = dot(hidden_two, fc_in_w, NT) + fc_in_bias
    active = low(exact_gelu(preact))
    state = resid + dot(active, fc_out_w) + fc_out_bias
    final = low(layer_norm(state, gain_end, shift_end))
    projected = dot(final, proj_w, NT)
    unit = low(normalize(projected))
    partners = lax.all_gather(partner_emb, ("img", "seq"), axis=0, tiled=True)
    count = partners.shape[0]
    logits = dot(unit, partners, NT) / SOFTMAX_SCALE
    onehot = (jnp.arange(count, dtype=jnp.int32)[None] == partner_index[:, None]).astype(F32)
    total = jax.nn.logsumexp(logits, axis=-1)
    loss_part = jnp.sum(total - jnp.sum(logits * onehot, axis=-1)) / count
    d_logits = (jax.nn.softmax(logits, axis=-1) - onehot) / count
    d_unit = dot(low(d_logits / SOFTMAX_SCALE), partners)
    d_projected = low(jax.vjp(normalize, projected)[1](d_unit)[0])
    d_final = dot(d_projected, proj_w)
    d_state, d_gain_end, d_shift_end = jax.vjp(layer_norm, state, gain_end, shift_end)[1](d_final)
    d_state_low = low(d_state)
    d_active = dot(d_state_low, fc_out_w, NT)
    d_preact = low(jax.vjp(exact_gelu, preact)[1](d_active)[0])
    d_hidden_two = dot(d_preact, fc_in_w)
    d_norm, d_gain_two, d_shift_two = jax.vjp(layer_norm, resid, gain_two, shift_two)[1](
        d_hidden_two
    )
    d_resid = d_state + d_norm
    d_resid_low = low(d_resid)
    d_attended = low(dot(d_resid_low, output_w, NT))
    wide = jnp.where(mask16, d_attended[:, None, :], jnp.zeros((), BF))
    d_pooled = low(dot(wide.reshape(-1, WIDTH), value_w, NT)).reshape(images, HEADS, WIDTH)
    d_weights = jnp.einsum("ihd,itd->iht", d_pooled, hidden, preferred_element_type=F32)
    d_weights = d_weights + jnp.sum(wide.astype(F32) * value_bias, axis=-1)[:, :, None]
    d_scores = low(weights * (d_weights - jnp.sum(weights * d_weights, axis=-1, keepdims=True)))
    d_hidden = jnp.einsum("iht,ihd->itd", weights_low, d_pooled, preferred_element_type=F32)
    d_hidden = d_hidden + jnp.einsum("iht,hd->itd", d_scores, qk, preferred_element_type=F32)
    pull = jnp.einsum("iht,itd->hd", d_scores, hidden, preferred_element_type=F32)
    d_query = jnp.sum(jnp.where(mask16, dot(low(pull), key_w), 0.0), axis=0) * SCALE
    d_class_hidden = dot(low(d_query)[None], query_w, NT)
    d_tokens, d_gain_one, d_shift_one = jax.vjp(layer_norm, tokens, gain_one, shift_one)[1](
        d_hidden
    )
    d_class, d_gain_cls, d_shift_cls = jax.vjp(layer_norm, class_state[None], gain_one, shift_one)[
        1
    ](d_class_hidden)
    d_class = d_class[0] + jnp.sum(d_tokens[:, 0], axis=0) + jnp.sum(d_resid, axis=0)
    d_patch = d_tokens[:, 1:]
    d_embed_w = jnp.einsum("itp,itd->pd", pixels, low(d_patch), preferred_element_type=F32)
    d_value_w = dot(pooled.reshape(-1, WIDTH), wide.reshape(-1, WIDTH), TN)
    d_key_w = dot(pull, query_heads.astype(F32), TN, precision=lax.Precision.HIGHEST)
    small_local = jnp.concatenate(
        [
            d_class[None],
            d_class[None],
            jnp.sum(d_patch, axis=0),
            jnp.sum(d_patch, axis=(0, 1))[None],
            (d_gain_one + d_gain_cls)[None],
            (d_shift_one + d_shift_cls)[None],
            d_query[None],
            jnp.sum(wide.astype(F32) * mass[:, :, None], axis=(0, 1))[None],
            jnp.sum(d_resid, axis=0)[None],
            d_gain_two[None],
            d_shift_two[None],
            jnp.sum(d_preact.astype(F32), axis=0).reshape(FF // WIDTH, WIDTH),
            jnp.sum(d_state, axis=0)[None],
            d_gain_end[None],
            d_shift_end[None],
        ],
        axis=0,
    )
    grad_table = jnp.concatenate(
        [
            d_embed_w,
            class_hidden.astype(F32)[:, None] * d_query[None, :],
            d_key_w,
            d_value_w,
            dot(attended, d_resid_low, TN),
            dot(d_preact, hidden_two, TN),
            dot(active, d_state_low, TN),
            dot(d_projected, final, TN),
            jnp.zeros(((chips * slots - UNIT_COUNT) * ROWS_PER_UNIT, WIDTH), F32),
        ],
        axis=0,
    ).reshape(chips * slots, ROWS_PER_UNIT, WIDTH)
    small_grad, loss = lax.psum((small_local, loss_part), ("img", "seq"))
    core_half = lax.psum_scatter(low(grad_table), "seq", scatter_dimension=1, tiled=True)
    own_grad = lax.psum_scatter(core_half.astype(F32), "img", scatter_dimension=0, tiled=True)
    owner_total = lax.psum(jnp.sum(own_grad * own_grad), ("img", "seq"))
    grad_norm = jnp.sqrt(owner_total + jnp.sum(small_grad * small_grad))
    factor = 1.0 / jnp.maximum(grad_norm, 1.0)
    slot_grad = to_slots(own_grad, near, img, chips)
    step_value = step_count.astype(F32)
    new_masters, new_first, new_second = adamw(
        masters, slot_grad * factor, first_moment_slots, second_moment_slots, step_value
    )
    new_small, new_small_first, new_small_second = adamw(
        small_params, small_grad * factor, small_first, small_second, step_value
    )
    return (
        new_masters, new_first, new_second, new_small, new_small_first, new_small_second,
        loss, grad_norm,
    )


def solution(mesh):
    sixteen = mesh.shape["img"] == CHIPS and mesh.shape["seq"] == 2
    return jax.shard_map(
        per_device_16 if sixteen else per_device_any,
        mesh=mesh,
        in_specs=(
            P(("img", "seq"), None, None),
            P(("img", "seq"), None),
            P(("img", "seq")),
            P(("img", "seq"), None),
            P("img", "seq", None),
            P("img", "seq", None),
            P("img", "seq", None),
            P(),
            P(),
            P(),
            P(),
            P(),
        ),
        out_specs=(
            P("img", "seq", None),
            P("img", "seq", None),
            P("img", "seq", None),
            P(),
            P(),
            P(),
            P(),
            P(),
        ),
        check_vma=False,
    )
```

```python
import functools
import math

import jax
import jax.numpy as jnp
from jax import lax
from jax.experimental import pallas as pl
from jax.experimental.pallas import tpu as pltpu
from jax.sharding import PartitionSpec as P

WIDTH = 1024
HEADS = 16
HEAD_DIM = 64
FF = 4096
PIX = 3072
PROJ = 768
TOKS = 50
PATCHES = TOKS - 1
ROWS_PER_UNIT = 32
UNIT_COUNT = 504
JITTER = 2

EPS_NORM = 1e-06
SOFTMAX_SCALE = 0.07
LEARN_RATE = 0.03
BETA_ONE = 0.5
BETA_TWO = 0.5
DECAY_RATE = 0.05
ADAM_EPS = 1e-08
MASKED = -1000000000.0
SCALE = HEAD_DIM ** (-0.5)

F32 = jnp.float32
BF = jnp.bfloat16
ROW_BASE = 1 + TOKS
ROW_TAIL = ROW_BASE + 8 + FF // WIDTH
SLOT = 64


def low(values):
    return values.astype(BF)


def dot(a, b, dims=((1,), (0,)), precision=None):
    return lax.dot_general(a, b, (dims, ((), ())), precision=precision, preferred_element_type=F32)


NN = ((1,), (0,))
NT = ((1,), (1,))
TN = ((0,), (0,))


def layer_norm(values, gain, shift):
    center = values - jnp.mean(values, axis=-1, keepdims=True)
    spread = jnp.mean(center * center, axis=-1, keepdims=True)
    return center * lax.rsqrt(spread + EPS_NORM) * gain + shift


def normalize(values):
    return values * lax.rsqrt(jnp.sum(values * values, axis=-1, keepdims=True) + EPS_NORM)


def exact_gelu(values):
    return jax.nn.gelu(values, approximate=False)


def small_parts(small):
    base, tail = ROW_BASE, ROW_TAIL
    return (
        small[0],
        small[1:base],
        small[base],
        small[base + 1],
        small[base + 2],
        small[base + 3],
        small[base + 4],
        small[base + 5],
        small[base + 6],
        small[base + 7],
        small[base + 8 : tail].reshape(FF),
        small[tail],
        small[tail + 1],
        small[tail + 2],
    )


def adamw(weight, grad, first, second, step):
    first_new = BETA_ONE * first + (1.0 - BETA_ONE) * grad
    second_new = BETA_TWO * second + (1.0 - BETA_TWO) * grad * grad
    first_hat = first_new / (1.0 - jnp.power(BETA_ONE, step))
    second_hat = second_new / (1.0 - jnp.power(BETA_TWO, step))
    weight_new = weight - LEARN_RATE * (
        first_hat / (jnp.sqrt(second_hat) + ADAM_EPS) + DECAY_RATE * weight
    )
    return (weight_new, first_new, second_new)


def halo(values, chips, axes):
    before = lax.ppermute(values[-JITTER:], axes, [(i, i + 1) for i in range(chips - 1)])
    behind = lax.ppermute(values[:JITTER], axes, [(i + 1, i) for i in range(chips - 1)])
    return before, behind


def with_halo(values, chips, axes):
    before, behind = halo(values, chips, axes)
    return jnp.concatenate([before, values, behind], axis=0)


def slots_near(slot_unit_index, img, slots):
    padded = jnp.pad(slot_unit_index, (JITTER, JITTER), constant_values=-1)
    return lax.dynamic_slice(padded, (img * slots,), (slots + 2 * JITTER,))


def pick(ext, matches, slots):
    out = jnp.zeros((slots,) + ext.shape[1:], ext.dtype)
    for shift in range(2 * JITTER + 1):
        out = jnp.where(matches[shift][:, None, None], ext[shift : shift + slots], out)
    return out


def to_units(values, near, img, chips, axes="img"):
    slots = values.shape[0]
    ids = img * slots + jnp.arange(slots, dtype=jnp.int32)
    matches = [near[s : s + slots] == ids for s in range(2 * JITTER + 1)]
    return pick(with_halo(values, chips, axes), matches, slots)


def to_slots(values, near, img, chips, axes="img"):
    slots = values.shape[0]
    here = near[JITTER : JITTER + slots]
    ids = img * slots + jnp.arange(slots, dtype=jnp.int32)
    matches = [
        (here == ids + (s - JITTER)) & (here < UNIT_COUNT) for s in range(2 * JITTER + 1)
    ]
    return pick(with_halo(values, chips, axes), matches, slots)


def shuffle_matrix():
    source = lax.broadcasted_iota(jnp.int32, (256, 256), 0)
    target = lax.broadcasted_iota(jnp.int32, (256, 256), 1)
    moved = ((source // 16) % 2) * 128 + (source // 32) * 16 + source % 16
    return (moved == target).astype(F32).astype(BF)


def vmem():
    return pl.BlockSpec(memory_space=pltpu.VMEM)


def smem():
    return pl.BlockSpec(memory_space=pltpu.SMEM)


def shape(dims, dtype):
    return jax.ShapeDtypeStruct(dims, dtype)


def call(kernel, name, scalars, arrays, outs, scratch=(), mib=40, flops=10**9):
    moved = sum(a.size * a.dtype.itemsize for a in list(arrays) + list(outs))
    return pl.pallas_call(
        kernel,
        in_specs=[smem()] * len(scalars) + [vmem()] * len(arrays),
        out_specs=[vmem()] * len(outs),
        out_shape=list(outs),
        scratch_shapes=list(scratch),
        compiler_params=pltpu.CompilerParams(vmem_limit_bytes=mib * 2**20),
        cost_estimate=pl.CostEstimate(flops=flops, bytes_accessed=moved, transcendentals=0),
        name=name,
    )(*scalars, *arrays)


def prep_kernel(pix_ref, shuffle_ref, out_ref):
    shuffle = shuffle_ref[...]
    for block in range(PIX // 256):
        moved = dot(pix_ref[0, :, 256 * block : 256 * block + 256], shuffle).astype(BF)
        out_ref[0, 0, :, 128 * block : 128 * block + 128] = moved[:, :128]
        out_ref[1, 0, :, 128 * block : 128 * block + 128] = moved[:, 128:]


def prep(padded, shuffle):
    images = padded.shape[0]
    return pl.pallas_call(
        prep_kernel,
        grid=(images,),
        in_specs=[
            pl.BlockSpec((1, SLOT, PIX), lambda i: (i, 0, 0)),
            pl.BlockSpec((256, 256), lambda i: (0, 0)),
        ],
        out_specs=pl.BlockSpec((2, 1, SLOT, PIX // 2), lambda i: (0, i, 0, 0)),
        out_shape=jax.ShapeDtypeStruct((2, images, SLOT, PIX // 2), BF),
        compiler_params=pltpu.CompilerParams(vmem_limit_bytes=24 * 2**20),
        cost_estimate=pl.CostEstimate(flops=8 * 10**8, bytes_accessed=6 * 2**20, transcendentals=0),
        name="prep",
    )(padded, shuffle)


def head_mask(rows):
    lane = lax.broadcasted_iota(jnp.int32, (rows, WIDTH), 1) // HEAD_DIM
    row = lax.broadcasted_iota(jnp.int32, (rows, WIDTH), 0) % HEADS
    return lane == row


def norm_parts(values):
    center = values - jnp.mean(values, axis=-1, keepdims=True)
    rstd = lax.rsqrt(jnp.mean(center * center, axis=-1, keepdims=True) + EPS_NORM)
    return center * rstd, rstd


def norm_back(grad, gain, xhat, rstd):
    gy = grad * gain
    return rstd * (
        gy - jnp.mean(gy, axis=-1, keepdims=True) - xhat * jnp.mean(gy * xhat, axis=-1, keepdims=True)
    )


def rowsum(values):
    return jnp.sum(values, axis=0, keepdims=True)


def to_halves(values, shuffle):
    first, second = [], []
    for block in range(values.shape[1] // 256):
        moved = low(dot(values[:, 256 * block : 256 * block + 256], shuffle))
        first.append(moved[:, :128])
        second.append(moved[:, 128:])
    return jnp.concatenate(first, axis=1), jnp.concatenate(second, axis=1)


def to_natural(first, second, shuffle):
    out = []
    for block in range(first.shape[1] // 128):
        lanes = slice(128 * block, 128 * block + 128)
        both = jnp.concatenate([first[:, lanes], second[:, lanes]], axis=1)
        out.append(low(dot(both, shuffle, NT)))
    return jnp.concatenate(out, axis=1)


R_PATCH, R_GAIN1, R_SHIFT1, R_VB, R_OB, R_GAIN2, R_SHIFT2 = 51, 52, 53, 55, 56, 57, 58
R_C2, R_GAINF, R_SHIFTF, R_SMALL = 63, 64, 65, 66
LATE = 128


def forward_kernel(segments, images, where_ref, pix_ref, *refs):
    count = len(segments)
    own, peer = refs[:count], refs[count : 2 * count]
    rows_ref, qk_ref, valid_ref, shuffle_ref = refs[2 * count : 2 * count + 4]
    hid_ref, xhat_ref, rstd_ref, p_ref, pooled_ref, mass_ref, wv_ref, o_ref = refs[
        2 * count + 4 : 2 * count + 12
    ]
    acc_ref, pool_ref = refs[2 * count + 12 :]
    col, core = where_ref[0], where_ref[1]
    patch = rows_ref[2 : 1 + TOKS] + rows_ref[R_PATCH : R_PATCH + 1]
    class_state = rows_ref[0:1] + rows_ref[1:2]
    for i in range(images):
        acc_ref[SLOT * i : SLOT * i + PATCHES] = patch
        acc_ref[SLOT * i + PATCHES : SLOT * i + TOKS] = class_state
        acc_ref[SLOT * i + TOKS : SLOT * (i + 1)] = jnp.zeros((SLOT - TOKS, WIDTH), F32)
    for flip, group in ((0, own), (1, peer)):
        half = core ^ flip
        for (source, parts), ref in zip(segments, group):
            block = col ^ source

            @pl.when(block < 3)
            def _():
                for row, lane, rows in parts:
                    lanes = pl.ds(pl.multiple_of(block * 512 + lane, 128), rows)
                    acc_ref[...] += dot(pix_ref[half, :, lanes], ref[row : row + rows])

            @pl.when(block == 3)
            def _():
                for row, lane, rows in parts:
                    wv_ref[half, lane : lane + rows] = ref[row : row + rows]

    gain, shift, value_bias = (rows_ref[r : r + 1] for r in (R_GAIN1, R_SHIFT1, R_VB))
    valid = valid_ref[...] > 0
    qk = qk_ref[...]
    for i in range(images):
        part = slice(SLOT * i, SLOT * (i + 1))
        xhat, rstd = norm_parts(acc_ref[part])
        hid = low(xhat * gain + shift)
        xhat_ref[part] = xhat
        rstd_ref[part] = jnp.broadcast_to(rstd, (SLOT, 128))
        hid_ref[part] = hid
        scores = jnp.where(valid[part], dot(hid, qk, NT), MASKED)
        e = jnp.exp(scores - jnp.max(scores, axis=0, keepdims=True))
        p = e / jnp.sum(e, axis=0, keepdims=True)
        p_ref[part] = p
        pb = low(p)
        pool_ref[HEADS * i : HEADS * (i + 1)] = low(dot(pb, hid, TN))
        mass_ref[HEADS * i : HEADS * (i + 1)] = dot(pb, jnp.ones((SLOT, 128), BF), TN)
    shuffle = shuffle_ref[...]
    pooled_ref[0], pooled_ref[1] = to_halves(pool_ref[...], shuffle)
    rows = images * HEADS
    mixed = dot(pooled_ref[0], wv_ref[0]) + dot(pooled_ref[1], wv_ref[1])
    mixed = mixed + mass_ref[:, 0:1] * value_bias
    mixed = jnp.where(head_mask(rows), mixed, 0.0)
    joined = low(jnp.sum(mixed.reshape(images, HEADS, WIDTH), axis=1))
    first, second = to_halves(joined, shuffle)
    o_ref[:, : WIDTH // 2] = first
    o_ref[:, WIDTH // 2 :] = second


def forward_call(segments, images, where, pix, own, peer, rows, qk, valid, shuffle):
    tokens = images * SLOT
    outs = [
        shape((tokens, WIDTH), BF),
        shape((tokens, WIDTH), F32),
        shape((tokens, 128), F32),
        shape((tokens, HEADS), F32),
        shape((2, images * HEADS, WIDTH // 2), BF),
        shape((images * HEADS, 128), F32),
        shape((2, WIDTH // 2, WIDTH), BF),
        shape((images, WIDTH), BF),
    ]
    return call(
        functools.partial(forward_kernel, segments, images), "forward", [where],
        [pix, *own, *peer, rows, qk, valid, shuffle], outs,
        [pltpu.VMEM((tokens, WIDTH), F32), pltpu.VMEM((images * HEADS, WIDTH), BF)], mib=50,
    )


def late_lanes(where_ref, flip, source, rows=LATE):
    at = ((where_ref[1] ^ flip) * 4 + (where_ref[0] ^ source)) * rows
    return pl.ds(pl.multiple_of(at, 128), rows)


def resid_kernel(where_ref, att_ref, rows_ref, *refs):
    late, (resid_ref, low_ref) = refs[:8], refs[8:]
    resid = rows_ref[0:1] + rows_ref[1:2] + rows_ref[R_OB : R_OB + 1]
    for number, piece in enumerate(late):
        lanes = late_lanes(where_ref, number // 4, number % 4)
        resid = resid + dot(att_ref[:, lanes], piece[:LATE])
    resid_ref[...] = resid
    xhat, _ = norm_parts(resid)
    hidden = low(xhat * rows_ref[R_GAIN2 : R_GAIN2 + 1] + rows_ref[R_SHIFT2 : R_SHIFT2 + 1])
    low_ref[...] = jnp.broadcast_to(hidden[None], low_ref.shape)


def fetch(pick_ref, slot, candidates, out_ref, sem):
    for number, candidate in enumerate(candidates):

        @pl.when(pick_ref[slot] == number)
        def _():
            pltpu.make_async_copy(candidate, out_ref, sem).start()


def arrived(candidate, out_ref, sem):
    pltpu.make_async_copy(candidate, out_ref, sem).wait()


def ff_kernel(pick_ref, hid_ref, bias_ref, *refs):
    candidates, (pre_ref, act_ref, part_ref, w1_ref, w2_ref, sems) = refs[:6], refs[6:]
    fetch(pick_ref, 0, candidates, w1_ref, sems.at[0])
    fetch(pick_ref, 1, candidates, w2_ref, sems.at[1])
    hidden = hid_ref[...].reshape(-1, WIDTH)
    arrived(candidates[0], w1_ref, sems.at[0])
    pre = dot(hidden, w1_ref[...], NT) + bias_ref[...]
    pre_ref[...] = pre
    active = low(0.5 * pre * (1.0 + lax.erf(pre * (0.5**0.5))))
    act_ref[...] = active
    arrived(candidates[0], w2_ref, sems.at[1])
    part_ref[...] = low(dot(active, w2_ref[...])).reshape(part_ref.shape)


def ff_back_kernel(pick_ref, dst_ref, pre_ref, *refs):
    candidates, (dpre_ref, sum_ref, part_ref, w1_ref, w2_ref, sems) = refs[:6], refs[6:]
    fetch(pick_ref, 1, candidates, w2_ref, sems.at[1])
    fetch(pick_ref, 0, candidates, w1_ref, sems.at[0])
    d_state = dst_ref[...].reshape(-1, WIDTH)
    pre = pre_ref[...]
    slope = 0.5 * (1.0 + lax.erf(pre * (0.5**0.5))) + pre * jnp.exp(-0.5 * pre * pre) * (
        1.0 / (2.0 * math.pi) ** 0.5
    )
    arrived(candidates[0], w2_ref, sems.at[1])
    d_pre = low(dot(d_state, w2_ref[...], NT) * slope)
    dpre_ref[...] = d_pre
    sum_ref[...] = rowsum(d_pre.astype(F32))
    arrived(candidates[0], w1_ref, sems.at[0])
    part_ref[...] = low(dot(d_pre, w1_ref[...])).reshape(part_ref.shape)


def ff_call(kernel, name, pick, arrays, candidates, outs):
    moved = sum(a.size * a.dtype.itemsize for a in list(arrays) + list(outs))
    return pl.pallas_call(
        kernel,
        in_specs=[smem()]
        + [vmem()] * len(arrays)
        + [pl.BlockSpec(memory_space=pl.ANY)] * len(candidates),
        out_specs=[vmem()] * len(outs),
        out_shape=list(outs),
        scratch_shapes=[
            pltpu.VMEM((512, WIDTH), BF),
            pltpu.VMEM((512, WIDTH), BF),
            pltpu.SemaphoreType.DMA((2,)),
        ],
        compiler_params=pltpu.CompilerParams(vmem_limit_bytes=24 * 2**20),
        cost_estimate=pl.CostEstimate(
            flops=2 * 10**8, bytes_accessed=moved + 2 * 2**20, transcendentals=0
        ),
        name=name,
    )(pick, *arrays, *candidates)


def head_kernel(
    where_ref, part_ref, resid_ref, partners_ref, target_ref, rows_ref, *refs
):
    late, (state_ref, low_ref, final_ref, dz_ref, vec_ref, z_ref) = refs[:8], refs[8:]
    images = resid_ref.shape[0]
    state = resid_ref[...] + jnp.sum(part_ref[...].astype(F32), axis=0) + rows_ref[R_C2 : R_C2 + 1]
    gain = rows_ref[R_GAINF : R_GAINF + 1]
    xhat, rstd = norm_parts(state)
    final = low(xhat * gain + rows_ref[R_SHIFTF : R_SHIFTF + 1])
    final_ref[...] = final
    for number, piece in enumerate(late):
        z_ref[:, late_lanes(where_ref, number // 4, number % 4)] = dot(final, piece[LATE:], NT)
    z = z_ref[...]
    inv = lax.rsqrt(jnp.sum(z * z, axis=-1, keepdims=True) + EPS_NORM)
    partners = partners_ref[...]
    logits = dot(low(z * inv), partners, NT) / SOFTMAX_SCALE
    total = logits.shape[1]
    hit = lax.broadcasted_iota(jnp.int32, (images, total), 1) == target_ref[...]
    top = jnp.max(logits, axis=-1, keepdims=True)
    e = jnp.exp(logits - top)
    mass = jnp.sum(e, axis=-1, keepdims=True)
    aim = jnp.sum(jnp.where(hit, logits, 0.0), axis=-1, keepdims=True)
    losses = jnp.log(mass) + top - aim
    d_logits = (e / mass - jnp.where(hit, 1.0, 0.0)) / total
    d_unit = dot(low(d_logits / SOFTMAX_SCALE), partners)
    along = jnp.sum(d_unit * z, axis=-1, keepdims=True)
    dz_ref[...] = low(d_unit * inv - z * (along * inv * inv * inv))
    d_final = jnp.zeros((images, WIDTH), F32)
    for number, piece in enumerate(late):
        lanes = late_lanes(where_ref, number // 4, number % 4)
        d_final = d_final + dot(dz_ref[:, lanes], piece[LATE:])
    d_state = norm_back(d_final, gain, xhat, rstd)
    state_ref[...] = d_state
    low_ref[...] = jnp.broadcast_to(low(d_state)[None], low_ref.shape)
    vec_ref[...] = jnp.zeros_like(vec_ref)
    vec_ref[0:1] = rowsum(d_state)
    vec_ref[1:2] = rowsum(d_final * xhat)
    vec_ref[2:3] = rowsum(d_final)
    vec_ref[3:4] = jnp.broadcast_to(rowsum(losses) / total, (1, WIDTH))


def backward_kernel(
    images, where_ref, part_ref, dstate_ref, resid_ref, wv_ref, hid_ref, xhat_ref,
    rstd_ref, p_ref, mass_ref, qk_ref, rows_ref, shuffle_ref, *refs,
):
    late = refs[:8]
    de_ref, do_ref, dres_ref, pos_ref, vec_ref, pull_ref, dom_ref, da_ref, att_ref = refs[8:]
    rows = images * HEADS
    gain, value_bias = rows_ref[R_GAIN1 : R_GAIN1 + 1], rows_ref[R_VB : R_VB + 1]
    shuffle = shuffle_ref[...]
    vec_ref[...] = jnp.zeros_like(vec_ref)
    d_two = jnp.sum(part_ref[...].astype(F32), axis=0)
    xhat2, rstd2 = norm_parts(resid_ref[...])
    d_resid = dstate_ref[...] + norm_back(d_two, rows_ref[R_GAIN2 : R_GAIN2 + 1], xhat2, rstd2)
    vec_ref[3:4] = rowsum(d_resid)
    vec_ref[4:5] = rowsum(d_two * xhat2)
    vec_ref[5:6] = rowsum(d_two)
    d_low = low(d_resid)
    dres_ref[...] = d_low
    for number, piece in enumerate(late):
        att_ref[:, late_lanes(where_ref, number // 4, number % 4)] = dot(d_low, piece[:LATE], NT)
    half = WIDTH // 2
    d_att = to_natural(low(att_ref[:, :half]), low(att_ref[:, half:]), shuffle)
    do_ref[...] = d_att
    spread = jnp.broadcast_to(d_att.reshape(images, 1, WIDTH).astype(F32), (images, HEADS, WIDTH))
    wide = jnp.where(head_mask(rows), spread.reshape(rows, WIDTH), 0.0)
    dom_ref[...] = low(wide)
    vec_ref[2:3] = rowsum(wide * mass_ref[:, 0:1])
    da_ref[...] = to_natural(
        low(dot(dom_ref[...], wv_ref[0], NT)), low(dot(dom_ref[...], wv_ref[1], NT)), shuffle
    )
    qk = qk_ref[...]
    bias_rows = low(jnp.broadcast_to(value_bias, (8, WIDTH)))
    real = lax.broadcasted_iota(jnp.int32, (SLOT, WIDTH), 0) < PATCHES
    for i in range(images):
        part = slice(SLOT * i, SLOT * (i + 1))
        mine = slice(HEADS * i, HEADS * (i + 1))
        hid, p, da = hid_ref[part], p_ref[part], da_ref[mine]
        dp = dot(hid, da, NT) + dot(bias_rows, dom_ref[mine], NT)[0:1]
        ds = low(p * (dp - rowsum(p * dp)))
        dh = dot(low(p), da) + dot(ds, qk)
        pull = dot(ds, hid, TN)
        xhat, rstd = xhat_ref[part], rstd_ref[part, 0:1]
        dx = norm_back(dh, gain, xhat, rstd)
        de_ref[part] = low(jnp.where(real, dx, 0.0))
        vec_ref[0:1] += rowsum(dh * xhat)
        vec_ref[1:2] += rowsum(dh)
        if i == 0:
            pos_ref[...] = dx
            pull_ref[...] = pull
        else:
            pos_ref[...] += dx
            pull_ref[...] += pull


def backward_call(images, where, arrays):
    tokens = images * SLOT
    outs = [
        shape((tokens, WIDTH), BF),
        shape((images, WIDTH), BF),
        shape((images, WIDTH), BF),
        shape((SLOT, WIDTH), F32),
        shape((8, WIDTH), F32),
        shape((HEADS, WIDTH), F32),
    ]
    scratch = [pltpu.VMEM((images * HEADS, WIDTH), BF)] * 2 + [pltpu.VMEM((images, WIDTH), F32)]
    return call(
        functools.partial(backward_kernel, images), "backward", [where], arrays, outs, scratch
    )


def embed_grad_kernel(
    images, plan, where_ref, pix_ref, pixp_ref, de_ref, dep_ref, pooled_ref, pooledp_ref,
    do_ref, dop_ref, *out_refs,
):
    col = where_ref[0]
    heads = images * HEADS
    for (source, first, rows), out_ref in zip(plan, out_refs):
        block = col ^ source

        @pl.when(block < 3)
        def _():
            lanes = pl.ds(pl.multiple_of(block * 512 + first, 128), rows)
            total = dot(pix_ref[:, lanes], de_ref[...], TN) + dot(pixp_ref[:, lanes], dep_ref[...], TN)
            out_ref[...] = total.astype(out_ref.dtype)

        @pl.when(block == 3)
        def _():
            total = None
            for pooled, do in ((pooled_ref, do_ref), (pooledp_ref, dop_ref)):
                spread = jnp.broadcast_to(
                    do[...].reshape(images, 1, WIDTH).astype(F32), (images, HEADS, WIDTH)
                )
                wide = low(jnp.where(head_mask(heads), spread.reshape(heads, WIDTH), 0.0))
                term = dot(pooled[:, first : first + rows], wide, TN)
                total = term if total is None else total + term
            out_ref[...] = total.astype(out_ref.dtype)


def embed_grad_call(images, name, plan, where, arrays):
    outs = [shape((rows, WIDTH), F32 if source == 0 else BF) for source, _, rows in plan]
    return call(
        functools.partial(embed_grad_kernel, images, plan), name, [where], arrays, outs
    )


def to_natural_exact(first, second, shuffle):
    wide = shuffle.astype(F32)
    out = []
    for block in range(first.shape[1] // 128):
        lanes = slice(128 * block, 128 * block + 128)
        both = jnp.concatenate([first[:, lanes], second[:, lanes]], axis=1)
        out.append(dot(both, wide, NT, precision=lax.Precision.HIGHEST))
    return jnp.concatenate(out, axis=1)


def collect_kernel(where_ref, pos_ref, vec_ref, head_ref, sum_ref, pull_ref, shuffle_ref, out_ref):
    col, core = where_ref[0], where_ref[1]
    out_ref[...] = jnp.zeros_like(out_ref)
    top = pos_ref[PATCHES:TOKS] + vec_ref[3:4]
    out_ref[0:1] = top
    out_ref[1:2] = top
    patches = pos_ref[0:PATCHES]
    out_ref[2 : 1 + TOKS] = patches
    out_ref[R_PATCH : R_PATCH + 1] = rowsum(patches)
    out_ref[R_GAIN1 : R_SHIFT1 + 1] = vec_ref[0:2]
    out_ref[R_VB : R_VB + 1] = vec_ref[2:3]
    out_ref[R_OB : R_SHIFT2 + 1] = vec_ref[3:6]
    sums = jnp.broadcast_to(sum_ref[...], (8, WIDTH // 2))
    nothing = jnp.zeros_like(sums)
    row = to_natural_exact(
        jnp.where(core == 0, sums, nothing), jnp.where(core == 0, nothing, sums), shuffle_ref[...]
    )
    for block in range(4):
        mine = (col + 1) % 4 == block
        out_ref[R_SHIFT2 + 1 + block : R_SHIFT2 + 2 + block] = jnp.where(mine, row[0:1], 0.0)
    out_ref[R_C2 : R_SHIFTF + 1] = head_ref[0:3]
    out_ref[R_SMALL : R_SMALL + HEADS] = pull_ref[...]
    out_ref[R_SMALL + HEADS : R_SMALL + HEADS + 1] = head_ref[3:4]


def complete_kernel(total_ref, path_ref, rows_ref, shuffle_ref, out_ref, square_ref):
    out_ref[...] = total_ref[0:R_SMALL]
    half = WIDTH // 2
    first = jnp.broadcast_to(path_ref[1:2, :half], (8, half))
    second = jnp.broadcast_to(path_ref[3:4, :half], (8, half))
    d_hidden = to_natural_exact(first, second, shuffle_ref[...])[0:1]
    xhat, rstd = norm_parts(rows_ref[0:1] + rows_ref[1:2])
    d_class = norm_back(d_hidden, rows_ref[R_GAIN1 : R_GAIN1 + 1], xhat, rstd)
    out_ref[0:1] += d_class
    out_ref[1:2] += d_class
    out_ref[R_GAIN1 : R_GAIN1 + 1] += d_hidden * xhat
    out_ref[R_SHIFT1 : R_SHIFT1 + 1] += d_hidden
    out_ref[R_SHIFT1 + 1 : R_SHIFT1 + 2] = path_ref[0:1]
    grads = out_ref[...]
    square_ref[...] = jnp.broadcast_to(
        jnp.sum(jnp.sum(grads * grads, axis=0, keepdims=True), axis=1, keepdims=True), (8, 128)
    )


def owner_kernel(role_ref, extra_ref, pull_ref, heads_ref, class_ref, dq_ref, *refs):
    ff, out_ref = refs[:6], refs[6]
    chip, core = role_ref[0], role_ref[1]
    half = WIDTH // 2

    @pl.when((chip >= 7) & (chip <= 14))
    def _():
        is_two = chip >= 11
        total = None
        for piece in ff:
            left = jnp.where(is_two, piece[:, :half], piece[:, half:WIDTH])
            right = jnp.where(is_two, piece[:, 2 * WIDTH :], piece[:, WIDTH : 2 * WIDTH])
            term = dot(left, right, TN)
            total = term if total is None else total + term
        out_ref[...] = total

    @pl.when(chip == 6)
    def _():
        lanes = pl.ds(pl.multiple_of(core * half, 128), half)
        out_ref[...] = dot(extra_ref[:, lanes], extra_ref[:, WIDTH : 2 * WIDTH], TN)

    @pl.when(chip == 15)
    def _():
        lanes = pl.ds(pl.multiple_of(2 * WIDTH + core * half, 128), half)
        wide = dot(extra_ref[:, lanes], extra_ref[:, 3 * WIDTH :], TN)
        for quarter in range(4):
            out_ref[96 * quarter : 96 * quarter + 96] = wide[128 * quarter : 128 * quarter + 96]
        out_ref[384:] = jnp.zeros((128, WIDTH), F32)

    @pl.when(chip == 4)
    def _():
        out_ref[...] = dot(
            pull_ref[...], heads_ref[...].astype(F32), TN, precision=lax.Precision.HIGHEST
        )

    @pl.when(chip == 3)
    def _():
        outer = dot(
            class_ref[...].astype(F32), jnp.concatenate([dq_ref[0:1], jnp.zeros((7, WIDTH), F32)]),
            TN, precision=lax.Precision.HIGHEST,
        )
        out_ref[...] = outer


def finish_kernel(role_ref, formed_ref, *refs):
    parts, (out_ref, square_ref) = refs[:-2], refs[-2:]
    chip = role_ref[0]
    rows = parts[0].shape[0]

    @pl.when(chip < 3)
    def _():
        for number in range(len(parts) // 2):
            out_ref[rows * number : rows * (number + 1)] = (
                parts[2 * number][...] + parts[2 * number + 1][...].astype(F32)
            )

    @pl.when(chip == 5)
    def _():
        for number in range(len(parts) // 2):
            out_ref[rows * number : rows * (number + 1)] = parts[2 * number + 1][...].astype(F32)

    @pl.when((chip >= 3) & (chip != 5))
    def _():
        out_ref[...] = formed_ref[...]

    grads = out_ref[...]
    square_ref[...] = jnp.broadcast_to(
        jnp.sum(jnp.sum(grads * grads, axis=0, keepdims=True), axis=1, keepdims=True), (8, 128)
    )


def update_kernel(
    source_ref, scalar_ref, before_ref, grad_ref, behind_ref, w_ref, m_ref, v_ref,
    nw_ref, nm_ref, nv_ref,
):
    step = pl.program_id(0)
    slots = grad_ref.shape[0]
    factor, fix_one, fix_two = scalar_ref[0], scalar_ref[1], scalar_ref[2]
    for k in range(w_ref.shape[0]):
        at = source_ref[step * w_ref.shape[0] + k]
        inside = (at >= 0) & (at < slots)
        grad = jnp.where(
            inside,
            grad_ref[jnp.clip(at, 0, slots - 1)],
            jnp.where(
                at < 0,
                before_ref[jnp.clip(at + JITTER, 0, JITTER - 1)],
                behind_ref[jnp.clip(at - slots, 0, JITTER - 1)],
            ),
        )
        grad = grad * jnp.where(at >= -JITTER, factor, 0.0)
        weight = w_ref[k]
        first = BETA_ONE * m_ref[k] + (1.0 - BETA_ONE) * grad
        second = BETA_TWO * v_ref[k] + (1.0 - BETA_TWO) * grad * grad
        nm_ref[k] = first
        nv_ref[k] = second
        nw_ref[k] = weight - LEARN_RATE * (
            (first * fix_one) / (jnp.sqrt(second * fix_two) + ADAM_EPS) + DECAY_RATE * weight
        )


def update_call(source, scalars, before, grads, behind, masters, first, second):
    slots, part, width = masters.shape
    block = 4
    spec = pl.BlockSpec((block, part, width), lambda i: (i, 0, 0))
    return pl.pallas_call(
        update_kernel,
        grid=(slots // block,),
        in_specs=[smem(), smem(), vmem(), vmem(), vmem(), spec, spec, spec],
        out_specs=[spec] * 3,
        out_shape=[shape(masters.shape, F32)] * 3,
        compiler_params=pltpu.CompilerParams(vmem_limit_bytes=24 * 2**20),
        cost_estimate=pl.CostEstimate(
            flops=2 * 10**7, bytes_accessed=7 * masters.size * 4, transcendentals=0
        ),
        name="update",
    )(source, scalars, before, grads, behind, masters, first, second)


CHIPS = 16
CHIP = ("z", "y", "x")
ALL = ("z", "y", "x", "c")
PLANE = ("y", "x", "c")
FLIP_X = [(i, i ^ 1) for i in range(CHIPS)]
FLIP_Y = [(i, i ^ 2) for i in range(CHIPS)]
FLIP_CORE = [(0, 1), (1, 0)]


def hop(values, pairs):
    return lax.ppermute(values, CHIP, pairs)


def swap(values):
    return lax.ppermute(values, "c", FLIP_CORE)


def after(values, *others):
    return lax.optimization_barrier((values,) + others)[0]


def among(img, chips):
    hit = img == chips[0]
    for chip in chips[1:]:
        hit = hit | (img == chip)
    return hit


def choose(img, cases, otherwise):
    out = otherwise
    for chips, values in cases:
        out = jnp.where(among(img, chips), values, out)
    return out


def together(*values):
    return lax.optimization_barrier(values)


def plane_gather(block, diagonal_by_x):
    by_x, by_y = hop(block, FLIP_X), hop(block, FLIP_Y)
    diagonal = hop(by_y, FLIP_X) if diagonal_by_x else hop(by_x, FLIP_Y)
    return [block, by_x, by_y, diagonal]


def in_plane(values):
    return lax.all_to_all(values, PLANE, 0, 0, tiled=True)


def from_all(values):
    sent = jnp.broadcast_to(values[None], (2 * CHIPS,) + values.shape)
    return lax.all_to_all(sent, ALL, 0, 0, tiled=True)


def natural(values):
    lead = values.shape[:-2]
    units = values.shape[-1] // 16
    split = values.reshape(lead + (2, units, 16))
    return jnp.swapaxes(split, -3, -2).reshape(lead + (units * 32,))


def halves(values):
    lead = values.shape[:-1]
    units = values.shape[-1] // 32
    return jnp.swapaxes(values.reshape(lead + (units, 2, 16)), -3, -2).reshape(
        lead + (2, units * 16)
    )


def per_device_16(
    pixels, keep_mask, partner_index, partner_emb, masters, first_moment_slots,
    second_moment_slots, slot_unit_index, small_params, small_first, small_second, step_count,
):
    img, core = lax.axis_index(CHIP), lax.axis_index("c")
    col, plane = img % 4, img // 4
    images = pixels.shape[0]
    slots = masters.shape[0]
    is_one = core == 1
    where = jnp.stack([col, core]).astype(jnp.int32)
    shuffle = shuffle_matrix()
    rows = small_params
    class_state = small_params[0] + small_params[1]

    def mine_of(pair):
        return jnp.where(is_one, pair[1], pair[0])

    def theirs_of(pair):
        return jnp.where(is_one, pair[0], pair[1])

    near = slots_near(slot_unit_index, img, slots)
    held = low(masters)
    ids = img * slots + jnp.arange(slots, dtype=jnp.int32)
    matches = [near[s : s + slots] == ids for s in range(2 * JITTER + 1)]
    middle = pick(held[6:26], [m[8:24] for m in matches], 16)
    before, behind = halo(after(held, middle), CHIPS, CHIP)
    lower = pick(jnp.concatenate([before, held[:10]]), [m[:8] for m in matches], 8)
    upper = pick(jnp.concatenate([held[22:], behind]), [m[24:] for m in matches], 8)
    outer = jnp.concatenate([lower, upper]).reshape(256, WIDTH)
    middle = middle.reshape(256, WIDTH)
    own_w = jnp.concatenate([outer[:128], middle, outer[128:]])

    class_hidden = low(layer_norm(class_state, small_params[R_GAIN1], small_params[R_SHIFT1]))
    class_half = mine_of(halves(class_hidden))
    by_quarter = halves(partner_emb).reshape(images, 2, 4, PROJ // 8)
    by_quarter = jnp.pad(by_quarter, ((0, 0), (0, 0), (0, 0), (0, LATE - PROJ // 8)))
    partners = from_all(by_quarter.reshape(images, WIDTH)).reshape(-1, WIDTH)

    one_a = hop(middle, [(0, 4), (1, 5), (2, 6), (5, 7)])
    query_parts = from_all(dot(class_half[None], own_w))
    filler = jnp.zeros((LATE - PROJ // 8, WIDTH), BF)

    def late_quarter(number):
        proj = jnp.concatenate([own_w[96 * number : 96 * number + 96], filler])
        return jnp.where(img == 15, proj, own_w[LATE * number : LATE * (number + 1)])

    quarters = [late_quarter(number) for number in range(4)]
    late = jnp.where(img == 6, quarters[2], quarters[3])
    for flip in (1, 2, 3):
        mine = jnp.where(img == 6, quarters[2 ^ flip], quarters[3 ^ flip])
        got = hop(mine, [(6, 6 ^ flip), (15, 15 ^ flip)])
        late = jnp.where(among(img, (6 ^ flip, 15 ^ flip)), got, late)
    down_one = hop(
        own_w, [(12, 8), (13, 9), (14, 10), (11, 7), (8, 4), (9, 5), (10, 6), (7, 3)]
    )
    one_a, outer, query_parts, late, partners = together(
        one_a, outer, query_parts, late, partners
    )
    one_b = hop(outer, [(0, 4), (1, 5), (2, 6), (5, 7)])
    two_a = hop(one_a, [(4, 8), (5, 9), (6, 10), (7, 11)])
    query = low((query_parts[6, 0] + query_parts[7, 0] + small_params[R_SHIFT1 + 1]) * SCALE)
    query_heads = jnp.where(head_mask(HEADS), query[None], jnp.zeros((), BF))
    pulled = from_all(low(dot(query_heads, own_w, NT)))
    late_one = hop(late, [(4, 0), (5, 1), (6, 2), (7, 3), (12, 8), (13, 9), (14, 10), (15, 11)])
    one_b, two_a, pulled, late_one, down_one = together(one_b, two_a, pulled, late_one, down_one)
    two_b = hop(one_b, [(4, 8), (5, 9), (6, 10), (7, 11)])
    three_a = hop(
        jnp.where(img == 7, one_a, two_a), [(8, 12), (9, 13), (10, 14), (11, 15), (7, 3)]
    )
    late_two = hop(
        jnp.where(plane == 1, late, late_one),
        [(4, 8), (5, 9), (6, 10), (7, 11), (8, 4), (9, 5), (10, 6), (11, 7)],
    )
    down_two = hop(down_one, [(8, 4), (9, 5), (10, 6), (7, 3), (4, 0), (5, 1), (6, 2)])
    two_b, three_a, late_two = together(two_b, three_a, late_two)
    block_a = jnp.where(img < 3, middle, one_a + two_a + three_a)
    x_a, y_a = hop(block_a, FLIP_X), hop(block_a, FLIP_Y)
    three_b = hop(
        jnp.where(img == 7, one_b, two_b), [(8, 12), (9, 13), (10, 14), (11, 15), (7, 3)]
    )
    late_three = hop(
        late_two, [(8, 12), (9, 13), (10, 14), (11, 15), (4, 0), (5, 1), (6, 2), (7, 3)]
    )
    x_a, y_a, three_b, late_three, down_two = together(x_a, y_a, three_b, late_three, down_two)
    block_b = jnp.where(img < 3, outer, one_b + two_b + three_b)
    x_b, y_b = hop(block_b, FLIP_X), hop(block_b, FLIP_Y)
    d_a = hop(y_a, FLIP_X)
    down_three = hop(down_two, [(4, 0), (5, 1), (6, 2)])
    up_one = hop(own_w, [(8, 12), (9, 13), (10, 14), (7, 11), (11, 15)])
    x_b, y_b, d_a, late_three = together(x_b, y_b, d_a, late_three)
    d_b = hop(x_b, FLIP_Y)
    wo_part = choose(plane, [((0,), late_one), ((1,), late), ((2,), late_two)], late_three)
    proj_part = choose(plane, [((3,), late), ((2,), late_one), ((1,), late_two)], late_three)
    late_own = jnp.concatenate([wo_part, proj_part])
    late_x, late_y = hop(late_own, FLIP_X), hop(late_own, FLIP_Y)
    up_two = hop(up_one, [(11, 15)])

    segments, own_pieces, peer_pieces = [], [], []
    for pieces, spans in (
        ((block_a, x_a, y_a, d_a), ((0, 128, 256),)),
        ((block_b, x_b, y_b, d_b), ((0, 0, 128), (128, 384, 128))),
    ):
        segments += [(source, spans) for source in range(4)]
        own_pieces += pieces
        peer_pieces += [swap(piece) for piece in pieces]
    late_d = jnp.concatenate([hop(late_y[:LATE], FLIP_X), hop(late_x[LATE:], FLIP_Y)])
    late_pieces = [late_own, late_x, late_y, late_d]
    late_pieces += [swap(piece) for piece in late_pieces]
    qk = natural(jnp.stack([pulled[8], pulled[9]], axis=1))

    padded = jnp.pad(pixels, ((0, 0), (0, SLOT - PATCHES), (0, 0)))
    pix = prep(padded, shuffle).reshape(2, images * SLOT, PIX // 2)
    pix_own = mine_of(pix)
    pix_peer = swap(theirs_of(pix))
    valid = jnp.concatenate(
        [
            keep_mask,
            jnp.ones((images, 1), jnp.int32),
            jnp.zeros((images, SLOT - TOKS), jnp.int32),
        ],
        axis=1,
    ).reshape(images * SLOT, 1)
    hid, xhat, rstd, p, pooled, mass, wv, attended = forward_call(
        segments, images, where, pix, own_pieces, peer_pieces, rows, qk, valid, shuffle
    )

    pooled_own = mine_of(pooled)
    pooled_peer = swap(theirs_of(pooled))

    resid, hidden_sent = call(
        resid_kernel, "resid", [where], [attended, rows, *late_pieces],
        [shape((images, WIDTH), F32), shape((8, images, WIDTH), BF)],
    )
    hidden_all = in_plane(hidden_sent)
    ff_block = (col + 1) % 4
    bias_part = lax.dynamic_slice(
        small_params[R_SHIFT2 + 1 : R_C2].reshape(4, 32, 2, 16),
        (ff_block, 0, core, 0),
        (1, 32, 1, 16),
    ).reshape(1, 512)
    candidates = [own_w, up_one, up_two, down_one, down_two, down_three]
    pick_one = choose(
        img, [((15,), 2), ((12, 13, 14, 11), 1), ((4, 5, 6, 3), 3), ((0, 1, 2), 4)], 0
    )
    pick_two = choose(
        img, [((15,), 1), ((8, 9, 10, 7), 3), ((4, 5, 6, 3), 4), ((0, 1, 2), 5)], 0
    )
    picks = jnp.stack([pick_one, pick_two]).astype(jnp.int32)
    preact, active, part = ff_call(
        ff_kernel, "ff", picks, [hidden_all, bias_part], candidates,
        [shape((8 * images, 512), F32), shape((8 * images, 512), BF), shape((8, images, WIDTH), BF)],
    )
    part = in_plane(part)
    d_state, d_state_sent, final, d_projected, head_vec = call(
        head_kernel, "head", [where],
        [part, resid, partners, partner_index[:, None], rows, *late_pieces],
        [
            shape((images, WIDTH), F32), shape((8, images, WIDTH), BF), shape((images, WIDTH), BF),
            shape((images, WIDTH), BF), shape((8, WIDTH), F32),
        ],
        [pltpu.VMEM((images, WIDTH), F32)],
    )
    d_state_all = in_plane(d_state_sent)
    d_preact, d_preact_sum, part = ff_call(
        ff_back_kernel, "ff_back", picks, [d_state_all, preact], candidates,
        [shape((8 * images, 512), BF), shape((1, 512), F32), shape((8, images, WIDTH), BF)],
    )
    part = in_plane(part)

    d_embed, d_attended, d_resid, d_pos, d_vec, pull = backward_call(
        images, where,
        [part, d_state, resid, wv, hid, xhat, rstd, p, mass, qk, rows, shuffle, *late_pieces],
    )
    arrays = [
        pix_own, pix_peer, d_embed, swap(d_embed), pooled_own, pooled_peer, d_attended,
        swap(d_attended),
    ]
    quads = [(3, 128 * number, 128) for number in range(4)]
    grad_d = embed_grad_call(images, "embed_grad_far", quads, where, arrays)
    pairs = [(source, first, 256) for source in (1, 2, 0) for first in (0, 256)]
    grads = embed_grad_call(images, "embed_grad_near", pairs, after(where, grad_d[0]), arrays)
    grad_x, grad_y, grad_own = grads[0:2], grads[2:4], grads[4:6]
    sums = []
    gate = None
    for number in range(2):
        for_y, for_x = grad_d[2 * number], grad_d[2 * number + 1]
        if number:
            for_y, for_x = after(for_y, gate), after(for_x, gate)
        got_y, got_x = hop(for_y, FLIP_X), hop(for_x, FLIP_Y)
        part_x, part_y = grad_x[number], grad_y[number]
        part_y = jnp.concatenate([low(part_y[:128].astype(F32) + got_y.astype(F32)), part_y[128:]])
        part_x = jnp.concatenate([part_x[:128], low(part_x[128:].astype(F32) + got_x.astype(F32))])
        gate = got_x
        got_x, got_y = hop(part_x, FLIP_X), hop(part_y, FLIP_Y)
        sums.append(grad_own[number] + got_x.astype(F32) + got_y.astype(F32))
    reduced = []
    for acc in sums:
        got = hop(low(acc), [(12, 8), (13, 9), (14, 10), (15, 11), (3, 7)])
        acc = acc + got.astype(F32)
        got = hop(low(acc), [(8, 4), (9, 5), (10, 6), (11, 7)])
        acc = acc + got.astype(F32)
        reduced += [acc, hop(low(acc), [(4, 0), (5, 1), (6, 2), (7, 5)])]

    d_pos, d_vec, head_vec, d_preact_sum, pull, active, attended, _ = together(
        d_pos, d_vec, head_vec, d_preact_sum, pull, active, attended, grad_own[0]
    )
    (small_local,) = call(
        collect_kernel, "collect", [where], [d_pos, d_vec, head_vec, d_preact_sum, pull, shuffle],
        [shape((96, WIDTH), F32)],
    )
    shares = lax.all_to_all(small_local.reshape(32, 3, WIDTH), ALL, 0, 0, tiled=True)
    small_total = from_all(jnp.sum(shares, axis=0)).reshape(96, WIDTH)
    pull_total, loss = small_total[R_SMALL : R_SMALL + HEADS], small_total[R_SMALL + HEADS, 0]
    pull_half = halves(pull_total)
    pull_half = mine_of((pull_half[:, 0], pull_half[:, 1]))
    d_query = jnp.where(head_mask(HEADS), dot(low(pull_half), own_w), 0.0)
    d_query = jnp.sum(d_query, axis=0, keepdims=True) * SCALE
    d_query = hop(d_query + swap(d_query), [(4, 3)])
    toward = dot(low(d_query), own_w, NT)
    path = jnp.concatenate([d_query, jnp.pad(toward, ((0, 0), (0, WIDTH // 2)))])
    path = from_all(path)
    small_grad, small_square = call(
        complete_kernel, "complete", [], [small_total, path[6:8].reshape(4, WIDTH), rows, shuffle],
        [shape((R_SMALL, WIDTH), F32), shape((8, 128), F32)],
    )

    ff_rows = jnp.concatenate(
        [
            active,
            d_preact,
            hidden_all.reshape(-1, WIDTH),
            d_state_all.reshape(-1, WIDTH),
        ],
        axis=1,
    )
    rise = [(i, i + 4) for i in range(12)]
    up_one = hop(ff_rows, rise)
    up_two = hop(up_one, rise[4:])
    up_three = hop(up_two, rise[8:])
    down_one = hop(ff_rows, [(12, 8), (13, 9), (14, 10), (15, 11), (11, 7)])
    down_two = hop(down_one, [(11, 7)])
    every = [ff_rows, up_one, up_two, up_three, down_one, down_two]
    extra = jnp.concatenate([attended, d_resid, d_projected, final], axis=1)
    extra = after(extra, small_total)
    sent = jnp.broadcast_to(extra[None], (CHIPS,) + extra.shape)
    extra = lax.all_to_all(sent, CHIP, 0, 0, tiled=True).reshape(CHIPS * images, -1)
    extra = jnp.concatenate([extra, swap(extra)], axis=0)
    class_rows = jnp.concatenate([class_half[None], jnp.zeros((7, WIDTH // 2), BF)])
    role = jnp.stack([img, core]).astype(jnp.int32)
    (formed,) = call(
        owner_kernel, "owner", [role],
        [extra, pull_half, query_heads, class_rows, d_query, *every],
        [shape((512, WIDTH), F32)],
    )
    own_grad, square = call(
        finish_kernel, "finish", [role], [formed, *reduced],
        [shape((512, WIDTH), F32), shape((8, 128), F32)],
    )
    owner_total = jnp.sum(from_all(square[0:1])[:, 0, 0])
    grad_norm = jnp.sqrt(owner_total + small_square[0, 0])
    factor = 1.0 / jnp.maximum(grad_norm, 1.0)
    own_grad = own_grad.reshape(slots, 16, WIDTH)
    before, behind = halo(own_grad, CHIPS, CHIP)
    here = near[JITTER : JITTER + slots]
    source = jnp.where(here < UNIT_COUNT, here - img * slots, -100)
    step_value = step_count.astype(F32)
    scalars = jnp.stack(
        [
            factor,
            1.0 / (1.0 - jnp.power(BETA_ONE, step_value)),
            1.0 / (1.0 - jnp.power(BETA_TWO, step_value)),
        ]
    )
    new_masters, new_first, new_second = update_call(
        source, scalars, before, own_grad, behind, masters, first_moment_slots,
        second_moment_slots,
    )
    new_small, new_small_first, new_small_second = adamw(
        small_params, small_grad * factor, small_first, small_second, step_value
    )
    return (
        new_masters, new_first, new_second, new_small, new_small_first, new_small_second,
        loss, grad_norm,
    )


def per_device_any(
    pixels, keep_mask, partner_index, partner_emb, masters, first_moment_slots,
    second_moment_slots, slot_unit_index, small_params, small_first, small_second, step_count,
):
    chips, seq = lax.axis_size("img"), lax.axis_size("seq")
    img = lax.axis_index("img")
    images = pixels.shape[0]
    slots, part = masters.shape[0], masters.shape[1]
    near = slots_near(slot_unit_index, img, slots)
    own_w = to_units(low(masters), near, img, chips)
    gathered = lax.all_gather(own_w, ("img", "seq"), axis=0, tiled=False)
    flat = gathered.reshape(chips, seq, slots, part, WIDTH).transpose(0, 2, 1, 3, 4)
    flat = flat.reshape(chips * slots * ROWS_PER_UNIT, WIDTH)
    bounds = [0, PIX, WIDTH, WIDTH, WIDTH, WIDTH, FF, FF, PROJ]
    parts, offset = [], 0
    for size in bounds[1:]:
        parts.append(flat[offset : offset + size])
        offset += size
    embed_w, query_w, key_w, value_w, output_w, fc_in_w, fc_out_w, proj_w = parts
    (
        class_row, pos_rows, patch_bias, gain_one, shift_one, query_bias, value_bias, out_bias,
        gain_two, shift_two, fc_in_bias, fc_out_bias, gain_end, shift_end,
    ) = small_parts(small_params)
    class_state = class_row + pos_rows[0]
    embedded = jnp.einsum("itp,pd->itd", pixels, embed_w, preferred_element_type=F32)
    tokens = jnp.concatenate(
        [
            jnp.broadcast_to(class_state, (images, 1, WIDTH)),
            embedded + patch_bias + pos_rows[1:],
        ],
        axis=1,
    )
    hidden = low(layer_norm(tokens, gain_one, shift_one))
    class_hidden = hidden[0, 0]
    mask16 = head_mask(HEADS)
    query = low((dot(class_hidden[None], query_w)[0] + query_bias) * SCALE)
    query_heads = jnp.where(mask16, query[None], jnp.zeros((), BF))
    qk = low(dot(query_heads, key_w, NT))
    scores = jnp.einsum("hd,itd->iht", qk, hidden, preferred_element_type=F32)
    keep = jnp.concatenate([jnp.ones((images, 1), jnp.int32), keep_mask], axis=1)
    scores = jnp.where(keep[:, None, :] > 0, scores, MASKED)
    weights = jax.nn.softmax(scores, axis=-1)
    weights_low = low(weights)
    pooled = low(jnp.einsum("iht,itd->ihd", weights_low, hidden, preferred_element_type=F32))
    mass = jnp.sum(weights_low.astype(F32), axis=-1)
    mixed = dot(pooled.reshape(-1, WIDTH), value_w).reshape(images, HEADS, WIDTH)
    mixed = mixed + mass[:, :, None] * value_bias
    attended = low(jnp.sum(jnp.where(mask16, mixed, 0.0), axis=1))
    resid = class_state + dot(attended, output_w) + out_bias
    hidden_two = low(layer_norm(resid, gain_two, shift_two))
    preact = dot(hidden_two, fc_in_w, NT) + fc_in_bias
    active = low(exact_gelu(preact))
    state = resid + dot(active, fc_out_w) + fc_out_bias
    final = low(layer_norm(state, gain_end, shift_end))
    projected = dot(final, proj_w, NT)
    unit = low(normalize(projected))
    partners = lax.all_gather(partner_emb, ("img", "seq"), axis=0, tiled=True)
    count = partners.shape[0]
    logits = dot(unit, partners, NT) / SOFTMAX_SCALE
    onehot = (jnp.arange(count, dtype=jnp.int32)[None] == partner_index[:, None]).astype(F32)
    total = jax.nn.logsumexp(logits, axis=-1)
    loss_part = jnp.sum(total - jnp.sum(logits * onehot, axis=-1)) / count
    d_logits = (jax.nn.softmax(logits, axis=-1) - onehot) / count
    d_unit = dot(low(d_logits / SOFTMAX_SCALE), partners)
    d_projected = low(jax.vjp(normalize, projected)[1](d_unit)[0])
    d_final = dot(d_projected, proj_w)
    d_state, d_gain_end, d_shift_end = jax.vjp(layer_norm, state, gain_end, shift_end)[1](d_final)
    d_state_low = low(d_state)
    d_active = dot(d_state_low, fc_out_w, NT)
    d_preact = low(jax.vjp(exact_gelu, preact)[1](d_active)[0])
    d_hidden_two = dot(d_preact, fc_in_w)
    d_norm, d_gain_two, d_shift_two = jax.vjp(layer_norm, resid, gain_two, shift_two)[1](
        d_hidden_two
    )
    d_resid = d_state + d_norm
    d_resid_low = low(d_resid)
    d_attended = low(dot(d_resid_low, output_w, NT))
    wide = jnp.where(mask16, d_attended[:, None, :], jnp.zeros((), BF))
    d_pooled = low(dot(wide.reshape(-1, WIDTH), value_w, NT)).reshape(images, HEADS, WIDTH)
    d_weights = jnp.einsum("ihd,itd->iht", d_pooled, hidden, preferred_element_type=F32)
    d_weights = d_weights + jnp.sum(wide.astype(F32) * value_bias, axis=-1)[:, :, None]
    d_scores = low(weights * (d_weights - jnp.sum(weights * d_weights, axis=-1, keepdims=True)))
    d_hidden = jnp.einsum("iht,ihd->itd", weights_low, d_pooled, preferred_element_type=F32)
    d_hidden = d_hidden + jnp.einsum("iht,hd->itd", d_scores, qk, preferred_element_type=F32)
    pull = jnp.einsum("iht,itd->hd", d_scores, hidden, preferred_element_type=F32)
    d_query = jnp.sum(jnp.where(mask16, dot(low(pull), key_w), 0.0), axis=0) * SCALE
    d_class_hidden = dot(low(d_query)[None], query_w, NT)
    d_tokens, d_gain_one, d_shift_one = jax.vjp(layer_norm, tokens, gain_one, shift_one)[1](
        d_hidden
    )
    d_class, d_gain_cls, d_shift_cls = jax.vjp(layer_norm, class_state[None], gain_one, shift_one)[
        1
    ](d_class_hidden)
    d_class = d_class[0] + jnp.sum(d_tokens[:, 0], axis=0) + jnp.sum(d_resid, axis=0)
    d_patch = d_tokens[:, 1:]
    d_embed_w = jnp.einsum("itp,itd->pd", pixels, low(d_patch), preferred_element_type=F32)
    d_value_w = dot(pooled.reshape(-1, WIDTH), wide.reshape(-1, WIDTH), TN)
    d_key_w = dot(pull, query_heads.astype(F32), TN, precision=lax.Precision.HIGHEST)
    small_local = jnp.concatenate(
        [
            d_class[None],
            d_class[None],
            jnp.sum(d_patch, axis=0),
            jnp.sum(d_patch, axis=(0, 1))[None],
            (d_gain_one + d_gain_cls)[None],
            (d_shift_one + d_shift_cls)[None],
            d_query[None],
            jnp.sum(wide.astype(F32) * mass[:, :, None], axis=(0, 1))[None],
            jnp.sum(d_resid, axis=0)[None],
            d_gain_two[None],
            d_shift_two[None],
            jnp.sum(d_preact.astype(F32), axis=0).reshape(FF // WIDTH, WIDTH),
            jnp.sum(d_state, axis=0)[None],
            d_gain_end[None],
            d_shift_end[None],
        ],
        axis=0,
    )
    grad_table = jnp.concatenate(
        [
            d_embed_w,
            class_hidden.astype(F32)[:, None] * d_query[None, :],
            d_key_w,
            d_value_w,
            dot(attended, d_resid_low, TN),
            dot(d_preact, hidden_two, TN),
            dot(active, d_state_low, TN),
            dot(d_projected, final, TN),
            jnp.zeros(((chips * slots - UNIT_COUNT) * ROWS_PER_UNIT, WIDTH), F32),
        ],
        axis=0,
    ).reshape(chips * slots, ROWS_PER_UNIT, WIDTH)
    small_grad, loss = lax.psum((small_local, loss_part), ("img", "seq"))
    core_half = lax.psum_scatter(low(grad_table), "seq", scatter_dimension=1, tiled=True)
    own_grad = lax.psum_scatter(core_half.astype(F32), "img", scatter_dimension=0, tiled=True)
    owner_total = lax.psum(jnp.sum(own_grad * own_grad), ("img", "seq"))
    grad_norm = jnp.sqrt(owner_total + jnp.sum(small_grad * small_grad))
    factor = 1.0 / jnp.maximum(grad_norm, 1.0)
    slot_grad = to_slots(own_grad, near, img, chips)
    step_value = step_count.astype(F32)
    new_masters, new_first, new_second = adamw(
        masters, slot_grad * factor, first_moment_slots, second_moment_slots, step_value
    )
    new_small, new_small_first, new_small_second = adamw(
        small_params, small_grad * factor, small_first, small_second, step_value
    )
    return (
        new_masters, new_first, new_second, new_small, new_small_first, new_small_second,
        loss, grad_norm,
    )


def solution(mesh):
    chip, devices = "img", ("img", "seq")
    core, body = "seq", per_device_any
    if mesh.shape["img"] == CHIPS and mesh.shape["seq"] == 2:
        mesh = jax.sharding.Mesh(mesh.devices.reshape(4, 2, 2, 2), ALL)
        chip, devices, core, body = CHIP, ALL, "c", per_device_16
    weights = P(chip, core, None)
    return jax.shard_map(
        body,
        mesh=mesh,
        in_specs=(
            P(devices, None, None),
            P(devices, None),
            P(devices),
            P(devices, None),
            weights,
            weights,
            weights,
            P(),
            P(),
            P(),
            P(),
            P(),
        ),
        out_specs=(weights, weights, weights, P(), P(), P(), P(), P()),
        check_vma=False,
    )
```

```python
import functools
import math

import jax
import jax.numpy as jnp
from jax import lax
from jax.experimental import pallas as pl
from jax.experimental.pallas import tpu as pltpu
from jax.sharding import PartitionSpec as P

WIDTH = 1024
HEADS = 16
HEAD_DIM = 64
FF = 4096
PIX = 3072
PROJ = 768
TOKS = 50
PATCHES = TOKS - 1
ROWS_PER_UNIT = 32
UNIT_COUNT = 504
JITTER = 2

EPS_NORM = 1e-06
SOFTMAX_SCALE = 0.07
LEARN_RATE = 0.03
BETA_ONE = 0.5
BETA_TWO = 0.5
DECAY_RATE = 0.05
ADAM_EPS = 1e-08
MASKED = -1000000000.0
SCALE = HEAD_DIM ** (-0.5)

F32 = jnp.float32
BF = jnp.bfloat16
ROW_BASE = 1 + TOKS
ROW_TAIL = ROW_BASE + 8 + FF // WIDTH
SLOT = 64


def low(values):
    return values.astype(BF)


def dot(a, b, dims=((1,), (0,)), precision=None):
    return lax.dot_general(a, b, (dims, ((), ())), precision=precision, preferred_element_type=F32)


NN = ((1,), (0,))
NT = ((1,), (1,))
TN = ((0,), (0,))


def layer_norm(values, gain, shift):
    center = values - jnp.mean(values, axis=-1, keepdims=True)
    spread = jnp.mean(center * center, axis=-1, keepdims=True)
    return center * lax.rsqrt(spread + EPS_NORM) * gain + shift


def normalize(values):
    return values * lax.rsqrt(jnp.sum(values * values, axis=-1, keepdims=True) + EPS_NORM)


def exact_gelu(values):
    return jax.nn.gelu(values, approximate=False)


def small_parts(small):
    base, tail = ROW_BASE, ROW_TAIL
    return (
        small[0],
        small[1:base],
        small[base],
        small[base + 1],
        small[base + 2],
        small[base + 3],
        small[base + 4],
        small[base + 5],
        small[base + 6],
        small[base + 7],
        small[base + 8 : tail].reshape(FF),
        small[tail],
        small[tail + 1],
        small[tail + 2],
    )


def adamw(weight, grad, first, second, step):
    first_new = BETA_ONE * first + (1.0 - BETA_ONE) * grad
    second_new = BETA_TWO * second + (1.0 - BETA_TWO) * grad * grad
    first_hat = first_new / (1.0 - jnp.power(BETA_ONE, step))
    second_hat = second_new / (1.0 - jnp.power(BETA_TWO, step))
    weight_new = weight - LEARN_RATE * (
        first_hat / (jnp.sqrt(second_hat) + ADAM_EPS) + DECAY_RATE * weight
    )
    return (weight_new, first_new, second_new)


def halo(values, chips, axes):
    before = lax.ppermute(values[-JITTER:], axes, [(i, i + 1) for i in range(chips - 1)])
    behind = lax.ppermute(values[:JITTER], axes, [(i + 1, i) for i in range(chips - 1)])
    return before, behind


def with_halo(values, chips, axes):
    before, behind = halo(values, chips, axes)
    return jnp.concatenate([before, values, behind], axis=0)


def slots_near(slot_unit_index, img, slots):
    padded = jnp.pad(slot_unit_index, (JITTER, JITTER), constant_values=-1)
    return lax.dynamic_slice(padded, (img * slots,), (slots + 2 * JITTER,))


def pick(ext, matches, slots):
    out = jnp.zeros((slots,) + ext.shape[1:], ext.dtype)
    for shift in range(2 * JITTER + 1):
        out = jnp.where(matches[shift][:, None, None], ext[shift : shift + slots], out)
    return out


def to_units(values, near, img, chips, axes="img"):
    slots = values.shape[0]
    ids = img * slots + jnp.arange(slots, dtype=jnp.int32)
    matches = [near[s : s + slots] == ids for s in range(2 * JITTER + 1)]
    return pick(with_halo(values, chips, axes), matches, slots)


def to_slots(values, near, img, chips, axes="img"):
    slots = values.shape[0]
    here = near[JITTER : JITTER + slots]
    ids = img * slots + jnp.arange(slots, dtype=jnp.int32)
    matches = [
        (here == ids + (s - JITTER)) & (here < UNIT_COUNT) for s in range(2 * JITTER + 1)
    ]
    return pick(with_halo(values, chips, axes), matches, slots)


def shuffle_matrix():
    source = lax.broadcasted_iota(jnp.int32, (256, 256), 0)
    target = lax.broadcasted_iota(jnp.int32, (256, 256), 1)
    moved = ((source // 16) % 2) * 128 + (source // 32) * 16 + source % 16
    return (moved == target).astype(F32).astype(BF)


def vmem():
    return pl.BlockSpec(memory_space=pltpu.VMEM)


def smem():
    return pl.BlockSpec(memory_space=pltpu.SMEM)


def shape(dims, dtype):
    return jax.ShapeDtypeStruct(dims, dtype)


def call(kernel, name, scalars, arrays, outs, scratch=(), mib=40, flops=10**9, far=()):
    moved = sum(a.size * a.dtype.itemsize for a in [*arrays, *outs, *far])
    return pl.pallas_call(
        kernel,
        in_specs=[smem()] * len(scalars)
        + [vmem()] * len(arrays)
        + [pl.BlockSpec(memory_space=pl.ANY)] * len(far),
        out_specs=[vmem()] * len(outs),
        out_shape=list(outs),
        scratch_shapes=list(scratch),
        compiler_params=pltpu.CompilerParams(vmem_limit_bytes=mib * 2**20),
        cost_estimate=pl.CostEstimate(flops=flops, bytes_accessed=moved, transcendentals=0),
        name=name,
    )(*scalars, *arrays, *far)


def prep_kernel(pix_ref, shuffle_ref, out_ref):
    shuffle = shuffle_ref[...]
    out_ref[...] = jnp.zeros_like(out_ref)
    for block in range(PIX // 256):
        moved = dot(pix_ref[0, :, 256 * block : 256 * block + 256], shuffle).astype(BF)
        out_ref[0, 0, :PATCHES, 128 * block : 128 * block + 128] = moved[:, :128]
        out_ref[1, 0, :PATCHES, 128 * block : 128 * block + 128] = moved[:, 128:]


def prep(pixels, shuffle):
    images = pixels.shape[0]
    return pl.pallas_call(
        prep_kernel,
        grid=(images,),
        in_specs=[
            pl.BlockSpec((1, PATCHES, PIX), lambda i: (i, 0, 0)),
            pl.BlockSpec((256, 256), lambda i: (0, 0)),
        ],
        out_specs=pl.BlockSpec((2, 1, SLOT, PIX // 2), lambda i: (0, i, 0, 0)),
        out_shape=jax.ShapeDtypeStruct((2, images, SLOT, PIX // 2), BF),
        compiler_params=pltpu.CompilerParams(vmem_limit_bytes=24 * 2**20),
        cost_estimate=pl.CostEstimate(flops=8 * 10**8, bytes_accessed=6 * 2**20, transcendentals=0),
        name="prep",
    )(pixels, shuffle)


def head_mask(rows):
    lane = lax.broadcasted_iota(jnp.int32, (rows, WIDTH), 1) // HEAD_DIM
    row = lax.broadcasted_iota(jnp.int32, (rows, WIDTH), 0) % HEADS
    return lane == row


def norm_parts(values):
    center = values - jnp.mean(values, axis=-1, keepdims=True)
    rstd = lax.rsqrt(jnp.mean(center * center, axis=-1, keepdims=True) + EPS_NORM)
    return center * rstd, rstd


def norm_back(grad, gain, xhat, rstd):
    gy = grad * gain
    return rstd * (
        gy - jnp.mean(gy, axis=-1, keepdims=True) - xhat * jnp.mean(gy * xhat, axis=-1, keepdims=True)
    )


def rowsum(values):
    return jnp.sum(values, axis=0, keepdims=True)


def to_halves(values, shuffle):
    first, second = [], []
    for block in range(values.shape[1] // 256):
        moved = low(dot(values[:, 256 * block : 256 * block + 256], shuffle))
        first.append(moved[:, :128])
        second.append(moved[:, 128:])
    return jnp.concatenate(first, axis=1), jnp.concatenate(second, axis=1)


def to_natural(first, second, shuffle):
    out = []
    for block in range(first.shape[1] // 128):
        lanes = slice(128 * block, 128 * block + 128)
        both = jnp.concatenate([first[:, lanes], second[:, lanes]], axis=1)
        out.append(low(dot(both, shuffle, NT)))
    return jnp.concatenate(out, axis=1)


R_PATCH, R_GAIN1, R_SHIFT1, R_VB, R_OB, R_GAIN2, R_SHIFT2 = 51, 52, 53, 55, 56, 57, 58
R_C2, R_GAINF, R_SHIFTF, R_SMALL = 63, 64, 65, 66
QUARTER = 128


def partner_kernel(raw_ref, out_ref):
    source = lax.broadcasted_iota(jnp.int32, (PROJ, PROJ), 0)
    target = lax.broadcasted_iota(jnp.int32, (PROJ, PROJ), 1)
    moved = ((source // 16) % 2) * (PROJ // 2) + (source // 32) * 16 + source % 16
    select = low((moved == target).astype(F32))
    out_ref[...] = low(dot(raw_ref[...].reshape(-1, PROJ), select))


def forward_kernel(segments, images, where_ref, pix_ref, rows_ref, valid_ref, shuffle_ref, *refs):
    count = len(segments)
    own, peer = refs[:count], refs[count : 2 * count]
    (
        hid_ref, xhat_ref, rstd_ref, p_ref, pooled_ref, mass_ref, wv_ref, wo_ref, qk_ref, o_ref,
        resid_ref, low_ref, acc_ref, pool_ref, half_ref, table_ref, sems,
    ) = refs[2 * count :]
    col, core = where_ref[0], where_ref[1]
    waits = ([], [])
    for flip, group in ((0, own), (1, peer)):
        half = core ^ flip
        for (source, parts, late), ref in zip(segments, group):
            block = col ^ source
            for row, lane, rows in parts:
                part = ref.at[pl.ds(row, rows)]
                line = pl.multiple_of(block * 512 + lane, 128)
                copy = pltpu.make_async_copy(part, table_ref.at[half, pl.ds(line, rows)], sems.at[flip])
                copy.start()
                waits[flip].append(copy)
            if late >= 0:
                part = ref.at[pl.ds(late, QUARTER)]
                line = pl.multiple_of(block * QUARTER, QUARTER)
                copy = pltpu.make_async_copy(part, wo_ref.at[half, pl.ds(line, QUARTER)], sems.at[2])
                copy.start()
                waits[1].append(copy)
                part = ref.at[pl.ds(late + QUARTER, HEADS)]
                copy = pltpu.make_async_copy(part, half_ref.at[half, block], sems.at[3])
                copy.start()
                waits[1].append(copy)
    patch = rows_ref[2 : 1 + TOKS] + rows_ref[R_PATCH : R_PATCH + 1]
    class_state = rows_ref[0:1] + rows_ref[1:2]
    for i in range(images):
        acc_ref[SLOT * i : SLOT * i + PATCHES] = patch
        acc_ref[SLOT * i + PATCHES : SLOT * i + TOKS] = class_state
        acc_ref[SLOT * i + TOKS : SLOT * (i + 1)] = jnp.zeros((SLOT - TOKS, WIDTH), F32)
    for copy in waits[0]:
        copy.wait()
    acc_ref[...] += dot(pix_ref[core], table_ref[core, :1536])
    for copy in waits[1]:
        copy.wait()
    acc_ref[...] += dot(pix_ref[1 - core], table_ref[1 - core, :1536])
    wv_ref[...] = table_ref[:, 1536:]
    shuffle = shuffle_ref[...]
    gain, shift, value_bias = (rows_ref[r : r + 1] for r in (R_GAIN1, R_SHIFT1, R_VB))
    half = WIDTH // 2
    qk = to_natural(half_ref[0, 0, :, :half], half_ref[1, 0, :, :half], shuffle)
    qk_ref[...] = qk
    valid = valid_ref[...] > 0
    for i in range(images):
        part = slice(SLOT * i, SLOT * (i + 1))
        xhat, rstd = norm_parts(acc_ref[part])
        hid = low(xhat * gain + shift)
        xhat_ref[part] = xhat
        rstd_ref[part] = jnp.broadcast_to(rstd, (SLOT, 128))
        hid_ref[part] = hid
        scores = jnp.where(valid[part], dot(hid, qk, NT), MASKED)
        e = jnp.exp(scores - jnp.max(scores, axis=0, keepdims=True))
        p = e / jnp.sum(e, axis=0, keepdims=True)
        p_ref[part] = p
        pb = low(p)
        pool_ref[HEADS * i : HEADS * (i + 1)] = low(dot(pb, hid, TN))
        mass_ref[HEADS * i : HEADS * (i + 1)] = dot(pb, jnp.ones((SLOT, 128), BF), TN)
    pooled_ref[0], pooled_ref[1] = to_halves(pool_ref[...], shuffle)
    rows = images * HEADS
    mixed = dot(pooled_ref[0], wv_ref[0]) + dot(pooled_ref[1], wv_ref[1])
    mixed = mixed + mass_ref[:, 0:1] * value_bias
    mixed = jnp.where(head_mask(rows), mixed, 0.0)
    joined = low(jnp.sum(mixed.reshape(images, HEADS, WIDTH), axis=1))
    first, second = to_halves(joined, shuffle)
    o_ref[:, : WIDTH // 2] = first
    o_ref[:, WIDTH // 2 :] = second
    resid = class_state + dot(first, wo_ref[0]) + dot(second, wo_ref[1])
    resid = resid + rows_ref[R_OB : R_OB + 1]
    resid_ref[...] = resid
    xhat, _ = norm_parts(resid)
    hidden = low(xhat * rows_ref[R_GAIN2 : R_GAIN2 + 1] + rows_ref[R_SHIFT2 : R_SHIFT2 + 1])
    low_ref[...] = jnp.broadcast_to(hidden[None], low_ref.shape)


def forward_call(segments, images, where, pix, own, peer, rows, valid, shuffle):
    tokens = images * SLOT
    outs = [
        shape((tokens, WIDTH), BF),
        shape((tokens, WIDTH), F32),
        shape((tokens, 128), F32),
        shape((tokens, HEADS), F32),
        shape((2, images * HEADS, WIDTH // 2), BF),
        shape((images * HEADS, 128), F32),
        shape((2, WIDTH // 2, WIDTH), BF),
        shape((2, WIDTH // 2, WIDTH), BF),
        shape((HEADS, WIDTH), BF),
        shape((images, WIDTH), BF),
        shape((images, WIDTH), F32),
        shape((8, images, WIDTH), BF),
    ]
    scratch = [
        pltpu.VMEM((tokens, WIDTH), F32),
        pltpu.VMEM((images * HEADS, WIDTH), BF),
        pltpu.VMEM((2, 4, HEADS, WIDTH), BF),
        pltpu.VMEM((2, 2048, WIDTH), BF),
        pltpu.SemaphoreType.DMA((4,)),
    ]
    return call(
        functools.partial(forward_kernel, segments, images), "forward", [where],
        [pix, rows, valid, shuffle], outs, scratch, mib=52, flops=4 * 10**9,
        far=[*own, *peer],
    )


def fetch(pick_ref, slot, candidates, out_ref, sem):
    for number, candidate in enumerate(candidates):

        @pl.when(pick_ref[slot] == number)
        def _():
            pltpu.make_async_copy(candidate, out_ref, sem).start()


def arrived(candidate, out_ref, sem):
    pltpu.make_async_copy(candidate, out_ref, sem).wait()


def ff_kernel(pick_ref, hid_ref, bias_ref, *refs):
    candidates, (pre_ref, act_ref, part_ref, w1_ref, w2_ref, sems) = refs[:6], refs[6:]
    fetch(pick_ref, 0, candidates, w1_ref, sems.at[0])
    fetch(pick_ref, 1, candidates, w2_ref, sems.at[1])
    hidden = hid_ref[...].reshape(-1, WIDTH)
    arrived(candidates[0], w1_ref, sems.at[0])
    pre = dot(hidden, w1_ref[...], NT) + bias_ref[...]
    pre_ref[...] = pre
    active = low(0.5 * pre * (1.0 + lax.erf(pre * (0.5**0.5))))
    act_ref[...] = active
    arrived(candidates[0], w2_ref, sems.at[1])
    part_ref[...] = low(dot(active, w2_ref[...])).reshape(part_ref.shape)


def ff_back_kernel(pick_ref, dst_ref, pre_ref, *refs):
    candidates, (dpre_ref, sum_ref, part_ref, w1_ref, w2_ref, sems) = refs[:6], refs[6:]
    fetch(pick_ref, 1, candidates, w2_ref, sems.at[1])
    fetch(pick_ref, 0, candidates, w1_ref, sems.at[0])
    d_state = dst_ref[...].reshape(-1, WIDTH)
    pre = pre_ref[...]
    slope = 0.5 * (1.0 + lax.erf(pre * (0.5**0.5))) + pre * jnp.exp(-0.5 * pre * pre) * (
        1.0 / (2.0 * math.pi) ** 0.5
    )
    arrived(candidates[0], w2_ref, sems.at[1])
    d_pre = low(dot(d_state, w2_ref[...], NT) * slope)
    dpre_ref[...] = d_pre
    sum_ref[...] = rowsum(d_pre.astype(F32))
    arrived(candidates[0], w1_ref, sems.at[0])
    part_ref[...] = low(dot(d_pre, w1_ref[...])).reshape(part_ref.shape)


def ff_call(kernel, name, pick, arrays, candidates, outs):
    moved = sum(a.size * a.dtype.itemsize for a in list(arrays) + list(outs))
    return pl.pallas_call(
        kernel,
        in_specs=[smem()]
        + [vmem()] * len(arrays)
        + [pl.BlockSpec(memory_space=pl.ANY)] * len(candidates),
        out_specs=[vmem()] * len(outs),
        out_shape=list(outs),
        scratch_shapes=[
            pltpu.VMEM((512, WIDTH), BF),
            pltpu.VMEM((512, WIDTH), BF),
            pltpu.SemaphoreType.DMA((2,)),
        ],
        compiler_params=pltpu.CompilerParams(vmem_limit_bytes=24 * 2**20),
        cost_estimate=pl.CostEstimate(
            flops=2 * 10**8, bytes_accessed=moved + 2 * 2**20, transcendentals=0
        ),
        name=name,
    )(pick, *arrays, *candidates)


def head_kernel(
    where_ref, part_ref, resid_ref, pj_ref, pjp_ref, partners_ref, target_ref, rows_ref,
    state_ref, low_ref, final_ref, dz_ref, vec_ref,
):
    images = resid_ref.shape[0]
    state = resid_ref[...] + jnp.sum(part_ref[...].astype(F32), axis=0) + rows_ref[R_C2 : R_C2 + 1]
    gain = rows_ref[R_GAINF : R_GAINF + 1]
    xhat, rstd = norm_parts(state)
    final = low(xhat * gain + rows_ref[R_SHIFTF : R_SHIFTF + 1])
    final_ref[...] = final
    z_own, z_peer = dot(final, pj_ref[...], NT), dot(final, pjp_ref[...], NT)
    square = jnp.sum(z_own * z_own, axis=-1, keepdims=True) + jnp.sum(
        z_peer * z_peer, axis=-1, keepdims=True
    )
    inv = lax.rsqrt(square + EPS_NORM)
    core = where_ref[1]
    half = PROJ // 2
    own_lanes = pl.ds(pl.multiple_of(core * half, 128), half)
    peer_lanes = pl.ds(pl.multiple_of((1 - core) * half, 128), half)
    ptn_own, ptn_peer = partners_ref[:, own_lanes], partners_ref[:, peer_lanes]
    logits = dot(low(z_own * inv), ptn_own, NT) + dot(low(z_peer * inv), ptn_peer, NT)
    logits = logits / SOFTMAX_SCALE
    total = logits.shape[1]
    hit = lax.broadcasted_iota(jnp.int32, (images, total), 1) == target_ref[...]
    top = jnp.max(logits, axis=-1, keepdims=True)
    e = jnp.exp(logits - top)
    mass = jnp.sum(e, axis=-1, keepdims=True)
    aim = jnp.sum(jnp.where(hit, logits, 0.0), axis=-1, keepdims=True)
    losses = jnp.log(mass) + top - aim
    d_logits = (e / mass - jnp.where(hit, 1.0, 0.0)) / total
    g_logits = low(d_logits / SOFTMAX_SCALE)
    d_own, d_peer = dot(g_logits, ptn_own), dot(g_logits, ptn_peer)
    along = jnp.sum(d_own * z_own, axis=-1, keepdims=True) + jnp.sum(
        d_peer * z_peer, axis=-1, keepdims=True
    )
    shrink = along * inv * inv * inv
    dz_own, dz_peer = low(d_own * inv - z_own * shrink), low(d_peer * inv - z_peer * shrink)
    dz_ref[:, own_lanes] = dz_own
    dz_ref[:, peer_lanes] = dz_peer
    d_final = dot(dz_own, pj_ref[...]) + dot(dz_peer, pjp_ref[...])
    d_state = norm_back(d_final, gain, xhat, rstd)
    state_ref[...] = d_state
    low_ref[...] = jnp.broadcast_to(low(d_state)[None], low_ref.shape)
    vec_ref[...] = jnp.zeros_like(vec_ref)
    vec_ref[0:1] = rowsum(d_state)
    vec_ref[1:2] = rowsum(d_final * xhat)
    vec_ref[2:3] = rowsum(d_final)
    vec_ref[3:4] = jnp.broadcast_to(rowsum(losses) / total, (1, WIDTH))


def backward_kernel(
    images, where_ref, part_ref, dstate_ref, resid_ref, wo_ref, wv_ref, hid_ref, xhat_ref,
    rstd_ref, p_ref, mass_ref, qk_ref, rows_ref, shuffle_ref,
    de_ref, do_ref, dres_ref, pos_ref, vec_ref, pull_ref, dom_ref, da_ref,
):
    rows = images * HEADS
    gain, value_bias = rows_ref[R_GAIN1 : R_GAIN1 + 1], rows_ref[R_VB : R_VB + 1]
    shuffle = shuffle_ref[...]
    vec_ref[...] = jnp.zeros_like(vec_ref)
    d_two = jnp.sum(part_ref[...].astype(F32), axis=0)
    xhat2, rstd2 = norm_parts(resid_ref[...])
    d_resid = dstate_ref[...] + norm_back(d_two, rows_ref[R_GAIN2 : R_GAIN2 + 1], xhat2, rstd2)
    vec_ref[3:4] = rowsum(d_resid)
    vec_ref[4:5] = rowsum(d_two * xhat2)
    vec_ref[5:6] = rowsum(d_two)
    d_low = low(d_resid)
    dres_ref[...] = d_low
    d_att = to_natural(
        low(dot(d_low, wo_ref[0], NT)), low(dot(d_low, wo_ref[1], NT)), shuffle
    )
    do_ref[...] = d_att
    spread = jnp.broadcast_to(d_att.reshape(images, 1, WIDTH).astype(F32), (images, HEADS, WIDTH))
    wide = jnp.where(head_mask(rows), spread.reshape(rows, WIDTH), 0.0)
    dom_ref[...] = low(wide)
    vec_ref[2:3] = rowsum(wide * mass_ref[:, 0:1])
    da_ref[...] = to_natural(
        low(dot(dom_ref[...], wv_ref[0], NT)), low(dot(dom_ref[...], wv_ref[1], NT)), shuffle
    )
    qk = qk_ref[...]
    bias_rows = low(jnp.broadcast_to(value_bias, (8, WIDTH)))
    real = lax.broadcasted_iota(jnp.int32, (SLOT, WIDTH), 0) < PATCHES
    for i in range(images):
        part = slice(SLOT * i, SLOT * (i + 1))
        mine = slice(HEADS * i, HEADS * (i + 1))
        hid, p, da = hid_ref[part], p_ref[part], da_ref[mine]
        dp = dot(hid, da, NT) + dot(bias_rows, dom_ref[mine], NT)[0:1]
        ds = low(p * (dp - rowsum(p * dp)))
        dh = dot(low(p), da) + dot(ds, qk)
        pull = dot(ds, hid, TN)
        xhat, rstd = xhat_ref[part], rstd_ref[part, 0:1]
        dx = norm_back(dh, gain, xhat, rstd)
        de_ref[part] = low(jnp.where(real, dx, 0.0))
        vec_ref[0:1] += rowsum(dh * xhat)
        vec_ref[1:2] += rowsum(dh)
        if i == 0:
            pos_ref[...] = dx
            pull_ref[...] = pull
        else:
            pos_ref[...] += dx
            pull_ref[...] += pull


def backward_call(images, where, arrays):
    tokens = images * SLOT
    outs = [
        shape((tokens, WIDTH), BF),
        shape((images, WIDTH), BF),
        shape((images, WIDTH), BF),
        shape((SLOT, WIDTH), F32),
        shape((8, WIDTH), F32),
        shape((HEADS, WIDTH), F32),
    ]
    scratch = [pltpu.VMEM((images * HEADS, WIDTH), BF)] * 2
    return call(
        functools.partial(backward_kernel, images), "backward", [where], arrays, outs, scratch
    )


def embed_grad_kernel(
    images, plan, where_ref, pix_ref, pixp_ref, de_ref, dep_ref, pooled_ref, pooledp_ref,
    do_ref, dop_ref, *refs,
):
    came = sum(entry[3] >= 0 for entry in plan)
    got_refs, out_refs = list(refs[:came]), refs[came:]
    col = where_ref[0]
    heads = images * HEADS
    for (source, first, rows, at), out_ref in zip(plan, out_refs):
        block = col ^ source
        got_ref = got_refs.pop(0) if at >= 0 else None

        def store(total, got_ref=got_ref, at=at, out_ref=out_ref):
            if got_ref is None:
                out_ref[...] = total.astype(out_ref.dtype)
                return
            end = at + got_ref.shape[0]
            out_ref[at:end] = (total[at:end] + got_ref[...].astype(F32)).astype(out_ref.dtype)
            if at > 0:
                out_ref[:at] = total[:at].astype(out_ref.dtype)
            if end < total.shape[0]:
                out_ref[end:] = total[end:].astype(out_ref.dtype)

        @pl.when(block < 3)
        def _():
            lanes = pl.ds(pl.multiple_of(block * 512 + first, 128), rows)
            store(dot(pix_ref[:, lanes], de_ref[...], TN) + dot(pixp_ref[:, lanes], dep_ref[...], TN))

        @pl.when(block == 3)
        def _():
            total = None
            for pooled, do in ((pooled_ref, do_ref), (pooledp_ref, dop_ref)):
                spread = jnp.broadcast_to(
                    do[...].reshape(images, 1, WIDTH).astype(F32), (images, HEADS, WIDTH)
                )
                wide = low(jnp.where(head_mask(heads), spread.reshape(heads, WIDTH), 0.0))
                term = dot(pooled[:, first : first + rows], wide, TN)
                total = term if total is None else total + term
            store(total)


def embed_grad_call(images, name, plan, where, arrays, got=()):
    outs = [shape((rows, WIDTH), F32 if source == 0 else BF) for source, _, rows, _ in plan]
    return call(
        functools.partial(embed_grad_kernel, images, plan), name, [where], [*arrays, *got], outs
    )


def to_natural_exact(first, second, shuffle):
    wide = shuffle.astype(F32)
    out = []
    for block in range(first.shape[1] // 128):
        lanes = slice(128 * block, 128 * block + 128)
        both = jnp.concatenate([first[:, lanes], second[:, lanes]], axis=1)
        out.append(dot(both, wide, NT, precision=lax.Precision.HIGHEST))
    return jnp.concatenate(out, axis=1)


def collect_kernel(
    where_ref, pos_ref, vec_ref, head_ref, sum_ref, pull_ref, shuffle_ref, sent_ref, out_ref
):
    col, core = where_ref[0], where_ref[1]
    out_ref[...] = jnp.zeros_like(out_ref)
    top = pos_ref[PATCHES:TOKS] + vec_ref[3:4]
    out_ref[0:1] = top
    out_ref[1:2] = top
    patches = pos_ref[0:PATCHES]
    out_ref[2 : 1 + TOKS] = patches
    out_ref[R_PATCH : R_PATCH + 1] = rowsum(patches)
    out_ref[R_GAIN1 : R_SHIFT1 + 1] = vec_ref[0:2]
    out_ref[R_VB : R_VB + 1] = vec_ref[2:3]
    out_ref[R_OB : R_SHIFT2 + 1] = vec_ref[3:6]
    sums = jnp.broadcast_to(sum_ref[...], (8, WIDTH // 2))
    nothing = jnp.zeros_like(sums)
    row = to_natural_exact(
        jnp.where(core == 0, sums, nothing), jnp.where(core == 0, nothing, sums), shuffle_ref[...]
    )
    for block in range(4):
        mine = (col + 1) % 4 == block
        out_ref[R_SHIFT2 + 1 + block : R_SHIFT2 + 2 + block] = jnp.where(mine, row[0:1], 0.0)
    out_ref[R_C2 : R_SHIFTF + 1] = head_ref[0:3]
    out_ref[R_SMALL : R_SMALL + HEADS] = pull_ref[...]
    out_ref[R_SMALL + HEADS : R_SMALL + HEADS + 1] = head_ref[3:4]
    for number in range(sent_ref.shape[0]):
        sent_ref[number] = out_ref[3 * number : 3 * number + 3]


def share_kernel(got_ref, sent_ref):
    sent_ref[...] = jnp.broadcast_to(jnp.sum(got_ref[...], axis=0, keepdims=True), sent_ref.shape)


def query_back_kernel(core_ref, got_ref, w_ref, shuffle_ref, dq_ref, pull_ref, total_ref):
    for number in range(got_ref.shape[0]):
        total_ref[3 * number : 3 * number + 3] = got_ref[number]
    wide = shuffle_ref[...].astype(F32)
    pull = total_ref[R_SMALL : R_SMALL + HEADS]
    is_one = core_ref[0] == 1
    out = []
    for block in range(WIDTH // 256):
        moved = dot(pull[:, 256 * block : 256 * block + 256], wide, precision=lax.Precision.HIGHEST)
        out.append(jnp.where(is_one, moved[:, 128:], moved[:, :128]))
    half = jnp.concatenate(out, axis=1)
    pull_ref[...] = half
    d_query = jnp.where(head_mask(HEADS), dot(low(half), w_ref[...]), 0.0)
    dq_ref[...] = jnp.broadcast_to(rowsum(d_query) * SCALE, dq_ref.shape)


def complete_kernel(total_ref, reports_ref, rows_ref, shuffle_ref, out_ref, norm_ref):
    out_ref[...] = total_ref[0:R_SMALL]
    half = WIDTH // 2
    first = jnp.broadcast_to(reports_ref[6, 2:3, :half], (8, half))
    second = jnp.broadcast_to(reports_ref[7, 2:3, :half], (8, half))
    d_hidden = to_natural_exact(first, second, shuffle_ref[...])[0:1]
    xhat, rstd = norm_parts(rows_ref[0:1] + rows_ref[1:2])
    d_class = norm_back(d_hidden, rows_ref[R_GAIN1 : R_GAIN1 + 1], xhat, rstd)
    out_ref[0:1] += d_class
    out_ref[1:2] += d_class
    out_ref[R_GAIN1 : R_GAIN1 + 1] += d_hidden * xhat
    out_ref[R_SHIFT1 : R_SHIFT1 + 1] += d_hidden
    out_ref[R_SHIFT1 + 1 : R_SHIFT1 + 2] = reports_ref[6, 1:2]
    grads = out_ref[...]
    square = jnp.sum(jnp.sum(grads * grads, axis=0, keepdims=True), axis=1, keepdims=True)
    for number in range(reports_ref.shape[0]):
        square = square + reports_ref[number, 0:1, 0:1]
    norm_ref[...] = jnp.broadcast_to(jnp.sqrt(square), (8, 128))


def owner_kernel(role_ref, pull_ref, heads_ref, class_ref, dq_ref, *refs):
    rows, out_ref = refs[:6], refs[6]
    chip, core = role_ref[0], role_ref[1]
    half = WIDTH // 2
    base = 3 * WIDTH

    def product(left, right):
        total = None
        for piece in rows:
            term = dot(left(piece), right(piece), TN)
            total = term if total is None else total + term
        return total

    @pl.when((chip >= 7) & (chip <= 14))
    def _():
        is_two = chip >= 11
        out_ref[...] = product(
            lambda piece: jnp.where(is_two, piece[:, :half], piece[:, half:WIDTH]),
            lambda piece: jnp.where(is_two, piece[:, 2 * WIDTH : base], piece[:, WIDTH : 2 * WIDTH]),
        )

    @pl.when(chip == 6)
    def _():
        lanes = pl.ds(pl.multiple_of(base + core * half, 128), half)
        out_ref[...] = product(lambda piece: piece[:, lanes], lambda piece: piece[:, base + WIDTH :])

    @pl.when(chip == 15)
    def _():
        lanes = pl.ds(pl.multiple_of(base + core * (PROJ // 2), 128), PROJ // 2)
        out_ref[: PROJ // 2] = product(
            lambda piece: piece[:, lanes],
            lambda piece: piece[:, base + PROJ : base + PROJ + WIDTH],
        )
        out_ref[PROJ // 2 :] = jnp.zeros((512 - PROJ // 2, WIDTH), F32)

    @pl.when(chip == 4)
    def _():
        out_ref[...] = dot(
            pull_ref[...], heads_ref[...].astype(F32), TN, precision=lax.Precision.HIGHEST
        )

    @pl.when(chip == 3)
    def _():
        out_ref[...] = dot(
            class_ref[...].astype(F32), jnp.concatenate([dq_ref[0:1], jnp.zeros((7, WIDTH), F32)]),
            TN, precision=lax.Precision.HIGHEST,
        )


def finish_kernel(
    role_ref, formed_ref, dq_ref, toward_ref, total_ref, first_ref, second_ref, aside_ref, third_ref,
    out_ref, top_ref, end_ref, report_ref,
):
    chip = role_ref[0]

    @pl.when(chip < 3)
    def _():
        out_ref[...] = total_ref[...] + first_ref[...].astype(F32) + second_ref[...].astype(F32)

    @pl.when(chip == 5)
    def _():
        out_ref[...] = (
            second_ref[...].astype(F32) + aside_ref[...].astype(F32) + third_ref[...].astype(F32)
        )

    @pl.when((chip >= 3) & (chip != 5))
    def _():
        out_ref[...] = formed_ref[...]

    edge = top_ref.shape[0]
    top_ref[...] = out_ref[:edge]
    end_ref[...] = out_ref[-edge:]
    grads = out_ref[...]
    report_ref[0:1] = jnp.broadcast_to(
        jnp.sum(jnp.sum(grads * grads, axis=0, keepdims=True), axis=1, keepdims=True), (1, WIDTH)
    )
    report_ref[1:2] = dq_ref[...]
    report_ref[2:3] = jnp.concatenate([toward_ref[...], jnp.zeros((1, WIDTH // 2), F32)], axis=1)


def update_kernel(
    source_ref, scalar_ref, before_ref, grad_ref, behind_ref, w_ref, m_ref, v_ref,
    nw_ref, nm_ref, nv_ref,
):
    step = pl.program_id(0)
    slots = grad_ref.shape[0]
    factor, fix_one, fix_two = scalar_ref[0], scalar_ref[1], scalar_ref[2]
    for k in range(w_ref.shape[0]):
        at = source_ref[step * w_ref.shape[0] + k]
        inside = (at >= 0) & (at < slots)
        grad = jnp.where(
            inside,
            grad_ref[jnp.clip(at, 0, slots - 1)],
            jnp.where(
                at < 0,
                before_ref[jnp.clip(at + JITTER, 0, JITTER - 1)],
                behind_ref[jnp.clip(at - slots, 0, JITTER - 1)],
            ),
        )
        grad = grad * jnp.where(at >= -JITTER, factor, 0.0)
        weight = w_ref[k]
        first = BETA_ONE * m_ref[k] + (1.0 - BETA_ONE) * grad
        second = BETA_TWO * v_ref[k] + (1.0 - BETA_TWO) * grad * grad
        nm_ref[k] = first
        nv_ref[k] = second
        nw_ref[k] = weight - LEARN_RATE * (
            (first * fix_one) / (jnp.sqrt(second * fix_two) + ADAM_EPS) + DECAY_RATE * weight
        )


def update_call(source, scalars, before, grads, behind, masters, first, second):
    slots, part, width = masters.shape
    block = 4
    spec = pl.BlockSpec((block, part, width), lambda i: (i, 0, 0))
    return pl.pallas_call(
        update_kernel,
        grid=(slots // block,),
        in_specs=[smem(), smem(), vmem(), vmem(), vmem(), spec, spec, spec],
        out_specs=[spec] * 3,
        out_shape=[shape(masters.shape, F32)] * 3,
        compiler_params=pltpu.CompilerParams(vmem_limit_bytes=58 * 2**20),
        cost_estimate=pl.CostEstimate(
            flops=2 * 10**7, bytes_accessed=7 * masters.size * 4, transcendentals=0
        ),
        name="update",
    )(source, scalars, before, grads, behind, masters, first, second)


CHIPS = 16
CHIP = ("z", "y", "x")
ALL = ("z", "y", "x", "c")
PLANE = ("y", "x", "c")
FLIP_X = [(i, i ^ 1) for i in range(CHIPS)]
FLIP_Y = [(i, i ^ 2) for i in range(CHIPS)]
FLIP_CORE = [(0, 1), (1, 0)]


def hop(values, pairs):
    return lax.ppermute(values, CHIP, pairs)


def swap(values):
    return lax.ppermute(values, "c", FLIP_CORE)


def after(values, *others):
    return lax.optimization_barrier((values,) + others)[0]


def among(img, chips):
    hit = img == chips[0]
    for chip in chips[1:]:
        hit = hit | (img == chip)
    return hit


def choose(img, cases, otherwise):
    out = otherwise
    for chips, values in cases:
        out = jnp.where(among(img, chips), values, out)
    return out


def together(*values):
    return lax.optimization_barrier(values)


def plane_gather(block, diagonal_by_x):
    by_x, by_y, block_peer = hop(block, FLIP_X), hop(block, FLIP_Y), swap(block)
    proj_top = jnp.where(img == 15, corner[0], corner[1] + corner[2] + corner[3])
    proj_one = hop(proj_top, [(12, 4), (13, 5), (14, 6), (15, 7)])
    diagonal = hop(by_y, FLIP_X) if diagonal_by_x else hop(by_x, FLIP_Y)
    return [block, by_x, by_y, diagonal]


def in_plane(values):
    return lax.all_to_all(values, PLANE, 0, 0, tiled=True)


def from_all(values):
    sent = jnp.broadcast_to(values[None], (2 * CHIPS,) + values.shape)
    return lax.all_to_all(sent, ALL, 0, 0, tiled=True)


def natural(values):
    lead = values.shape[:-2]
    units = values.shape[-1] // 16
    split = values.reshape(lead + (2, units, 16))
    return jnp.swapaxes(split, -3, -2).reshape(lead + (units * 32,))


def halves(values):
    lead = values.shape[:-1]
    units = values.shape[-1] // 32
    return jnp.swapaxes(values.reshape(lead + (units, 2, 16)), -3, -2).reshape(
        lead + (2, units * 16)
    )


def per_device_16(
    pixels, keep_mask, partner_index, partner_emb, masters, first_moment_slots,
    second_moment_slots, slot_unit_index, small_params, small_first, small_second, step_count,
):
    img, core = lax.axis_index(CHIP), lax.axis_index("c")
    col, plane = img % 4, img // 4
    images = pixels.shape[0]
    slots = masters.shape[0]
    is_one = core == 1
    where = jnp.stack([col, core]).astype(jnp.int32)
    shuffle = shuffle_matrix()
    rows = small_params
    class_state = small_params[0] + small_params[1]

    def mine_of(pair):
        return jnp.where(is_one, pair[1], pair[0])

    def theirs_of(pair):
        return jnp.where(is_one, pair[0], pair[1])

    partners = from_all(partner_emb)
    near = slots_near(slot_unit_index, img, slots)
    held = low(masters)
    ids = img * slots + jnp.arange(slots, dtype=jnp.int32)
    matches = [near[s : s + slots] == ids for s in range(2 * JITTER + 1)]
    middle = pick(held[6:26], [m[8:24] for m in matches], 16).reshape(256, WIDTH)
    one_a = hop(middle, [(0, 4), (1, 5), (2, 6), (5, 7)])
    before, behind = halo(after(held, middle), CHIPS, CHIP)
    lower = pick(jnp.concatenate([before, held[:10]]), [m[:8] for m in matches], 8)
    upper = pick(jnp.concatenate([held[22:], behind]), [m[24:] for m in matches], 8)
    outer = jnp.concatenate([lower, upper]).reshape(256, WIDTH)
    own_w = jnp.concatenate([outer[:128], middle, outer[128:]])
    class_hidden = low(layer_norm(class_state, small_params[R_GAIN1], small_params[R_SHIFT1]))
    class_half = mine_of(halves(class_hidden))
    query = dot(class_half[None], own_w)
    query = hop(query + swap(query), [(3, 4)])
    wo_quarter = hop(own_w[384:], [(6, 7)]) + hop(own_w[:128], [(6, 4)])
    wo_quarter = wo_quarter + hop(own_w[128:256], [(6, 5)])
    wo_quarter = jnp.where(img == 6, own_w[256:384], wo_quarter)
    down_one = hop(
        own_w,
        [(12, 8), (13, 9), (14, 10), (11, 7), (8, 4), (9, 5), (10, 6), (7, 3)],
    )
    one_a, outer = together(one_a, outer)
    one_b = hop(outer, [(0, 4), (1, 5), (2, 6), (5, 7)])
    two_a = hop(one_a, [(4, 8), (5, 9), (6, 10), (7, 11)])
    pix = prep(after(pixels, one_a), shuffle).reshape(2, images * SLOT, PIX // 2)
    corner = after(own_w[: PROJ // 2], one_a)
    corner = [corner] + [hop(corner, [(15, 15 ^ flip)]) for flip in (1, 2, 3)]
    query = low((query + small_params[R_SHIFT1 + 1 : R_SHIFT1 + 2]) * SCALE)
    query_heads = jnp.where(head_mask(HEADS), query, jnp.zeros((), BF))
    pulled = jnp.pad(low(dot(query_heads, own_w, NT)), ((0, 0), (0, WIDTH // 2)))
    one_b, two_a, wo_quarter, pulled, down_one = together(
        one_b, two_a, wo_quarter, pulled, down_one
    )
    mid_b = jnp.concatenate([one_b, wo_quarter, pulled])
    two_b = hop(mid_b, [(4, 8), (5, 9), (6, 10), (7, 11)])
    three_a = hop(
        jnp.where(img == 7, one_a, two_a), [(8, 12), (9, 13), (10, 14), (11, 15), (7, 3)]
    )
    low_b = hop(mid_b[256:], [(4, 0), (5, 1), (6, 2)])
    two_b, three_a, low_b, pix, partners = together(two_b, three_a, low_b, pix, partners)
    block_a = jnp.where(img < 3, middle, one_a + two_a + three_a)
    x_a, y_a = hop(block_a, FLIP_X), hop(block_a, FLIP_Y)
    three_b = hop(
        jnp.where(img == 7, mid_b, two_b), [(8, 12), (9, 13), (10, 14), (11, 15), (7, 3)]
    )
    pix_own, pix_send = mine_of(pix), theirs_of(pix)
    x_a, y_a, three_b, pix_own, pix_send, *corner = together(
        x_a, y_a, three_b, pix_own, pix_send, *corner
    )
    block_b = jnp.where(
        img < 3,
        jnp.concatenate([outer, low_b]),
        jnp.where(plane == 1, mid_b, jnp.where(plane == 2, two_b, three_b)),
    )
    x_b, y_b = hop(block_b, FLIP_X), hop(block_b, FLIP_Y)
    d_a = hop(y_a, FLIP_X)
    down_two = hop(
        after(down_one, three_b), [(8, 4), (9, 5), (10, 6), (7, 3), (4, 0), (5, 1), (6, 2)]
    )
    proj_top = jnp.where(img == 15, corner[0], corner[1] + corner[2] + corner[3])
    proj_one = hop(proj_top, [(12, 4), (13, 5), (14, 6), (15, 7)])
    (partners,) = call(
        partner_kernel, "partners", [], [partners], [shape((2 * CHIPS * images, PROJ), BF)]
    )
    x_b, y_b, d_a = together(x_b, y_b, d_a)
    d_b = hop(x_b, FLIP_Y)
    up_one = hop(
        after(own_w, x_b), [(8, 12), (9, 13), (10, 14), (7, 11), (11, 15)]
    )

    down_three = hop(after(down_two, y_b), [(4, 0), (5, 1), (6, 2)])
    proj_mid = hop(
        after(jnp.where(plane == 3, proj_top, proj_one), x_b),
        [(12, 8), (13, 9), (14, 10), (15, 11), (4, 0), (5, 1), (6, 2), (7, 3)],
    )

    segments, own_pieces, peer_pieces = [], [], []
    for pieces, spans, late in (
        ((block_a, x_a, y_a, d_a), ((0, 128, 256),), -1),
        ((block_b, x_b, y_b, d_b), ((0, 0, 128), (128, 384, 128)), 256),
    ):
        segments += [(source, spans, late) for source in range(4)]
        own_pieces += pieces
        peer_pieces += [swap(piece) for piece in pieces]
    pix_peer = swap(pix_send)
    valid = jnp.concatenate(
        [
            keep_mask,
            jnp.ones((images, 1), jnp.int32),
            jnp.zeros((images, SLOT - TOKS), jnp.int32),
        ],
        axis=1,
    ).reshape(images * SLOT, 1)
    (
        hid, xhat, rstd, p, pooled, mass, wv, wo, qk, attended, resid, hidden_sent,
    ) = forward_call(
        segments, images, where, pix, own_pieces, peer_pieces, rows, valid, shuffle
    )
    pooled_own = mine_of(pooled)
    pooled_peer = swap(theirs_of(pooled))

    hidden_all = in_plane(hidden_sent)
    up_two = hop(after(up_one, hidden_sent), [(11, 15)])
    ff_block = (col + 1) % 4
    bias_part = lax.dynamic_slice(
        small_params[R_SHIFT2 + 1 : R_C2].reshape(4, 32, 2, 16),
        (ff_block, 0, core, 0),
        (1, 32, 1, 16),
    ).reshape(1, 512)
    candidates = [own_w, up_one, up_two, down_one, down_two, down_three]
    pick_one = choose(
        img, [((15,), 2), ((12, 13, 14, 11), 1), ((4, 5, 6, 3), 3), ((0, 1, 2), 4)], 0
    )
    pick_two = choose(
        img, [((15,), 1), ((8, 9, 10, 7), 3), ((4, 5, 6, 3), 4), ((0, 1, 2), 5)], 0
    )
    picks = jnp.stack([pick_one, pick_two]).astype(jnp.int32)
    preact, active, part = ff_call(
        ff_kernel, "ff", picks, [hidden_all, bias_part], candidates,
        [shape((8 * images, 512), F32), shape((8 * images, 512), BF), shape((8, images, WIDTH), BF)],
    )
    proj = choose(
        plane, [((3,), proj_top), ((1,), proj_one)], after(proj_mid, hidden_sent)
    )
    proj_peer = swap(proj)
    part = in_plane(part)
    d_state, d_state_sent, final, d_projected, head_vec = call(
        head_kernel, "head", [where],
        [part, resid, proj, proj_peer, partners, partner_index[:, None], rows],
        [
            shape((images, WIDTH), F32), shape((8, images, WIDTH), BF), shape((images, WIDTH), BF),
            shape((images, PROJ), BF), shape((8, WIDTH), F32),
        ],
    )
    d_state_all = in_plane(d_state_sent)
    d_preact, d_preact_sum, part = ff_call(
        ff_back_kernel, "ff_back", picks, [d_state_all, preact], candidates,
        [shape((8 * images, 512), BF), shape((1, 512), F32), shape((8, images, WIDTH), BF)],
    )
    part = in_plane(part)

    d_embed, d_attended, d_resid, d_pos, d_vec, pull = backward_call(
        images, where,
        [part, d_state, resid, wo, wv, hid, xhat, rstd, p, mass, qk, rows, shuffle],
    )
    arrays = [
        pix_own, pix_peer, d_embed, swap(d_embed), pooled_own, pooled_peer, d_attended,
        swap(d_attended),
    ]
    far_x, far_y = embed_grad_call(
        images, "embed_grad_far", [(3, 0, 256, -1), (3, 256, 256, -1)], where, arrays
    )
    got_y, got_x = hop(far_x, FLIP_X), hop(far_y, FLIP_Y)
    (own_part,) = embed_grad_call(
        images, "embed_grad_own", [(0, 0, 512, -1)], after(where, far_x), arrays
    )
    extra = after(jnp.concatenate([attended, d_resid, d_projected, final], axis=1), far_x)
    extra = in_plane(jnp.broadcast_to(extra[None], (8,) + extra.shape)).reshape(8 * images, -1)
    d_pos, d_vec, head_vec, d_preact_sum, pull, _ = together(
        d_pos, d_vec, head_vec, d_preact_sum, pull, far_x
    )
    (small_sent,) = call(
        collect_kernel, "collect", [where], [d_pos, d_vec, head_vec, d_preact_sum, pull, shuffle],
        [shape((32, 3, WIDTH), F32)], [pltpu.VMEM((96, WIDTH), F32)],
    )
    got_x, got_y, own_part, extra, small_sent = together(got_x, got_y, own_part, extra, small_sent)
    part_x, part_y = embed_grad_call(
        images, "embed_grad_near", [(1, 0, 512, 256), (2, 0, 512, 0)], where, arrays, (got_x, got_y)
    )
    sum_x, sum_y = hop(part_x, FLIP_X), hop(part_y, FLIP_Y)
    shares = lax.all_to_all(small_sent, ALL, 0, 0, tiled=True)
    roles = jnp.where(
        col == 2,
        extra[:, : 2 * WIDTH],
        jnp.pad(extra[:, 2 * WIDTH :], ((0, 0), (0, WIDTH - PROJ))),
    )
    ff_rows = jnp.concatenate(
        [
            active,
            d_preact,
            hidden_all.reshape(-1, WIDTH),
            d_state_all.reshape(-1, WIDTH),
            roles,
        ],
        axis=1,
    )
    rise = [(i, i + 4) for i in range(12)]
    fall = [(12, 8), (13, 9), (14, 10), (15, 11), (10, 6), (11, 7)]
    up_one, down_one = hop(ff_rows, rise), hop(ff_rows, fall)
    sum_x, sum_y, shares, up_one, down_one = together(sum_x, sum_y, shares, up_one, down_one)
    total = own_part + sum_x.astype(F32) + sum_y.astype(F32)
    sent = low(total)
    first = hop(sent, [(12, 8), (13, 9), (14, 10), (15, 11), (4, 0), (5, 1), (6, 2)])
    aside = hop(sent, [(3, 1), (7, 5)])
    (small_sent,) = call(share_kernel, "share", [], [shares], [shape((32, 3, WIDTH), F32)])
    shares = lax.all_to_all(small_sent, ALL, 0, 0, tiled=True)
    up_two = hop(up_one, rise[4:])
    first, aside, shares, up_two, total = together(first, aside, shares, up_two, total)
    partial = low(total + first.astype(F32))
    second = hop(partial, [(8, 0), (9, 1), (10, 2), (11, 5)])
    third = hop(aside, [(1, 5)])
    up_three = hop(up_two, rise[8:])
    down_two = hop(down_one, fall[4:])
    d_query, pull_half, small_total = call(
        query_back_kernel, "query_back", [core.reshape(1).astype(jnp.int32)],
        [shares, own_w, shuffle],
        [shape((8, WIDTH), F32), shape((HEADS, WIDTH // 2), F32), shape((96, WIDTH), F32)],
    )
    loss = small_total[R_SMALL + HEADS, 0]
    d_query = d_query[0:1]
    d_query = hop(d_query + swap(d_query), [(4, 3)])
    toward = dot(low(d_query), own_w, NT)
    second, third, up_three, down_two, toward = together(second, third, up_three, down_two, toward)

    every = [ff_rows, up_one, up_two, up_three, down_one, down_two]
    class_rows = jnp.concatenate([class_half[None], jnp.zeros((7, WIDTH // 2), BF)])
    role = jnp.stack([img, core]).astype(jnp.int32)
    (formed,) = call(
        owner_kernel, "owner", [role], [pull_half, query_heads, class_rows, d_query, *every],
        [shape((512, WIDTH), F32)],
    )
    edge = shape((JITTER * 16, WIDTH), F32)
    own_grad, top, end, report = call(
        finish_kernel, "finish", [role],
        [formed, d_query, toward, total, first, second, aside, third],
        [shape((512, WIDTH), F32), edge, edge, shape((3, WIDTH), F32)],
    )
    reports = from_all(report)
    before = hop(end, [(i, i + 1) for i in range(CHIPS - 1)]).reshape(JITTER, 16, WIDTH)
    behind = hop(top, [(i + 1, i) for i in range(CHIPS - 1)]).reshape(JITTER, 16, WIDTH)
    small_grad, norm = call(
        complete_kernel, "complete", [], [small_total, reports, rows, shuffle],
        [shape((R_SMALL, WIDTH), F32), shape((8, 128), F32)],
    )
    grad_norm = norm[0, 0]
    factor = 1.0 / jnp.maximum(grad_norm, 1.0)
    own_grad = own_grad.reshape(slots, 16, WIDTH)
    here = near[JITTER : JITTER + slots]
    source = jnp.where(here < UNIT_COUNT, here - img * slots, -100)
    step_value = step_count.astype(F32)
    scalars = jnp.stack(
        [
            factor,
            1.0 / (1.0 - jnp.power(BETA_ONE, step_value)),
            1.0 / (1.0 - jnp.power(BETA_TWO, step_value)),
        ]
    )
    new_masters, new_first, new_second = update_call(
        source, scalars, before, own_grad, behind, masters, first_moment_slots,
        second_moment_slots,
    )
    new_small, new_small_first, new_small_second = adamw(
        small_params, small_grad * factor, small_first, small_second, step_value
    )
    return (
        new_masters, new_first, new_second, new_small, new_small_first, new_small_second,
        loss, grad_norm,
    )


def per_device_any(
    pixels, keep_mask, partner_index, partner_emb, masters, first_moment_slots,
    second_moment_slots, slot_unit_index, small_params, small_first, small_second, step_count,
):
    chips, seq = lax.axis_size("img"), lax.axis_size("seq")
    img = lax.axis_index("img")
    images = pixels.shape[0]
    slots, part = masters.shape[0], masters.shape[1]
    near = slots_near(slot_unit_index, img, slots)
    own_w = to_units(low(masters), near, img, chips)
    gathered = lax.all_gather(own_w, ("img", "seq"), axis=0, tiled=False)
    flat = gathered.reshape(chips, seq, slots, part, WIDTH).transpose(0, 2, 1, 3, 4)
    flat = flat.reshape(chips * slots * ROWS_PER_UNIT, WIDTH)
    bounds = [0, PIX, WIDTH, WIDTH, WIDTH, WIDTH, FF, FF, PROJ]
    parts, offset = [], 0
    for size in bounds[1:]:
        parts.append(flat[offset : offset + size])
        offset += size
    embed_w, query_w, key_w, value_w, output_w, fc_in_w, fc_out_w, proj_w = parts
    (
        class_row, pos_rows, patch_bias, gain_one, shift_one, query_bias, value_bias, out_bias,
        gain_two, shift_two, fc_in_bias, fc_out_bias, gain_end, shift_end,
    ) = small_parts(small_params)
    class_state = class_row + pos_rows[0]
    embedded = jnp.einsum("itp,pd->itd", pixels, embed_w, preferred_element_type=F32)
    tokens = jnp.concatenate(
        [
            jnp.broadcast_to(class_state, (images, 1, WIDTH)),
            embedded + patch_bias + pos_rows[1:],
        ],
        axis=1,
    )
    hidden = low(layer_norm(tokens, gain_one, shift_one))
    class_hidden = hidden[0, 0]
    mask16 = head_mask(HEADS)
    query = low((dot(class_hidden[None], query_w)[0] + query_bias) * SCALE)
    query_heads = jnp.where(mask16, query[None], jnp.zeros((), BF))
    qk = low(dot(query_heads, key_w, NT))
    scores = jnp.einsum("hd,itd->iht", qk, hidden, preferred_element_type=F32)
    keep = jnp.concatenate([jnp.ones((images, 1), jnp.int32), keep_mask], axis=1)
    scores = jnp.where(keep[:, None, :] > 0, scores, MASKED)
    weights = jax.nn.softmax(scores, axis=-1)
    weights_low = low(weights)
    pooled = low(jnp.einsum("iht,itd->ihd", weights_low, hidden, preferred_element_type=F32))
    mass = jnp.sum(weights_low.astype(F32), axis=-1)
    mixed = dot(pooled.reshape(-1, WIDTH), value_w).reshape(images, HEADS, WIDTH)
    mixed = mixed + mass[:, :, None] * value_bias
    attended = low(jnp.sum(jnp.where(mask16, mixed, 0.0), axis=1))
    resid = class_state + dot(attended, output_w) + out_bias
    hidden_two = low(layer_norm(resid, gain_two, shift_two))
    preact = dot(hidden_two, fc_in_w, NT) + fc_in_bias
    active = low(exact_gelu(preact))
    state = resid + dot(active, fc_out_w) + fc_out_bias
    final = low(layer_norm(state, gain_end, shift_end))
    projected = dot(final, proj_w, NT)
    unit = low(normalize(projected))
    partners = lax.all_gather(partner_emb, ("img", "seq"), axis=0, tiled=True)
    count = partners.shape[0]
    logits = dot(unit, partners, NT) / SOFTMAX_SCALE
    onehot = (jnp.arange(count, dtype=jnp.int32)[None] == partner_index[:, None]).astype(F32)
    total = jax.nn.logsumexp(logits, axis=-1)
    loss_part = jnp.sum(total - jnp.sum(logits * onehot, axis=-1)) / count
    d_logits = (jax.nn.softmax(logits, axis=-1) - onehot) / count
    d_unit = dot(low(d_logits / SOFTMAX_SCALE), partners)
    d_projected = low(jax.vjp(normalize, projected)[1](d_unit)[0])
    d_final = dot(d_projected, proj_w)
    d_state, d_gain_end, d_shift_end = jax.vjp(layer_norm, state, gain_end, shift_end)[1](d_final)
    d_state_low = low(d_state)
    d_active = dot(d_state_low, fc_out_w, NT)
    d_preact = low(jax.vjp(exact_gelu, preact)[1](d_active)[0])
    d_hidden_two = dot(d_preact, fc_in_w)
    d_norm, d_gain_two, d_shift_two = jax.vjp(layer_norm, resid, gain_two, shift_two)[1](
        d_hidden_two
    )
    d_resid = d_state + d_norm
    d_resid_low = low(d_resid)
    d_attended = low(dot(d_resid_low, output_w, NT))
    wide = jnp.where(mask16, d_attended[:, None, :], jnp.zeros((), BF))
    d_pooled = low(dot(wide.reshape(-1, WIDTH), value_w, NT)).reshape(images, HEADS, WIDTH)
    d_weights = jnp.einsum("ihd,itd->iht", d_pooled, hidden, preferred_element_type=F32)
    d_weights = d_weights + jnp.sum(wide.astype(F32) * value_bias, axis=-1)[:, :, None]
    d_scores = low(weights * (d_weights - jnp.sum(weights * d_weights, axis=-1, keepdims=True)))
    d_hidden = jnp.einsum("iht,ihd->itd", weights_low, d_pooled, preferred_element_type=F32)
    d_hidden = d_hidden + jnp.einsum("iht,hd->itd", d_scores, qk, preferred_element_type=F32)
    pull = jnp.einsum("iht,itd->hd", d_scores, hidden, preferred_element_type=F32)
    d_query = jnp.sum(jnp.where(mask16, dot(low(pull), key_w), 0.0), axis=0) * SCALE
    d_class_hidden = dot(low(d_query)[None], query_w, NT)
    d_tokens, d_gain_one, d_shift_one = jax.vjp(layer_norm, tokens, gain_one, shift_one)[1](
        d_hidden
    )
    d_class, d_gain_cls, d_shift_cls = jax.vjp(layer_norm, class_state[None], gain_one, shift_one)[
        1
    ](d_class_hidden)
    d_class = d_class[0] + jnp.sum(d_tokens[:, 0], axis=0) + jnp.sum(d_resid, axis=0)
    d_patch = d_tokens[:, 1:]
    d_embed_w = jnp.einsum("itp,itd->pd", pixels, low(d_patch), preferred_element_type=F32)
    d_value_w = dot(pooled.reshape(-1, WIDTH), wide.reshape(-1, WIDTH), TN)
    d_key_w = dot(pull, query_heads.astype(F32), TN, precision=lax.Precision.HIGHEST)
    small_local = jnp.concatenate(
        [
            d_class[None],
            d_class[None],
            jnp.sum(d_patch, axis=0),
            jnp.sum(d_patch, axis=(0, 1))[None],
            (d_gain_one + d_gain_cls)[None],
            (d_shift_one + d_shift_cls)[None],
            d_query[None],
            jnp.sum(wide.astype(F32) * mass[:, :, None], axis=(0, 1))[None],
            jnp.sum(d_resid, axis=0)[None],
            d_gain_two[None],
            d_shift_two[None],
            jnp.sum(d_preact.astype(F32), axis=0).reshape(FF // WIDTH, WIDTH),
            jnp.sum(d_state, axis=0)[None],
            d_gain_end[None],
            d_shift_end[None],
        ],
        axis=0,
    )
    grad_table = jnp.concatenate(
        [
            d_embed_w,
            class_hidden.astype(F32)[:, None] * d_query[None, :],
            d_key_w,
            d_value_w,
            dot(attended, d_resid_low, TN),
            dot(d_preact, hidden_two, TN),
            dot(active, d_state_low, TN),
            dot(d_projected, final, TN),
            jnp.zeros(((chips * slots - UNIT_COUNT) * ROWS_PER_UNIT, WIDTH), F32),
        ],
        axis=0,
    ).reshape(chips * slots, ROWS_PER_UNIT, WIDTH)
    small_grad, loss = lax.psum((small_local, loss_part), ("img", "seq"))
    core_half = lax.psum_scatter(low(grad_table), "seq", scatter_dimension=1, tiled=True)
    own_grad = lax.psum_scatter(core_half.astype(F32), "img", scatter_dimension=0, tiled=True)
    owner_total = lax.psum(jnp.sum(own_grad * own_grad), ("img", "seq"))
    grad_norm = jnp.sqrt(owner_total + jnp.sum(small_grad * small_grad))
    factor = 1.0 / jnp.maximum(grad_norm, 1.0)
    slot_grad = to_slots(own_grad, near, img, chips)
    step_value = step_count.astype(F32)
    new_masters, new_first, new_second = adamw(
        masters, slot_grad * factor, first_moment_slots, second_moment_slots, step_value
    )
    new_small, new_small_first, new_small_second = adamw(
        small_params, small_grad * factor, small_first, small_second, step_value
    )
    return (
        new_masters, new_first, new_second, new_small, new_small_first, new_small_second,
        loss, grad_norm,
    )


def solution(mesh):
    chip, devices = "img", ("img", "seq")
    core, body = "seq", per_device_any
    if mesh.shape["img"] == CHIPS and mesh.shape["seq"] == 2:
        mesh = jax.sharding.Mesh(mesh.devices.reshape(4, 2, 2, 2), ALL)
        chip, devices, core, body = CHIP, ALL, "c", per_device_16
    weights = P(chip, core, None)
    return jax.shard_map(
        body,
        mesh=mesh,
        in_specs=(
            P(devices, None, None),
            P(devices, None),
            P(devices),
            P(devices, None),
            weights,
            weights,
            weights,
            P(),
            P(),
            P(),
            P(),
            P(),
        ),
        out_specs=(weights, weights, weights, P(), P(), P(), P(), P()),
        check_vma=False,
    )
```

```python
import functools
import math

import jax
import jax.numpy as jnp
from jax import lax
from jax.experimental import pallas as pl
from jax.experimental.pallas import tpu as pltpu
from jax.sharding import PartitionSpec as P

WIDTH = 1024
HEADS = 16
HEAD_DIM = 64
FF = 4096
PIX = 3072
PROJ = 768
TOKS = 50
PATCHES = TOKS - 1
ROWS_PER_UNIT = 32
UNIT_COUNT = 504
JITTER = 2

EPS_NORM = 1e-06
SOFTMAX_SCALE = 0.07
LEARN_RATE = 0.03
BETA_ONE = 0.5
BETA_TWO = 0.5
DECAY_RATE = 0.05
ADAM_EPS = 1e-08
MASKED = -1000000000.0
SCALE = HEAD_DIM ** (-0.5)

F32 = jnp.float32
BF = jnp.bfloat16
ROW_BASE = 1 + TOKS
ROW_TAIL = ROW_BASE + 8 + FF // WIDTH
SLOT = 64


def low(values):
    return values.astype(BF)


def dot(a, b, dims=((1,), (0,)), precision=None):
    return lax.dot_general(a, b, (dims, ((), ())), precision=precision, preferred_element_type=F32)


NN = ((1,), (0,))
NT = ((1,), (1,))
TN = ((0,), (0,))


def layer_norm(values, gain, shift):
    center = values - jnp.mean(values, axis=-1, keepdims=True)
    spread = jnp.mean(center * center, axis=-1, keepdims=True)
    return center * lax.rsqrt(spread + EPS_NORM) * gain + shift


def normalize(values):
    return values * lax.rsqrt(jnp.sum(values * values, axis=-1, keepdims=True) + EPS_NORM)


def exact_gelu(values):
    return jax.nn.gelu(values, approximate=False)


def small_parts(small):
    base, tail = ROW_BASE, ROW_TAIL
    return (
        small[0],
        small[1:base],
        small[base],
        small[base + 1],
        small[base + 2],
        small[base + 3],
        small[base + 4],
        small[base + 5],
        small[base + 6],
        small[base + 7],
        small[base + 8 : tail].reshape(FF),
        small[tail],
        small[tail + 1],
        small[tail + 2],
    )


def adamw(weight, grad, first, second, step):
    first_new = BETA_ONE * first + (1.0 - BETA_ONE) * grad
    second_new = BETA_TWO * second + (1.0 - BETA_TWO) * grad * grad
    first_hat = first_new / (1.0 - jnp.power(BETA_ONE, step))
    second_hat = second_new / (1.0 - jnp.power(BETA_TWO, step))
    weight_new = weight - LEARN_RATE * (
        first_hat / (jnp.sqrt(second_hat) + ADAM_EPS) + DECAY_RATE * weight
    )
    return (weight_new, first_new, second_new)


def halo(values, chips, axes):
    before = lax.ppermute(values[-JITTER:], axes, [(i, i + 1) for i in range(chips - 1)])
    behind = lax.ppermute(values[:JITTER], axes, [(i + 1, i) for i in range(chips - 1)])
    return before, behind


def with_halo(values, chips, axes):
    before, behind = halo(values, chips, axes)
    return jnp.concatenate([before, values, behind], axis=0)


def slots_near(slot_unit_index, img, slots):
    padded = jnp.pad(slot_unit_index, (JITTER, JITTER), constant_values=-1)
    return lax.dynamic_slice(padded, (img * slots,), (slots + 2 * JITTER,))


def pick(ext, matches, slots):
    out = jnp.zeros((slots,) + ext.shape[1:], ext.dtype)
    for shift in range(2 * JITTER + 1):
        out = jnp.where(matches[shift][:, None, None], ext[shift : shift + slots], out)
    return out


def to_units(values, near, img, chips, axes="img"):
    slots = values.shape[0]
    ids = img * slots + jnp.arange(slots, dtype=jnp.int32)
    matches = [near[s : s + slots] == ids for s in range(2 * JITTER + 1)]
    return pick(with_halo(values, chips, axes), matches, slots)


def to_slots(values, near, img, chips, axes="img"):
    slots = values.shape[0]
    here = near[JITTER : JITTER + slots]
    ids = img * slots + jnp.arange(slots, dtype=jnp.int32)
    matches = [
        (here == ids + (s - JITTER)) & (here < UNIT_COUNT) for s in range(2 * JITTER + 1)
    ]
    return pick(with_halo(values, chips, axes), matches, slots)


def shuffle_matrix():
    source = lax.broadcasted_iota(jnp.int32, (256, 256), 0)
    target = lax.broadcasted_iota(jnp.int32, (256, 256), 1)
    moved = ((source // 16) % 2) * 128 + (source // 32) * 16 + source % 16
    return (moved == target).astype(F32).astype(BF)


def vmem():
    return pl.BlockSpec(memory_space=pltpu.VMEM)


def smem():
    return pl.BlockSpec(memory_space=pltpu.SMEM)


def shape(dims, dtype):
    return jax.ShapeDtypeStruct(dims, dtype)


def call(kernel, name, scalars, arrays, outs, scratch=(), mib=40, flops=10**9, far=()):
    moved = sum(a.size * a.dtype.itemsize for a in [*arrays, *outs, *far])
    return pl.pallas_call(
        kernel,
        in_specs=[smem()] * len(scalars)
        + [vmem()] * len(arrays)
        + [pl.BlockSpec(memory_space=pl.ANY)] * len(far),
        out_specs=[vmem()] * len(outs),
        out_shape=list(outs),
        scratch_shapes=list(scratch),
        compiler_params=pltpu.CompilerParams(vmem_limit_bytes=mib * 2**20),
        cost_estimate=pl.CostEstimate(flops=flops, bytes_accessed=moved, transcendentals=0),
        name=name,
    )(*scalars, *arrays, *far)


def prep_kernel(pix_ref, shuffle_ref, out_ref):
    shuffle = shuffle_ref[...]
    out_ref[...] = jnp.zeros_like(out_ref)
    for block in range(PIX // 256):
        moved = dot(pix_ref[0, :, 256 * block : 256 * block + 256], shuffle).astype(BF)
        out_ref[0, 0, :PATCHES, 128 * block : 128 * block + 128] = moved[:, :128]
        out_ref[1, 0, :PATCHES, 128 * block : 128 * block + 128] = moved[:, 128:]


def prep(pixels, shuffle):
    images = pixels.shape[0]
    return pl.pallas_call(
        prep_kernel,
        grid=(images,),
        in_specs=[
            pl.BlockSpec((1, PATCHES, PIX), lambda i: (i, 0, 0)),
            pl.BlockSpec((256, 256), lambda i: (0, 0)),
        ],
        out_specs=pl.BlockSpec((2, 1, SLOT, PIX // 2), lambda i: (0, i, 0, 0)),
        out_shape=jax.ShapeDtypeStruct((2, images, SLOT, PIX // 2), BF),
        compiler_params=pltpu.CompilerParams(vmem_limit_bytes=24 * 2**20),
        cost_estimate=pl.CostEstimate(flops=8 * 10**8, bytes_accessed=6 * 2**20, transcendentals=0),
        name="prep",
    )(pixels, shuffle)


def head_mask(rows):
    lane = lax.broadcasted_iota(jnp.int32, (rows, WIDTH), 1) // HEAD_DIM
    row = lax.broadcasted_iota(jnp.int32, (rows, WIDTH), 0) % HEADS
    return lane == row


def norm_parts(values):
    center = values - jnp.mean(values, axis=-1, keepdims=True)
    rstd = lax.rsqrt(jnp.mean(center * center, axis=-1, keepdims=True) + EPS_NORM)
    return center * rstd, rstd


def norm_back(grad, gain, xhat, rstd):
    gy = grad * gain
    return rstd * (
        gy - jnp.mean(gy, axis=-1, keepdims=True) - xhat * jnp.mean(gy * xhat, axis=-1, keepdims=True)
    )


def rowsum(values):
    return jnp.sum(values, axis=0, keepdims=True)


def to_halves(values, shuffle):
    first, second = [], []
    for block in range(values.shape[1] // 256):
        moved = low(dot(values[:, 256 * block : 256 * block + 256], shuffle))
        first.append(moved[:, :128])
        second.append(moved[:, 128:])
    return jnp.concatenate(first, axis=1), jnp.concatenate(second, axis=1)


def to_natural(first, second, shuffle):
    out = []
    for block in range(first.shape[1] // 128):
        lanes = slice(128 * block, 128 * block + 128)
        both = jnp.concatenate([first[:, lanes], second[:, lanes]], axis=1)
        out.append(low(dot(both, shuffle, NT)))
    return jnp.concatenate(out, axis=1)


R_PATCH, R_GAIN1, R_SHIFT1, R_VB, R_OB, R_GAIN2, R_SHIFT2 = 51, 52, 53, 55, 56, 57, 58
R_C2, R_GAINF, R_SHIFTF, R_SMALL = 63, 64, 65, 66
QUARTER = 128


def partner_kernel(raw_ref, out_ref):
    source = lax.broadcasted_iota(jnp.int32, (PROJ, PROJ), 0)
    target = lax.broadcasted_iota(jnp.int32, (PROJ, PROJ), 1)
    moved = ((source // 16) % 2) * (PROJ // 2) + (source // 32) * 16 + source % 16
    select = low((moved == target).astype(F32))
    out_ref[...] = low(dot(raw_ref[...].reshape(-1, PROJ), select))


def forward_kernel(segments, images, where_ref, pix_ref, rows_ref, valid_ref, shuffle_ref, *refs):
    count = len(segments)
    own, peer = refs[:count], refs[count : 2 * count]
    (
        hid_ref, xhat_ref, rstd_ref, p_ref, pooled_ref, mass_ref, wv_ref, wo_ref, qk_ref,
        resid_ref, low_ref, acc_ref, pool_ref, half_ref, table_ref, sems,
    ) = refs[2 * count :]
    col, core = where_ref[0], where_ref[1]
    waits = ([], [])
    for flip, group in ((0, own), (1, peer)):
        half = core ^ flip
        for (source, parts, late), ref in zip(segments, group):
            block = col ^ source
            for row, lane, rows in parts:
                part = ref.at[pl.ds(row, rows)]
                line = pl.multiple_of(block * 512 + lane, 128)
                copy = pltpu.make_async_copy(part, table_ref.at[half, pl.ds(line, rows)], sems.at[flip])
                copy.start()
                waits[flip].append(copy)
            if late >= 0:
                part = ref.at[pl.ds(late, QUARTER)]
                line = pl.multiple_of(block * QUARTER, QUARTER)
                copy = pltpu.make_async_copy(part, wo_ref.at[half, pl.ds(line, QUARTER)], sems.at[2])
                copy.start()
                waits[1].append(copy)
                part = ref.at[pl.ds(late + QUARTER, HEADS)]
                copy = pltpu.make_async_copy(part, half_ref.at[half, block], sems.at[3])
                copy.start()
                waits[1].append(copy)
    patch = rows_ref[2 : 1 + TOKS] + rows_ref[R_PATCH : R_PATCH + 1]
    class_state = rows_ref[0:1] + rows_ref[1:2]
    for i in range(images):
        acc_ref[SLOT * i : SLOT * i + PATCHES] = patch
        acc_ref[SLOT * i + PATCHES : SLOT * i + TOKS] = class_state
        acc_ref[SLOT * i + TOKS : SLOT * (i + 1)] = jnp.zeros((SLOT - TOKS, WIDTH), F32)
    for copy in waits[0]:
        copy.wait()
    acc_ref[...] += dot(pix_ref[core], table_ref[core, :1536])
    for copy in waits[1]:
        copy.wait()
    acc_ref[...] += dot(pix_ref[1 - core], table_ref[1 - core, :1536])
    wv_ref[...] = table_ref[:, 1536:]
    shuffle = shuffle_ref[...]
    gain, shift, value_bias = (rows_ref[r : r + 1] for r in (R_GAIN1, R_SHIFT1, R_VB))
    half = WIDTH // 2
    qk = to_natural(half_ref[0, 0, :, :half], half_ref[1, 0, :, :half], shuffle)
    qk_ref[...] = qk
    valid = valid_ref[...] > 0
    for i in range(images):
        part = slice(SLOT * i, SLOT * (i + 1))
        xhat, rstd = norm_parts(acc_ref[part])
        hid = low(xhat * gain + shift)
        xhat_ref[part] = xhat
        rstd_ref[part] = jnp.broadcast_to(rstd, (SLOT, 128))
        hid_ref[part] = hid
        scores = jnp.where(valid[part], dot(hid, qk, NT), MASKED)
        e = jnp.exp(scores - jnp.max(scores, axis=0, keepdims=True))
        p = e / jnp.sum(e, axis=0, keepdims=True)
        p_ref[part] = p
        pb = low(p)
        pool_ref[HEADS * i : HEADS * (i + 1)] = low(dot(pb, hid, TN))
        mass_ref[HEADS * i : HEADS * (i + 1)] = dot(pb, jnp.ones((SLOT, 128), BF), TN)
    pooled_ref[0], pooled_ref[1] = to_halves(pool_ref[...], shuffle)
    rows = images * HEADS
    mixed = dot(pooled_ref[0], wv_ref[0]) + dot(pooled_ref[1], wv_ref[1])
    mixed = mixed + mass_ref[:, 0:1] * value_bias
    mixed = jnp.where(head_mask(rows), mixed, 0.0)
    joined = low(jnp.sum(mixed.reshape(images, HEADS, WIDTH), axis=1))
    first, second = to_halves(joined, shuffle)
    resid = class_state + dot(first, wo_ref[0]) + dot(second, wo_ref[1])
    resid = resid + rows_ref[R_OB : R_OB + 1]
    resid_ref[...] = resid
    xhat, _ = norm_parts(resid)
    hidden = low(xhat * rows_ref[R_GAIN2 : R_GAIN2 + 1] + rows_ref[R_SHIFT2 : R_SHIFT2 + 1])
    sent = jnp.concatenate([hidden, first, second], axis=1)
    low_ref[...] = jnp.broadcast_to(sent[None], low_ref.shape)


def forward_call(segments, images, where, pix, own, peer, rows, valid, shuffle):
    tokens = images * SLOT
    outs = [
        shape((tokens, WIDTH), BF),
        shape((tokens, WIDTH), F32),
        shape((tokens, 128), F32),
        shape((tokens, HEADS), F32),
        shape((2, images * HEADS, WIDTH // 2), BF),
        shape((images * HEADS, 128), F32),
        shape((2, WIDTH // 2, WIDTH), BF),
        shape((2, WIDTH // 2, WIDTH), BF),
        shape((HEADS, WIDTH), BF),
        shape((images, WIDTH), F32),
        shape((8, images, 2 * WIDTH), BF),
    ]
    scratch = [
        pltpu.VMEM((tokens, WIDTH), F32),
        pltpu.VMEM((images * HEADS, WIDTH), BF),
        pltpu.VMEM((2, 4, HEADS, WIDTH), BF),
        pltpu.VMEM((2, 2048, WIDTH), BF),
        pltpu.SemaphoreType.DMA((4,)),
    ]
    return call(
        functools.partial(forward_kernel, segments, images), "forward", [where],
        [pix, rows, valid, shuffle], outs, scratch, mib=52, flops=4 * 10**9,
        far=[*own, *peer],
    )


def fetch(pick_ref, slot, candidates, out_ref, sem):
    for number, candidate in enumerate(candidates):

        @pl.when(pick_ref[slot] == number)
        def _():
            pltpu.make_async_copy(candidate, out_ref, sem).start()


def arrived(candidate, out_ref, sem):
    pltpu.make_async_copy(candidate, out_ref, sem).wait()


def ff_kernel(pick_ref, hid_ref, bias_ref, *refs):
    candidates, (pre_ref, act_ref, part_ref, w1_ref, w2_ref, sems) = refs[:6], refs[6:]
    fetch(pick_ref, 0, candidates, w1_ref, sems.at[0])
    fetch(pick_ref, 1, candidates, w2_ref, sems.at[1])
    hidden = hid_ref[:, :, :WIDTH].reshape(-1, WIDTH)
    arrived(candidates[0], w1_ref, sems.at[0])
    pre = dot(hidden, w1_ref[...], NT) + bias_ref[...]
    pre_ref[...] = pre
    active = low(0.5 * pre * (1.0 + lax.erf(pre * (0.5**0.5))))
    act_ref[...] = active
    arrived(candidates[0], w2_ref, sems.at[1])
    part_ref[...] = low(dot(active, w2_ref[...])).reshape(part_ref.shape)


def ff_back_kernel(pick_ref, dst_ref, pre_ref, *refs):
    candidates, (dpre_ref, sum_ref, part_ref, w1_ref, w2_ref, sems) = refs[:6], refs[6:]
    fetch(pick_ref, 1, candidates, w2_ref, sems.at[1])
    fetch(pick_ref, 0, candidates, w1_ref, sems.at[0])
    d_state = dst_ref[:, :, :WIDTH].reshape(-1, WIDTH)
    pre = pre_ref[...]
    slope = 0.5 * (1.0 + lax.erf(pre * (0.5**0.5))) + pre * jnp.exp(-0.5 * pre * pre) * (
        1.0 / (2.0 * math.pi) ** 0.5
    )
    arrived(candidates[0], w2_ref, sems.at[1])
    d_pre = low(dot(d_state, w2_ref[...], NT) * slope)
    dpre_ref[...] = d_pre
    sum_ref[...] = rowsum(d_pre.astype(F32))
    arrived(candidates[0], w1_ref, sems.at[0])
    part_ref[...] = low(dot(d_pre, w1_ref[...])).reshape(part_ref.shape)


def ff_call(kernel, name, pick, arrays, candidates, outs):
    moved = sum(a.size * a.dtype.itemsize for a in list(arrays) + list(outs))
    return pl.pallas_call(
        kernel,
        in_specs=[smem()]
        + [vmem()] * len(arrays)
        + [pl.BlockSpec(memory_space=pl.ANY)] * len(candidates),
        out_specs=[vmem()] * len(outs),
        out_shape=list(outs),
        scratch_shapes=[
            pltpu.VMEM((512, WIDTH), BF),
            pltpu.VMEM((512, WIDTH), BF),
            pltpu.SemaphoreType.DMA((2,)),
        ],
        compiler_params=pltpu.CompilerParams(vmem_limit_bytes=24 * 2**20),
        cost_estimate=pl.CostEstimate(
            flops=2 * 10**8, bytes_accessed=moved + 2 * 2**20, transcendentals=0
        ),
        name=name,
    )(pick, *arrays, *candidates)


def head_kernel(
    where_ref, part_ref, resid_ref, pj_ref, pjp_ref, partners_ref, target_ref, rows_ref,
    state_ref, low_ref, vec_ref, dz_ref,
):
    images = resid_ref.shape[0]
    state = resid_ref[...] + jnp.sum(part_ref[...].astype(F32), axis=0) + rows_ref[R_C2 : R_C2 + 1]
    gain = rows_ref[R_GAINF : R_GAINF + 1]
    xhat, rstd = norm_parts(state)
    final = low(xhat * gain + rows_ref[R_SHIFTF : R_SHIFTF + 1])
    z_own, z_peer = dot(final, pj_ref[...], NT), dot(final, pjp_ref[...], NT)
    square = jnp.sum(z_own * z_own, axis=-1, keepdims=True) + jnp.sum(
        z_peer * z_peer, axis=-1, keepdims=True
    )
    inv = lax.rsqrt(square + EPS_NORM)
    core = where_ref[1]
    half = PROJ // 2
    own_lanes = pl.ds(pl.multiple_of(core * half, 128), half)
    peer_lanes = pl.ds(pl.multiple_of((1 - core) * half, 128), half)
    ptn_own, ptn_peer = partners_ref[:, own_lanes], partners_ref[:, peer_lanes]
    logits = dot(low(z_own * inv), ptn_own, NT) + dot(low(z_peer * inv), ptn_peer, NT)
    logits = logits / SOFTMAX_SCALE
    total = logits.shape[1]
    hit = lax.broadcasted_iota(jnp.int32, (images, total), 1) == target_ref[...]
    top = jnp.max(logits, axis=-1, keepdims=True)
    e = jnp.exp(logits - top)
    mass = jnp.sum(e, axis=-1, keepdims=True)
    aim = jnp.sum(jnp.where(hit, logits, 0.0), axis=-1, keepdims=True)
    losses = jnp.log(mass) + top - aim
    d_logits = (e / mass - jnp.where(hit, 1.0, 0.0)) / total
    g_logits = low(d_logits / SOFTMAX_SCALE)
    d_own, d_peer = dot(g_logits, ptn_own), dot(g_logits, ptn_peer)
    along = jnp.sum(d_own * z_own, axis=-1, keepdims=True) + jnp.sum(
        d_peer * z_peer, axis=-1, keepdims=True
    )
    shrink = along * inv * inv * inv
    dz_own, dz_peer = low(d_own * inv - z_own * shrink), low(d_peer * inv - z_peer * shrink)
    dz_ref[:, own_lanes] = dz_own
    dz_ref[:, peer_lanes] = dz_peer
    d_final = dot(dz_own, pj_ref[...]) + dot(dz_peer, pjp_ref[...])
    d_state = norm_back(d_final, gain, xhat, rstd)
    state_ref[...] = d_state
    sent = jnp.concatenate([low(d_state), dz_ref[...], final], axis=1)
    low_ref[...] = jnp.broadcast_to(sent[None], low_ref.shape)
    vec_ref[...] = jnp.zeros_like(vec_ref)
    vec_ref[0:1] = rowsum(d_state)
    vec_ref[1:2] = rowsum(d_final * xhat)
    vec_ref[2:3] = rowsum(d_final)
    vec_ref[3:4] = jnp.broadcast_to(rowsum(losses) / total, (1, WIDTH))


def backward_kernel(
    images, where_ref, part_ref, dstate_ref, resid_ref, wo_ref, wv_ref, hid_ref, xhat_ref,
    rstd_ref, p_ref, mass_ref, qk_ref, rows_ref, shuffle_ref,
    de_ref, do_ref, dres_ref, pos_ref, vec_ref, pull_ref, dom_ref, da_ref,
):
    rows = images * HEADS
    gain, value_bias = rows_ref[R_GAIN1 : R_GAIN1 + 1], rows_ref[R_VB : R_VB + 1]
    shuffle = shuffle_ref[...]
    vec_ref[...] = jnp.zeros_like(vec_ref)
    d_two = jnp.sum(part_ref[...].astype(F32), axis=0)
    xhat2, rstd2 = norm_parts(resid_ref[...])
    d_resid = dstate_ref[...] + norm_back(d_two, rows_ref[R_GAIN2 : R_GAIN2 + 1], xhat2, rstd2)
    vec_ref[3:4] = rowsum(d_resid)
    vec_ref[4:5] = rowsum(d_two * xhat2)
    vec_ref[5:6] = rowsum(d_two)
    d_low = low(d_resid)
    dres_ref[...] = jnp.broadcast_to(d_low[None], dres_ref.shape)
    d_att = to_natural(
        low(dot(d_low, wo_ref[0], NT)), low(dot(d_low, wo_ref[1], NT)), shuffle
    )
    do_ref[...] = d_att
    spread = jnp.broadcast_to(d_att.reshape(images, 1, WIDTH).astype(F32), (images, HEADS, WIDTH))
    wide = jnp.where(head_mask(rows), spread.reshape(rows, WIDTH), 0.0)
    dom_ref[...] = low(wide)
    vec_ref[2:3] = rowsum(wide * mass_ref[:, 0:1])
    da_ref[...] = to_natural(
        low(dot(dom_ref[...], wv_ref[0], NT)), low(dot(dom_ref[...], wv_ref[1], NT)), shuffle
    )
    qk = qk_ref[...]
    bias_rows = low(jnp.broadcast_to(value_bias, (8, WIDTH)))
    real = lax.broadcasted_iota(jnp.int32, (SLOT, WIDTH), 0) < PATCHES
    for i in range(images):
        part = slice(SLOT * i, SLOT * (i + 1))
        mine = slice(HEADS * i, HEADS * (i + 1))
        hid, p, da = hid_ref[part], p_ref[part], da_ref[mine]
        dp = dot(hid, da, NT) + dot(bias_rows, dom_ref[mine], NT)[0:1]
        ds = low(p * (dp - rowsum(p * dp)))
        dh = dot(low(p), da) + dot(ds, qk)
        pull = dot(ds, hid, TN)
        xhat, rstd = xhat_ref[part], rstd_ref[part, 0:1]
        dx = norm_back(dh, gain, xhat, rstd)
        de_ref[part] = low(jnp.where(real, dx, 0.0))
        vec_ref[0:1] += rowsum(dh * xhat)
        vec_ref[1:2] += rowsum(dh)
        if i == 0:
            pos_ref[...] = dx
            pull_ref[...] = pull
        else:
            pos_ref[...] += dx
            pull_ref[...] += pull


def backward_call(images, where, arrays):
    tokens = images * SLOT
    outs = [
        shape((tokens, WIDTH), BF),
        shape((images, WIDTH), BF),
        shape((8, images, WIDTH), BF),
        shape((SLOT, WIDTH), F32),
        shape((8, WIDTH), F32),
        shape((HEADS, WIDTH), F32),
    ]
    scratch = [pltpu.VMEM((images * HEADS, WIDTH), BF)] * 2
    return call(
        functools.partial(backward_kernel, images), "backward", [where], arrays, outs, scratch
    )


def rows_kernel(where_ref, act_ref, dpre_ref, hid_ref, dst_ref, dres_ref, out_ref):
    half = WIDTH // 2
    base = 3 * WIDTH
    out_ref[:, :half] = act_ref[...]
    out_ref[:, half:WIDTH] = dpre_ref[...]
    count = out_ref.shape[0]
    out_ref[:, WIDTH : 2 * WIDTH] = hid_ref[:, :, :WIDTH].reshape(count, WIDTH)
    out_ref[:, 2 * WIDTH : base] = dst_ref[:, :, :WIDTH].reshape(count, WIDTH)

    @pl.when(where_ref[0] == 2)
    def _():
        out_ref[:, base : base + WIDTH] = hid_ref[:, :, WIDTH:].reshape(count, WIDTH)
        out_ref[:, base + WIDTH :] = dres_ref[...].reshape(count, WIDTH)

    @pl.when(where_ref[0] != 2)
    def _():
        out_ref[:, base : base + WIDTH + PROJ] = dst_ref[:, :, WIDTH:].reshape(count, WIDTH + PROJ)
        out_ref[:, base + WIDTH + PROJ :] = jnp.zeros((count, WIDTH - PROJ), BF)


def embed_grad_kernel(
    images, plan, where_ref, pix_ref, pixp_ref, de_ref, dep_ref, pooled_ref, pooledp_ref,
    do_ref, dop_ref, *refs,
):
    came = sum(entry[3] >= 0 for entry in plan)
    got_refs, out_refs = list(refs[:came]), refs[came:]
    col = where_ref[0]
    heads = images * HEADS
    for (source, first, rows, at), out_ref in zip(plan, out_refs):
        block = col ^ source
        got_ref = got_refs.pop(0) if at >= 0 else None

        def store(total, got_ref=got_ref, at=at, out_ref=out_ref):
            if got_ref is None:
                out_ref[...] = total.astype(out_ref.dtype)
                return
            end = at + got_ref.shape[0]
            out_ref[at:end] = (total[at:end] + got_ref[...].astype(F32)).astype(out_ref.dtype)
            if at > 0:
                out_ref[:at] = total[:at].astype(out_ref.dtype)
            if end < total.shape[0]:
                out_ref[end:] = total[end:].astype(out_ref.dtype)

        @pl.when(block < 3)
        def _():
            lanes = pl.ds(pl.multiple_of(block * 512 + first, 128), rows)
            store(dot(pix_ref[:, lanes], de_ref[...], TN) + dot(pixp_ref[:, lanes], dep_ref[...], TN))

        @pl.when(block == 3)
        def _():
            total = None
            for pooled, do in ((pooled_ref, do_ref), (pooledp_ref, dop_ref)):
                spread = jnp.broadcast_to(
                    do[...].reshape(images, 1, WIDTH).astype(F32), (images, HEADS, WIDTH)
                )
                wide = low(jnp.where(head_mask(heads), spread.reshape(heads, WIDTH), 0.0))
                term = dot(pooled[:, first : first + rows], wide, TN)
                total = term if total is None else total + term
            store(total)


def embed_grad_call(images, name, plan, where, arrays, got=()):
    outs = [shape((rows, WIDTH), F32 if source == 0 else BF) for source, _, rows, _ in plan]
    return call(
        functools.partial(embed_grad_kernel, images, plan), name, [where], [*arrays, *got], outs
    )


def to_natural_exact(first, second, shuffle):
    wide = shuffle.astype(F32)
    out = []
    for block in range(first.shape[1] // 128):
        lanes = slice(128 * block, 128 * block + 128)
        both = jnp.concatenate([first[:, lanes], second[:, lanes]], axis=1)
        out.append(dot(both, wide, NT, precision=lax.Precision.HIGHEST))
    return jnp.concatenate(out, axis=1)


def collect_kernel(
    where_ref, pos_ref, vec_ref, head_ref, sum_ref, pull_ref, shuffle_ref, sent_ref, out_ref
):
    col, core = where_ref[0], where_ref[1]
    out_ref[...] = jnp.zeros_like(out_ref)
    top = pos_ref[PATCHES:TOKS] + vec_ref[3:4]
    out_ref[0:1] = top
    out_ref[1:2] = top
    patches = pos_ref[0:PATCHES]
    out_ref[2 : 1 + TOKS] = patches
    out_ref[R_PATCH : R_PATCH + 1] = rowsum(patches)
    out_ref[R_GAIN1 : R_SHIFT1 + 1] = vec_ref[0:2]
    out_ref[R_VB : R_VB + 1] = vec_ref[2:3]
    out_ref[R_OB : R_SHIFT2 + 1] = vec_ref[3:6]
    sums = jnp.broadcast_to(sum_ref[...], (8, WIDTH // 2))
    nothing = jnp.zeros_like(sums)
    row = to_natural_exact(
        jnp.where(core == 0, sums, nothing), jnp.where(core == 0, nothing, sums), shuffle_ref[...]
    )
    for block in range(4):
        mine = (col + 1) % 4 == block
        out_ref[R_SHIFT2 + 1 + block : R_SHIFT2 + 2 + block] = jnp.where(mine, row[0:1], 0.0)
    out_ref[R_C2 : R_SHIFTF + 1] = head_ref[0:3]
    out_ref[R_SMALL : R_SMALL + HEADS] = pull_ref[...]
    out_ref[R_SMALL + HEADS : R_SMALL + HEADS + 1] = head_ref[3:4]
    for number in range(sent_ref.shape[0]):
        sent_ref[number] = out_ref[3 * number : 3 * number + 3]


def share_kernel(got_ref, sent_ref):
    sent_ref[...] = jnp.broadcast_to(jnp.sum(got_ref[...], axis=0, keepdims=True), sent_ref.shape)


def query_back_kernel(core_ref, got_ref, w_ref, shuffle_ref, dq_ref, pull_ref, total_ref):
    for number in range(got_ref.shape[0]):
        total_ref[3 * number : 3 * number + 3] = got_ref[number]
    wide = shuffle_ref[...].astype(F32)
    pull = total_ref[R_SMALL : R_SMALL + HEADS]
    is_one = core_ref[0] == 1
    out = []
    for block in range(WIDTH // 256):
        moved = dot(pull[:, 256 * block : 256 * block + 256], wide, precision=lax.Precision.HIGHEST)
        out.append(jnp.where(is_one, moved[:, 128:], moved[:, :128]))
    half = jnp.concatenate(out, axis=1)
    pull_ref[...] = half
    d_query = jnp.where(head_mask(HEADS), dot(low(half), w_ref[...]), 0.0)
    dq_ref[...] = jnp.broadcast_to(rowsum(d_query) * SCALE, dq_ref.shape)


def complete_kernel(total_ref, reports_ref, rows_ref, shuffle_ref, out_ref, norm_ref):
    out_ref[...] = total_ref[0:R_SMALL]
    half = WIDTH // 2
    first = jnp.broadcast_to(reports_ref[6, :, WIDTH : WIDTH + half], (8, half))
    second = jnp.broadcast_to(reports_ref[7, :, WIDTH : WIDTH + half], (8, half))
    d_hidden = to_natural_exact(first, second, shuffle_ref[...])[0:1]
    xhat, rstd = norm_parts(rows_ref[0:1] + rows_ref[1:2])
    d_class = norm_back(d_hidden, rows_ref[R_GAIN1 : R_GAIN1 + 1], xhat, rstd)
    out_ref[0:1] += d_class
    out_ref[1:2] += d_class
    out_ref[R_GAIN1 : R_GAIN1 + 1] += d_hidden * xhat
    out_ref[R_SHIFT1 : R_SHIFT1 + 1] += d_hidden
    out_ref[R_SHIFT1 + 1 : R_SHIFT1 + 2] = reports_ref[6, :, :WIDTH]
    grads = out_ref[...]
    square = jnp.sum(jnp.sum(grads * grads, axis=0, keepdims=True), axis=1, keepdims=True)
    for number in range(reports_ref.shape[0]):
        square = square + reports_ref[number, :, WIDTH + half : WIDTH + half + 1]
    norm_ref[...] = jnp.broadcast_to(jnp.sqrt(square), (8, 128))


def owner_kernel(role_ref, pull_ref, heads_ref, class_ref, dq_ref, *refs):
    rows, out_ref = refs[:6], refs[6]
    chip, core = role_ref[0], role_ref[1]
    half = WIDTH // 2
    base = 3 * WIDTH

    def product(left, right):
        total = None
        for piece in rows:
            term = dot(left(piece), right(piece), TN)
            total = term if total is None else total + term
        return total

    @pl.when((chip >= 7) & (chip <= 14))
    def _():
        is_two = chip >= 11
        out_ref[...] = product(
            lambda piece: jnp.where(is_two, piece[:, :half], piece[:, half:WIDTH]),
            lambda piece: jnp.where(is_two, piece[:, 2 * WIDTH : base], piece[:, WIDTH : 2 * WIDTH]),
        )

    @pl.when(chip == 6)
    def _():
        lanes = pl.ds(pl.multiple_of(base + core * half, 128), half)
        out_ref[...] = product(lambda piece: piece[:, lanes], lambda piece: piece[:, base + WIDTH :])

    @pl.when(chip == 15)
    def _():
        lanes = pl.ds(pl.multiple_of(base + core * (PROJ // 2), 128), PROJ // 2)
        out_ref[: PROJ // 2] = product(
            lambda piece: piece[:, lanes],
            lambda piece: piece[:, base + PROJ : base + PROJ + WIDTH],
        )
        out_ref[PROJ // 2 :] = jnp.zeros((512 - PROJ // 2, WIDTH), F32)

    @pl.when(chip == 4)
    def _():
        out_ref[...] = dot(
            pull_ref[...], heads_ref[...].astype(F32), TN, precision=lax.Precision.HIGHEST
        )

    @pl.when(chip == 3)
    def _():
        out_ref[...] = dot(
            class_ref[...].astype(F32), jnp.concatenate([dq_ref[0:1], jnp.zeros((7, WIDTH), F32)]),
            TN, precision=lax.Precision.HIGHEST,
        )


def finish_kernel(
    role_ref, formed_ref, dq_ref, toward_ref, total_ref, first_ref, second_ref, aside_ref, third_ref,
    out_ref, top_ref, end_ref, report_ref,
):
    chip = role_ref[0]

    @pl.when(chip < 3)
    def _():
        out_ref[...] = total_ref[...] + first_ref[...].astype(F32) + second_ref[...].astype(F32)

    @pl.when(chip == 5)
    def _():
        out_ref[...] = (
            second_ref[...].astype(F32) + aside_ref[...].astype(F32) + third_ref[...].astype(F32)
        )

    @pl.when((chip >= 3) & (chip != 5))
    def _():
        out_ref[...] = formed_ref[...]

    edge = top_ref.shape[0]
    top_ref[...] = out_ref[:edge]
    end_ref[...] = out_ref[-edge:]
    grads = out_ref[...]
    square = jnp.sum(jnp.sum(grads * grads, axis=0, keepdims=True), axis=1, keepdims=True)
    report_ref[...] = jnp.concatenate(
        [dq_ref[...], toward_ref[...], jnp.broadcast_to(square, (1, 128))], axis=1
    )


def update_kernel(
    source_ref, scalar_ref, before_ref, grad_ref, behind_ref, w_ref, m_ref, v_ref,
    nw_ref, nm_ref, nv_ref,
):
    step = pl.program_id(0)
    slots = grad_ref.shape[0]
    factor, fix_one, fix_two = scalar_ref[0], scalar_ref[1], scalar_ref[2]
    for k in range(w_ref.shape[0]):
        at = source_ref[step * w_ref.shape[0] + k]
        inside = (at >= 0) & (at < slots)
        grad = jnp.where(
            inside,
            grad_ref[jnp.clip(at, 0, slots - 1)],
            jnp.where(
                at < 0,
                before_ref[jnp.clip(at + JITTER, 0, JITTER - 1)],
                behind_ref[jnp.clip(at - slots, 0, JITTER - 1)],
            ),
        )
        grad = grad * jnp.where(at >= -JITTER, factor, 0.0)
        weight = w_ref[k]
        first = BETA_ONE * m_ref[k] + (1.0 - BETA_ONE) * grad
        second = BETA_TWO * v_ref[k] + (1.0 - BETA_TWO) * grad * grad
        nm_ref[k] = first
        nv_ref[k] = second
        nw_ref[k] = weight - LEARN_RATE * (
            (first * fix_one) / (jnp.sqrt(second * fix_two) + ADAM_EPS) + DECAY_RATE * weight
        )


def update_call(source, scalars, before, grads, behind, masters, first, second):
    slots, part, width = masters.shape
    block = 4
    spec = pl.BlockSpec((block, part, width), lambda i: (i, 0, 0))
    return pl.pallas_call(
        update_kernel,
        grid=(slots // block,),
        in_specs=[smem(), smem(), vmem(), vmem(), vmem(), spec, spec, spec],
        out_specs=[spec] * 3,
        out_shape=[shape(masters.shape, F32)] * 3,
        compiler_params=pltpu.CompilerParams(vmem_limit_bytes=58 * 2**20),
        cost_estimate=pl.CostEstimate(
            flops=2 * 10**7, bytes_accessed=7 * masters.size * 4, transcendentals=0
        ),
        name="update",
    )(source, scalars, before, grads, behind, masters, first, second)


CHIPS = 16
CHIP = ("z", "y", "x")
ALL = ("z", "y", "x", "c")
PLANE = ("y", "x", "c")
FLIP_X = [(i, i ^ 1) for i in range(CHIPS)]
FLIP_Y = [(i, i ^ 2) for i in range(CHIPS)]
FLIP_CORE = [(0, 1), (1, 0)]


def hop(values, pairs):
    return lax.ppermute(values, CHIP, pairs)


def swap(values):
    return lax.ppermute(values, "c", FLIP_CORE)


def after(values, *others):
    return lax.optimization_barrier((values,) + others)[0]


def among(img, chips):
    hit = img == chips[0]
    for chip in chips[1:]:
        hit = hit | (img == chip)
    return hit


def choose(img, cases, otherwise):
    out = otherwise
    for chips, values in cases:
        out = jnp.where(among(img, chips), values, out)
    return out


def together(*values):
    return lax.optimization_barrier(values)


def plane_gather(block, diagonal_by_x):
    by_x, by_y, block_peer = hop(block, FLIP_X), hop(block, FLIP_Y), swap(block)
    proj_top = jnp.where(img == 15, corner[0], corner[1] + corner[2] + corner[3])
    proj_one = hop(proj_top, [(12, 4), (13, 5), (14, 6), (15, 7)])
    diagonal = hop(by_y, FLIP_X) if diagonal_by_x else hop(by_x, FLIP_Y)
    return [block, by_x, by_y, diagonal]


def in_plane(values):
    return lax.all_to_all(values, PLANE, 0, 0, tiled=True)


def from_all(values):
    sent = jnp.broadcast_to(values[None], (2 * CHIPS,) + values.shape)
    return lax.all_to_all(sent, ALL, 0, 0, tiled=True)


def natural(values):
    lead = values.shape[:-2]
    units = values.shape[-1] // 16
    split = values.reshape(lead + (2, units, 16))
    return jnp.swapaxes(split, -3, -2).reshape(lead + (units * 32,))


def halves(values):
    lead = values.shape[:-1]
    units = values.shape[-1] // 32
    return jnp.swapaxes(values.reshape(lead + (units, 2, 16)), -3, -2).reshape(
        lead + (2, units * 16)
    )


def per_device_16(
    pixels, keep_mask, partner_index, partner_emb, masters, first_moment_slots,
    second_moment_slots, slot_unit_index, small_params, small_first, small_second, step_count,
):
    img, core = lax.axis_index(CHIP), lax.axis_index("c")
    col, plane = img % 4, img // 4
    images = pixels.shape[0]
    slots = masters.shape[0]
    is_one = core == 1
    where = jnp.stack([col, core]).astype(jnp.int32)
    shuffle = shuffle_matrix()
    rows = small_params
    class_state = small_params[0] + small_params[1]

    def mine_of(pair):
        return jnp.where(is_one, pair[1], pair[0])

    def theirs_of(pair):
        return jnp.where(is_one, pair[0], pair[1])

    near = slots_near(slot_unit_index, img, slots)
    held = low(masters)
    ids = img * slots + jnp.arange(slots, dtype=jnp.int32)
    matches = [near[s : s + slots] == ids for s in range(2 * JITTER + 1)]
    middle = pick(held[6:26], [m[8:24] for m in matches], 16).reshape(256, WIDTH)
    one_a = hop(middle, [(0, 4), (1, 5), (2, 6), (5, 7)])
    partners = from_all(after(partner_emb, middle))
    before, behind = halo(after(held, middle), CHIPS, CHIP)
    lower = pick(jnp.concatenate([before, held[:10]]), [m[:8] for m in matches], 8)
    upper = pick(jnp.concatenate([held[22:], behind]), [m[24:] for m in matches], 8)
    outer = jnp.concatenate([lower, upper]).reshape(256, WIDTH)
    own_w = jnp.concatenate([outer[:128], middle, outer[128:]])
    class_hidden = low(layer_norm(class_state, small_params[R_GAIN1], small_params[R_SHIFT1]))
    class_half = mine_of(halves(class_hidden))
    query = dot(class_half[None], own_w)
    query = hop(query + swap(query), [(3, 4)])
    wo_quarter = hop(own_w[384:], [(6, 7)]) + hop(own_w[:128], [(6, 4)])
    wo_quarter = wo_quarter + hop(own_w[128:256], [(6, 5)])
    wo_quarter = jnp.where(img == 6, own_w[256:384], wo_quarter)
    down_one = hop(
        own_w,
        [(12, 8), (13, 9), (14, 10), (11, 7), (8, 4), (9, 5), (10, 6), (7, 3)],
    )
    one_a, outer = together(one_a, outer)
    one_b = hop(outer, [(0, 4), (1, 5), (2, 6), (5, 7)])
    two_a = hop(one_a, [(4, 8), (5, 9), (6, 10), (7, 11)])
    pix = prep(after(pixels, one_a), shuffle).reshape(2, images * SLOT, PIX // 2)
    corner = after(own_w[: PROJ // 2], one_a)
    corner = [corner] + [hop(corner, [(15, 15 ^ flip)]) for flip in (1, 2, 3)]
    query = low((query + small_params[R_SHIFT1 + 1 : R_SHIFT1 + 2]) * SCALE)
    query_heads = jnp.where(head_mask(HEADS), query, jnp.zeros((), BF))
    pulled = jnp.pad(low(dot(query_heads, own_w, NT)), ((0, 0), (0, WIDTH // 2)))
    one_b, two_a, wo_quarter, pulled, down_one = together(
        one_b, two_a, wo_quarter, pulled, down_one
    )
    mid_b = jnp.concatenate([one_b, wo_quarter, pulled])
    two_b = hop(mid_b, [(4, 8), (5, 9), (6, 10), (7, 11)])
    three_a = hop(
        jnp.where(img == 7, one_a, two_a), [(8, 12), (9, 13), (10, 14), (11, 15), (7, 3)]
    )
    low_b = hop(mid_b[256:], [(4, 0), (5, 1), (6, 2)])
    two_b, three_a, low_b, pix, partners = together(two_b, three_a, low_b, pix, partners)
    block_a = jnp.where(img < 3, middle, one_a + two_a + three_a)
    x_a, y_a = hop(block_a, FLIP_X), hop(block_a, FLIP_Y)
    three_b = hop(
        jnp.where(img == 7, mid_b, two_b), [(8, 12), (9, 13), (10, 14), (11, 15), (7, 3)]
    )
    pix_own, pix_send = mine_of(pix), theirs_of(pix)
    x_a, y_a, three_b, pix_own, pix_send, *corner = together(
        x_a, y_a, three_b, pix_own, pix_send, *corner
    )
    block_b = jnp.where(
        img < 3,
        jnp.concatenate([outer, low_b]),
        jnp.where(plane == 1, mid_b, jnp.where(plane == 2, two_b, three_b)),
    )
    x_b, y_b = hop(block_b, FLIP_X), hop(block_b, FLIP_Y)
    down_two = hop(
        after(down_one, three_b), [(8, 4), (9, 5), (10, 6), (7, 3), (4, 0), (5, 1), (6, 2)]
    )
    proj_top = jnp.where(img == 15, corner[0], corner[1] + corner[2] + corner[3])
    proj_one = hop(proj_top, [(12, 4), (13, 5), (14, 6), (15, 7)])
    (partners,) = call(
        partner_kernel, "partners", [], [partners], [shape((2 * CHIPS * images, PROJ), BF)]
    )
    x_b, y_b = together(x_b, y_b)
    d_a, d_b = hop(y_a, FLIP_X), hop(x_b, FLIP_Y)
    up_one = hop(
        after(own_w, x_b), [(8, 12), (9, 13), (10, 14), (7, 11), (11, 15)]
    )

    down_three = hop(after(down_two, y_b), [(4, 0), (5, 1), (6, 2)])
    segments, own_pieces, peer_pieces = [], [], []
    for pieces, spans, late in (
        ((block_a, x_a, y_a, d_a), ((0, 128, 256),), -1),
        ((block_b, x_b, y_b, d_b), ((0, 0, 128), (128, 384, 128)), 256),
    ):
        segments += [(source, spans, late) for source in range(4)]
        own_pieces += pieces
        peer_pieces += [swap(piece) for piece in pieces]
    pix_peer = swap(pix_send)
    valid = jnp.concatenate(
        [
            keep_mask,
            jnp.ones((images, 1), jnp.int32),
            jnp.zeros((images, SLOT - TOKS), jnp.int32),
        ],
        axis=1,
    ).reshape(images * SLOT, 1)
    (
        hid, xhat, rstd, p, pooled, mass, wv, wo, qk, resid, hidden_sent,
    ) = forward_call(
        segments, images, where, pix, own_pieces, peer_pieces, rows, valid, shuffle
    )
    pooled_own = mine_of(pooled)
    pooled_peer = swap(theirs_of(pooled))

    hidden_all = in_plane(hidden_sent)
    hidden_all, pooled_peer = together(hidden_all, pooled_peer)
    up_two = hop(after(up_one, hidden_sent), [(11, 15)])
    ff_block = (col + 1) % 4
    bias_part = lax.dynamic_slice(
        small_params[R_SHIFT2 + 1 : R_C2].reshape(4, 32, 2, 16),
        (ff_block, 0, core, 0),
        (1, 32, 1, 16),
    ).reshape(1, 512)
    candidates = [own_w, up_one, up_two, down_one, down_two, down_three]
    pick_one = choose(
        img, [((15,), 2), ((12, 13, 14, 11), 1), ((4, 5, 6, 3), 3), ((0, 1, 2), 4)], 0
    )
    pick_two = choose(
        img, [((15,), 1), ((8, 9, 10, 7), 3), ((4, 5, 6, 3), 4), ((0, 1, 2), 5)], 0
    )
    picks = jnp.stack([pick_one, pick_two]).astype(jnp.int32)
    preact, active, part = ff_call(
        ff_kernel, "ff", picks, [hidden_all, bias_part], candidates,
        [shape((8 * images, 512), F32), shape((8 * images, 512), BF), shape((8, images, WIDTH), BF)],
    )
    proj_mid = hop(
        after(jnp.where(plane == 3, proj_top, proj_one), hidden_sent),
        [(12, 8), (13, 9), (14, 10), (15, 11), (4, 0), (5, 1), (6, 2), (7, 3)],
    )
    hidden_all = in_plane(hidden_sent)
    up_two = hop(after(up_one, hidden_sent), [(11, 15)])
    ff_block = (col + 1) % 4
    bias_part = lax.dynamic_slice(
        small_params[R_SHIFT2 + 1 : R_C2].reshape(4, 32, 2, 16),
        (ff_block, 0, core, 0),
        (1, 32, 1, 16),
    ).reshape(1, 512)
    candidates = [own_w, up_one, up_two, down_one, down_two, down_three]
    pick_one = choose(
        img, [((15,), 2), ((12, 13, 14, 11), 1), ((4, 5, 6, 3), 3), ((0, 1, 2), 4)], 0
    )
    pick_two = choose(
        img, [((15,), 1), ((8, 9, 10, 7), 3), ((4, 5, 6, 3), 4), ((0, 1, 2), 5)], 0
    )
    picks = jnp.stack([pick_one, pick_two]).astype(jnp.int32)
    preact, active, part = ff_call(
        ff_kernel, "ff", picks, [hidden_all, bias_part], candidates,
        [shape((8 * images, 512), F32), shape((8 * images, 512), BF), shape((8, images, WIDTH), BF)],
    )
    proj = choose(
        plane, [((3,), proj_top), ((1,), proj_one)], after(proj_mid, hidden_sent)
    )
    proj_peer = swap(proj)
    proj = choose(plane, [((3,), proj_top), ((1,), proj_one)], after(proj_mid, active))
    proj_peer = swap(proj)
    part = in_plane(part)
    d_state, d_state_sent, head_vec = call(
        head_kernel, "head", [where],
        [part, resid, proj, proj_peer, partners, partner_index[:, None], rows],
        [
            shape((images, WIDTH), F32), shape((8, images, 2 * WIDTH + PROJ), BF),
            shape((8, WIDTH), F32),
        ],
        [pltpu.VMEM((images, PROJ), BF)],
    )
    d_state_all = in_plane(d_state_sent)
    d_preact, d_preact_sum, part = ff_call(
        ff_back_kernel, "ff_back", picks, [d_state_all, preact], candidates,
        [shape((8 * images, 512), BF), shape((1, 512), F32), shape((8, images, WIDTH), BF)],
    )
    part = in_plane(part)

    d_embed, d_attended, d_resid, d_pos, d_vec, pull = backward_call(
        images, where,
        [part, d_state, resid, wo, wv, hid, xhat, rstd, p, mass, qk, rows, shuffle],
    )
    arrays = [
        pix_own, pix_peer, d_embed, swap(d_embed), pooled_own, pooled_peer, d_attended,
        swap(d_attended),
    ]
    far_x, far_y = embed_grad_call(
        images, "embed_grad_far", [(3, 0, 256, -1), (3, 256, 256, -1)], where, arrays
    )
    got_y, got_x = hop(far_x, FLIP_X), hop(far_y, FLIP_Y)
    (own_part,) = embed_grad_call(
        images, "embed_grad_own", [(0, 0, 512, -1)], after(where, far_x), arrays
    )
    d_resid = in_plane(after(d_resid, far_x))
    d_pos, d_vec, head_vec, d_preact_sum, pull, _ = together(
        d_pos, d_vec, head_vec, d_preact_sum, pull, far_x
    )
    (small_sent,) = call(
        collect_kernel, "collect", [where], [d_pos, d_vec, head_vec, d_preact_sum, pull, shuffle],
        [shape((32, 3, WIDTH), F32)], [pltpu.VMEM((96, WIDTH), F32)],
    )
    shares = lax.all_to_all(small_sent, ALL, 0, 0, tiled=True)
    got_x, got_y, own_part, d_resid, shares = together(got_x, got_y, own_part, d_resid, shares)
    part_x, part_y = embed_grad_call(
        images, "embed_grad_near", [(1, 0, 512, 256), (2, 0, 512, 0)], where, arrays, (got_x, got_y)
    )
    sum_x, sum_y = hop(part_x, FLIP_X), hop(part_y, FLIP_Y)
    (small_sent,) = call(share_kernel, "share", [], [shares], [shape((32, 3, WIDTH), F32)])
    shares = lax.all_to_all(small_sent, ALL, 0, 0, tiled=True)
    (ff_rows,) = call(
        rows_kernel, "rows", [where], [active, d_preact, hidden_all, d_state_all, d_resid],
        [shape((8 * images, 5 * WIDTH), BF)],
    )
    rise = [(i, i + 4) for i in range(12)]
    fall = [(12, 8), (13, 9), (14, 10), (15, 11), (10, 6), (11, 7)]
    up_one, down_one = hop(ff_rows, rise), hop(ff_rows, fall)
    sum_x, sum_y, shares, up_one, down_one = together(sum_x, sum_y, shares, up_one, down_one)
    total = own_part + sum_x.astype(F32) + sum_y.astype(F32)
    sent = low(total)
    first = hop(sent, [(12, 8), (13, 9), (14, 10), (15, 11), (4, 0), (5, 1), (6, 2)])
    aside = hop(sent, [(3, 1), (7, 5)])
    d_query, pull_half, small_total = call(
        query_back_kernel, "query_back", [core.reshape(1).astype(jnp.int32)],
        [shares, own_w, shuffle],
        [shape((8, WIDTH), F32), shape((HEADS, WIDTH // 2), F32), shape((96, WIDTH), F32)],
    )
    loss = small_total[R_SMALL + HEADS, 0]
    d_query = d_query[0:1]
    d_query = d_query + swap(d_query)
    up_two, down_two = hop(up_one, rise[4:]), hop(down_one, fall[4:])
    first, aside, d_query, up_two, down_two, total = together(
        first, aside, d_query, up_two, down_two, total
    )
    partial = low(total + first.astype(F32))
    second = hop(partial, [(8, 0), (9, 1), (10, 2), (11, 5)])
    third = hop(aside, [(1, 5)])
    up_three = hop(up_two, rise[8:])
    d_query = hop(d_query, [(4, 3)])
    toward = dot(low(d_query), own_w, NT)
    second, third, up_three, toward = together(second, third, up_three, toward)

    every = [ff_rows, up_one, up_two, up_three, down_one, down_two]
    class_rows = jnp.concatenate([class_half[None], jnp.zeros((7, WIDTH // 2), BF)])
    role = jnp.stack([img, core]).astype(jnp.int32)
    (formed,) = call(
        owner_kernel, "owner", [role], [pull_half, query_heads, class_rows, d_query, *every],
        [shape((512, WIDTH), F32)],
    )
    edge = shape((JITTER * 16, WIDTH), F32)
    own_grad, top, end, report = call(
        finish_kernel, "finish", [role],
        [formed, d_query, toward, total, first, second, aside, third],
        [shape((512, WIDTH), F32), edge, edge, shape((1, WIDTH + 640), F32)],
    )
    reports = from_all(report)
    before = hop(end, [(i, i + 1) for i in range(CHIPS - 1)]).reshape(JITTER, 16, WIDTH)
    behind = hop(top, [(i + 1, i) for i in range(CHIPS - 1)]).reshape(JITTER, 16, WIDTH)
    small_grad, norm = call(
        complete_kernel, "complete", [], [small_total, reports, rows, shuffle],
        [shape((R_SMALL, WIDTH), F32), shape((8, 128), F32)],
    )
    grad_norm = norm[0, 0]
    factor = 1.0 / jnp.maximum(grad_norm, 1.0)
    own_grad = own_grad.reshape(slots, 16, WIDTH)
    here = near[JITTER : JITTER + slots]
    source = jnp.where(here < UNIT_COUNT, here - img * slots, -100)
    step_value = step_count.astype(F32)
    scalars = jnp.stack(
        [
            factor,
            1.0 / (1.0 - jnp.power(BETA_ONE, step_value)),
            1.0 / (1.0 - jnp.power(BETA_TWO, step_value)),
        ]
    )
    new_masters, new_first, new_second = update_call(
        source, scalars, before, own_grad, behind, masters, first_moment_slots,
        second_moment_slots,
    )
    new_small, new_small_first, new_small_second = adamw(
        small_params, small_grad * factor, small_first, small_second, step_value
    )
    return (
        new_masters, new_first, new_second, new_small, new_small_first, new_small_second,
        loss, grad_norm,
    )


def per_device_any(
    pixels, keep_mask, partner_index, partner_emb, masters, first_moment_slots,
    second_moment_slots, slot_unit_index, small_params, small_first, small_second, step_count,
):
    chips, seq = lax.axis_size("img"), lax.axis_size("seq")
    img = lax.axis_index("img")
    images = pixels.shape[0]
    slots, part = masters.shape[0], masters.shape[1]
    near = slots_near(slot_unit_index, img, slots)
    own_w = to_units(low(masters), near, img, chips)
    gathered = lax.all_gather(own_w, ("img", "seq"), axis=0, tiled=False)
    flat = gathered.reshape(chips, seq, slots, part, WIDTH).transpose(0, 2, 1, 3, 4)
    flat = flat.reshape(chips * slots * ROWS_PER_UNIT, WIDTH)
    bounds = [0, PIX, WIDTH, WIDTH, WIDTH, WIDTH, FF, FF, PROJ]
    parts, offset = [], 0
    for size in bounds[1:]:
        parts.append(flat[offset : offset + size])
        offset += size
    embed_w, query_w, key_w, value_w, output_w, fc_in_w, fc_out_w, proj_w = parts
    (
        class_row, pos_rows, patch_bias, gain_one, shift_one, query_bias, value_bias, out_bias,
        gain_two, shift_two, fc_in_bias, fc_out_bias, gain_end, shift_end,
    ) = small_parts(small_params)
    class_state = class_row + pos_rows[0]
    embedded = jnp.einsum("itp,pd->itd", pixels, embed_w, preferred_element_type=F32)
    tokens = jnp.concatenate(
        [
            jnp.broadcast_to(class_state, (images, 1, WIDTH)),
            embedded + patch_bias + pos_rows[1:],
        ],
        axis=1,
    )
    hidden = low(layer_norm(tokens, gain_one, shift_one))
    class_hidden = hidden[0, 0]
    mask16 = head_mask(HEADS)
    query = low((dot(class_hidden[None], query_w)[0] + query_bias) * SCALE)
    query_heads = jnp.where(mask16, query[None], jnp.zeros((), BF))
    qk = low(dot(query_heads, key_w, NT))
    scores = jnp.einsum("hd,itd->iht", qk, hidden, preferred_element_type=F32)
    keep = jnp.concatenate([jnp.ones((images, 1), jnp.int32), keep_mask], axis=1)
    scores = jnp.where(keep[:, None, :] > 0, scores, MASKED)
    weights = jax.nn.softmax(scores, axis=-1)
    weights_low = low(weights)
    pooled = low(jnp.einsum("iht,itd->ihd", weights_low, hidden, preferred_element_type=F32))
    mass = jnp.sum(weights_low.astype(F32), axis=-1)
    mixed = dot(pooled.reshape(-1, WIDTH), value_w).reshape(images, HEADS, WIDTH)
    mixed = mixed + mass[:, :, None] * value_bias
    attended = low(jnp.sum(jnp.where(mask16, mixed, 0.0), axis=1))
    resid = class_state + dot(attended, output_w) + out_bias
    hidden_two = low(layer_norm(resid, gain_two, shift_two))
    preact = dot(hidden_two, fc_in_w, NT) + fc_in_bias
    active = low(exact_gelu(preact))
    state = resid + dot(active, fc_out_w) + fc_out_bias
    final = low(layer_norm(state, gain_end, shift_end))
    projected = dot(final, proj_w, NT)
    unit = low(normalize(projected))
    partners = lax.all_gather(partner_emb, ("img", "seq"), axis=0, tiled=True)
    count = partners.shape[0]
    logits = dot(unit, partners, NT) / SOFTMAX_SCALE
    onehot = (jnp.arange(count, dtype=jnp.int32)[None] == partner_index[:, None]).astype(F32)
    total = jax.nn.logsumexp(logits, axis=-1)
    loss_part = jnp.sum(total - jnp.sum(logits * onehot, axis=-1)) / count
    d_logits = (jax.nn.softmax(logits, axis=-1) - onehot) / count
    d_unit = dot(low(d_logits / SOFTMAX_SCALE), partners)
    d_projected = low(jax.vjp(normalize, projected)[1](d_unit)[0])
    d_final = dot(d_projected, proj_w)
    d_state, d_gain_end, d_shift_end = jax.vjp(layer_norm, state, gain_end, shift_end)[1](d_final)
    d_state_low = low(d_state)
    d_active = dot(d_state_low, fc_out_w, NT)
    d_preact = low(jax.vjp(exact_gelu, preact)[1](d_active)[0])
    d_hidden_two = dot(d_preact, fc_in_w)
    d_norm, d_gain_two, d_shift_two = jax.vjp(layer_norm, resid, gain_two, shift_two)[1](
        d_hidden_two
    )
    d_resid = d_state + d_norm
    d_resid_low = low(d_resid)
    d_attended = low(dot(d_resid_low, output_w, NT))
    wide = jnp.where(mask16, d_attended[:, None, :], jnp.zeros((), BF))
    d_pooled = low(dot(wide.reshape(-1, WIDTH), value_w, NT)).reshape(images, HEADS, WIDTH)
    d_weights = jnp.einsum("ihd,itd->iht", d_pooled, hidden, preferred_element_type=F32)
    d_weights = d_weights + jnp.sum(wide.astype(F32) * value_bias, axis=-1)[:, :, None]
    d_scores = low(weights * (d_weights - jnp.sum(weights * d_weights, axis=-1, keepdims=True)))
    d_hidden = jnp.einsum("iht,ihd->itd", weights_low, d_pooled, preferred_element_type=F32)
    d_hidden = d_hidden + jnp.einsum("iht,hd->itd", d_scores, qk, preferred_element_type=F32)
    pull = jnp.einsum("iht,itd->hd", d_scores, hidden, preferred_element_type=F32)
    d_query = jnp.sum(jnp.where(mask16, dot(low(pull), key_w), 0.0), axis=0) * SCALE
    d_class_hidden = dot(low(d_query)[None], query_w, NT)
    d_tokens, d_gain_one, d_shift_one = jax.vjp(layer_norm, tokens, gain_one, shift_one)[1](
        d_hidden
    )
    d_class, d_gain_cls, d_shift_cls = jax.vjp(layer_norm, class_state[None], gain_one, shift_one)[
        1
    ](d_class_hidden)
    d_class = d_class[0] + jnp.sum(d_tokens[:, 0], axis=0) + jnp.sum(d_resid, axis=0)
    d_patch = d_tokens[:, 1:]
    d_embed_w = jnp.einsum("itp,itd->pd", pixels, low(d_patch), preferred_element_type=F32)
    d_value_w = dot(pooled.reshape(-1, WIDTH), wide.reshape(-1, WIDTH), TN)
    d_key_w = dot(pull, query_heads.astype(F32), TN, precision=lax.Precision.HIGHEST)
    small_local = jnp.concatenate(
        [
            d_class[None],
            d_class[None],
            jnp.sum(d_patch, axis=0),
            jnp.sum(d_patch, axis=(0, 1))[None],
            (d_gain_one + d_gain_cls)[None],
            (d_shift_one + d_shift_cls)[None],
            d_query[None],
            jnp.sum(wide.astype(F32) * mass[:, :, None], axis=(0, 1))[None],
            jnp.sum(d_resid, axis=0)[None],
            d_gain_two[None],
            d_shift_two[None],
            jnp.sum(d_preact.astype(F32), axis=0).reshape(FF // WIDTH, WIDTH),
            jnp.sum(d_state, axis=0)[None],
            d_gain_end[None],
            d_shift_end[None],
        ],
        axis=0,
    )
    grad_table = jnp.concatenate(
        [
            d_embed_w,
            class_hidden.astype(F32)[:, None] * d_query[None, :],
            d_key_w,
            d_value_w,
            dot(attended, d_resid_low, TN),
            dot(d_preact, hidden_two, TN),
            dot(active, d_state_low, TN),
            dot(d_projected, final, TN),
            jnp.zeros(((chips * slots - UNIT_COUNT) * ROWS_PER_UNIT, WIDTH), F32),
        ],
        axis=0,
    ).reshape(chips * slots, ROWS_PER_UNIT, WIDTH)
    small_grad, loss = lax.psum((small_local, loss_part), ("img", "seq"))
    core_half = lax.psum_scatter(low(grad_table), "seq", scatter_dimension=1, tiled=True)
    own_grad = lax.psum_scatter(core_half.astype(F32), "img", scatter_dimension=0, tiled=True)
    owner_total = lax.psum(jnp.sum(own_grad * own_grad), ("img", "seq"))
    grad_norm = jnp.sqrt(owner_total + jnp.sum(small_grad * small_grad))
    factor = 1.0 / jnp.maximum(grad_norm, 1.0)
    slot_grad = to_slots(own_grad, near, img, chips)
    step_value = step_count.astype(F32)
    new_masters, new_first, new_second = adamw(
        masters, slot_grad * factor, first_moment_slots, second_moment_slots, step_value
    )
    new_small, new_small_first, new_small_second = adamw(
        small_params, small_grad * factor, small_first, small_second, step_value
    )
    return (
        new_masters, new_first, new_second, new_small, new_small_first, new_small_second,
        loss, grad_norm,
    )


def solution(mesh):
    chip, devices = "img", ("img", "seq")
    core, body = "seq", per_device_any
    if mesh.shape["img"] == CHIPS and mesh.shape["seq"] == 2:
        mesh = jax.sharding.Mesh(mesh.devices.reshape(4, 2, 2, 2), ALL)
        chip, devices, core, body = CHIP, ALL, "c", per_device_16
    weights = P(chip, core, None)
    return jax.shard_map(
        body,
        mesh=mesh,
        in_specs=(
            P(devices, None, None),
            P(devices, None),
            P(devices),
            P(devices, None),
            weights,
            weights,
            weights,
            P(),
            P(),
            P(),
            P(),
            P(),
        ),
        out_specs=(weights, weights, weights, P(), P(), P(), P(), P()),
        check_vma=False,
    )
```

```python
import functools
import math

import jax
import jax.numpy as jnp
from jax import lax
from jax.experimental import pallas as pl
from jax.experimental.pallas import tpu as pltpu
from jax.sharding import PartitionSpec as P

WIDTH = 1024
HEADS = 16
HEAD_DIM = 64
FF = 4096
PIX = 3072
PROJ = 768
TOKS = 50
PATCHES = TOKS - 1
ROWS_PER_UNIT = 32
UNIT_COUNT = 504
JITTER = 2

EPS_NORM = 1e-06
SOFTMAX_SCALE = 0.07
LEARN_RATE = 0.03
BETA_ONE = 0.5
BETA_TWO = 0.5
DECAY_RATE = 0.05
ADAM_EPS = 1e-08
MASKED = -1000000000.0
SCALE = HEAD_DIM ** (-0.5)

F32 = jnp.float32
BF = jnp.bfloat16
ROW_BASE = 1 + TOKS
ROW_TAIL = ROW_BASE + 8 + FF // WIDTH
SLOT = 64


def low(values):
    return values.astype(BF)


def dot(a, b, dims=((1,), (0,)), precision=None):
    return lax.dot_general(a, b, (dims, ((), ())), precision=precision, preferred_element_type=F32)


NN = ((1,), (0,))
NT = ((1,), (1,))
TN = ((0,), (0,))


def layer_norm(values, gain, shift):
    center = values - jnp.mean(values, axis=-1, keepdims=True)
    spread = jnp.mean(center * center, axis=-1, keepdims=True)
    return center * lax.rsqrt(spread + EPS_NORM) * gain + shift


def normalize(values):
    return values * lax.rsqrt(jnp.sum(values * values, axis=-1, keepdims=True) + EPS_NORM)


def exact_gelu(values):
    return jax.nn.gelu(values, approximate=False)


def small_parts(small):
    base, tail = ROW_BASE, ROW_TAIL
    return (
        small[0],
        small[1:base],
        small[base],
        small[base + 1],
        small[base + 2],
        small[base + 3],
        small[base + 4],
        small[base + 5],
        small[base + 6],
        small[base + 7],
        small[base + 8 : tail].reshape(FF),
        small[tail],
        small[tail + 1],
        small[tail + 2],
    )


def adamw(weight, grad, first, second, step):
    first_new = BETA_ONE * first + (1.0 - BETA_ONE) * grad
    second_new = BETA_TWO * second + (1.0 - BETA_TWO) * grad * grad
    first_hat = first_new / (1.0 - jnp.power(BETA_ONE, step))
    second_hat = second_new / (1.0 - jnp.power(BETA_TWO, step))
    weight_new = weight - LEARN_RATE * (
        first_hat / (jnp.sqrt(second_hat) + ADAM_EPS) + DECAY_RATE * weight
    )
    return (weight_new, first_new, second_new)


def halo(values, chips, axes):
    before = lax.ppermute(values[-JITTER:], axes, [(i, i + 1) for i in range(chips - 1)])
    behind = lax.ppermute(values[:JITTER], axes, [(i + 1, i) for i in range(chips - 1)])
    return before, behind


def with_halo(values, chips, axes):
    before, behind = halo(values, chips, axes)
    return jnp.concatenate([before, values, behind], axis=0)


def slots_near(slot_unit_index, img, slots):
    padded = jnp.pad(slot_unit_index, (JITTER, JITTER), constant_values=-1)
    return lax.dynamic_slice(padded, (img * slots,), (slots + 2 * JITTER,))


def pick(ext, matches, slots):
    out = jnp.zeros((slots,) + ext.shape[1:], ext.dtype)
    for shift in range(2 * JITTER + 1):
        out = jnp.where(matches[shift][:, None, None], ext[shift : shift + slots], out)
    return out


def to_units(values, near, img, chips, axes="img"):
    slots = values.shape[0]
    ids = img * slots + jnp.arange(slots, dtype=jnp.int32)
    matches = [near[s : s + slots] == ids for s in range(2 * JITTER + 1)]
    return pick(with_halo(values, chips, axes), matches, slots)


def to_slots(values, near, img, chips, axes="img"):
    slots = values.shape[0]
    here = near[JITTER : JITTER + slots]
    ids = img * slots + jnp.arange(slots, dtype=jnp.int32)
    matches = [
        (here == ids + (s - JITTER)) & (here < UNIT_COUNT) for s in range(2 * JITTER + 1)
    ]
    return pick(with_halo(values, chips, axes), matches, slots)


def shuffle_matrix():
    source = lax.broadcasted_iota(jnp.int32, (256, 256), 0)
    target = lax.broadcasted_iota(jnp.int32, (256, 256), 1)
    moved = ((source // 16) % 2) * 128 + (source // 32) * 16 + source % 16
    return (moved == target).astype(F32).astype(BF)


def vmem():
    return pl.BlockSpec(memory_space=pltpu.VMEM)


def smem():
    return pl.BlockSpec(memory_space=pltpu.SMEM)


def shape(dims, dtype):
    return jax.ShapeDtypeStruct(dims, dtype)


def call(kernel, name, scalars, arrays, outs, scratch=(), mib=16, flops=10**9, far=()):
    moved = sum(a.size * a.dtype.itemsize for a in [*arrays, *outs, *far])
    return pl.pallas_call(
        kernel,
        in_specs=[smem()] * len(scalars)
        + [vmem()] * len(arrays)
        + [pl.BlockSpec(memory_space=pl.ANY)] * len(far),
        out_specs=[vmem()] * len(outs),
        out_shape=list(outs),
        scratch_shapes=list(scratch),
        compiler_params=pltpu.CompilerParams(vmem_limit_bytes=mib * 2**20),
        cost_estimate=pl.CostEstimate(flops=flops, bytes_accessed=moved, transcendentals=0),
        name=name,
    )(*scalars, *arrays, *far)


def prep_kernel(pix_ref, shuffle_ref, out_ref):
    shuffle = shuffle_ref[...]
    out_ref[...] = jnp.zeros_like(out_ref)
    for block in range(PIX // 256):
        moved = dot(pix_ref[0, :, 256 * block : 256 * block + 256], shuffle).astype(BF)
        out_ref[0, 0, :PATCHES, 128 * block : 128 * block + 128] = moved[:, :128]
        out_ref[1, 0, :PATCHES, 128 * block : 128 * block + 128] = moved[:, 128:]


def prep(pixels, shuffle):
    images = pixels.shape[0]
    return pl.pallas_call(
        prep_kernel,
        grid=(images,),
        in_specs=[
            pl.BlockSpec((1, PATCHES, PIX), lambda i: (i, 0, 0)),
            pl.BlockSpec((256, 256), lambda i: (0, 0)),
        ],
        out_specs=pl.BlockSpec((2, 1, SLOT, PIX // 2), lambda i: (0, i, 0, 0)),
        out_shape=jax.ShapeDtypeStruct((2, images, SLOT, PIX // 2), BF),
        compiler_params=pltpu.CompilerParams(vmem_limit_bytes=24 * 2**20),
        cost_estimate=pl.CostEstimate(flops=8 * 10**8, bytes_accessed=6 * 2**20, transcendentals=0),
        name="prep",
    )(pixels, shuffle)


def head_mask(rows):
    lane = lax.broadcasted_iota(jnp.int32, (rows, WIDTH), 1) // HEAD_DIM
    row = lax.broadcasted_iota(jnp.int32, (rows, WIDTH), 0) % HEADS
    return lane == row


def norm_parts(values):
    center = values - jnp.mean(values, axis=-1, keepdims=True)
    rstd = lax.rsqrt(jnp.mean(center * center, axis=-1, keepdims=True) + EPS_NORM)
    return center * rstd, rstd


def norm_back(grad, gain, xhat, rstd):
    gy = grad * gain
    return rstd * (
        gy - jnp.mean(gy, axis=-1, keepdims=True) - xhat * jnp.mean(gy * xhat, axis=-1, keepdims=True)
    )


def rowsum(values):
    return jnp.sum(values, axis=0, keepdims=True)


def to_halves(values, shuffle):
    first, second = [], []
    for block in range(values.shape[1] // 256):
        moved = low(dot(values[:, 256 * block : 256 * block + 256], shuffle))
        first.append(moved[:, :128])
        second.append(moved[:, 128:])
    return jnp.concatenate(first, axis=1), jnp.concatenate(second, axis=1)


def to_natural(first, second, shuffle):
    out = []
    for block in range(first.shape[1] // 128):
        lanes = slice(128 * block, 128 * block + 128)
        both = jnp.concatenate([first[:, lanes], second[:, lanes]], axis=1)
        out.append(low(dot(both, shuffle, NT)))
    return jnp.concatenate(out, axis=1)


R_PATCH, R_GAIN1, R_SHIFT1, R_VB, R_OB, R_GAIN2, R_SHIFT2 = 51, 52, 53, 55, 56, 57, 58
R_C2, R_GAINF, R_SHIFTF, R_SMALL = 63, 64, 65, 66
QUARTER = 128


def partner_kernel(raw_ref, out_ref):
    source = lax.broadcasted_iota(jnp.int32, (PROJ, PROJ), 0)
    target = lax.broadcasted_iota(jnp.int32, (PROJ, PROJ), 1)
    moved = ((source // 16) % 2) * (PROJ // 2) + (source // 32) * 16 + source % 16
    select = low((moved == target).astype(F32))
    out_ref[...] = low(dot(raw_ref[...].reshape(-1, PROJ), select))


def second_block_kernel(role_ref, outer_ref, low_ref, mid_ref, two_ref, three_ref, out_ref, sems):
    chip, plane = role_ref[0], role_ref[1]
    first = out_ref.at[pl.ds(0, 256)]
    last = out_ref.at[pl.ds(256, QUARTER + HEADS)]

    @pl.when(chip < 3)
    def _():
        head = pltpu.make_async_copy(outer_ref, first, sems.at[0])
        tail = pltpu.make_async_copy(low_ref, last, sems.at[1])
        head.start()
        tail.start()
        head.wait()
        tail.wait()

    for number, ref in ((1, mid_ref), (2, two_ref), (3, three_ref)):
        here = (plane == number) | (chip == 3) if number == 3 else plane == number

        @pl.when(here)
        def _():
            whole = pltpu.make_async_copy(ref, out_ref, sems.at[0])
            whole.start()
            whole.wait()


def second_block(role, pieces):
    any_place = pl.BlockSpec(memory_space=pl.ANY)
    return pl.pallas_call(
        second_block_kernel,
        in_specs=[smem()] + [any_place] * len(pieces),
        out_specs=pl.BlockSpec(memory_space=pltpu.HBM),
        out_shape=shape((256 + QUARTER + HEADS, WIDTH), BF),
        scratch_shapes=[pltpu.SemaphoreType.DMA((2,))],
        compiler_params=pltpu.CompilerParams(vmem_limit_bytes=4 * 2**20),
        cost_estimate=pl.CostEstimate(flops=0, bytes_accessed=2 * 2**20, transcendentals=0),
        name="second_block",
    )(role, *pieces)


def forward_kernel(segments, images, where_ref, pix_ref, rows_ref, valid_ref, shuffle_ref, *refs):
    count = len(segments)
    own, peer = refs[:count], refs[count : 2 * count]
    (
        hid_ref, xhat_ref, rstd_ref, p_ref, pooled_ref, mass_ref, wv_ref, wo_ref, qk_ref,
        resid_ref, low_ref, acc_ref, pool_ref, half_ref, table_ref, sems,
    ) = refs[2 * count :]
    col, core = where_ref[0], where_ref[1]
    waits = ([], [])
    for flip, group in ((0, own), (1, peer)):
        half = core ^ flip
        for (source, parts, late), ref in zip(segments, group):
            block = col ^ source
            for row, lane, rows in parts:
                part = ref.at[pl.ds(row, rows)]
                line = pl.multiple_of(block * 512 + lane, 128)
                copy = pltpu.make_async_copy(part, table_ref.at[half, pl.ds(line, rows)], sems.at[flip])
                copy.start()
                waits[flip].append(copy)
            if late >= 0:
                part = ref.at[pl.ds(late, QUARTER)]
                line = pl.multiple_of(block * QUARTER, QUARTER)
                copy = pltpu.make_async_copy(part, wo_ref.at[half, pl.ds(line, QUARTER)], sems.at[2])
                copy.start()
                waits[1].append(copy)
                part = ref.at[pl.ds(late + QUARTER, HEADS)]
                copy = pltpu.make_async_copy(part, half_ref.at[half, block], sems.at[3])
                copy.start()
                waits[1].append(copy)
    patch = rows_ref[2 : 1 + TOKS] + rows_ref[R_PATCH : R_PATCH + 1]
    class_state = rows_ref[0:1] + rows_ref[1:2]
    for i in range(images):
        acc_ref[SLOT * i : SLOT * i + PATCHES] = patch
        acc_ref[SLOT * i + PATCHES : SLOT * i + TOKS] = class_state
        acc_ref[SLOT * i + TOKS : SLOT * (i + 1)] = jnp.zeros((SLOT - TOKS, WIDTH), F32)
    for copy in waits[0]:
        copy.wait()
    acc_ref[...] += dot(pix_ref[core], table_ref[core, :1536])
    for copy in waits[1]:
        copy.wait()
    acc_ref[...] += dot(pix_ref[1 - core], table_ref[1 - core, :1536])
    wv_ref[...] = table_ref[:, 1536:]
    shuffle = shuffle_ref[...]
    gain, shift, value_bias = (rows_ref[r : r + 1] for r in (R_GAIN1, R_SHIFT1, R_VB))
    half = WIDTH // 2
    qk = to_natural(half_ref[0, 0, :, :half], half_ref[1, 0, :, :half], shuffle)
    qk_ref[...] = qk
    valid = valid_ref[...] > 0
    for i in range(images):
        part = slice(SLOT * i, SLOT * (i + 1))
        xhat, rstd = norm_parts(acc_ref[part])
        hid = low(xhat * gain + shift)
        xhat_ref[part] = xhat
        rstd_ref[part] = jnp.broadcast_to(rstd, (SLOT, 128))
        hid_ref[part] = hid
        scores = jnp.where(valid[part], dot(hid, qk, NT), MASKED)
        e = jnp.exp(scores - jnp.max(scores, axis=0, keepdims=True))
        p = e / jnp.sum(e, axis=0, keepdims=True)
        p_ref[part] = p
        pb = low(p)
        pool_ref[HEADS * i : HEADS * (i + 1)] = low(dot(pb, hid, TN))
        mass_ref[HEADS * i : HEADS * (i + 1)] = dot(pb, jnp.ones((SLOT, 128), BF), TN)
    pooled_ref[0], pooled_ref[1] = to_halves(pool_ref[...], shuffle)
    rows = images * HEADS
    mixed = dot(pooled_ref[0], wv_ref[0]) + dot(pooled_ref[1], wv_ref[1])
    mixed = mixed + mass_ref[:, 0:1] * value_bias
    mixed = jnp.where(head_mask(rows), mixed, 0.0)
    joined = low(jnp.sum(mixed.reshape(images, HEADS, WIDTH), axis=1))
    first, second = to_halves(joined, shuffle)
    resid = class_state + dot(first, wo_ref[0]) + dot(second, wo_ref[1])
    resid = resid + rows_ref[R_OB : R_OB + 1]
    resid_ref[...] = resid
    xhat, _ = norm_parts(resid)
    hidden = low(xhat * rows_ref[R_GAIN2 : R_GAIN2 + 1] + rows_ref[R_SHIFT2 : R_SHIFT2 + 1])
    sent = jnp.concatenate([hidden, first, second], axis=1)
    low_ref[...] = jnp.broadcast_to(sent[None], low_ref.shape)


def forward_call(segments, images, where, pix, own, peer, rows, valid, shuffle):
    tokens = images * SLOT
    outs = [
        shape((tokens, WIDTH), BF),
        shape((tokens, WIDTH), F32),
        shape((tokens, 128), F32),
        shape((tokens, HEADS), F32),
        shape((2, images * HEADS, WIDTH // 2), BF),
        shape((images * HEADS, 128), F32),
        shape((2, WIDTH // 2, WIDTH), BF),
        shape((2, WIDTH // 2, WIDTH), BF),
        shape((HEADS, WIDTH), BF),
        shape((images, WIDTH), F32),
        shape((8, images, 2 * WIDTH), BF),
    ]
    scratch = [
        pltpu.VMEM((tokens, WIDTH), F32),
        pltpu.VMEM((images * HEADS, WIDTH), BF),
        pltpu.VMEM((2, 4, HEADS, WIDTH), BF),
        pltpu.VMEM((2, 2048, WIDTH), BF),
        pltpu.SemaphoreType.DMA((4,)),
    ]
    return call(
        functools.partial(forward_kernel, segments, images), "forward", [where],
        [pix, rows, valid, shuffle], outs, scratch, mib=52, flops=4 * 10**9,
        far=[*own, *peer],
    )


def fetch(pick_ref, slot, candidates, out_ref, sem):
    for number, candidate in enumerate(candidates):

        @pl.when(pick_ref[slot] == number)
        def _():
            pltpu.make_async_copy(candidate, out_ref, sem).start()


def arrived(candidate, out_ref, sem):
    pltpu.make_async_copy(candidate, out_ref, sem).wait()


def ff_kernel(pick_ref, hid_ref, bias_ref, *refs):
    candidates, (pre_ref, act_ref, part_ref, w1_ref, w2_ref, sems) = refs[:6], refs[6:]
    fetch(pick_ref, 0, candidates, w1_ref, sems.at[0])
    fetch(pick_ref, 1, candidates, w2_ref, sems.at[1])
    hidden = hid_ref[:, :, :WIDTH].reshape(-1, WIDTH)
    arrived(candidates[0], w1_ref, sems.at[0])
    pre = dot(hidden, w1_ref[...], NT) + bias_ref[...]
    pre_ref[...] = pre
    active = low(0.5 * pre * (1.0 + lax.erf(pre * (0.5**0.5))))
    act_ref[...] = active
    arrived(candidates[0], w2_ref, sems.at[1])
    part_ref[...] = low(dot(active, w2_ref[...])).reshape(part_ref.shape)


def ff_back_kernel(pick_ref, dst_ref, pre_ref, *refs):
    candidates, (dpre_ref, sum_ref, part_ref, w1_ref, w2_ref, sems) = refs[:6], refs[6:]
    fetch(pick_ref, 1, candidates, w2_ref, sems.at[1])
    fetch(pick_ref, 0, candidates, w1_ref, sems.at[0])
    d_state = dst_ref[:, :, :WIDTH].reshape(-1, WIDTH)
    pre = pre_ref[...]
    slope = 0.5 * (1.0 + lax.erf(pre * (0.5**0.5))) + pre * jnp.exp(-0.5 * pre * pre) * (
        1.0 / (2.0 * math.pi) ** 0.5
    )
    arrived(candidates[0], w2_ref, sems.at[1])
    d_pre = low(dot(d_state, w2_ref[...], NT) * slope)
    dpre_ref[...] = d_pre
    sum_ref[...] = rowsum(d_pre.astype(F32))
    arrived(candidates[0], w1_ref, sems.at[0])
    part_ref[...] = low(dot(d_pre, w1_ref[...])).reshape(part_ref.shape)


def ff_call(kernel, name, pick, arrays, candidates, outs):
    moved = sum(a.size * a.dtype.itemsize for a in list(arrays) + list(outs))
    return pl.pallas_call(
        kernel,
        in_specs=[smem()]
        + [vmem()] * len(arrays)
        + [pl.BlockSpec(memory_space=pl.ANY)] * len(candidates),
        out_specs=[vmem()] * len(outs),
        out_shape=list(outs),
        scratch_shapes=[
            pltpu.VMEM((512, WIDTH), BF),
            pltpu.VMEM((512, WIDTH), BF),
            pltpu.SemaphoreType.DMA((2,)),
        ],
        compiler_params=pltpu.CompilerParams(vmem_limit_bytes=24 * 2**20),
        cost_estimate=pl.CostEstimate(
            flops=2 * 10**8, bytes_accessed=moved + 2 * 2**20, transcendentals=0
        ),
        name=name,
    )(pick, *arrays, *candidates)


def head_kernel(
    where_ref, part_ref, resid_ref, pj_ref, pjp_ref, partners_ref, target_ref, rows_ref,
    state_ref, low_ref, vec_ref, dz_ref,
):
    images = resid_ref.shape[0]
    state = resid_ref[...] + jnp.sum(part_ref[...].astype(F32), axis=0) + rows_ref[R_C2 : R_C2 + 1]
    gain = rows_ref[R_GAINF : R_GAINF + 1]
    xhat, rstd = norm_parts(state)
    final = low(xhat * gain + rows_ref[R_SHIFTF : R_SHIFTF + 1])
    z_own, z_peer = dot(final, pj_ref[...], NT), dot(final, pjp_ref[...], NT)
    square = jnp.sum(z_own * z_own, axis=-1, keepdims=True) + jnp.sum(
        z_peer * z_peer, axis=-1, keepdims=True
    )
    inv = lax.rsqrt(square + EPS_NORM)
    core = where_ref[1]
    half = PROJ // 2
    own_lanes = pl.ds(pl.multiple_of(core * half, 128), half)
    peer_lanes = pl.ds(pl.multiple_of((1 - core) * half, 128), half)
    ptn_own, ptn_peer = partners_ref[:, own_lanes], partners_ref[:, peer_lanes]
    logits = dot(low(z_own * inv), ptn_own, NT) + dot(low(z_peer * inv), ptn_peer, NT)
    logits = logits / SOFTMAX_SCALE
    total = logits.shape[1]
    hit = lax.broadcasted_iota(jnp.int32, (images, total), 1) == target_ref[...]
    top = jnp.max(logits, axis=-1, keepdims=True)
    e = jnp.exp(logits - top)
    mass = jnp.sum(e, axis=-1, keepdims=True)
    aim = jnp.sum(jnp.where(hit, logits, 0.0), axis=-1, keepdims=True)
    losses = jnp.log(mass) + top - aim
    d_logits = (e / mass - jnp.where(hit, 1.0, 0.0)) / total
    g_logits = low(d_logits / SOFTMAX_SCALE)
    d_own, d_peer = dot(g_logits, ptn_own), dot(g_logits, ptn_peer)
    along = jnp.sum(d_own * z_own, axis=-1, keepdims=True) + jnp.sum(
        d_peer * z_peer, axis=-1, keepdims=True
    )
    shrink = along * inv * inv * inv
    dz_own, dz_peer = low(d_own * inv - z_own * shrink), low(d_peer * inv - z_peer * shrink)
    dz_ref[:, own_lanes] = dz_own
    dz_ref[:, peer_lanes] = dz_peer
    d_final = dot(dz_own, pj_ref[...]) + dot(dz_peer, pjp_ref[...])
    d_state = norm_back(d_final, gain, xhat, rstd)
    state_ref[...] = d_state
    sent = jnp.concatenate([low(d_state), dz_ref[...], final], axis=1)
    low_ref[...] = jnp.broadcast_to(sent[None], low_ref.shape)
    vec_ref[...] = jnp.zeros_like(vec_ref)
    vec_ref[0:1] = rowsum(d_state)
    vec_ref[1:2] = rowsum(d_final * xhat)
    vec_ref[2:3] = rowsum(d_final)
    vec_ref[3:4] = jnp.broadcast_to(rowsum(losses) / total, (1, WIDTH))


def backward_kernel(
    images, where_ref, part_ref, dstate_ref, resid_ref, wo_ref, wv_ref, hid_ref, xhat_ref,
    rstd_ref, p_ref, mass_ref, qk_ref, rows_ref, shuffle_ref,
    de_ref, do_ref, dres_ref, pos_ref, vec_ref, pull_ref, dom_ref, da_ref,
):
    rows = images * HEADS
    gain, value_bias = rows_ref[R_GAIN1 : R_GAIN1 + 1], rows_ref[R_VB : R_VB + 1]
    shuffle = shuffle_ref[...]
    vec_ref[...] = jnp.zeros_like(vec_ref)
    d_two = jnp.sum(part_ref[...].astype(F32), axis=0)
    xhat2, rstd2 = norm_parts(resid_ref[...])
    d_resid = dstate_ref[...] + norm_back(d_two, rows_ref[R_GAIN2 : R_GAIN2 + 1], xhat2, rstd2)
    vec_ref[3:4] = rowsum(d_resid)
    vec_ref[4:5] = rowsum(d_two * xhat2)
    vec_ref[5:6] = rowsum(d_two)
    d_low = low(d_resid)
    dres_ref[...] = jnp.broadcast_to(d_low[None], dres_ref.shape)
    d_att = to_natural(
        low(dot(d_low, wo_ref[0], NT)), low(dot(d_low, wo_ref[1], NT)), shuffle
    )
    do_ref[...] = d_att
    spread = jnp.broadcast_to(d_att.reshape(images, 1, WIDTH).astype(F32), (images, HEADS, WIDTH))
    wide = jnp.where(head_mask(rows), spread.reshape(rows, WIDTH), 0.0)
    dom_ref[...] = low(wide)
    vec_ref[2:3] = rowsum(wide * mass_ref[:, 0:1])
    da_ref[...] = to_natural(
        low(dot(dom_ref[...], wv_ref[0], NT)), low(dot(dom_ref[...], wv_ref[1], NT)), shuffle
    )
    qk = qk_ref[...]
    bias_rows = low(jnp.broadcast_to(value_bias, (8, WIDTH)))
    real = lax.broadcasted_iota(jnp.int32, (SLOT, WIDTH), 0) < PATCHES
    for i in range(images):
        part = slice(SLOT * i, SLOT * (i + 1))
        mine = slice(HEADS * i, HEADS * (i + 1))
        hid, p, da = hid_ref[part], p_ref[part], da_ref[mine]
        dp = dot(hid, da, NT) + dot(bias_rows, dom_ref[mine], NT)[0:1]
        ds = low(p * (dp - rowsum(p * dp)))
        dh = dot(low(p), da) + dot(ds, qk)
        pull = dot(ds, hid, TN)
        xhat, rstd = xhat_ref[part], rstd_ref[part, 0:1]
        dx = norm_back(dh, gain, xhat, rstd)
        de_ref[part] = low(jnp.where(real, dx, 0.0))
        vec_ref[0:1] += rowsum(dh * xhat)
        vec_ref[1:2] += rowsum(dh)
        if i == 0:
            pos_ref[...] = dx
            pull_ref[...] = pull
        else:
            pos_ref[...] += dx
            pull_ref[...] += pull


def backward_call(images, where, arrays):
    tokens = images * SLOT
    outs = [
        shape((tokens, WIDTH), BF),
        shape((images, WIDTH), BF),
        shape((8, images, WIDTH), BF),
        shape((SLOT, WIDTH), F32),
        shape((8, WIDTH), F32),
        shape((HEADS, WIDTH), F32),
    ]
    scratch = [pltpu.VMEM((images * HEADS, WIDTH), BF)] * 2
    return call(
        functools.partial(backward_kernel, images), "backward", [where], arrays, outs, scratch
    )


def rows_kernel(where_ref, act_ref, dpre_ref, hid_ref, dst_ref, dres_ref, out_ref):
    half = WIDTH // 2
    base = 3 * WIDTH
    out_ref[:, :half] = act_ref[...]
    out_ref[:, half:WIDTH] = dpre_ref[...]
    count = out_ref.shape[0]
    out_ref[:, WIDTH : 2 * WIDTH] = hid_ref[:, :, :WIDTH].reshape(count, WIDTH)
    out_ref[:, 2 * WIDTH : base] = dst_ref[:, :, :WIDTH].reshape(count, WIDTH)

    @pl.when(where_ref[0] == 2)
    def _():
        out_ref[:, base : base + WIDTH] = hid_ref[:, :, WIDTH:].reshape(count, WIDTH)
        out_ref[:, base + WIDTH :] = dres_ref[...].reshape(count, WIDTH)

    @pl.when(where_ref[0] != 2)
    def _():
        out_ref[:, base : base + WIDTH + PROJ] = dst_ref[:, :, WIDTH:].reshape(count, WIDTH + PROJ)
        out_ref[:, base + WIDTH + PROJ :] = jnp.zeros((count, WIDTH - PROJ), BF)


def embed_grad_kernel(
    images, plan, where_ref, pix_ref, pixp_ref, de_ref, dep_ref, pooled_ref, pooledp_ref,
    do_ref, dop_ref, *out_refs,
):
    col = where_ref[0]
    heads = images * HEADS
    for (source, first, rows, _), out_ref in zip(plan, out_refs):
        block = col ^ source

        @pl.when(block < 3)
        def _():
            lanes = pl.ds(pl.multiple_of(block * 512 + first, 128), rows)
            total = dot(pix_ref[:, lanes], de_ref[...], TN) + dot(pixp_ref[:, lanes], dep_ref[...], TN)
            out_ref[...] = total.astype(out_ref.dtype)

        @pl.when(block == 3)
        def _():
            total = None
            for pooled, do in ((pooled_ref, do_ref), (pooledp_ref, dop_ref)):
                spread = jnp.broadcast_to(
                    do[...].reshape(images, 1, WIDTH).astype(F32), (images, HEADS, WIDTH)
                )
                wide = low(jnp.where(head_mask(heads), spread.reshape(heads, WIDTH), 0.0))
                term = dot(pooled[:, first : first + rows], wide, TN)
                total = term if total is None else total + term
            out_ref[...] = total.astype(out_ref.dtype)


def embed_grad_call(images, name, plan, where, arrays):
    outs = [shape((rows, WIDTH), dtype) for _, _, rows, dtype in plan]
    return call(
        functools.partial(embed_grad_kernel, images, plan), name, [where], arrays, outs
    )


def add_far_kernel(x_low_ref, x_high_ref, got_x_ref, y_low_ref, got_y_ref, y_high_ref, x_ref, y_ref):
    half = x_low_ref.shape[0]
    x_ref[:half] = x_low_ref[...]
    x_ref[half:] = low(x_high_ref[...] + got_x_ref[...].astype(F32))
    y_ref[:half] = low(y_low_ref[...] + got_y_ref[...].astype(F32))
    y_ref[half:] = y_high_ref[...]


def to_natural_exact(first, second, shuffle):
    wide = shuffle.astype(F32)
    out = []
    for block in range(first.shape[1] // 128):
        lanes = slice(128 * block, 128 * block + 128)
        both = jnp.concatenate([first[:, lanes], second[:, lanes]], axis=1)
        out.append(dot(both, wide, NT, precision=lax.Precision.HIGHEST))
    return jnp.concatenate(out, axis=1)


def collect_kernel(
    where_ref, pos_ref, vec_ref, head_ref, sum_ref, pull_ref, shuffle_ref, sent_ref, out_ref
):
    col, core = where_ref[0], where_ref[1]
    out_ref[...] = jnp.zeros_like(out_ref)
    top = pos_ref[PATCHES:TOKS] + vec_ref[3:4]
    out_ref[0:1] = top
    out_ref[1:2] = top
    patches = pos_ref[0:PATCHES]
    out_ref[2 : 1 + TOKS] = patches
    out_ref[R_PATCH : R_PATCH + 1] = rowsum(patches)
    out_ref[R_GAIN1 : R_SHIFT1 + 1] = vec_ref[0:2]
    out_ref[R_VB : R_VB + 1] = vec_ref[2:3]
    out_ref[R_OB : R_SHIFT2 + 1] = vec_ref[3:6]
    sums = jnp.broadcast_to(sum_ref[...], (8, WIDTH // 2))
    nothing = jnp.zeros_like(sums)
    row = to_natural_exact(
        jnp.where(core == 0, sums, nothing), jnp.where(core == 0, nothing, sums), shuffle_ref[...]
    )
    for block in range(4):
        mine = (col + 1) % 4 == block
        out_ref[R_SHIFT2 + 1 + block : R_SHIFT2 + 2 + block] = jnp.where(mine, row[0:1], 0.0)
    out_ref[R_C2 : R_SHIFTF + 1] = head_ref[0:3]
    out_ref[R_SMALL : R_SMALL + HEADS] = pull_ref[...]
    out_ref[R_SMALL + HEADS : R_SMALL + HEADS + 1] = head_ref[3:4]
    for number in range(sent_ref.shape[0]):
        sent_ref[number] = out_ref[3 * number : 3 * number + 3]


def share_kernel(got_ref, sent_ref):
    sent_ref[...] = jnp.broadcast_to(jnp.sum(got_ref[...], axis=0, keepdims=True), sent_ref.shape)


def query_back_kernel(core_ref, got_ref, w_ref, shuffle_ref, dq_ref, pull_ref, total_ref):
    for number in range(got_ref.shape[0]):
        total_ref[3 * number : 3 * number + 3] = got_ref[number]
    wide = shuffle_ref[...].astype(F32)
    pull = total_ref[R_SMALL : R_SMALL + HEADS]
    is_one = core_ref[0] == 1
    out = []
    for block in range(WIDTH // 256):
        moved = dot(pull[:, 256 * block : 256 * block + 256], wide, precision=lax.Precision.HIGHEST)
        out.append(jnp.where(is_one, moved[:, 128:], moved[:, :128]))
    half = jnp.concatenate(out, axis=1)
    pull_ref[...] = half
    d_query = jnp.where(head_mask(HEADS), dot(low(half), w_ref[...]), 0.0)
    dq_ref[...] = jnp.broadcast_to(rowsum(d_query) * SCALE, dq_ref.shape)


def complete_kernel(total_ref, reports_ref, rows_ref, shuffle_ref, out_ref, norm_ref):
    out_ref[...] = total_ref[0:R_SMALL]
    half = WIDTH // 2
    first = jnp.broadcast_to(reports_ref[6, :, WIDTH : WIDTH + half], (8, half))
    second = jnp.broadcast_to(reports_ref[7, :, WIDTH : WIDTH + half], (8, half))
    d_hidden = to_natural_exact(first, second, shuffle_ref[...])[0:1]
    xhat, rstd = norm_parts(rows_ref[0:1] + rows_ref[1:2])
    d_class = norm_back(d_hidden, rows_ref[R_GAIN1 : R_GAIN1 + 1], xhat, rstd)
    out_ref[0:1] += d_class
    out_ref[1:2] += d_class
    out_ref[R_GAIN1 : R_GAIN1 + 1] += d_hidden * xhat
    out_ref[R_SHIFT1 : R_SHIFT1 + 1] += d_hidden
    out_ref[R_SHIFT1 + 1 : R_SHIFT1 + 2] = reports_ref[6, :, :WIDTH]
    grads = out_ref[...]
    square = jnp.sum(jnp.sum(grads * grads, axis=0, keepdims=True), axis=1, keepdims=True)
    for number in range(reports_ref.shape[0]):
        square = square + reports_ref[number, :, WIDTH + half : WIDTH + half + 1]
    norm_ref[...] = jnp.broadcast_to(jnp.sqrt(square), (8, 128))


def owner_kernel(role_ref, pull_ref, heads_ref, class_ref, dq_ref, *refs):
    rows, out_ref = refs[:6], refs[6]
    chip, core = role_ref[0], role_ref[1]
    half = WIDTH // 2
    base = 3 * WIDTH

    def product(left, right):
        total = None
        for piece in rows:
            term = dot(left(piece), right(piece), TN)
            total = term if total is None else total + term
        return total

    @pl.when((chip >= 7) & (chip <= 14))
    def _():
        is_two = chip >= 11
        out_ref[...] = product(
            lambda piece: jnp.where(is_two, piece[:, :half], piece[:, half:WIDTH]),
            lambda piece: jnp.where(is_two, piece[:, 2 * WIDTH : base], piece[:, WIDTH : 2 * WIDTH]),
        )

    @pl.when(chip == 6)
    def _():
        lanes = pl.ds(pl.multiple_of(base + core * half, 128), half)
        out_ref[...] = product(lambda piece: piece[:, lanes], lambda piece: piece[:, base + WIDTH :])

    @pl.when(chip == 15)
    def _():
        lanes = pl.ds(pl.multiple_of(base + core * (PROJ // 2), 128), PROJ // 2)
        out_ref[: PROJ // 2] = product(
            lambda piece: piece[:, lanes],
            lambda piece: piece[:, base + PROJ : base + PROJ + WIDTH],
        )
        out_ref[PROJ // 2 :] = jnp.zeros((512 - PROJ // 2, WIDTH), F32)

    @pl.when(chip == 4)
    def _():
        out_ref[...] = dot(
            pull_ref[...], heads_ref[...].astype(F32), TN, precision=lax.Precision.HIGHEST
        )

    @pl.when(chip == 3)
    def _():
        out_ref[...] = dot(
            class_ref[...].astype(F32), jnp.concatenate([dq_ref[0:1], jnp.zeros((7, WIDTH), F32)]),
            TN, precision=lax.Precision.HIGHEST,
        )


def finish_kernel(
    role_ref, formed_ref, dq_ref, toward_ref, total_ref, first_ref, second_ref, aside_ref, third_ref,
    out_ref, top_ref, end_ref, report_ref,
):
    chip = role_ref[0]

    @pl.when(chip < 3)
    def _():
        out_ref[...] = total_ref[...] + first_ref[...].astype(F32) + second_ref[...].astype(F32)

    @pl.when(chip == 5)
    def _():
        out_ref[...] = (
            second_ref[...].astype(F32) + aside_ref[...].astype(F32) + third_ref[...].astype(F32)
        )

    @pl.when((chip >= 3) & (chip != 5))
    def _():
        out_ref[...] = formed_ref[...]

    edge = top_ref.shape[0]
    top_ref[...] = out_ref[:edge]
    end_ref[...] = out_ref[-edge:]
    grads = out_ref[...]
    square = jnp.sum(jnp.sum(grads * grads, axis=0, keepdims=True), axis=1, keepdims=True)
    report_ref[...] = jnp.concatenate(
        [dq_ref[...], toward_ref[...], jnp.broadcast_to(square, (1, 128))], axis=1
    )


def update_kernel(
    source_ref, scalar_ref, before_ref, grad_ref, behind_ref, w_ref, m_ref, v_ref,
    nw_ref, nm_ref, nv_ref,
):
    step = pl.program_id(0)
    slots = grad_ref.shape[0]
    factor, fix_one, fix_two = scalar_ref[0], scalar_ref[1], scalar_ref[2]
    for k in range(w_ref.shape[0]):
        at = source_ref[step * w_ref.shape[0] + k]
        inside = (at >= 0) & (at < slots)
        grad = jnp.where(
            inside,
            grad_ref[jnp.clip(at, 0, slots - 1)],
            jnp.where(
                at < 0,
                before_ref[jnp.clip(at + JITTER, 0, JITTER - 1)],
                behind_ref[jnp.clip(at - slots, 0, JITTER - 1)],
            ),
        )
        grad = grad * jnp.where(at >= -JITTER, factor, 0.0)
        weight = w_ref[k]
        first = BETA_ONE * m_ref[k] + (1.0 - BETA_ONE) * grad
        second = BETA_TWO * v_ref[k] + (1.0 - BETA_TWO) * grad * grad
        nm_ref[k] = first
        nv_ref[k] = second
        nw_ref[k] = weight - LEARN_RATE * (
            (first * fix_one) / (jnp.sqrt(second * fix_two) + ADAM_EPS) + DECAY_RATE * weight
        )


def update_call(source, scalars, before, grads, behind, masters, first, second):
    slots, part, width = masters.shape
    block = 4
    spec = pl.BlockSpec((block, part, width), lambda i: (i, 0, 0))
    return pl.pallas_call(
        update_kernel,
        grid=(slots // block,),
        in_specs=[smem(), smem(), vmem(), vmem(), vmem(), spec, spec, spec],
        out_specs=[spec] * 3,
        out_shape=[shape(masters.shape, F32)] * 3,
        compiler_params=pltpu.CompilerParams(vmem_limit_bytes=58 * 2**20),
        cost_estimate=pl.CostEstimate(
            flops=2 * 10**7, bytes_accessed=7 * masters.size * 4, transcendentals=0
        ),
        name="update",
    )(source, scalars, before, grads, behind, masters, first, second)


CHIPS = 16
CHIP = ("z", "y", "x")
ALL = ("z", "y", "x", "c")
PLANE = ("y", "x", "c")
FLIP_X = [(i, i ^ 1) for i in range(CHIPS)]
FLIP_Y = [(i, i ^ 2) for i in range(CHIPS)]
FLIP_CORE = [(0, 1), (1, 0)]


def hop(values, pairs):
    return lax.ppermute(values, CHIP, pairs)


def swap(values):
    return lax.ppermute(values, "c", FLIP_CORE)


def after(values, *others):
    return lax.optimization_barrier((values,) + others)[0]


def among(img, chips):
    hit = img == chips[0]
    for chip in chips[1:]:
        hit = hit | (img == chip)
    return hit


def choose(img, cases, otherwise):
    out = otherwise
    for chips, values in cases:
        out = jnp.where(among(img, chips), values, out)
    return out


def together(*values):
    return lax.optimization_barrier(values)


def plane_gather(block, diagonal_by_x):
    by_x, by_y, block_peer = hop(block, FLIP_X), hop(block, FLIP_Y), swap(block)
    proj_top = jnp.where(img == 15, corner[0], corner[1] + corner[2] + corner[3])
    diagonal = hop(by_y, FLIP_X) if diagonal_by_x else hop(by_x, FLIP_Y)
    return [block, by_x, by_y, diagonal]


def in_plane(values):
    return lax.all_to_all(values, PLANE, 0, 0, tiled=True)


def from_all(values):
    sent = jnp.broadcast_to(values[None], (2 * CHIPS,) + values.shape)
    return lax.all_to_all(sent, ALL, 0, 0, tiled=True)


def natural(values):
    lead = values.shape[:-2]
    units = values.shape[-1] // 16
    split = values.reshape(lead + (2, units, 16))
    return jnp.swapaxes(split, -3, -2).reshape(lead + (units * 32,))


def halves(values):
    lead = values.shape[:-1]
    units = values.shape[-1] // 32
    return jnp.swapaxes(values.reshape(lead + (units, 2, 16)), -3, -2).reshape(
        lead + (2, units * 16)
    )


def per_device_16(
    pixels, keep_mask, partner_index, partner_emb, masters, first_moment_slots,
    second_moment_slots, slot_unit_index, small_params, small_first, small_second, step_count,
):
    img, core = lax.axis_index(CHIP), lax.axis_index("c")
    col, plane = img % 4, img // 4
    images = pixels.shape[0]
    slots = masters.shape[0]
    is_one = core == 1
    where = jnp.stack([col, core]).astype(jnp.int32)
    shuffle = shuffle_matrix()
    rows = small_params
    class_state = small_params[0] + small_params[1]

    def mine_of(pair):
        return jnp.where(is_one, pair[1], pair[0])

    def theirs_of(pair):
        return jnp.where(is_one, pair[0], pair[1])

    near = slots_near(slot_unit_index, img, slots)
    held = low(masters)
    ids = img * slots + jnp.arange(slots, dtype=jnp.int32)
    matches = [near[s : s + slots] == ids for s in range(2 * JITTER + 1)]
    middle = pick(held[6:26], [m[8:24] for m in matches], 16).reshape(256, WIDTH)
    one_a = hop(middle, [(0, 4), (1, 5), (2, 6), (5, 7)])
    partners = from_all(after(partner_emb, middle))
    before, behind = halo(after(held, middle), CHIPS, CHIP)
    lower = pick(jnp.concatenate([before, held[:10]]), [m[:8] for m in matches], 8)
    upper = pick(jnp.concatenate([held[22:], behind]), [m[24:] for m in matches], 8)
    outer = jnp.concatenate([lower, upper]).reshape(256, WIDTH)
    own_w = jnp.concatenate([outer[:128], middle, outer[128:]])
    class_hidden = low(layer_norm(class_state, small_params[R_GAIN1], small_params[R_SHIFT1]))
    class_half = mine_of(halves(class_hidden))
    query = dot(class_half[None], own_w)
    query = query + swap(query)
    wo_quarter = hop(own_w[384:], [(6, 7)]) + hop(own_w[:128], [(6, 4)])
    wo_quarter = wo_quarter + hop(own_w[128:256], [(6, 5)])
    wo_quarter = jnp.where(img == 6, own_w[256:384], wo_quarter)
    down_one = hop(
        own_w,
        [(12, 8), (13, 9), (14, 10), (11, 7), (8, 4), (9, 5), (10, 6), (7, 3)],
    )
    one_a, outer, query = together(one_a, outer, query)
    query = hop(query, [(3, 4)])
    one_b = hop(outer, [(0, 4), (1, 5), (2, 6), (5, 7)])
    two_a = hop(one_a, [(4, 8), (5, 9), (6, 10), (7, 11)])
    pix = prep(after(pixels, one_a), shuffle).reshape(2, images * SLOT, PIX // 2)
    corner = after(own_w[: PROJ // 2], one_a)
    corner = [corner] + [hop(corner, [(15, 15 ^ flip)]) for flip in (1, 2, 3)]
    query = low((query + small_params[R_SHIFT1 + 1 : R_SHIFT1 + 2]) * SCALE)
    query_heads = jnp.where(head_mask(HEADS), query, jnp.zeros((), BF))
    pulled = jnp.pad(low(dot(query_heads, own_w, NT)), ((0, 0), (0, WIDTH // 2)))
    one_b, two_a, wo_quarter, pulled, down_one = together(
        one_b, two_a, wo_quarter, pulled, down_one
    )
    mid_b = jnp.concatenate([one_b, wo_quarter, pulled])
    two_b = hop(mid_b, [(4, 8), (5, 9), (6, 10), (7, 11)])
    three_a = hop(
        jnp.where(img == 7, one_a, two_a), [(8, 12), (9, 13), (10, 14), (11, 15), (7, 3)]
    )
    low_b = hop(mid_b[256:], [(4, 0), (5, 1), (6, 2)])
    two_b, three_a, low_b, pix, partners, *corner = together(
        two_b, three_a, low_b, pix, partners, *corner
    )
    block_a = jnp.where(img < 3, middle, one_a + two_a + three_a)
    x_a, y_a = hop(block_a, FLIP_X), hop(block_a, FLIP_Y)
    three_b = hop(
        jnp.where(img == 7, mid_b, two_b), [(8, 12), (9, 13), (10, 14), (11, 15), (7, 3)]
    )
    pix_own, pix_send = mine_of(pix), theirs_of(pix)
    x_a, y_a, three_b, pix_own, pix_send = together(x_a, y_a, three_b, pix_own, pix_send)
    spot = jnp.stack([img, plane]).astype(jnp.int32)
    block_b = second_block(spot, [outer, low_b, mid_b, two_b, three_b])
    x_b, y_b = hop(block_b, FLIP_X), hop(block_b, FLIP_Y)
    down_two = hop(
        after(down_one, three_b), [(8, 4), (9, 5), (10, 6), (7, 3), (4, 0), (5, 1), (6, 2)]
    )
    proj_top = jnp.where(img == 15, corner[0], corner[1] + corner[2] + corner[3])
    (partners,) = call(
        partner_kernel, "partners", [], [partners], [shape((2 * CHIPS * images, PROJ), BF)]
    )
    up_one = hop(
        after(own_w, three_b), [(8, 12), (9, 13), (10, 14), (7, 11), (11, 15)]
    )
    x_b, y_b, up_one, down_two = together(x_b, y_b, up_one, down_two)
    up_two = hop(up_one, [(11, 15)])
    proj_one = hop(after(proj_top, x_b), [(12, 4), (13, 5), (14, 6), (15, 7)])
    d_a, d_b = hop(y_a, FLIP_X), hop(x_b, FLIP_Y)
    down_three = hop(after(down_two, y_b), [(4, 0), (5, 1), (6, 2)])
    segments, own_pieces, peer_pieces = [], [], []
    for pieces, spans, late in (
        ((block_a, x_a, y_a, d_a), ((0, 128, 256),), -1),
        ((block_b, x_b, y_b, d_b), ((0, 0, 128), (128, 384, 128)), 256),
    ):
        segments += [(source, spans, late) for source in range(4)]
        own_pieces += pieces
        peer_pieces += [swap(piece) for piece in pieces]
    pix_peer = swap(pix_send)
    valid = jnp.concatenate(
        [
            keep_mask,
            jnp.ones((images, 1), jnp.int32),
            jnp.zeros((images, SLOT - TOKS), jnp.int32),
        ],
        axis=1,
    ).reshape(images * SLOT, 1)
    (
        hid, xhat, rstd, p, pooled, mass, wv, wo, qk, resid, hidden_sent,
    ) = forward_call(
        segments, images, where, pix, own_pieces, peer_pieces, rows, valid, shuffle
    )
    pooled_own = mine_of(pooled)
    pooled_peer = swap(theirs_of(pooled))

    hidden_all = in_plane(hidden_sent)
    hidden_all, pooled_peer = together(hidden_all, pooled_peer)
    ff_block = (col + 1) % 4
    bias_part = lax.dynamic_slice(
        small_params[R_SHIFT2 + 1 : R_C2].reshape(4, 32, 2, 16),
        (ff_block, 0, core, 0),
        (1, 32, 1, 16),
    ).reshape(1, 512)
    candidates = [own_w, up_one, up_two, down_one, down_two, down_three]
    pick_one = choose(
        img, [((15,), 2), ((12, 13, 14, 11), 1), ((4, 5, 6, 3), 3), ((0, 1, 2), 4)], 0
    )
    pick_two = choose(
        img, [((15,), 1), ((8, 9, 10, 7), 3), ((4, 5, 6, 3), 4), ((0, 1, 2), 5)], 0
    )
    picks = jnp.stack([pick_one, pick_two]).astype(jnp.int32)
    preact, active, part = ff_call(
        ff_kernel, "ff", picks, [hidden_all, bias_part], candidates,
        [shape((8 * images, 512), F32), shape((8 * images, 512), BF), shape((8, images, WIDTH), BF)],
    )
    proj_mid = hop(
        after(jnp.where(plane == 3, proj_top, proj_one), hidden_sent),
        [(12, 8), (13, 9), (14, 10), (15, 11), (4, 0), (5, 1), (6, 2), (7, 3)],
    )
    hidden_all = in_plane(hidden_sent)
    ff_block = (col + 1) % 4
    bias_part = lax.dynamic_slice(
        small_params[R_SHIFT2 + 1 : R_C2].reshape(4, 32, 2, 16),
        (ff_block, 0, core, 0),
        (1, 32, 1, 16),
    ).reshape(1, 512)
    candidates = [own_w, up_one, up_two, down_one, down_two, down_three]
    pick_one = choose(
        img, [((15,), 2), ((12, 13, 14, 11), 1), ((4, 5, 6, 3), 3), ((0, 1, 2), 4)], 0
    )
    pick_two = choose(
        img, [((15,), 1), ((8, 9, 10, 7), 3), ((4, 5, 6, 3), 4), ((0, 1, 2), 5)], 0
    )
    picks = jnp.stack([pick_one, pick_two]).astype(jnp.int32)
    preact, active, part = ff_call(
        ff_kernel, "ff", picks, [hidden_all, bias_part], candidates,
        [shape((8 * images, 512), F32), shape((8 * images, 512), BF), shape((8, images, WIDTH), BF)],
    )
    proj = choose(
        plane, [((3,), proj_top), ((1,), proj_one)], after(proj_mid, hidden_sent)
    )
    proj_peer = swap(proj)
    part = in_plane(part)
    proj = choose(plane, [((3,), proj_top), ((1,), proj_one)], after(proj_mid, part))
    proj_peer = swap(proj)
    d_state, d_state_sent, head_vec = call(
        head_kernel, "head", [where],
        [part, resid, proj, proj_peer, partners, partner_index[:, None], rows],
        [
            shape((images, WIDTH), F32), shape((8, images, 2 * WIDTH + PROJ), BF),
            shape((8, WIDTH), F32),
        ],
        [pltpu.VMEM((images, PROJ), BF)],
    )
    d_state_all = in_plane(d_state_sent)
    d_preact, d_preact_sum, part = ff_call(
        ff_back_kernel, "ff_back", picks, [d_state_all, preact], candidates,
        [shape((8 * images, 512), BF), shape((1, 512), F32), shape((8, images, WIDTH), BF)],
    )
    part = in_plane(part)

    d_embed, d_attended, d_resid, d_pos, d_vec, pull = backward_call(
        images, where,
        [part, d_state, resid, wo, wv, hid, xhat, rstd, p, mass, qk, rows, shuffle],
    )
    arrays = [
        pix_own, pix_peer, d_embed, swap(d_embed), pooled_own, pooled_peer, d_attended,
        swap(d_attended),
    ]
    far_x, far_y = embed_grad_call(
        images, "embed_grad_far", [(3, 0, 256, BF), (3, 256, 256, BF)], where, arrays
    )
    got_y, got_x = hop(far_x, FLIP_X), hop(far_y, FLIP_Y)
    own_part, x_low, x_high, y_low, y_high = embed_grad_call(
        images, "embed_grad_near",
        [(0, 0, 512, F32), (1, 0, 256, BF), (1, 256, 256, F32), (2, 0, 256, F32), (2, 256, 256, BF)],
        after(where, far_x), arrays,
    )
    d_resid = in_plane(after(d_resid, far_x))
    d_pos, d_vec, head_vec, d_preact_sum, pull, _ = together(
        d_pos, d_vec, head_vec, d_preact_sum, pull, far_x
    )
    (small_sent,) = call(
        collect_kernel, "collect", [where], [d_pos, d_vec, head_vec, d_preact_sum, pull, shuffle],
        [shape((32, 3, WIDTH), F32)], [pltpu.VMEM((96, WIDTH), F32)],
    )
    got_x, got_y, own_part, x_low, x_high, y_low, y_high, d_resid, small_sent = together(
        got_x, got_y, own_part, x_low, x_high, y_low, y_high, d_resid, small_sent
    )
    part_x, part_y = call(
        add_far_kernel, "add_far", [], [x_low, x_high, got_x, y_low, got_y, y_high],
        [shape((512, WIDTH), BF)] * 2,
    )
    sum_x, sum_y = hop(part_x, FLIP_X), hop(part_y, FLIP_Y)
    shares = lax.all_to_all(small_sent, ALL, 0, 0, tiled=True)
    (ff_rows,) = call(
        rows_kernel, "rows", [where], [active, d_preact, hidden_all, d_state_all, d_resid],
        [shape((8 * images, 5 * WIDTH), BF)],
    )
    rise = [(i, i + 4) for i in range(12)]
    fall = [(12, 8), (13, 9), (14, 10), (15, 11), (10, 6), (11, 7)]
    up_one, down_one = hop(ff_rows, rise), hop(ff_rows, fall)
    sum_x, sum_y, shares, up_one, down_one = together(sum_x, sum_y, shares, up_one, down_one)
    total = own_part + sum_x.astype(F32) + sum_y.astype(F32)
    sent = low(total)
    first = hop(sent, [(12, 8), (13, 9), (14, 10), (15, 11), (4, 0), (5, 1), (6, 2)])
    aside = hop(sent, [(3, 1), (7, 5)])
    (small_sent,) = call(share_kernel, "share", [], [shares], [shape((32, 3, WIDTH), F32)])
    shares = lax.all_to_all(small_sent, ALL, 0, 0, tiled=True)
    up_two, down_two = hop(up_one, rise[4:]), hop(down_one, fall[4:])
    first, aside, shares, up_two, down_two, total = together(
        first, aside, shares, up_two, down_two, total
    )
    partial = low(total + first.astype(F32))
    second = hop(partial, [(8, 0), (9, 1), (10, 2), (11, 5)])
    third = hop(aside, [(1, 5)])
    up_three = hop(up_two, rise[8:])
    d_query, pull_half, small_total = call(
        query_back_kernel, "query_back", [core.reshape(1).astype(jnp.int32)],
        [shares, own_w, shuffle],
        [shape((8, WIDTH), F32), shape((HEADS, WIDTH // 2), F32), shape((96, WIDTH), F32)],
    )
    loss = small_total[R_SMALL + HEADS, 0]
    d_query = d_query[0:1]
    d_query = d_query + swap(d_query)
    d_query = hop(d_query, [(4, 3)])
    toward = dot(low(d_query), own_w, NT)

    every = [ff_rows, up_one, up_two, up_three, down_one, down_two]
    class_rows = jnp.concatenate([class_half[None], jnp.zeros((7, WIDTH // 2), BF)])
    role = jnp.stack([img, core]).astype(jnp.int32)
    (formed,) = call(
        owner_kernel, "owner", [role], [pull_half, query_heads, class_rows, d_query, *every],
        [shape((512, WIDTH), F32)],
    )
    edge = shape((JITTER * 16, WIDTH), F32)
    own_grad, top, end, report = call(
        finish_kernel, "finish", [role],
        [formed, d_query, toward, total, first, second, aside, third],
        [shape((512, WIDTH), F32), edge, edge, shape((1, WIDTH + 640), F32)],
    )
    reports = from_all(report)
    before = hop(end, [(i, i + 1) for i in range(CHIPS - 1)]).reshape(JITTER, 16, WIDTH)
    behind = hop(top, [(i + 1, i) for i in range(CHIPS - 1)]).reshape(JITTER, 16, WIDTH)
    small_grad, norm = call(
        complete_kernel, "complete", [], [small_total, reports, rows, shuffle],
        [shape((R_SMALL, WIDTH), F32), shape((8, 128), F32)],
    )
    grad_norm = norm[0, 0]
    factor = 1.0 / jnp.maximum(grad_norm, 1.0)
    own_grad = own_grad.reshape(slots, 16, WIDTH)
    here = near[JITTER : JITTER + slots]
    source = jnp.where(here < UNIT_COUNT, here - img * slots, -100)
    step_value = step_count.astype(F32)
    scalars = jnp.stack(
        [
            factor,
            1.0 / (1.0 - jnp.power(BETA_ONE, step_value)),
            1.0 / (1.0 - jnp.power(BETA_TWO, step_value)),
        ]
    )
    new_masters, new_first, new_second = update_call(
        source, scalars, before, own_grad, behind, masters, first_moment_slots,
        second_moment_slots,
    )
    new_small, new_small_first, new_small_second = adamw(
        small_params, small_grad * factor, small_first, small_second, step_value
    )
    return (
        new_masters, new_first, new_second, new_small, new_small_first, new_small_second,
        loss, grad_norm,
    )


def per_device_any(
    pixels, keep_mask, partner_index, partner_emb, masters, first_moment_slots,
    second_moment_slots, slot_unit_index, small_params, small_first, small_second, step_count,
):
    chips, seq = lax.axis_size("img"), lax.axis_size("seq")
    img = lax.axis_index("img")
    images = pixels.shape[0]
    slots, part = masters.shape[0], masters.shape[1]
    near = slots_near(slot_unit_index, img, slots)
    own_w = to_units(low(masters), near, img, chips)
    gathered = lax.all_gather(own_w, ("img", "seq"), axis=0, tiled=False)
    flat = gathered.reshape(chips, seq, slots, part, WIDTH).transpose(0, 2, 1, 3, 4)
    flat = flat.reshape(chips * slots * ROWS_PER_UNIT, WIDTH)
    bounds = [0, PIX, WIDTH, WIDTH, WIDTH, WIDTH, FF, FF, PROJ]
    parts, offset = [], 0
    for size in bounds[1:]:
        parts.append(flat[offset : offset + size])
        offset += size
    embed_w, query_w, key_w, value_w, output_w, fc_in_w, fc_out_w, proj_w = parts
    (
        class_row, pos_rows, patch_bias, gain_one, shift_one, query_bias, value_bias, out_bias,
        gain_two, shift_two, fc_in_bias, fc_out_bias, gain_end, shift_end,
    ) = small_parts(small_params)
    class_state = class_row + pos_rows[0]
    embedded = jnp.einsum("itp,pd->itd", pixels, embed_w, preferred_element_type=F32)
    tokens = jnp.concatenate(
        [
            jnp.broadcast_to(class_state, (images, 1, WIDTH)),
            embedded + patch_bias + pos_rows[1:],
        ],
        axis=1,
    )
    hidden = low(layer_norm(tokens, gain_one, shift_one))
    class_hidden = hidden[0, 0]
    mask16 = head_mask(HEADS)
    query = low((dot(class_hidden[None], query_w)[0] + query_bias) * SCALE)
    query_heads = jnp.where(mask16, query[None], jnp.zeros((), BF))
    qk = low(dot(query_heads, key_w, NT))
    scores = jnp.einsum("hd,itd->iht", qk, hidden, preferred_element_type=F32)
    keep = jnp.concatenate([jnp.ones((images, 1), jnp.int32), keep_mask], axis=1)
    scores = jnp.where(keep[:, None, :] > 0, scores, MASKED)
    weights = jax.nn.softmax(scores, axis=-1)
    weights_low = low(weights)
    pooled = low(jnp.einsum("iht,itd->ihd", weights_low, hidden, preferred_element_type=F32))
    mass = jnp.sum(weights_low.astype(F32), axis=-1)
    mixed = dot(pooled.reshape(-1, WIDTH), value_w).reshape(images, HEADS, WIDTH)
    mixed = mixed + mass[:, :, None] * value_bias
    attended = low(jnp.sum(jnp.where(mask16, mixed, 0.0), axis=1))
    resid = class_state + dot(attended, output_w) + out_bias
    hidden_two = low(layer_norm(resid, gain_two, shift_two))
    preact = dot(hidden_two, fc_in_w, NT) + fc_in_bias
    active = low(exact_gelu(preact))
    state = resid + dot(active, fc_out_w) + fc_out_bias
    final = low(layer_norm(state, gain_end, shift_end))
    projected = dot(final, proj_w, NT)
    unit = low(normalize(projected))
    partners = lax.all_gather(partner_emb, ("img", "seq"), axis=0, tiled=True)
    count = partners.shape[0]
    logits = dot(unit, partners, NT) / SOFTMAX_SCALE
    onehot = (jnp.arange(count, dtype=jnp.int32)[None] == partner_index[:, None]).astype(F32)
    total = jax.nn.logsumexp(logits, axis=-1)
    loss_part = jnp.sum(total - jnp.sum(logits * onehot, axis=-1)) / count
    d_logits = (jax.nn.softmax(logits, axis=-1) - onehot) / count
    d_unit = dot(low(d_logits / SOFTMAX_SCALE), partners)
    d_projected = low(jax.vjp(normalize, projected)[1](d_unit)[0])
    d_final = dot(d_projected, proj_w)
    d_state, d_gain_end, d_shift_end = jax.vjp(layer_norm, state, gain_end, shift_end)[1](d_final)
    d_state_low = low(d_state)
    d_active = dot(d_state_low, fc_out_w, NT)
    d_preact = low(jax.vjp(exact_gelu, preact)[1](d_active)[0])
    d_hidden_two = dot(d_preact, fc_in_w)
    d_norm, d_gain_two, d_shift_two = jax.vjp(layer_norm, resid, gain_two, shift_two)[1](
        d_hidden_two
    )
    d_resid = d_state + d_norm
    d_resid_low = low(d_resid)
    d_attended = low(dot(d_resid_low, output_w, NT))
    wide = jnp.where(mask16, d_attended[:, None, :], jnp.zeros((), BF))
    d_pooled = low(dot(wide.reshape(-1, WIDTH), value_w, NT)).reshape(images, HEADS, WIDTH)
    d_weights = jnp.einsum("ihd,itd->iht", d_pooled, hidden, preferred_element_type=F32)
    d_weights = d_weights + jnp.sum(wide.astype(F32) * value_bias, axis=-1)[:, :, None]
    d_scores = low(weights * (d_weights - jnp.sum(weights * d_weights, axis=-1, keepdims=True)))
    d_hidden = jnp.einsum("iht,ihd->itd", weights_low, d_pooled, preferred_element_type=F32)
    d_hidden = d_hidden + jnp.einsum("iht,hd->itd", d_scores, qk, preferred_element_type=F32)
    pull = jnp.einsum("iht,itd->hd", d_scores, hidden, preferred_element_type=F32)
    d_query = jnp.sum(jnp.where(mask16, dot(low(pull), key_w), 0.0), axis=0) * SCALE
    d_class_hidden = dot(low(d_query)[None], query_w, NT)
    d_tokens, d_gain_one, d_shift_one = jax.vjp(layer_norm, tokens, gain_one, shift_one)[1](
        d_hidden
    )
    d_class, d_gain_cls, d_shift_cls = jax.vjp(layer_norm, class_state[None], gain_one, shift_one)[
        1
    ](d_class_hidden)
    d_class = d_class[0] + jnp.sum(d_tokens[:, 0], axis=0) + jnp.sum(d_resid, axis=0)
    d_patch = d_tokens[:, 1:]
    d_embed_w = jnp.einsum("itp,itd->pd", pixels, low(d_patch), preferred_element_type=F32)
    d_value_w = dot(pooled.reshape(-1, WIDTH), wide.reshape(-1, WIDTH), TN)
    d_key_w = dot(pull, query_heads.astype(F32), TN, precision=lax.Precision.HIGHEST)
    small_local = jnp.concatenate(
        [
            d_class[None],
            d_class[None],
            jnp.sum(d_patch, axis=0),
            jnp.sum(d_patch, axis=(0, 1))[None],
            (d_gain_one + d_gain_cls)[None],
            (d_shift_one + d_shift_cls)[None],
            d_query[None],
            jnp.sum(wide.astype(F32) * mass[:, :, None], axis=(0, 1))[None],
            jnp.sum(d_resid, axis=0)[None],
            d_gain_two[None],
            d_shift_two[None],
            jnp.sum(d_preact.astype(F32), axis=0).reshape(FF // WIDTH, WIDTH),
            jnp.sum(d_state, axis=0)[None],
            d_gain_end[None],
            d_shift_end[None],
        ],
        axis=0,
    )
    grad_table = jnp.concatenate(
        [
            d_embed_w,
            class_hidden.astype(F32)[:, None] * d_query[None, :],
            d_key_w,
            d_value_w,
            dot(attended, d_resid_low, TN),
            dot(d_preact, hidden_two, TN),
            dot(active, d_state_low, TN),
            dot(d_projected, final, TN),
            jnp.zeros(((chips * slots - UNIT_COUNT) * ROWS_PER_UNIT, WIDTH), F32),
        ],
        axis=0,
    ).reshape(chips * slots, ROWS_PER_UNIT, WIDTH)
    small_grad, loss = lax.psum((small_local, loss_part), ("img", "seq"))
    core_half = lax.psum_scatter(low(grad_table), "seq", scatter_dimension=1, tiled=True)
    own_grad = lax.psum_scatter(core_half.astype(F32), "img", scatter_dimension=0, tiled=True)
    owner_total = lax.psum(jnp.sum(own_grad * own_grad), ("img", "seq"))
    grad_norm = jnp.sqrt(owner_total + jnp.sum(small_grad * small_grad))
    factor = 1.0 / jnp.maximum(grad_norm, 1.0)
    slot_grad = to_slots(own_grad, near, img, chips)
    step_value = step_count.astype(F32)
    new_masters, new_first, new_second = adamw(
        masters, slot_grad * factor, first_moment_slots, second_moment_slots, step_value
    )
    new_small, new_small_first, new_small_second = adamw(
        small_params, small_grad * factor, small_first, small_second, step_value
    )
    return (
        new_masters, new_first, new_second, new_small, new_small_first, new_small_second,
        loss, grad_norm,
    )


def solution(mesh):
    chip, devices = "img", ("img", "seq")
    core, body = "seq", per_device_any
    if mesh.shape["img"] == CHIPS and mesh.shape["seq"] == 2:
        mesh = jax.sharding.Mesh(mesh.devices.reshape(4, 2, 2, 2), ALL)
        chip, devices, core, body = CHIP, ALL, "c", per_device_16
    weights = P(chip, core, None)
    return jax.shard_map(
        body,
        mesh=mesh,
        in_specs=(
            P(devices, None, None),
            P(devices, None),
            P(devices),
            P(devices, None),
            weights,
            weights,
            weights,
            P(),
            P(),
            P(),
            P(),
            P(),
        ),
        out_specs=(weights, weights, weights, P(), P(), P(), P(), P()),
        check_vma=False,
    )
```

```python
import functools
import math

import jax
import jax.numpy as jnp
from jax import lax
from jax.experimental import pallas as pl
from jax.experimental.pallas import tpu as pltpu
from jax.sharding import PartitionSpec as P

WIDTH = 1024
HEADS = 16
HEAD_DIM = 64
FF = 4096
PIX = 3072
PROJ = 768
TOKS = 50
PATCHES = TOKS - 1
ROWS_PER_UNIT = 32
UNIT_COUNT = 504
JITTER = 2

EPS_NORM = 1e-06
SOFTMAX_SCALE = 0.07
LEARN_RATE = 0.03
BETA_ONE = 0.5
BETA_TWO = 0.5
DECAY_RATE = 0.05
ADAM_EPS = 1e-08
MASKED = -1000000000.0
SCALE = HEAD_DIM ** (-0.5)

F32 = jnp.float32
BF = jnp.bfloat16
ROW_BASE = 1 + TOKS
ROW_TAIL = ROW_BASE + 8 + FF // WIDTH
SLOT = 64


def low(values):
    return values.astype(BF)


def dot(a, b, dims=((1,), (0,)), precision=None):
    return lax.dot_general(a, b, (dims, ((), ())), precision=precision, preferred_element_type=F32)


NN = ((1,), (0,))
NT = ((1,), (1,))
TN = ((0,), (0,))


def layer_norm(values, gain, shift):
    center = values - jnp.mean(values, axis=-1, keepdims=True)
    spread = jnp.mean(center * center, axis=-1, keepdims=True)
    return center * lax.rsqrt(spread + EPS_NORM) * gain + shift


def normalize(values):
    return values * lax.rsqrt(jnp.sum(values * values, axis=-1, keepdims=True) + EPS_NORM)


def exact_gelu(values):
    return jax.nn.gelu(values, approximate=False)


def small_parts(small):
    base, tail = ROW_BASE, ROW_TAIL
    return (
        small[0],
        small[1:base],
        small[base],
        small[base + 1],
        small[base + 2],
        small[base + 3],
        small[base + 4],
        small[base + 5],
        small[base + 6],
        small[base + 7],
        small[base + 8 : tail].reshape(FF),
        small[tail],
        small[tail + 1],
        small[tail + 2],
    )


def adamw(weight, grad, first, second, step):
    first_new = BETA_ONE * first + (1.0 - BETA_ONE) * grad
    second_new = BETA_TWO * second + (1.0 - BETA_TWO) * grad * grad
    first_hat = first_new / (1.0 - jnp.power(BETA_ONE, step))
    second_hat = second_new / (1.0 - jnp.power(BETA_TWO, step))
    weight_new = weight - LEARN_RATE * (
        first_hat / (jnp.sqrt(second_hat) + ADAM_EPS) + DECAY_RATE * weight
    )
    return (weight_new, first_new, second_new)


def halo(values, chips, axes):
    before = lax.ppermute(values[-JITTER:], axes, [(i, i + 1) for i in range(chips - 1)])
    behind = lax.ppermute(values[:JITTER], axes, [(i + 1, i) for i in range(chips - 1)])
    return before, behind


def with_halo(values, chips, axes):
    before, behind = halo(values, chips, axes)
    return jnp.concatenate([before, values, behind], axis=0)


def slots_near(slot_unit_index, img, slots):
    padded = jnp.pad(slot_unit_index, (JITTER, JITTER), constant_values=-1)
    return lax.dynamic_slice(padded, (img * slots,), (slots + 2 * JITTER,))


def pick(ext, matches, slots):
    out = jnp.zeros((slots,) + ext.shape[1:], ext.dtype)
    for shift in range(2 * JITTER + 1):
        out = jnp.where(matches[shift][:, None, None], ext[shift : shift + slots], out)
    return out


def to_units(values, near, img, chips, axes="img"):
    slots = values.shape[0]
    ids = img * slots + jnp.arange(slots, dtype=jnp.int32)
    matches = [near[s : s + slots] == ids for s in range(2 * JITTER + 1)]
    return pick(with_halo(values, chips, axes), matches, slots)


def to_slots(values, near, img, chips, axes="img"):
    slots = values.shape[0]
    here = near[JITTER : JITTER + slots]
    ids = img * slots + jnp.arange(slots, dtype=jnp.int32)
    matches = [
        (here == ids + (s - JITTER)) & (here < UNIT_COUNT) for s in range(2 * JITTER + 1)
    ]
    return pick(with_halo(values, chips, axes), matches, slots)


def shuffle_matrix():
    source = lax.broadcasted_iota(jnp.int32, (256, 256), 0)
    target = lax.broadcasted_iota(jnp.int32, (256, 256), 1)
    moved = ((source // 16) % 2) * 128 + (source // 32) * 16 + source % 16
    return (moved == target).astype(F32).astype(BF)


def vmem():
    return pl.BlockSpec(memory_space=pltpu.VMEM)


def smem():
    return pl.BlockSpec(memory_space=pltpu.SMEM)


def shape(dims, dtype):
    return jax.ShapeDtypeStruct(dims, dtype)


def call(kernel, name, scalars, arrays, outs, scratch=(), mib=16, flops=10**9, far=()):
    moved = sum(a.size * a.dtype.itemsize for a in [*arrays, *outs, *far])
    return pl.pallas_call(
        kernel,
        in_specs=[smem()] * len(scalars)
        + [vmem()] * len(arrays)
        + [pl.BlockSpec(memory_space=pl.ANY)] * len(far),
        out_specs=[vmem()] * len(outs),
        out_shape=list(outs),
        scratch_shapes=list(scratch),
        compiler_params=pltpu.CompilerParams(vmem_limit_bytes=mib * 2**20),
        cost_estimate=pl.CostEstimate(flops=flops, bytes_accessed=moved, transcendentals=0),
        name=name,
    )(*scalars, *arrays, *far)


def prep_kernel(pix_ref, shuffle_ref, out_ref):
    shuffle = shuffle_ref[...]
    out_ref[...] = jnp.zeros_like(out_ref)
    for block in range(PIX // 256):
        moved = dot(pix_ref[0, :, 256 * block : 256 * block + 256], shuffle).astype(BF)
        out_ref[0, 0, :PATCHES, 128 * block : 128 * block + 128] = moved[:, :128]
        out_ref[1, 0, :PATCHES, 128 * block : 128 * block + 128] = moved[:, 128:]


def prep(pixels, shuffle):
    images = pixels.shape[0]
    return pl.pallas_call(
        prep_kernel,
        grid=(images,),
        in_specs=[
            pl.BlockSpec((1, PATCHES, PIX), lambda i: (i, 0, 0)),
            pl.BlockSpec((256, 256), lambda i: (0, 0)),
        ],
        out_specs=pl.BlockSpec((2, 1, SLOT, PIX // 2), lambda i: (0, i, 0, 0)),
        out_shape=jax.ShapeDtypeStruct((2, images, SLOT, PIX // 2), BF),
        compiler_params=pltpu.CompilerParams(vmem_limit_bytes=24 * 2**20),
        cost_estimate=pl.CostEstimate(flops=8 * 10**8, bytes_accessed=6 * 2**20, transcendentals=0),
        name="prep",
    )(pixels, shuffle)


def head_mask(rows):
    lane = lax.broadcasted_iota(jnp.int32, (rows, WIDTH), 1) // HEAD_DIM
    row = lax.broadcasted_iota(jnp.int32, (rows, WIDTH), 0) % HEADS
    return lane == row


def norm_parts(values):
    center = values - jnp.mean(values, axis=-1, keepdims=True)
    rstd = lax.rsqrt(jnp.mean(center * center, axis=-1, keepdims=True) + EPS_NORM)
    return center * rstd, rstd


def norm_back(grad, gain, xhat, rstd):
    gy = grad * gain
    return rstd * (
        gy - jnp.mean(gy, axis=-1, keepdims=True) - xhat * jnp.mean(gy * xhat, axis=-1, keepdims=True)
    )


def rowsum(values):
    return jnp.sum(values, axis=0, keepdims=True)


def to_halves(values, shuffle):
    first, second = [], []
    for block in range(values.shape[1] // 256):
        moved = low(dot(values[:, 256 * block : 256 * block + 256], shuffle))
        first.append(moved[:, :128])
        second.append(moved[:, 128:])
    return jnp.concatenate(first, axis=1), jnp.concatenate(second, axis=1)


def to_natural(first, second, shuffle):
    out = []
    for block in range(first.shape[1] // 128):
        lanes = slice(128 * block, 128 * block + 128)
        both = jnp.concatenate([first[:, lanes], second[:, lanes]], axis=1)
        out.append(low(dot(both, shuffle, NT)))
    return jnp.concatenate(out, axis=1)


R_PATCH, R_GAIN1, R_SHIFT1, R_VB, R_OB, R_GAIN2, R_SHIFT2 = 51, 52, 53, 55, 56, 57, 58
R_C2, R_GAINF, R_SHIFTF, R_SMALL = 63, 64, 65, 66
QUARTER = 128


def partner_kernel(raw_ref, out_ref):
    source = lax.broadcasted_iota(jnp.int32, (PROJ, PROJ), 0)
    target = lax.broadcasted_iota(jnp.int32, (PROJ, PROJ), 1)
    moved = ((source // 16) % 2) * (PROJ // 2) + (source // 32) * 16 + source % 16
    select = low((moved == target).astype(F32))
    out_ref[...] = low(dot(raw_ref[...].reshape(-1, PROJ), select))


def second_block_kernel(
    role_ref, outer_ref, low_ref, mid_ref, two_ref, three_ref, out_ref, held_ref, sems
):
    chip, plane = role_ref[0], role_ref[1]

    @pl.when(chip < 3)
    def _():
        head = pltpu.make_async_copy(outer_ref, held_ref.at[pl.ds(0, 256)], sems.at[0])
        tail = pltpu.make_async_copy(low_ref, held_ref.at[pl.ds(256, QUARTER + HEADS)], sems.at[1])
        head.start()
        tail.start()
        head.wait()
        tail.wait()

    for number, ref in ((1, mid_ref), (2, two_ref), (3, three_ref)):
        here = (plane == number) | (chip == 3) if number == 3 else plane == number

        @pl.when(here)
        def _():
            whole = pltpu.make_async_copy(ref, held_ref, sems.at[0])
            whole.start()
            whole.wait()

    out = pltpu.make_async_copy(held_ref, out_ref, sems.at[0])
    out.start()
    out.wait()


def second_block(role, pieces):
    any_place = pl.BlockSpec(memory_space=pl.ANY)
    return pl.pallas_call(
        second_block_kernel,
        in_specs=[smem()] + [any_place] * len(pieces),
        out_specs=pl.BlockSpec(memory_space=pltpu.HBM),
        out_shape=shape((256 + QUARTER + HEADS, WIDTH), BF),
        scratch_shapes=[
            pltpu.VMEM((256 + QUARTER + HEADS, WIDTH), BF),
            pltpu.SemaphoreType.DMA((2,)),
        ],
        compiler_params=pltpu.CompilerParams(vmem_limit_bytes=4 * 2**20),
        cost_estimate=pl.CostEstimate(flops=0, bytes_accessed=2 * 2**20, transcendentals=0),
        name="second_block",
    )(role, *pieces)


def forward_kernel(segments, images, where_ref, pix_ref, rows_ref, valid_ref, shuffle_ref, *refs):
    count = len(segments)
    own, peer = refs[:count], refs[count : 2 * count]
    (
        hid_ref, xhat_ref, rstd_ref, p_ref, pooled_ref, mass_ref, wv_ref, wo_ref, qk_ref,
        resid_ref, low_ref, acc_ref, pool_ref, half_ref, table_ref, sems,
    ) = refs[2 * count :]
    col, core = where_ref[0], where_ref[1]
    waits = ([], [])
    for flip, group in ((0, own), (1, peer)):
        half = core ^ flip
        for (source, parts, late), ref in zip(segments, group):
            block = col ^ source
            for row, lane, rows in parts:
                part = ref.at[pl.ds(row, rows)]
                line = pl.multiple_of(block * 512 + lane, 128)
                copy = pltpu.make_async_copy(part, table_ref.at[half, pl.ds(line, rows)], sems.at[flip])
                copy.start()
                waits[flip].append(copy)
            if late >= 0:
                part = ref.at[pl.ds(late, QUARTER)]
                line = pl.multiple_of(block * QUARTER, QUARTER)
                copy = pltpu.make_async_copy(part, wo_ref.at[half, pl.ds(line, QUARTER)], sems.at[2])
                copy.start()
                waits[1].append(copy)
                part = ref.at[pl.ds(late + QUARTER, HEADS)]
                copy = pltpu.make_async_copy(part, half_ref.at[half, block], sems.at[3])
                copy.start()
                waits[1].append(copy)
    patch = rows_ref[2 : 1 + TOKS] + rows_ref[R_PATCH : R_PATCH + 1]
    class_state = rows_ref[0:1] + rows_ref[1:2]
    for i in range(images):
        acc_ref[SLOT * i : SLOT * i + PATCHES] = patch
        acc_ref[SLOT * i + PATCHES : SLOT * i + TOKS] = class_state
        acc_ref[SLOT * i + TOKS : SLOT * (i + 1)] = jnp.zeros((SLOT - TOKS, WIDTH), F32)
    for copy in waits[0]:
        copy.wait()
    acc_ref[...] += dot(pix_ref[core], table_ref[core, :1536])
    for copy in waits[1]:
        copy.wait()
    acc_ref[...] += dot(pix_ref[1 - core], table_ref[1 - core, :1536])
    wv_ref[...] = table_ref[:, 1536:]
    shuffle = shuffle_ref[...]
    gain, shift, value_bias = (rows_ref[r : r + 1] for r in (R_GAIN1, R_SHIFT1, R_VB))
    half = WIDTH // 2
    qk = to_natural(half_ref[0, 0, :, :half], half_ref[1, 0, :, :half], shuffle)
    qk_ref[...] = qk
    valid = valid_ref[...] > 0
    for i in range(images):
        part = slice(SLOT * i, SLOT * (i + 1))
        xhat, rstd = norm_parts(acc_ref[part])
        hid = low(xhat * gain + shift)
        xhat_ref[part] = xhat
        rstd_ref[part] = jnp.broadcast_to(rstd, (SLOT, 128))
        hid_ref[part] = hid
        scores = jnp.where(valid[part], dot(hid, qk, NT), MASKED)
        e = jnp.exp(scores - jnp.max(scores, axis=0, keepdims=True))
        p = e / jnp.sum(e, axis=0, keepdims=True)
        p_ref[part] = p
        pb = low(p)
        pool_ref[HEADS * i : HEADS * (i + 1)] = low(dot(pb, hid, TN))
        mass_ref[HEADS * i : HEADS * (i + 1)] = dot(pb, jnp.ones((SLOT, 128), BF), TN)
    pooled_ref[0], pooled_ref[1] = to_halves(pool_ref[...], shuffle)
    rows = images * HEADS
    mixed = dot(pooled_ref[0], wv_ref[0]) + dot(pooled_ref[1], wv_ref[1])
    mixed = mixed + mass_ref[:, 0:1] * value_bias
    mixed = jnp.where(head_mask(rows), mixed, 0.0)
    joined = low(jnp.sum(mixed.reshape(images, HEADS, WIDTH), axis=1))
    first, second = to_halves(joined, shuffle)
    resid = class_state + dot(first, wo_ref[0]) + dot(second, wo_ref[1])
    resid = resid + rows_ref[R_OB : R_OB + 1]
    resid_ref[...] = resid
    xhat, _ = norm_parts(resid)
    hidden = low(xhat * rows_ref[R_GAIN2 : R_GAIN2 + 1] + rows_ref[R_SHIFT2 : R_SHIFT2 + 1])
    sent = jnp.concatenate([hidden, first, second], axis=1)
    low_ref[...] = jnp.broadcast_to(sent[None], low_ref.shape)


def forward_call(segments, images, where, pix, own, peer, rows, valid, shuffle):
    tokens = images * SLOT
    outs = [
        shape((tokens, WIDTH), BF),
        shape((tokens, WIDTH), F32),
        shape((tokens, 128), F32),
        shape((tokens, HEADS), F32),
        shape((2, images * HEADS, WIDTH // 2), BF),
        shape((images * HEADS, 128), F32),
        shape((2, WIDTH // 2, WIDTH), BF),
        shape((2, WIDTH // 2, WIDTH), BF),
        shape((HEADS, WIDTH), BF),
        shape((images, WIDTH), F32),
        shape((8, images, 2 * WIDTH), BF),
    ]
    scratch = [
        pltpu.VMEM((tokens, WIDTH), F32),
        pltpu.VMEM((images * HEADS, WIDTH), BF),
        pltpu.VMEM((2, 4, HEADS, WIDTH), BF),
        pltpu.VMEM((2, 2048, WIDTH), BF),
        pltpu.SemaphoreType.DMA((4,)),
    ]
    return call(
        functools.partial(forward_kernel, segments, images), "forward", [where],
        [pix, rows, valid, shuffle], outs, scratch, mib=52, flops=4 * 10**9,
        far=[*own, *peer],
    )


def fetch(pick_ref, slot, candidates, out_ref, sem):
    for number, candidate in enumerate(candidates):

        @pl.when(pick_ref[slot] == number)
        def _():
            pltpu.make_async_copy(candidate, out_ref, sem).start()


def arrived(candidate, out_ref, sem):
    pltpu.make_async_copy(candidate, out_ref, sem).wait()


def ff_kernel(pick_ref, hid_ref, bias_ref, *refs):
    candidates, (pre_ref, act_ref, part_ref, w1_ref, w2_ref, sems) = refs[:6], refs[6:]
    fetch(pick_ref, 0, candidates, w1_ref, sems.at[0])
    fetch(pick_ref, 1, candidates, w2_ref, sems.at[1])
    hidden = hid_ref[:, :, :WIDTH].reshape(-1, WIDTH)
    arrived(candidates[0], w1_ref, sems.at[0])
    pre = dot(hidden, w1_ref[...], NT) + bias_ref[...]
    pre_ref[...] = pre
    active = low(0.5 * pre * (1.0 + lax.erf(pre * (0.5**0.5))))
    act_ref[...] = active
    arrived(candidates[0], w2_ref, sems.at[1])
    part_ref[...] = low(dot(active, w2_ref[...])).reshape(part_ref.shape)


def ff_back_kernel(pick_ref, dst_ref, pre_ref, *refs):
    candidates, (dpre_ref, sum_ref, part_ref, w1_ref, w2_ref, sems) = refs[:6], refs[6:]
    fetch(pick_ref, 1, candidates, w2_ref, sems.at[1])
    fetch(pick_ref, 0, candidates, w1_ref, sems.at[0])
    d_state = dst_ref[:, :, :WIDTH].reshape(-1, WIDTH)
    pre = pre_ref[...]
    slope = 0.5 * (1.0 + lax.erf(pre * (0.5**0.5))) + pre * jnp.exp(-0.5 * pre * pre) * (
        1.0 / (2.0 * math.pi) ** 0.5
    )
    arrived(candidates[0], w2_ref, sems.at[1])
    d_pre = low(dot(d_state, w2_ref[...], NT) * slope)
    dpre_ref[...] = d_pre
    sum_ref[...] = rowsum(d_pre.astype(F32))
    arrived(candidates[0], w1_ref, sems.at[0])
    part_ref[...] = low(dot(d_pre, w1_ref[...])).reshape(part_ref.shape)


def ff_call(kernel, name, pick, arrays, candidates, outs):
    moved = sum(a.size * a.dtype.itemsize for a in list(arrays) + list(outs))
    return pl.pallas_call(
        kernel,
        in_specs=[smem()]
        + [vmem()] * len(arrays)
        + [pl.BlockSpec(memory_space=pl.ANY)] * len(candidates),
        out_specs=[vmem()] * len(outs),
        out_shape=list(outs),
        scratch_shapes=[
            pltpu.VMEM((512, WIDTH), BF),
            pltpu.VMEM((512, WIDTH), BF),
            pltpu.SemaphoreType.DMA((2,)),
        ],
        compiler_params=pltpu.CompilerParams(vmem_limit_bytes=24 * 2**20),
        cost_estimate=pl.CostEstimate(
            flops=2 * 10**8, bytes_accessed=moved + 2 * 2**20, transcendentals=0
        ),
        name=name,
    )(pick, *arrays, *candidates)


def head_kernel(
    where_ref, part_ref, resid_ref, pj_ref, pjp_ref, partners_ref, target_ref, rows_ref,
    state_ref, low_ref, vec_ref, dz_ref,
):
    images = resid_ref.shape[0]
    state = resid_ref[...] + jnp.sum(part_ref[...].astype(F32), axis=0) + rows_ref[R_C2 : R_C2 + 1]
    gain = rows_ref[R_GAINF : R_GAINF + 1]
    xhat, rstd = norm_parts(state)
    final = low(xhat * gain + rows_ref[R_SHIFTF : R_SHIFTF + 1])
    z_own, z_peer = dot(final, pj_ref[...], NT), dot(final, pjp_ref[...], NT)
    square = jnp.sum(z_own * z_own, axis=-1, keepdims=True) + jnp.sum(
        z_peer * z_peer, axis=-1, keepdims=True
    )
    inv = lax.rsqrt(square + EPS_NORM)
    core = where_ref[1]
    half = PROJ // 2
    own_lanes = pl.ds(pl.multiple_of(core * half, 128), half)
    peer_lanes = pl.ds(pl.multiple_of((1 - core) * half, 128), half)
    ptn_own, ptn_peer = partners_ref[:, own_lanes], partners_ref[:, peer_lanes]
    logits = dot(low(z_own * inv), ptn_own, NT) + dot(low(z_peer * inv), ptn_peer, NT)
    logits = logits / SOFTMAX_SCALE
    total = logits.shape[1]
    hit = lax.broadcasted_iota(jnp.int32, (images, total), 1) == target_ref[...]
    top = jnp.max(logits, axis=-1, keepdims=True)
    e = jnp.exp(logits - top)
    mass = jnp.sum(e, axis=-1, keepdims=True)
    aim = jnp.sum(jnp.where(hit, logits, 0.0), axis=-1, keepdims=True)
    losses = jnp.log(mass) + top - aim
    d_logits = (e / mass - jnp.where(hit, 1.0, 0.0)) / total
    g_logits = low(d_logits / SOFTMAX_SCALE)
    d_own, d_peer = dot(g_logits, ptn_own), dot(g_logits, ptn_peer)
    along = jnp.sum(d_own * z_own, axis=-1, keepdims=True) + jnp.sum(
        d_peer * z_peer, axis=-1, keepdims=True
    )
    shrink = along * inv * inv * inv
    dz_own, dz_peer = low(d_own * inv - z_own * shrink), low(d_peer * inv - z_peer * shrink)
    dz_ref[:, own_lanes] = dz_own
    dz_ref[:, peer_lanes] = dz_peer
    d_final = dot(dz_own, pj_ref[...]) + dot(dz_peer, pjp_ref[...])
    d_state = norm_back(d_final, gain, xhat, rstd)
    state_ref[...] = d_state
    sent = jnp.concatenate([low(d_state), dz_ref[...], final], axis=1)
    low_ref[...] = jnp.broadcast_to(sent[None], low_ref.shape)
    vec_ref[...] = jnp.zeros_like(vec_ref)
    vec_ref[0:1] = rowsum(d_state)
    vec_ref[1:2] = rowsum(d_final * xhat)
    vec_ref[2:3] = rowsum(d_final)
    vec_ref[3:4] = jnp.broadcast_to(rowsum(losses) / total, (1, WIDTH))


def backward_kernel(
    images, where_ref, part_ref, dstate_ref, resid_ref, wo_ref, wv_ref, hid_ref, xhat_ref,
    rstd_ref, p_ref, mass_ref, qk_ref, rows_ref, shuffle_ref,
    de_ref, do_ref, dres_ref, pos_ref, vec_ref, pull_ref, dom_ref, da_ref,
):
    rows = images * HEADS
    gain, value_bias = rows_ref[R_GAIN1 : R_GAIN1 + 1], rows_ref[R_VB : R_VB + 1]
    shuffle = shuffle_ref[...]
    vec_ref[...] = jnp.zeros_like(vec_ref)
    d_two = jnp.sum(part_ref[...].astype(F32), axis=0)
    xhat2, rstd2 = norm_parts(resid_ref[...])
    d_resid = dstate_ref[...] + norm_back(d_two, rows_ref[R_GAIN2 : R_GAIN2 + 1], xhat2, rstd2)
    vec_ref[3:4] = rowsum(d_resid)
    vec_ref[4:5] = rowsum(d_two * xhat2)
    vec_ref[5:6] = rowsum(d_two)
    d_low = low(d_resid)
    dres_ref[...] = jnp.broadcast_to(d_low[None], dres_ref.shape)
    d_att = to_natural(
        low(dot(d_low, wo_ref[0], NT)), low(dot(d_low, wo_ref[1], NT)), shuffle
    )
    do_ref[...] = d_att
    spread = jnp.broadcast_to(d_att.reshape(images, 1, WIDTH).astype(F32), (images, HEADS, WIDTH))
    wide = jnp.where(head_mask(rows), spread.reshape(rows, WIDTH), 0.0)
    dom_ref[...] = low(wide)
    vec_ref[2:3] = rowsum(wide * mass_ref[:, 0:1])
    da_ref[...] = to_natural(
        low(dot(dom_ref[...], wv_ref[0], NT)), low(dot(dom_ref[...], wv_ref[1], NT)), shuffle
    )
    qk = qk_ref[...]
    bias_rows = low(jnp.broadcast_to(value_bias, (8, WIDTH)))
    real = lax.broadcasted_iota(jnp.int32, (SLOT, WIDTH), 0) < PATCHES
    for i in range(images):
        part = slice(SLOT * i, SLOT * (i + 1))
        mine = slice(HEADS * i, HEADS * (i + 1))
        hid, p, da = hid_ref[part], p_ref[part], da_ref[mine]
        dp = dot(hid, da, NT) + dot(bias_rows, dom_ref[mine], NT)[0:1]
        ds = low(p * (dp - rowsum(p * dp)))
        dh = dot(low(p), da) + dot(ds, qk)
        pull = dot(ds, hid, TN)
        xhat, rstd = xhat_ref[part], rstd_ref[part, 0:1]
        dx = norm_back(dh, gain, xhat, rstd)
        de_ref[part] = low(jnp.where(real, dx, 0.0))
        vec_ref[0:1] += rowsum(dh * xhat)
        vec_ref[1:2] += rowsum(dh)
        if i == 0:
            pos_ref[...] = dx
            pull_ref[...] = pull
        else:
            pos_ref[...] += dx
            pull_ref[...] += pull


def backward_call(images, where, arrays):
    tokens = images * SLOT
    outs = [
        shape((tokens, WIDTH), BF),
        shape((images, WIDTH), BF),
        shape((8, images, WIDTH), BF),
        shape((SLOT, WIDTH), F32),
        shape((8, WIDTH), F32),
        shape((HEADS, WIDTH), F32),
    ]
    scratch = [pltpu.VMEM((images * HEADS, WIDTH), BF)] * 2
    return call(
        functools.partial(backward_kernel, images), "backward", [where], arrays, outs, scratch
    )


def rows_kernel(where_ref, act_ref, dpre_ref, hid_ref, dst_ref, dres_ref, out_ref):
    half = WIDTH // 2
    base = 3 * WIDTH
    out_ref[:, :half] = act_ref[...]
    out_ref[:, half:WIDTH] = dpre_ref[...]
    count = out_ref.shape[0]
    out_ref[:, WIDTH : 2 * WIDTH] = hid_ref[:, :, :WIDTH].reshape(count, WIDTH)
    out_ref[:, 2 * WIDTH : base] = dst_ref[:, :, :WIDTH].reshape(count, WIDTH)

    @pl.when(where_ref[0] == 2)
    def _():
        out_ref[:, base : base + WIDTH] = hid_ref[:, :, WIDTH:].reshape(count, WIDTH)
        out_ref[:, base + WIDTH :] = dres_ref[...].reshape(count, WIDTH)

    @pl.when(where_ref[0] != 2)
    def _():
        out_ref[:, base : base + WIDTH + PROJ] = dst_ref[:, :, WIDTH:].reshape(count, WIDTH + PROJ)
        out_ref[:, base + WIDTH + PROJ :] = jnp.zeros((count, WIDTH - PROJ), BF)


def embed_grad_kernel(
    images, plan, where_ref, pix_ref, pixp_ref, de_ref, dep_ref, pooled_ref, pooledp_ref,
    do_ref, dop_ref, *out_refs,
):
    col = where_ref[0]
    heads = images * HEADS
    for (source, first, rows, _), out_ref in zip(plan, out_refs):
        block = col ^ source

        @pl.when(block < 3)
        def _():
            lanes = pl.ds(pl.multiple_of(block * 512 + first, 128), rows)
            total = dot(pix_ref[:, lanes], de_ref[...], TN) + dot(pixp_ref[:, lanes], dep_ref[...], TN)
            out_ref[...] = total.astype(out_ref.dtype)

        @pl.when(block == 3)
        def _():
            total = None
            for pooled, do in ((pooled_ref, do_ref), (pooledp_ref, dop_ref)):
                spread = jnp.broadcast_to(
                    do[...].reshape(images, 1, WIDTH).astype(F32), (images, HEADS, WIDTH)
                )
                wide = low(jnp.where(head_mask(heads), spread.reshape(heads, WIDTH), 0.0))
                term = dot(pooled[:, first : first + rows], wide, TN)
                total = term if total is None else total + term
            out_ref[...] = total.astype(out_ref.dtype)


def embed_grad_call(images, name, plan, where, arrays):
    outs = [shape((rows, WIDTH), dtype) for _, _, rows, dtype in plan]
    return call(
        functools.partial(embed_grad_kernel, images, plan), name, [where], arrays, outs
    )


def add_far_kernel(x_low_ref, x_high_ref, got_x_ref, y_low_ref, got_y_ref, y_high_ref, x_ref, y_ref):
    x_ref[0] = x_low_ref[...]
    x_ref[1] = low(x_high_ref[...] + got_x_ref[...].astype(F32))
    y_ref[0] = low(y_low_ref[...] + got_y_ref[...].astype(F32))
    y_ref[1] = y_high_ref[...]


def add_far(pieces):
    rows = pieces[0].shape[0]
    step = rows // 4
    out = shape((2, rows, WIDTH), BF)
    return pl.pallas_call(
        add_far_kernel,
        grid=(4,),
        in_specs=[pl.BlockSpec((step, WIDTH), lambda i: (i, 0))] * 6,
        out_specs=[pl.BlockSpec((2, step, WIDTH), lambda i: (0, i, 0))] * 2,
        out_shape=[out, out],
        compiler_params=pltpu.CompilerParams(vmem_limit_bytes=58 * 2**20),
        cost_estimate=pl.CostEstimate(flops=10**6, bytes_accessed=6 * 2**20, transcendentals=0),
        name="add_far",
    )(*pieces)


def to_natural_exact(first, second, shuffle):
    wide = shuffle.astype(F32)
    out = []
    for block in range(first.shape[1] // 128):
        lanes = slice(128 * block, 128 * block + 128)
        both = jnp.concatenate([first[:, lanes], second[:, lanes]], axis=1)
        out.append(dot(both, wide, NT, precision=lax.Precision.HIGHEST))
    return jnp.concatenate(out, axis=1)


def collect_kernel(
    where_ref, pos_ref, vec_ref, head_ref, sum_ref, pull_ref, shuffle_ref, sent_ref, out_ref
):
    col, core = where_ref[0], where_ref[1]
    out_ref[...] = jnp.zeros_like(out_ref)
    top = pos_ref[PATCHES:TOKS] + vec_ref[3:4]
    out_ref[0:1] = top
    out_ref[1:2] = top
    patches = pos_ref[0:PATCHES]
    out_ref[2 : 1 + TOKS] = patches
    out_ref[R_PATCH : R_PATCH + 1] = rowsum(patches)
    out_ref[R_GAIN1 : R_SHIFT1 + 1] = vec_ref[0:2]
    out_ref[R_VB : R_VB + 1] = vec_ref[2:3]
    out_ref[R_OB : R_SHIFT2 + 1] = vec_ref[3:6]
    sums = jnp.broadcast_to(sum_ref[...], (8, WIDTH // 2))
    nothing = jnp.zeros_like(sums)
    row = to_natural_exact(
        jnp.where(core == 0, sums, nothing), jnp.where(core == 0, nothing, sums), shuffle_ref[...]
    )
    for block in range(4):
        mine = (col + 1) % 4 == block
        out_ref[R_SHIFT2 + 1 + block : R_SHIFT2 + 2 + block] = jnp.where(mine, row[0:1], 0.0)
    out_ref[R_C2 : R_SHIFTF + 1] = head_ref[0:3]
    out_ref[R_SMALL : R_SMALL + HEADS] = pull_ref[...]
    out_ref[R_SMALL + HEADS : R_SMALL + HEADS + 1] = head_ref[3:4]
    for number in range(sent_ref.shape[0]):
        sent_ref[number] = out_ref[3 * number : 3 * number + 3]


def share_kernel(got_ref, sent_ref):
    sent_ref[...] = jnp.broadcast_to(jnp.sum(got_ref[...], axis=0, keepdims=True), sent_ref.shape)


def query_back_kernel(core_ref, got_ref, w_ref, shuffle_ref, dq_ref, pull_ref, total_ref):
    for number in range(got_ref.shape[0]):
        total_ref[3 * number : 3 * number + 3] = got_ref[number]
    wide = shuffle_ref[...].astype(F32)
    pull = total_ref[R_SMALL : R_SMALL + HEADS]
    is_one = core_ref[0] == 1
    out = []
    for block in range(WIDTH // 256):
        moved = dot(pull[:, 256 * block : 256 * block + 256], wide, precision=lax.Precision.HIGHEST)
        out.append(jnp.where(is_one, moved[:, 128:], moved[:, :128]))
    half = jnp.concatenate(out, axis=1)
    pull_ref[...] = half
    d_query = jnp.where(head_mask(HEADS), dot(low(half), w_ref[...]), 0.0)
    dq_ref[...] = jnp.broadcast_to(rowsum(d_query) * SCALE, dq_ref.shape)


def complete_kernel(total_ref, reports_ref, rows_ref, shuffle_ref, out_ref, norm_ref):
    out_ref[...] = total_ref[0:R_SMALL]
    half = WIDTH // 2
    first = jnp.broadcast_to(reports_ref[6, :, WIDTH : WIDTH + half], (8, half))
    second = jnp.broadcast_to(reports_ref[7, :, WIDTH : WIDTH + half], (8, half))
    d_hidden = to_natural_exact(first, second, shuffle_ref[...])[0:1]
    xhat, rstd = norm_parts(rows_ref[0:1] + rows_ref[1:2])
    d_class = norm_back(d_hidden, rows_ref[R_GAIN1 : R_GAIN1 + 1], xhat, rstd)
    out_ref[0:1] += d_class
    out_ref[1:2] += d_class
    out_ref[R_GAIN1 : R_GAIN1 + 1] += d_hidden * xhat
    out_ref[R_SHIFT1 : R_SHIFT1 + 1] += d_hidden
    out_ref[R_SHIFT1 + 1 : R_SHIFT1 + 2] = reports_ref[6, :, :WIDTH]
    grads = out_ref[...]
    square = jnp.sum(jnp.sum(grads * grads, axis=0, keepdims=True), axis=1, keepdims=True)
    for number in range(reports_ref.shape[0]):
        square = square + reports_ref[number, :, WIDTH + half : WIDTH + half + 1]
    norm_ref[...] = jnp.broadcast_to(jnp.sqrt(square), (8, 128))


def owner_kernel(role_ref, pull_ref, heads_ref, class_ref, dq_ref, *refs):
    rows, out_ref = refs[:6], refs[6]
    chip, core = role_ref[0], role_ref[1]
    half = WIDTH // 2
    base = 3 * WIDTH

    def product(left, right):
        total = None
        for piece in rows:
            term = dot(left(piece), right(piece), TN)
            total = term if total is None else total + term
        return total

    @pl.when((chip >= 7) & (chip <= 14))
    def _():
        is_two = chip >= 11
        out_ref[...] = product(
            lambda piece: jnp.where(is_two, piece[:, :half], piece[:, half:WIDTH]),
            lambda piece: jnp.where(is_two, piece[:, 2 * WIDTH : base], piece[:, WIDTH : 2 * WIDTH]),
        )

    @pl.when(chip == 6)
    def _():
        lanes = pl.ds(pl.multiple_of(base + core * half, 128), half)
        out_ref[...] = product(lambda piece: piece[:, lanes], lambda piece: piece[:, base + WIDTH :])

    @pl.when(chip == 15)
    def _():
        lanes = pl.ds(pl.multiple_of(base + core * (PROJ // 2), 128), PROJ // 2)
        out_ref[: PROJ // 2] = product(
            lambda piece: piece[:, lanes],
            lambda piece: piece[:, base + PROJ : base + PROJ + WIDTH],
        )
        out_ref[PROJ // 2 :] = jnp.zeros((512 - PROJ // 2, WIDTH), F32)

    @pl.when(chip == 4)
    def _():
        out_ref[...] = dot(
            pull_ref[...], heads_ref[...].astype(F32), TN, precision=lax.Precision.HIGHEST
        )

    @pl.when(chip == 3)
    def _():
        out_ref[...] = dot(
            class_ref[...].astype(F32), jnp.concatenate([dq_ref[0:1], jnp.zeros((7, WIDTH), F32)]),
            TN, precision=lax.Precision.HIGHEST,
        )


def finish_kernel(
    role_ref, formed_ref, dq_ref, toward_ref, total_ref, first_ref, second_ref, aside_ref, third_ref,
    out_ref, top_ref, end_ref, report_ref,
):
    chip = role_ref[0]

    @pl.when(chip < 3)
    def _():
        out_ref[...] = total_ref[...] + first_ref[...].astype(F32) + second_ref[...].astype(F32)

    @pl.when(chip == 5)
    def _():
        out_ref[...] = (
            second_ref[...].astype(F32) + aside_ref[...].astype(F32) + third_ref[...].astype(F32)
        )

    @pl.when((chip >= 3) & (chip != 5))
    def _():
        out_ref[...] = formed_ref[...]

    edge = top_ref.shape[0]
    top_ref[...] = out_ref[:edge]
    end_ref[...] = out_ref[-edge:]
    grads = out_ref[...]
    square = jnp.sum(jnp.sum(grads * grads, axis=0, keepdims=True), axis=1, keepdims=True)
    report_ref[...] = jnp.concatenate(
        [dq_ref[...], toward_ref[...], jnp.broadcast_to(square, (1, 128))], axis=1
    )


def update_kernel(
    source_ref, scalar_ref, before_ref, grad_ref, behind_ref, w_ref, m_ref, v_ref,
    nw_ref, nm_ref, nv_ref,
):
    step = pl.program_id(0)
    slots = grad_ref.shape[0]
    factor, fix_one, fix_two = scalar_ref[0], scalar_ref[1], scalar_ref[2]
    for k in range(w_ref.shape[0]):
        at = source_ref[step * w_ref.shape[0] + k]
        inside = (at >= 0) & (at < slots)
        grad = jnp.where(
            inside,
            grad_ref[jnp.clip(at, 0, slots - 1)],
            jnp.where(
                at < 0,
                before_ref[jnp.clip(at + JITTER, 0, JITTER - 1)],
                behind_ref[jnp.clip(at - slots, 0, JITTER - 1)],
            ),
        )
        grad = grad * jnp.where(at >= -JITTER, factor, 0.0)
        weight = w_ref[k]
        first = BETA_ONE * m_ref[k] + (1.0 - BETA_ONE) * grad
        second = BETA_TWO * v_ref[k] + (1.0 - BETA_TWO) * grad * grad
        nm_ref[k] = first
        nv_ref[k] = second
        nw_ref[k] = weight - LEARN_RATE * (
            (first * fix_one) / (jnp.sqrt(second * fix_two) + ADAM_EPS) + DECAY_RATE * weight
        )


def update_call(source, scalars, before, grads, behind, masters, first, second):
    slots, part, width = masters.shape
    block = 16
    spec = pl.BlockSpec((block, part, width), lambda i: (i, 0, 0))
    return pl.pallas_call(
        update_kernel,
        grid=(slots // block,),
        in_specs=[smem(), smem(), vmem(), vmem(), vmem(), spec, spec, spec],
        out_specs=[spec] * 3,
        out_shape=[shape(masters.shape, F32)] * 3,
        compiler_params=pltpu.CompilerParams(vmem_limit_bytes=58 * 2**20),
        cost_estimate=pl.CostEstimate(
            flops=2 * 10**7, bytes_accessed=7 * masters.size * 4, transcendentals=0
        ),
        name="update",
    )(source, scalars, before, grads, behind, masters, first, second)


CHIPS = 16
CHIP = ("z", "y", "x")
ALL = ("z", "y", "x", "c")
PLANE = ("y", "x", "c")
FLIP_X = [(i, i ^ 1) for i in range(CHIPS)]
FLIP_Y = [(i, i ^ 2) for i in range(CHIPS)]
FLIP_CORE = [(0, 1), (1, 0)]


def hop(values, pairs):
    return lax.ppermute(values, CHIP, pairs)


def swap(values):
    return lax.ppermute(values, "c", FLIP_CORE)


def after(values, *others):
    return lax.optimization_barrier((values,) + others)[0]


def among(img, chips):
    hit = img == chips[0]
    for chip in chips[1:]:
        hit = hit | (img == chip)
    return hit


def choose(img, cases, otherwise):
    out = otherwise
    for chips, values in cases:
        out = jnp.where(among(img, chips), values, out)
    return out


def together(*values):
    return lax.optimization_barrier(values)


def plane_gather(block, diagonal_by_x):
    by_x, by_y, block_peer = hop(block, FLIP_X), hop(block, FLIP_Y), swap(block)
    proj_top = jnp.where(img == 15, corner[0], corner[1] + corner[2] + corner[3])
    diagonal = hop(by_y, FLIP_X) if diagonal_by_x else hop(by_x, FLIP_Y)
    return [block, by_x, by_y, diagonal]


def in_plane(values):
    return lax.all_to_all(values, PLANE, 0, 0, tiled=True)


def from_all(values):
    sent = jnp.broadcast_to(values[None], (2 * CHIPS,) + values.shape)
    return lax.all_to_all(sent, ALL, 0, 0, tiled=True)


def natural(values):
    lead = values.shape[:-2]
    units = values.shape[-1] // 16
    split = values.reshape(lead + (2, units, 16))
    return jnp.swapaxes(split, -3, -2).reshape(lead + (units * 32,))


def halves(values):
    lead = values.shape[:-1]
    units = values.shape[-1] // 32
    return jnp.swapaxes(values.reshape(lead + (units, 2, 16)), -3, -2).reshape(
        lead + (2, units * 16)
    )


def per_device_16(
    pixels, keep_mask, partner_index, partner_emb, masters, first_moment_slots,
    second_moment_slots, slot_unit_index, small_params, small_first, small_second, step_count,
):
    img, core = lax.axis_index(CHIP), lax.axis_index("c")
    col, plane = img % 4, img // 4
    images = pixels.shape[0]
    slots = masters.shape[0]
    is_one = core == 1
    where = jnp.stack([col, core]).astype(jnp.int32)
    shuffle = shuffle_matrix()
    rows = small_params
    class_state = small_params[0] + small_params[1]

    def mine_of(pair):
        return jnp.where(is_one, pair[1], pair[0])

    def theirs_of(pair):
        return jnp.where(is_one, pair[0], pair[1])

    near = slots_near(slot_unit_index, img, slots)
    held = low(masters)
    ids = img * slots + jnp.arange(slots, dtype=jnp.int32)
    matches = [near[s : s + slots] == ids for s in range(2 * JITTER + 1)]
    middle = pick(held[6:26], [m[8:24] for m in matches], 16).reshape(256, WIDTH)
    one_a = hop(middle, [(0, 4), (1, 5), (2, 6), (5, 7)])
    partners = from_all(after(partner_emb, middle))
    before, behind = halo(after(held, middle), CHIPS, CHIP)
    lower = pick(jnp.concatenate([before, held[:10]]), [m[:8] for m in matches], 8)
    upper = pick(jnp.concatenate([held[22:], behind]), [m[24:] for m in matches], 8)
    outer = jnp.concatenate([lower, upper]).reshape(256, WIDTH)
    own_w = jnp.concatenate([outer[:128], middle, outer[128:]])
    class_hidden = low(layer_norm(class_state, small_params[R_GAIN1], small_params[R_SHIFT1]))
    class_half = mine_of(halves(class_hidden))
    query = dot(class_half[None], own_w)
    query = query + swap(query)
    wo_quarter = hop(own_w[384:], [(6, 7)]) + hop(own_w[:128], [(6, 4)])
    wo_quarter = wo_quarter + hop(own_w[128:256], [(6, 5)])
    wo_quarter = jnp.where(img == 6, own_w[256:384], wo_quarter)
    down_one = hop(
        own_w,
        [(12, 8), (13, 9), (14, 10), (11, 7), (8, 4), (9, 5), (10, 6), (7, 3)],
    )
    one_a, outer, query = together(one_a, outer, query)
    query = hop(query, [(3, 4)])
    one_b = hop(outer, [(0, 4), (1, 5), (2, 6), (5, 7)])
    two_a = hop(one_a, [(4, 8), (5, 9), (6, 10), (7, 11)])
    pix = prep(after(pixels, one_a), shuffle).reshape(2, images * SLOT, PIX // 2)
    corner = after(own_w[: PROJ // 2], one_a)
    corner = [corner] + [hop(corner, [(15, 15 ^ flip)]) for flip in (1, 2, 3)]
    query = low((query + small_params[R_SHIFT1 + 1 : R_SHIFT1 + 2]) * SCALE)
    query_heads = jnp.where(head_mask(HEADS), query, jnp.zeros((), BF))
    pulled = jnp.pad(low(dot(query_heads, own_w, NT)), ((0, 0), (0, WIDTH // 2)))
    one_b, two_a, wo_quarter, pulled, down_one = together(
        one_b, two_a, wo_quarter, pulled, down_one
    )
    mid_b = jnp.concatenate([one_b, wo_quarter, pulled])
    two_b = hop(mid_b, [(4, 8), (5, 9), (6, 10), (7, 11)])
    three_a = hop(
        jnp.where(img == 7, one_a, two_a), [(8, 12), (9, 13), (10, 14), (11, 15), (7, 3)]
    )
    low_b = hop(mid_b[256:], [(4, 0), (5, 1), (6, 2)])
    two_b, three_a, low_b, pix, partners, *corner = together(
        two_b, three_a, low_b, pix, partners, *corner
    )
    block_a = jnp.where(img < 3, middle, one_a + two_a + three_a)
    x_a, y_a = hop(block_a, FLIP_X), hop(block_a, FLIP_Y)
    three_b = hop(
        jnp.where(img == 7, mid_b, two_b), [(8, 12), (9, 13), (10, 14), (11, 15), (7, 3)]
    )
    pix_own, pix_send = mine_of(pix), theirs_of(pix)
    x_a, y_a, three_b, pix_own, pix_send = together(x_a, y_a, three_b, pix_own, pix_send)
    spot = jnp.stack([img, plane]).astype(jnp.int32)
    block_b = second_block(spot, [outer, low_b, mid_b, two_b, three_b])
    x_b, y_b = hop(block_b, FLIP_X), hop(block_b, FLIP_Y)
    down_two = hop(
        after(down_one, three_b), [(8, 4), (9, 5), (10, 6), (7, 3), (4, 0), (5, 1), (6, 2)]
    )
    proj_top = jnp.where(img == 15, corner[0], corner[1] + corner[2] + corner[3])
    (partners,) = call(
        partner_kernel, "partners", [], [partners], [shape((2 * CHIPS * images, PROJ), BF)]
    )
    up_one = hop(
        after(own_w, three_b), [(8, 12), (9, 13), (10, 14), (7, 11), (11, 15)]
    )
    peers_a = [swap(block_a), swap(x_a), swap(y_a), swap(block_b)]
    x_b, y_b, up_one, down_two, *peers_a = together(x_b, y_b, up_one, down_two, *peers_a)
    up_two = hop(up_one, [(11, 15)])
    proj_one = hop(after(proj_top, x_b), [(12, 4), (13, 5), (14, 6), (15, 7)])
    d_a, d_b = hop(y_a, FLIP_X), hop(x_b, FLIP_Y)
    down_three = hop(after(down_two, y_b), [(4, 0), (5, 1), (6, 2)])
    x_peer, y_peer = swap(x_b), swap(y_b)
    d_a, d_b, x_peer, y_peer = together(d_a, d_b, x_peer, y_peer)
    segments = [(source, ((0, 128, 256),), -1) for source in range(4)]
    segments += [(source, ((0, 0, 128), (128, 384, 128)), 256) for source in range(4)]
    own_pieces = [block_a, x_a, y_a, d_a, block_b, x_b, y_b, d_b]
    peer_pieces = [*peers_a[:3], swap(d_a), peers_a[3], x_peer, y_peer, swap(d_b)]
    pix_peer = swap(pix_send)
    valid = jnp.concatenate(
        [
            keep_mask,
            jnp.ones((images, 1), jnp.int32),
            jnp.zeros((images, SLOT - TOKS), jnp.int32),
        ],
        axis=1,
    ).reshape(images * SLOT, 1)
    (
        hid, xhat, rstd, p, pooled, mass, wv, wo, qk, resid, hidden_sent,
    ) = forward_call(
        segments, images, where, pix, own_pieces, peer_pieces, rows, valid, shuffle
    )
    pooled_own = mine_of(pooled)
    pooled_peer = swap(theirs_of(pooled))

    hidden_all = in_plane(hidden_sent)
    hidden_all, pooled_peer = together(hidden_all, pooled_peer)
    ff_block = (col + 1) % 4
    bias_part = lax.dynamic_slice(
        small_params[R_SHIFT2 + 1 : R_C2].reshape(4, 32, 2, 16),
        (ff_block, 0, core, 0),
        (1, 32, 1, 16),
    ).reshape(1, 512)
    candidates = [own_w, up_one, up_two, down_one, down_two, down_three]
    pick_one = choose(
        img, [((15,), 2), ((12, 13, 14, 11), 1), ((4, 5, 6, 3), 3), ((0, 1, 2), 4)], 0
    )
    pick_two = choose(
        img, [((15,), 1), ((8, 9, 10, 7), 3), ((4, 5, 6, 3), 4), ((0, 1, 2), 5)], 0
    )
    picks = jnp.stack([pick_one, pick_two]).astype(jnp.int32)
    preact, active, part = ff_call(
        ff_kernel, "ff", picks, [hidden_all, bias_part], candidates,
        [shape((8 * images, 512), F32), shape((8 * images, 512), BF), shape((8, images, WIDTH), BF)],
    )
    proj_mid = hop(
        after(jnp.where(plane == 3, proj_top, proj_one), hidden_sent),
        [(12, 8), (13, 9), (14, 10), (15, 11), (4, 0), (5, 1), (6, 2), (7, 3)],
    )
    hidden_all = in_plane(hidden_sent)
    ff_block = (col + 1) % 4
    bias_part = lax.dynamic_slice(
        small_params[R_SHIFT2 + 1 : R_C2].reshape(4, 32, 2, 16),
        (ff_block, 0, core, 0),
        (1, 32, 1, 16),
    ).reshape(1, 512)
    candidates = [own_w, up_one, up_two, down_one, down_two, down_three]
    pick_one = choose(
        img, [((15,), 2), ((12, 13, 14, 11), 1), ((4, 5, 6, 3), 3), ((0, 1, 2), 4)], 0
    )
    pick_two = choose(
        img, [((15,), 1), ((8, 9, 10, 7), 3), ((4, 5, 6, 3), 4), ((0, 1, 2), 5)], 0
    )
    picks = jnp.stack([pick_one, pick_two]).astype(jnp.int32)
    preact, active, part = ff_call(
        ff_kernel, "ff", picks, [hidden_all, bias_part], candidates,
        [shape((8 * images, 512), F32), shape((8 * images, 512), BF), shape((8, images, WIDTH), BF)],
    )
    proj = choose(
        plane, [((3,), proj_top), ((1,), proj_one)], after(proj_mid, hidden_sent)
    )
    proj_peer = swap(proj)
    part = in_plane(part)
    proj = choose(plane, [((3,), proj_top), ((1,), proj_one)], after(proj_mid, part))
    proj_peer = swap(proj)
    d_state, d_state_sent, head_vec = call(
        head_kernel, "head", [where],
        [part, resid, proj, proj_peer, partners, partner_index[:, None], rows],
        [
            shape((images, WIDTH), F32), shape((8, images, 2 * WIDTH + PROJ), BF),
            shape((8, WIDTH), F32),
        ],
        [pltpu.VMEM((images, PROJ), BF)],
    )
    d_state_all = in_plane(d_state_sent)
    d_preact, d_preact_sum, part = ff_call(
        ff_back_kernel, "ff_back", picks, [d_state_all, preact], candidates,
        [shape((8 * images, 512), BF), shape((1, 512), F32), shape((8, images, WIDTH), BF)],
    )
    part = in_plane(part)

    d_embed, d_attended, d_resid, d_pos, d_vec, pull = backward_call(
        images, where,
        [part, d_state, resid, wo, wv, hid, xhat, rstd, p, mass, qk, rows, shuffle],
    )
    arrays = [
        pix_own, pix_peer, d_embed, swap(d_embed), pooled_own, pooled_peer, d_attended,
        swap(d_attended),
    ]
    far_x, far_y = embed_grad_call(
        images, "embed_grad_far", [(3, 0, 256, BF), (3, 256, 256, BF)], where, arrays
    )
    got_y, got_x = hop(far_x, FLIP_X), hop(far_y, FLIP_Y)
    own_part, x_low, x_high, y_low, y_high = embed_grad_call(
        images, "embed_grad_near",
        [(0, 0, 512, F32), (1, 0, 256, BF), (1, 256, 256, F32), (2, 0, 256, F32), (2, 256, 256, BF)],
        after(where, far_x), arrays,
    )
    d_resid = in_plane(after(d_resid, far_x))
    d_pos, d_vec, head_vec, d_preact_sum, pull, _ = together(
        d_pos, d_vec, head_vec, d_preact_sum, pull, far_x
    )
    (small_sent,) = call(
        collect_kernel, "collect", [where], [d_pos, d_vec, head_vec, d_preact_sum, pull, shuffle],
        [shape((32, 3, WIDTH), F32)], [pltpu.VMEM((96, WIDTH), F32)],
    )
    got_x, got_y, own_part, x_low, x_high, y_low, y_high, d_resid, small_sent = together(
        got_x, got_y, own_part, x_low, x_high, y_low, y_high, d_resid, small_sent
    )
    part_x, part_y = add_far([x_low, x_high, got_x, y_low, got_y, y_high])
    part_x, part_y = part_x.reshape(512, WIDTH), part_y.reshape(512, WIDTH)
    sum_x, sum_y = hop(part_x, FLIP_X), hop(part_y, FLIP_Y)
    shares = lax.all_to_all(small_sent, ALL, 0, 0, tiled=True)
    (ff_rows,) = call(
        rows_kernel, "rows", [where], [active, d_preact, hidden_all, d_state_all, d_resid],
        [shape((8 * images, 5 * WIDTH), BF)],
    )
    rise = [(i, i + 4) for i in range(12)]
    fall = [(12, 8), (13, 9), (14, 10), (15, 11), (10, 6), (11, 7)]
    up_one, down_one = hop(ff_rows, rise), hop(ff_rows, fall)
    sum_x, sum_y, shares, up_one, down_one = together(sum_x, sum_y, shares, up_one, down_one)
    total = own_part + sum_x.astype(F32) + sum_y.astype(F32)
    sent = low(total)
    first = hop(sent, [(12, 8), (13, 9), (14, 10), (15, 11), (4, 0), (5, 1), (6, 2)])
    aside = hop(sent, [(3, 1), (7, 5)])
    (small_sent,) = call(share_kernel, "share", [], [shares], [shape((32, 3, WIDTH), F32)])
    shares = lax.all_to_all(small_sent, ALL, 0, 0, tiled=True)
    up_two, down_two = hop(up_one, rise[4:]), hop(down_one, fall[4:])
    first, aside, up_two, down_two, total = together(first, aside, up_two, down_two, total)
    partial = low(total + first.astype(F32))
    second = hop(partial, [(8, 0), (9, 1), (10, 2), (11, 5)])
    third = hop(aside, [(1, 5)])
    up_three = hop(up_two, rise[8:])
    d_query, pull_half, small_total = call(
        query_back_kernel, "query_back", [core.reshape(1).astype(jnp.int32)],
        [shares, own_w, shuffle],
        [shape((8, WIDTH), F32), shape((HEADS, WIDTH // 2), F32), shape((96, WIDTH), F32)],
    )
    loss = small_total[R_SMALL + HEADS, 0]
    d_query = d_query[0:1]
    d_query = d_query + swap(d_query)
    d_query = hop(d_query, [(4, 3)])
    toward = dot(low(d_query), own_w, NT)

    every = [ff_rows, up_one, up_two, up_three, down_one, down_two]
    class_rows = jnp.concatenate([class_half[None], jnp.zeros((7, WIDTH // 2), BF)])
    role = jnp.stack([img, core]).astype(jnp.int32)
    (formed,) = call(
        owner_kernel, "owner", [role], [pull_half, query_heads, class_rows, d_query, *every],
        [shape((512, WIDTH), F32)],
    )
    edge = shape((JITTER * 16, WIDTH), F32)
    own_grad, top, end, report = call(
        finish_kernel, "finish", [role],
        [formed, d_query, toward, total, first, second, aside, third],
        [shape((512, WIDTH), F32), edge, edge, shape((1, WIDTH + 640), F32)],
    )
    reports = from_all(report)
    before = hop(end, [(i, i + 1) for i in range(CHIPS - 1)]).reshape(JITTER, 16, WIDTH)
    behind = hop(top, [(i + 1, i) for i in range(CHIPS - 1)]).reshape(JITTER, 16, WIDTH)
    small_grad, norm = call(
        complete_kernel, "complete", [], [small_total, reports, rows, shuffle],
        [shape((R_SMALL, WIDTH), F32), shape((8, 128), F32)],
    )
    grad_norm = norm[0, 0]
    factor = 1.0 / jnp.maximum(grad_norm, 1.0)
    own_grad = own_grad.reshape(slots, 16, WIDTH)
    here = near[JITTER : JITTER + slots]
    source = jnp.where(here < UNIT_COUNT, here - img * slots, -100)
    step_value = step_count.astype(F32)
    scalars = jnp.stack(
        [
            factor,
            1.0 / (1.0 - jnp.power(BETA_ONE, step_value)),
            1.0 / (1.0 - jnp.power(BETA_TWO, step_value)),
        ]
    )
    new_masters, new_first, new_second = update_call(
        source, scalars, before, own_grad, behind, masters, first_moment_slots,
        second_moment_slots,
    )
    new_small, new_small_first, new_small_second = adamw(
        small_params, small_grad * factor, small_first, small_second, step_value
    )
    return (
        new_masters, new_first, new_second, new_small, new_small_first, new_small_second,
        loss, grad_norm,
    )


def per_device_any(
    pixels, keep_mask, partner_index, partner_emb, masters, first_moment_slots,
    second_moment_slots, slot_unit_index, small_params, small_first, small_second, step_count,
):
    chips, seq = lax.axis_size("img"), lax.axis_size("seq")
    img = lax.axis_index("img")
    images = pixels.shape[0]
    slots, part = masters.shape[0], masters.shape[1]
    near = slots_near(slot_unit_index, img, slots)
    own_w = to_units(low(masters), near, img, chips)
    gathered = lax.all_gather(own_w, ("img", "seq"), axis=0, tiled=False)
    flat = gathered.reshape(chips, seq, slots, part, WIDTH).transpose(0, 2, 1, 3, 4)
    flat = flat.reshape(chips * slots * ROWS_PER_UNIT, WIDTH)
    bounds = [0, PIX, WIDTH, WIDTH, WIDTH, WIDTH, FF, FF, PROJ]
    parts, offset = [], 0
    for size in bounds[1:]:
        parts.append(flat[offset : offset + size])
        offset += size
    embed_w, query_w, key_w, value_w, output_w, fc_in_w, fc_out_w, proj_w = parts
    (
        class_row, pos_rows, patch_bias, gain_one, shift_one, query_bias, value_bias, out_bias,
        gain_two, shift_two, fc_in_bias, fc_out_bias, gain_end, shift_end,
    ) = small_parts(small_params)
    class_state = class_row + pos_rows[0]
    embedded = jnp.einsum("itp,pd->itd", pixels, embed_w, preferred_element_type=F32)
    tokens = jnp.concatenate(
        [
            jnp.broadcast_to(class_state, (images, 1, WIDTH)),
            embedded + patch_bias + pos_rows[1:],
        ],
        axis=1,
    )
    hidden = low(layer_norm(tokens, gain_one, shift_one))
    class_hidden = hidden[0, 0]
    mask16 = head_mask(HEADS)
    query = low((dot(class_hidden[None], query_w)[0] + query_bias) * SCALE)
    query_heads = jnp.where(mask16, query[None], jnp.zeros((), BF))
    qk = low(dot(query_heads, key_w, NT))
    scores = jnp.einsum("hd,itd->iht", qk, hidden, preferred_element_type=F32)
    keep = jnp.concatenate([jnp.ones((images, 1), jnp.int32), keep_mask], axis=1)
    scores = jnp.where(keep[:, None, :] > 0, scores, MASKED)
    weights = jax.nn.softmax(scores, axis=-1)
    weights_low = low(weights)
    pooled = low(jnp.einsum("iht,itd->ihd", weights_low, hidden, preferred_element_type=F32))
    mass = jnp.sum(weights_low.astype(F32), axis=-1)
    mixed = dot(pooled.reshape(-1, WIDTH), value_w).reshape(images, HEADS, WIDTH)
    mixed = mixed + mass[:, :, None] * value_bias
    attended = low(jnp.sum(jnp.where(mask16, mixed, 0.0), axis=1))
    resid = class_state + dot(attended, output_w) + out_bias
    hidden_two = low(layer_norm(resid, gain_two, shift_two))
    preact = dot(hidden_two, fc_in_w, NT) + fc_in_bias
    active = low(exact_gelu(preact))
    state = resid + dot(active, fc_out_w) + fc_out_bias
    final = low(layer_norm(state, gain_end, shift_end))
    projected = dot(final, proj_w, NT)
    unit = low(normalize(projected))
    partners = lax.all_gather(partner_emb, ("img", "seq"), axis=0, tiled=True)
    count = partners.shape[0]
    logits = dot(unit, partners, NT) / SOFTMAX_SCALE
    onehot = (jnp.arange(count, dtype=jnp.int32)[None] == partner_index[:, None]).astype(F32)
    total = jax.nn.logsumexp(logits, axis=-1)
    loss_part = jnp.sum(total - jnp.sum(logits * onehot, axis=-1)) / count
    d_logits = (jax.nn.softmax(logits, axis=-1) - onehot) / count
    d_unit = dot(low(d_logits / SOFTMAX_SCALE), partners)
    d_projected = low(jax.vjp(normalize, projected)[1](d_unit)[0])
    d_final = dot(d_projected, proj_w)
    d_state, d_gain_end, d_shift_end = jax.vjp(layer_norm, state, gain_end, shift_end)[1](d_final)
    d_state_low = low(d_state)
    d_active = dot(d_state_low, fc_out_w, NT)
    d_preact = low(jax.vjp(exact_gelu, preact)[1](d_active)[0])
    d_hidden_two = dot(d_preact, fc_in_w)
    d_norm, d_gain_two, d_shift_two = jax.vjp(layer_norm, resid, gain_two, shift_two)[1](
        d_hidden_two
    )
    d_resid = d_state + d_norm
    d_resid_low = low(d_resid)
    d_attended = low(dot(d_resid_low, output_w, NT))
    wide = jnp.where(mask16, d_attended[:, None, :], jnp.zeros((), BF))
    d_pooled = low(dot(wide.reshape(-1, WIDTH), value_w, NT)).reshape(images, HEADS, WIDTH)
    d_weights = jnp.einsum("ihd,itd->iht", d_pooled, hidden, preferred_element_type=F32)
    d_weights = d_weights + jnp.sum(wide.astype(F32) * value_bias, axis=-1)[:, :, None]
    d_scores = low(weights * (d_weights - jnp.sum(weights * d_weights, axis=-1, keepdims=True)))
    d_hidden = jnp.einsum("iht,ihd->itd", weights_low, d_pooled, preferred_element_type=F32)
    d_hidden = d_hidden + jnp.einsum("iht,hd->itd", d_scores, qk, preferred_element_type=F32)
    pull = jnp.einsum("iht,itd->hd", d_scores, hidden, preferred_element_type=F32)
    d_query = jnp.sum(jnp.where(mask16, dot(low(pull), key_w), 0.0), axis=0) * SCALE
    d_class_hidden = dot(low(d_query)[None], query_w, NT)
    d_tokens, d_gain_one, d_shift_one = jax.vjp(layer_norm, tokens, gain_one, shift_one)[1](
        d_hidden
    )
    d_class, d_gain_cls, d_shift_cls = jax.vjp(layer_norm, class_state[None], gain_one, shift_one)[
        1
    ](d_class_hidden)
    d_class = d_class[0] + jnp.sum(d_tokens[:, 0], axis=0) + jnp.sum(d_resid, axis=0)
    d_patch = d_tokens[:, 1:]
    d_embed_w = jnp.einsum("itp,itd->pd", pixels, low(d_patch), preferred_element_type=F32)
    d_value_w = dot(pooled.reshape(-1, WIDTH), wide.reshape(-1, WIDTH), TN)
    d_key_w = dot(pull, query_heads.astype(F32), TN, precision=lax.Precision.HIGHEST)
    small_local = jnp.concatenate(
        [
            d_class[None],
            d_class[None],
            jnp.sum(d_patch, axis=0),
            jnp.sum(d_patch, axis=(0, 1))[None],
            (d_gain_one + d_gain_cls)[None],
            (d_shift_one + d_shift_cls)[None],
            d_query[None],
            jnp.sum(wide.astype(F32) * mass[:, :, None], axis=(0, 1))[None],
            jnp.sum(d_resid, axis=0)[None],
            d_gain_two[None],
            d_shift_two[None],
            jnp.sum(d_preact.astype(F32), axis=0).reshape(FF // WIDTH, WIDTH),
            jnp.sum(d_state, axis=0)[None],
            d_gain_end[None],
            d_shift_end[None],
        ],
        axis=0,
    )
    grad_table = jnp.concatenate(
        [
            d_embed_w,
            class_hidden.astype(F32)[:, None] * d_query[None, :],
            d_key_w,
            d_value_w,
            dot(attended, d_resid_low, TN),
            dot(d_preact, hidden_two, TN),
            dot(active, d_state_low, TN),
            dot(d_projected, final, TN),
            jnp.zeros(((chips * slots - UNIT_COUNT) * ROWS_PER_UNIT, WIDTH), F32),
        ],
        axis=0,
    ).reshape(chips * slots, ROWS_PER_UNIT, WIDTH)
    small_grad, loss = lax.psum((small_local, loss_part), ("img", "seq"))
    core_half = lax.psum_scatter(low(grad_table), "seq", scatter_dimension=1, tiled=True)
    own_grad = lax.psum_scatter(core_half.astype(F32), "img", scatter_dimension=0, tiled=True)
    owner_total = lax.psum(jnp.sum(own_grad * own_grad), ("img", "seq"))
    grad_norm = jnp.sqrt(owner_total + jnp.sum(small_grad * small_grad))
    factor = 1.0 / jnp.maximum(grad_norm, 1.0)
    slot_grad = to_slots(own_grad, near, img, chips)
    step_value = step_count.astype(F32)
    new_masters, new_first, new_second = adamw(
        masters, slot_grad * factor, first_moment_slots, second_moment_slots, step_value
    )
    new_small, new_small_first, new_small_second = adamw(
        small_params, small_grad * factor, small_first, small_second, step_value
    )
    return (
        new_masters, new_first, new_second, new_small, new_small_first, new_small_second,
        loss, grad_norm,
    )


def solution(mesh):
    chip, devices = "img", ("img", "seq")
    core, body = "seq", per_device_any
    if mesh.shape["img"] == CHIPS and mesh.shape["seq"] == 2:
        mesh = jax.sharding.Mesh(mesh.devices.reshape(4, 2, 2, 2), ALL)
        chip, devices, core, body = CHIP, ALL, "c", per_device_16
    weights = P(chip, core, None)
    return jax.shard_map(
        body,
        mesh=mesh,
        in_specs=(
            P(devices, None, None),
            P(devices, None),
            P(devices),
            P(devices, None),
            weights,
            weights,
            weights,
            P(),
            P(),
            P(),
            P(),
            P(),
        ),
        out_specs=(weights, weights, weights, P(), P(), P(), P(), P()),
        check_vma=False,
    )
```

```python
import functools
import math

import jax
import jax.numpy as jnp
from jax import lax
from jax.experimental import pallas as pl
from jax.experimental.pallas import tpu as pltpu
from jax.sharding import PartitionSpec as P

WIDTH = 1024
HEADS = 16
HEAD_DIM = 64
FF = 4096
PIX = 3072
PROJ = 768
TOKS = 50
PATCHES = TOKS - 1
ROWS_PER_UNIT = 32
UNIT_COUNT = 504
JITTER = 2

EPS_NORM = 1e-06
SOFTMAX_SCALE = 0.07
LEARN_RATE = 0.03
BETA_ONE = 0.5
BETA_TWO = 0.5
DECAY_RATE = 0.05
ADAM_EPS = 1e-08
MASKED = -1000000000.0
SCALE = HEAD_DIM ** (-0.5)

F32 = jnp.float32
BF = jnp.bfloat16
ROW_BASE = 1 + TOKS
ROW_TAIL = ROW_BASE + 8 + FF // WIDTH
SLOT = 64


def low(values):
    return values.astype(BF)


def dot(a, b, dims=((1,), (0,)), precision=None):
    return lax.dot_general(a, b, (dims, ((), ())), precision=precision, preferred_element_type=F32)


NN = ((1,), (0,))
NT = ((1,), (1,))
TN = ((0,), (0,))


def layer_norm(values, gain, shift):
    center = values - jnp.mean(values, axis=-1, keepdims=True)
    spread = jnp.mean(center * center, axis=-1, keepdims=True)
    return center * lax.rsqrt(spread + EPS_NORM) * gain + shift


def normalize(values):
    return values * lax.rsqrt(jnp.sum(values * values, axis=-1, keepdims=True) + EPS_NORM)


def exact_gelu(values):
    return jax.nn.gelu(values, approximate=False)


def small_parts(small):
    base, tail = ROW_BASE, ROW_TAIL
    return (
        small[0],
        small[1:base],
        small[base],
        small[base + 1],
        small[base + 2],
        small[base + 3],
        small[base + 4],
        small[base + 5],
        small[base + 6],
        small[base + 7],
        small[base + 8 : tail].reshape(FF),
        small[tail],
        small[tail + 1],
        small[tail + 2],
    )


def adamw(weight, grad, first, second, step):
    first_new = BETA_ONE * first + (1.0 - BETA_ONE) * grad
    second_new = BETA_TWO * second + (1.0 - BETA_TWO) * grad * grad
    first_hat = first_new / (1.0 - jnp.power(BETA_ONE, step))
    second_hat = second_new / (1.0 - jnp.power(BETA_TWO, step))
    weight_new = weight - LEARN_RATE * (
        first_hat / (jnp.sqrt(second_hat) + ADAM_EPS) + DECAY_RATE * weight
    )
    return (weight_new, first_new, second_new)


def halo(values, chips, axes):
    before = lax.ppermute(values[-JITTER:], axes, [(i, i + 1) for i in range(chips - 1)])
    behind = lax.ppermute(values[:JITTER], axes, [(i + 1, i) for i in range(chips - 1)])
    return before, behind


def with_halo(values, chips, axes):
    before, behind = halo(values, chips, axes)
    return jnp.concatenate([before, values, behind], axis=0)


def slots_near(slot_unit_index, img, slots):
    padded = jnp.pad(slot_unit_index, (JITTER, JITTER), constant_values=-1)
    return lax.dynamic_slice(padded, (img * slots,), (slots + 2 * JITTER,))


def pick(ext, matches, slots):
    out = jnp.zeros((slots,) + ext.shape[1:], ext.dtype)
    for shift in range(2 * JITTER + 1):
        out = jnp.where(matches[shift][:, None, None], ext[shift : shift + slots], out)
    return out


def to_units(values, near, img, chips, axes="img"):
    slots = values.shape[0]
    ids = img * slots + jnp.arange(slots, dtype=jnp.int32)
    matches = [near[s : s + slots] == ids for s in range(2 * JITTER + 1)]
    return pick(with_halo(values, chips, axes), matches, slots)


def to_slots(values, near, img, chips, axes="img"):
    slots = values.shape[0]
    here = near[JITTER : JITTER + slots]
    ids = img * slots + jnp.arange(slots, dtype=jnp.int32)
    matches = [
        (here == ids + (s - JITTER)) & (here < UNIT_COUNT) for s in range(2 * JITTER + 1)
    ]
    return pick(with_halo(values, chips, axes), matches, slots)


def shuffle_matrix():
    source = lax.broadcasted_iota(jnp.int32, (256, 256), 0)
    target = lax.broadcasted_iota(jnp.int32, (256, 256), 1)
    moved = ((source // 16) % 2) * 128 + (source // 32) * 16 + source % 16
    return (moved == target).astype(F32).astype(BF)


def vmem():
    return pl.BlockSpec(memory_space=pltpu.VMEM)


def smem():
    return pl.BlockSpec(memory_space=pltpu.SMEM)


def shape(dims, dtype):
    return jax.ShapeDtypeStruct(dims, dtype)


def call(kernel, name, scalars, arrays, outs, scratch=(), mib=16, flops=10**9, far=()):
    moved = sum(a.size * a.dtype.itemsize for a in [*arrays, *outs, *far])
    return pl.pallas_call(
        kernel,
        in_specs=[smem()] * len(scalars)
        + [vmem()] * len(arrays)
        + [pl.BlockSpec(memory_space=pl.ANY)] * len(far),
        out_specs=[vmem()] * len(outs),
        out_shape=list(outs),
        scratch_shapes=list(scratch),
        compiler_params=pltpu.CompilerParams(vmem_limit_bytes=mib * 2**20),
        cost_estimate=pl.CostEstimate(flops=flops, bytes_accessed=moved, transcendentals=0),
        name=name,
    )(*scalars, *arrays, *far)


def prep_kernel(pix_ref, shuffle_ref, out_ref):
    shuffle = shuffle_ref[...]
    out_ref[...] = jnp.zeros_like(out_ref)
    for block in range(PIX // 256):
        moved = dot(pix_ref[0, :, 256 * block : 256 * block + 256], shuffle).astype(BF)
        out_ref[0, 0, :PATCHES, 128 * block : 128 * block + 128] = moved[:, :128]
        out_ref[1, 0, :PATCHES, 128 * block : 128 * block + 128] = moved[:, 128:]


def prep(pixels, shuffle):
    images = pixels.shape[0]
    return pl.pallas_call(
        prep_kernel,
        grid=(images,),
        in_specs=[
            pl.BlockSpec((1, PATCHES, PIX), lambda i: (i, 0, 0)),
            pl.BlockSpec((256, 256), lambda i: (0, 0)),
        ],
        out_specs=pl.BlockSpec((2, 1, SLOT, PIX // 2), lambda i: (0, i, 0, 0)),
        out_shape=jax.ShapeDtypeStruct((2, images, SLOT, PIX // 2), BF),
        compiler_params=pltpu.CompilerParams(vmem_limit_bytes=24 * 2**20),
        cost_estimate=pl.CostEstimate(flops=8 * 10**8, bytes_accessed=6 * 2**20, transcendentals=0),
        name="prep",
    )(pixels, shuffle)


def head_mask(rows):
    lane = lax.broadcasted_iota(jnp.int32, (rows, WIDTH), 1) // HEAD_DIM
    row = lax.broadcasted_iota(jnp.int32, (rows, WIDTH), 0) % HEADS
    return lane == row


def norm_parts(values):
    center = values - jnp.mean(values, axis=-1, keepdims=True)
    rstd = lax.rsqrt(jnp.mean(center * center, axis=-1, keepdims=True) + EPS_NORM)
    return center * rstd, rstd


def norm_back(grad, gain, xhat, rstd):
    gy = grad * gain
    return rstd * (
        gy - jnp.mean(gy, axis=-1, keepdims=True) - xhat * jnp.mean(gy * xhat, axis=-1, keepdims=True)
    )


def rowsum(values):
    return jnp.sum(values, axis=0, keepdims=True)


def to_halves(values, shuffle):
    first, second = [], []
    for block in range(values.shape[1] // 256):
        moved = low(dot(values[:, 256 * block : 256 * block + 256], shuffle))
        first.append(moved[:, :128])
        second.append(moved[:, 128:])
    return jnp.concatenate(first, axis=1), jnp.concatenate(second, axis=1)


def to_natural(first, second, shuffle):
    out = []
    for block in range(first.shape[1] // 128):
        lanes = slice(128 * block, 128 * block + 128)
        both = jnp.concatenate([first[:, lanes], second[:, lanes]], axis=1)
        out.append(low(dot(both, shuffle, NT)))
    return jnp.concatenate(out, axis=1)


R_PATCH, R_GAIN1, R_SHIFT1, R_VB, R_OB, R_GAIN2, R_SHIFT2 = 51, 52, 53, 55, 56, 57, 58
R_C2, R_GAINF, R_SHIFTF, R_SMALL = 63, 64, 65, 66
QUARTER = 128


def partner_kernel(raw_ref, out_ref):
    source = lax.broadcasted_iota(jnp.int32, (PROJ, PROJ), 0)
    target = lax.broadcasted_iota(jnp.int32, (PROJ, PROJ), 1)
    moved = ((source // 16) % 2) * (PROJ // 2) + (source // 32) * 16 + source % 16
    select = low((moved == target).astype(F32))
    out_ref[...] = low(dot(raw_ref[...].reshape(-1, PROJ), select))


def second_block_kernel(
    role_ref, outer_ref, low_ref, mid_ref, two_ref, three_ref, out_ref, held_ref, sems
):
    chip, plane = role_ref[0], role_ref[1]

    @pl.when(chip < 3)
    def _():
        head = pltpu.make_async_copy(outer_ref, held_ref.at[pl.ds(0, 256)], sems.at[0])
        tail = pltpu.make_async_copy(low_ref, held_ref.at[pl.ds(256, QUARTER + HEADS)], sems.at[1])
        head.start()
        tail.start()
        head.wait()
        tail.wait()

    for number, ref in ((1, mid_ref), (2, two_ref), (3, three_ref)):
        here = (plane == number) | (chip == 3) if number == 3 else plane == number

        @pl.when(here)
        def _():
            whole = pltpu.make_async_copy(ref, held_ref, sems.at[0])
            whole.start()
            whole.wait()

    out = pltpu.make_async_copy(held_ref, out_ref, sems.at[0])
    out.start()
    out.wait()


def second_block(role, pieces):
    any_place = pl.BlockSpec(memory_space=pl.ANY)
    return pl.pallas_call(
        second_block_kernel,
        in_specs=[smem()] + [any_place] * len(pieces),
        out_specs=pl.BlockSpec(memory_space=pltpu.HBM),
        out_shape=shape((256 + QUARTER + HEADS, WIDTH), BF),
        scratch_shapes=[
            pltpu.VMEM((256 + QUARTER + HEADS, WIDTH), BF),
            pltpu.SemaphoreType.DMA((2,)),
        ],
        compiler_params=pltpu.CompilerParams(vmem_limit_bytes=4 * 2**20),
        cost_estimate=pl.CostEstimate(flops=0, bytes_accessed=2 * 2**20, transcendentals=0),
        name="second_block",
    )(role, *pieces)


def forward_kernel(segments, images, where_ref, pix_ref, rows_ref, valid_ref, shuffle_ref, *refs):
    count = len(segments)
    own, peer = refs[:count], refs[count : 2 * count]
    (
        hid_ref, xhat_ref, rstd_ref, p_ref, pooled_ref, mass_ref, wv_ref, wo_ref, qk_ref,
        resid_ref, low_ref, acc_ref, pool_ref, half_ref, table_ref, sems,
    ) = refs[2 * count :]
    col, core = where_ref[0], where_ref[1]
    waits = ([], [])
    for flip, group in ((0, own), (1, peer)):
        half = core ^ flip
        for (source, parts, late), ref in zip(segments, group):
            block = col ^ source
            for row, lane, rows in parts:
                part = ref.at[pl.ds(row, rows)]
                line = pl.multiple_of(block * 512 + lane, 128)
                copy = pltpu.make_async_copy(part, table_ref.at[half, pl.ds(line, rows)], sems.at[flip])
                copy.start()
                waits[flip].append(copy)
            if late >= 0:
                part = ref.at[pl.ds(late, QUARTER)]
                line = pl.multiple_of(block * QUARTER, QUARTER)
                copy = pltpu.make_async_copy(part, wo_ref.at[half, pl.ds(line, QUARTER)], sems.at[2])
                copy.start()
                waits[1].append(copy)
                part = ref.at[pl.ds(late + QUARTER, HEADS)]
                copy = pltpu.make_async_copy(part, half_ref.at[half, block], sems.at[3])
                copy.start()
                waits[1].append(copy)
    patch = rows_ref[2 : 1 + TOKS] + rows_ref[R_PATCH : R_PATCH + 1]
    class_state = rows_ref[0:1] + rows_ref[1:2]
    for i in range(images):
        acc_ref[SLOT * i : SLOT * i + PATCHES] = patch
        acc_ref[SLOT * i + PATCHES : SLOT * i + TOKS] = class_state
        acc_ref[SLOT * i + TOKS : SLOT * (i + 1)] = jnp.zeros((SLOT - TOKS, WIDTH), F32)
    for copy in waits[0]:
        copy.wait()
    acc_ref[...] += dot(pix_ref[core], table_ref[core, :1536])
    for copy in waits[1]:
        copy.wait()
    acc_ref[...] += dot(pix_ref[1 - core], table_ref[1 - core, :1536])
    wv_ref[...] = table_ref[:, 1536:]
    shuffle = shuffle_ref[...]
    gain, shift, value_bias = (rows_ref[r : r + 1] for r in (R_GAIN1, R_SHIFT1, R_VB))
    half = WIDTH // 2
    qk = to_natural(half_ref[0, 0, :, :half], half_ref[1, 0, :, :half], shuffle)
    qk_ref[...] = qk
    valid = valid_ref[...] > 0
    for i in range(images):
        part = slice(SLOT * i, SLOT * (i + 1))
        xhat, rstd = norm_parts(acc_ref[part])
        hid = low(xhat * gain + shift)
        xhat_ref[part] = xhat
        rstd_ref[part] = jnp.broadcast_to(rstd, (SLOT, 128))
        hid_ref[part] = hid
        scores = jnp.where(valid[part], dot(hid, qk, NT), MASKED)
        e = jnp.exp(scores - jnp.max(scores, axis=0, keepdims=True))
        p = e / jnp.sum(e, axis=0, keepdims=True)
        p_ref[part] = p
        pb = low(p)
        pool_ref[HEADS * i : HEADS * (i + 1)] = low(dot(pb, hid, TN))
        mass_ref[HEADS * i : HEADS * (i + 1)] = dot(pb, jnp.ones((SLOT, 128), BF), TN)
    pooled_ref[0], pooled_ref[1] = to_halves(pool_ref[...], shuffle)
    rows = images * HEADS
    mixed = dot(pooled_ref[0], wv_ref[0]) + dot(pooled_ref[1], wv_ref[1])
    mixed = mixed + mass_ref[:, 0:1] * value_bias
    mixed = jnp.where(head_mask(rows), mixed, 0.0)
    joined = low(jnp.sum(mixed.reshape(images, HEADS, WIDTH), axis=1))
    first, second = to_halves(joined, shuffle)
    resid = class_state + dot(first, wo_ref[0]) + dot(second, wo_ref[1])
    resid = resid + rows_ref[R_OB : R_OB + 1]
    resid_ref[...] = resid
    xhat, _ = norm_parts(resid)
    hidden = low(xhat * rows_ref[R_GAIN2 : R_GAIN2 + 1] + rows_ref[R_SHIFT2 : R_SHIFT2 + 1])
    sent = jnp.concatenate([hidden, first, second], axis=1)
    low_ref[...] = jnp.broadcast_to(sent[None], low_ref.shape)


def forward_call(segments, images, where, pix, own, peer, rows, valid, shuffle):
    tokens = images * SLOT
    outs = [
        shape((tokens, WIDTH), BF),
        shape((tokens, WIDTH), F32),
        shape((tokens, 128), F32),
        shape((tokens, HEADS), F32),
        shape((2, images * HEADS, WIDTH // 2), BF),
        shape((images * HEADS, 128), F32),
        shape((2, WIDTH // 2, WIDTH), BF),
        shape((2, WIDTH // 2, WIDTH), BF),
        shape((HEADS, WIDTH), BF),
        shape((images, WIDTH), F32),
        shape((8, images, 2 * WIDTH), BF),
    ]
    scratch = [
        pltpu.VMEM((tokens, WIDTH), F32),
        pltpu.VMEM((images * HEADS, WIDTH), BF),
        pltpu.VMEM((2, 4, HEADS, WIDTH), BF),
        pltpu.VMEM((2, 2048, WIDTH), BF),
        pltpu.SemaphoreType.DMA((4,)),
    ]
    return call(
        functools.partial(forward_kernel, segments, images), "forward", [where],
        [pix, rows, valid, shuffle], outs, scratch, mib=52, flops=4 * 10**9,
        far=[*own, *peer],
    )


def fetch(pick_ref, slot, candidates, out_ref, sem):
    for number, candidate in enumerate(candidates):

        @pl.when(pick_ref[slot] == number)
        def _():
            pltpu.make_async_copy(candidate, out_ref, sem).start()


def arrived(candidate, out_ref, sem):
    pltpu.make_async_copy(candidate, out_ref, sem).wait()


def ff_kernel(pick_ref, hid_ref, bias_ref, *refs):
    candidates, (pre_ref, act_ref, part_ref, w1_ref, w2_ref, sems) = refs[:6], refs[6:]
    fetch(pick_ref, 0, candidates, w1_ref, sems.at[0])
    fetch(pick_ref, 1, candidates, w2_ref, sems.at[1])
    hidden = hid_ref[:, :, :WIDTH].reshape(-1, WIDTH)
    arrived(candidates[0], w1_ref, sems.at[0])
    pre = dot(hidden, w1_ref[...], NT) + bias_ref[...]
    pre_ref[...] = pre
    active = low(0.5 * pre * (1.0 + lax.erf(pre * (0.5**0.5))))
    act_ref[...] = active
    arrived(candidates[0], w2_ref, sems.at[1])
    part_ref[...] = low(dot(active, w2_ref[...])).reshape(part_ref.shape)


def ff_back_kernel(pick_ref, dst_ref, pre_ref, *refs):
    candidates, (dpre_ref, sum_ref, part_ref, w1_ref, w2_ref, sems) = refs[:6], refs[6:]
    fetch(pick_ref, 1, candidates, w2_ref, sems.at[1])
    fetch(pick_ref, 0, candidates, w1_ref, sems.at[0])
    d_state = dst_ref[:, :, :WIDTH].reshape(-1, WIDTH)
    pre = pre_ref[...]
    slope = 0.5 * (1.0 + lax.erf(pre * (0.5**0.5))) + pre * jnp.exp(-0.5 * pre * pre) * (
        1.0 / (2.0 * math.pi) ** 0.5
    )
    arrived(candidates[0], w2_ref, sems.at[1])
    d_pre = low(dot(d_state, w2_ref[...], NT) * slope)
    dpre_ref[...] = d_pre
    sum_ref[...] = rowsum(d_pre.astype(F32))
    arrived(candidates[0], w1_ref, sems.at[0])
    part_ref[...] = low(dot(d_pre, w1_ref[...])).reshape(part_ref.shape)


def ff_call(kernel, name, pick, arrays, candidates, outs):
    moved = sum(a.size * a.dtype.itemsize for a in list(arrays) + list(outs))
    return pl.pallas_call(
        kernel,
        in_specs=[smem()]
        + [vmem()] * len(arrays)
        + [pl.BlockSpec(memory_space=pl.ANY)] * len(candidates),
        out_specs=[vmem()] * len(outs),
        out_shape=list(outs),
        scratch_shapes=[
            pltpu.VMEM((512, WIDTH), BF),
            pltpu.VMEM((512, WIDTH), BF),
            pltpu.SemaphoreType.DMA((2,)),
        ],
        compiler_params=pltpu.CompilerParams(vmem_limit_bytes=24 * 2**20),
        cost_estimate=pl.CostEstimate(
            flops=2 * 10**8, bytes_accessed=moved + 2 * 2**20, transcendentals=0
        ),
        name=name,
    )(pick, *arrays, *candidates)


def head_kernel(
    where_ref, part_ref, resid_ref, pj_ref, pjp_ref, partners_ref, target_ref, rows_ref,
    state_ref, low_ref, vec_ref, dz_ref,
):
    images = resid_ref.shape[0]
    state = resid_ref[...] + jnp.sum(part_ref[...].astype(F32), axis=0) + rows_ref[R_C2 : R_C2 + 1]
    gain = rows_ref[R_GAINF : R_GAINF + 1]
    xhat, rstd = norm_parts(state)
    final = low(xhat * gain + rows_ref[R_SHIFTF : R_SHIFTF + 1])
    z_own, z_peer = dot(final, pj_ref[...], NT), dot(final, pjp_ref[...], NT)
    square = jnp.sum(z_own * z_own, axis=-1, keepdims=True) + jnp.sum(
        z_peer * z_peer, axis=-1, keepdims=True
    )
    inv = lax.rsqrt(square + EPS_NORM)
    core = where_ref[1]
    half = PROJ // 2
    own_lanes = pl.ds(pl.multiple_of(core * half, 128), half)
    peer_lanes = pl.ds(pl.multiple_of((1 - core) * half, 128), half)
    ptn_own, ptn_peer = partners_ref[:, own_lanes], partners_ref[:, peer_lanes]
    logits = dot(low(z_own * inv), ptn_own, NT) + dot(low(z_peer * inv), ptn_peer, NT)
    logits = logits / SOFTMAX_SCALE
    total = logits.shape[1]
    hit = lax.broadcasted_iota(jnp.int32, (images, total), 1) == target_ref[...]
    top = jnp.max(logits, axis=-1, keepdims=True)
    e = jnp.exp(logits - top)
    mass = jnp.sum(e, axis=-1, keepdims=True)
    aim = jnp.sum(jnp.where(hit, logits, 0.0), axis=-1, keepdims=True)
    losses = jnp.log(mass) + top - aim
    d_logits = (e / mass - jnp.where(hit, 1.0, 0.0)) / total
    g_logits = low(d_logits / SOFTMAX_SCALE)
    d_own, d_peer = dot(g_logits, ptn_own), dot(g_logits, ptn_peer)
    along = jnp.sum(d_own * z_own, axis=-1, keepdims=True) + jnp.sum(
        d_peer * z_peer, axis=-1, keepdims=True
    )
    shrink = along * inv * inv * inv
    dz_own, dz_peer = low(d_own * inv - z_own * shrink), low(d_peer * inv - z_peer * shrink)
    dz_ref[:, own_lanes] = dz_own
    dz_ref[:, peer_lanes] = dz_peer
    d_final = dot(dz_own, pj_ref[...]) + dot(dz_peer, pjp_ref[...])
    d_state = norm_back(d_final, gain, xhat, rstd)
    state_ref[...] = d_state
    sent = jnp.concatenate([low(d_state), dz_ref[...], final], axis=1)
    low_ref[...] = jnp.broadcast_to(sent[None], low_ref.shape)
    vec_ref[...] = jnp.zeros_like(vec_ref)
    vec_ref[0:1] = rowsum(d_state)
    vec_ref[1:2] = rowsum(d_final * xhat)
    vec_ref[2:3] = rowsum(d_final)
    vec_ref[3:4] = jnp.broadcast_to(rowsum(losses) / total, (1, WIDTH))


def backward_kernel(
    images, where_ref, part_ref, dstate_ref, resid_ref, wo_ref, wv_ref, hid_ref, xhat_ref,
    rstd_ref, p_ref, mass_ref, qk_ref, rows_ref, shuffle_ref,
    de_ref, do_ref, dres_ref, pos_ref, vec_ref, pull_ref, dom_ref, da_ref,
):
    rows = images * HEADS
    gain, value_bias = rows_ref[R_GAIN1 : R_GAIN1 + 1], rows_ref[R_VB : R_VB + 1]
    shuffle = shuffle_ref[...]
    vec_ref[...] = jnp.zeros_like(vec_ref)
    d_two = jnp.sum(part_ref[...].astype(F32), axis=0)
    xhat2, rstd2 = norm_parts(resid_ref[...])
    d_resid = dstate_ref[...] + norm_back(d_two, rows_ref[R_GAIN2 : R_GAIN2 + 1], xhat2, rstd2)
    vec_ref[3:4] = rowsum(d_resid)
    vec_ref[4:5] = rowsum(d_two * xhat2)
    vec_ref[5:6] = rowsum(d_two)
    d_low = low(d_resid)
    dres_ref[...] = jnp.broadcast_to(d_low[None], dres_ref.shape)
    d_att = to_natural(
        low(dot(d_low, wo_ref[0], NT)), low(dot(d_low, wo_ref[1], NT)), shuffle
    )
    do_ref[...] = d_att
    spread = jnp.broadcast_to(d_att.reshape(images, 1, WIDTH).astype(F32), (images, HEADS, WIDTH))
    wide = jnp.where(head_mask(rows), spread.reshape(rows, WIDTH), 0.0)
    dom_ref[...] = low(wide)
    vec_ref[2:3] = rowsum(wide * mass_ref[:, 0:1])
    da_ref[...] = to_natural(
        low(dot(dom_ref[...], wv_ref[0], NT)), low(dot(dom_ref[...], wv_ref[1], NT)), shuffle
    )
    qk = qk_ref[...]
    bias_rows = low(jnp.broadcast_to(value_bias, (8, WIDTH)))
    real = lax.broadcasted_iota(jnp.int32, (SLOT, WIDTH), 0) < PATCHES
    for i in range(images):
        part = slice(SLOT * i, SLOT * (i + 1))
        mine = slice(HEADS * i, HEADS * (i + 1))
        hid, p, da = hid_ref[part], p_ref[part], da_ref[mine]
        dp = dot(hid, da, NT) + dot(bias_rows, dom_ref[mine], NT)[0:1]
        ds = low(p * (dp - rowsum(p * dp)))
        dh = dot(low(p), da) + dot(ds, qk)
        pull = dot(ds, hid, TN)
        xhat, rstd = xhat_ref[part], rstd_ref[part, 0:1]
        dx = norm_back(dh, gain, xhat, rstd)
        de_ref[part] = low(jnp.where(real, dx, 0.0))
        vec_ref[0:1] += rowsum(dh * xhat)
        vec_ref[1:2] += rowsum(dh)
        if i == 0:
            pos_ref[...] = dx
            pull_ref[...] = pull
        else:
            pos_ref[...] += dx
            pull_ref[...] += pull


def backward_call(images, where, arrays):
    tokens = images * SLOT
    outs = [
        shape((tokens, WIDTH), BF),
        shape((images, WIDTH), BF),
        shape((8, images, WIDTH), BF),
        shape((SLOT, WIDTH), F32),
        shape((8, WIDTH), F32),
        shape((HEADS, WIDTH), F32),
    ]
    scratch = [pltpu.VMEM((images * HEADS, WIDTH), BF)] * 2
    return call(
        functools.partial(backward_kernel, images), "backward", [where], arrays, outs, scratch
    )


def rows_kernel(where_ref, act_ref, dpre_ref, hid_ref, dst_ref, dres_ref, out_ref):
    half = WIDTH // 2
    base = 3 * WIDTH
    out_ref[:, :half] = act_ref[...]
    out_ref[:, half:WIDTH] = dpre_ref[...]
    count = out_ref.shape[0]
    out_ref[:, WIDTH : 2 * WIDTH] = hid_ref[:, :, :WIDTH].reshape(count, WIDTH)
    out_ref[:, 2 * WIDTH : base] = dst_ref[:, :, :WIDTH].reshape(count, WIDTH)

    @pl.when(where_ref[0] == 2)
    def _():
        out_ref[:, base : base + WIDTH] = hid_ref[:, :, WIDTH:].reshape(count, WIDTH)
        out_ref[:, base + WIDTH :] = dres_ref[...].reshape(count, WIDTH)

    @pl.when(where_ref[0] != 2)
    def _():
        out_ref[:, base : base + WIDTH + PROJ] = dst_ref[:, :, WIDTH:].reshape(count, WIDTH + PROJ)
        out_ref[:, base + WIDTH + PROJ :] = jnp.zeros((count, WIDTH - PROJ), BF)


def embed_grad_kernel(
    images, plan, where_ref, pix_ref, pixp_ref, de_ref, dep_ref, pooled_ref, pooledp_ref,
    do_ref, dop_ref, *out_refs,
):
    col = where_ref[0]
    heads = images * HEADS
    for (source, first, rows, _), out_ref in zip(plan, out_refs):
        block = col ^ source

        @pl.when(block < 3)
        def _():
            lanes = pl.ds(pl.multiple_of(block * 512 + first, 128), rows)
            total = dot(pix_ref[:, lanes], de_ref[...], TN) + dot(pixp_ref[:, lanes], dep_ref[...], TN)
            out_ref[...] = total.astype(out_ref.dtype)

        @pl.when(block == 3)
        def _():
            total = None
            for pooled, do in ((pooled_ref, do_ref), (pooledp_ref, dop_ref)):
                spread = jnp.broadcast_to(
                    do[...].reshape(images, 1, WIDTH).astype(F32), (images, HEADS, WIDTH)
                )
                wide = low(jnp.where(head_mask(heads), spread.reshape(heads, WIDTH), 0.0))
                term = dot(pooled[:, first : first + rows], wide, TN)
                total = term if total is None else total + term
            out_ref[...] = total.astype(out_ref.dtype)


def embed_grad_call(images, name, plan, where, arrays):
    outs = [shape((rows, WIDTH), dtype) for _, _, rows, dtype in plan]
    return call(
        functools.partial(embed_grad_kernel, images, plan), name, [where], arrays, outs
    )


def add_far_kernel(x_low_ref, x_high_ref, got_x_ref, y_low_ref, got_y_ref, y_high_ref, x_ref, y_ref):
    x_ref[0] = x_low_ref[...]
    x_ref[1] = low(x_high_ref[...] + got_x_ref[...].astype(F32))
    y_ref[0] = low(y_low_ref[...] + got_y_ref[...].astype(F32))
    y_ref[1] = y_high_ref[...]


def add_far(pieces):
    rows = pieces[0].shape[0]
    step = rows // 4
    out = shape((2, rows, WIDTH), BF)
    return pl.pallas_call(
        add_far_kernel,
        grid=(4,),
        in_specs=[pl.BlockSpec((step, WIDTH), lambda i: (i, 0))] * 6,
        out_specs=[pl.BlockSpec((2, step, WIDTH), lambda i: (0, i, 0))] * 2,
        out_shape=[out, out],
        compiler_params=pltpu.CompilerParams(vmem_limit_bytes=58 * 2**20),
        cost_estimate=pl.CostEstimate(flops=10**6, bytes_accessed=6 * 2**20, transcendentals=0),
        name="add_far",
    )(*pieces)


def to_natural_exact(first, second, shuffle):
    wide = shuffle.astype(F32)
    out = []
    for block in range(first.shape[1] // 128):
        lanes = slice(128 * block, 128 * block + 128)
        both = jnp.concatenate([first[:, lanes], second[:, lanes]], axis=1)
        out.append(dot(both, wide, NT, precision=lax.Precision.HIGHEST))
    return jnp.concatenate(out, axis=1)


def collect_kernel(
    where_ref, pos_ref, vec_ref, head_ref, sum_ref, pull_ref, shuffle_ref, sent_ref, out_ref
):
    col, core = where_ref[0], where_ref[1]
    out_ref[...] = jnp.zeros_like(out_ref)
    top = pos_ref[PATCHES:TOKS] + vec_ref[3:4]
    out_ref[0:1] = top
    out_ref[1:2] = top
    patches = pos_ref[0:PATCHES]
    out_ref[2 : 1 + TOKS] = patches
    out_ref[R_PATCH : R_PATCH + 1] = rowsum(patches)
    out_ref[R_GAIN1 : R_SHIFT1 + 1] = vec_ref[0:2]
    out_ref[R_VB : R_VB + 1] = vec_ref[2:3]
    out_ref[R_OB : R_SHIFT2 + 1] = vec_ref[3:6]
    sums = jnp.broadcast_to(sum_ref[...], (8, WIDTH // 2))
    nothing = jnp.zeros_like(sums)
    row = to_natural_exact(
        jnp.where(core == 0, sums, nothing), jnp.where(core == 0, nothing, sums), shuffle_ref[...]
    )
    for block in range(4):
        mine = (col + 1) % 4 == block
        out_ref[R_SHIFT2 + 1 + block : R_SHIFT2 + 2 + block] = jnp.where(mine, row[0:1], 0.0)
    out_ref[R_C2 : R_SHIFTF + 1] = head_ref[0:3]
    out_ref[R_SMALL : R_SMALL + HEADS] = pull_ref[...]
    out_ref[R_SMALL + HEADS : R_SMALL + HEADS + 1] = head_ref[3:4]
    for number in range(sent_ref.shape[0]):
        sent_ref[number] = out_ref[3 * number : 3 * number + 3]


def share_kernel(got_ref, sent_ref):
    sent_ref[...] = jnp.broadcast_to(jnp.sum(got_ref[...], axis=0, keepdims=True), sent_ref.shape)


def query_back_kernel(core_ref, got_ref, w_ref, shuffle_ref, dq_ref, pull_ref, total_ref):
    for number in range(got_ref.shape[0]):
        total_ref[3 * number : 3 * number + 3] = got_ref[number]
    wide = shuffle_ref[...].astype(F32)
    pull = total_ref[R_SMALL : R_SMALL + HEADS]
    is_one = core_ref[0] == 1
    out = []
    for block in range(WIDTH // 256):
        moved = dot(pull[:, 256 * block : 256 * block + 256], wide, precision=lax.Precision.HIGHEST)
        out.append(jnp.where(is_one, moved[:, 128:], moved[:, :128]))
    half = jnp.concatenate(out, axis=1)
    pull_ref[...] = half
    d_query = jnp.where(head_mask(HEADS), dot(low(half), w_ref[...]), 0.0)
    dq_ref[...] = jnp.broadcast_to(rowsum(d_query) * SCALE, dq_ref.shape)


def complete_kernel(total_ref, reports_ref, rows_ref, shuffle_ref, out_ref, norm_ref):
    out_ref[...] = total_ref[0:R_SMALL]
    half = WIDTH // 2
    first = jnp.broadcast_to(reports_ref[6, :, WIDTH : WIDTH + half], (8, half))
    second = jnp.broadcast_to(reports_ref[7, :, WIDTH : WIDTH + half], (8, half))
    d_hidden = to_natural_exact(first, second, shuffle_ref[...])[0:1]
    xhat, rstd = norm_parts(rows_ref[0:1] + rows_ref[1:2])
    d_class = norm_back(d_hidden, rows_ref[R_GAIN1 : R_GAIN1 + 1], xhat, rstd)
    out_ref[0:1] += d_class
    out_ref[1:2] += d_class
    out_ref[R_GAIN1 : R_GAIN1 + 1] += d_hidden * xhat
    out_ref[R_SHIFT1 : R_SHIFT1 + 1] += d_hidden
    out_ref[R_SHIFT1 + 1 : R_SHIFT1 + 2] = reports_ref[6, :, :WIDTH]
    grads = out_ref[...]
    square = jnp.sum(jnp.sum(grads * grads, axis=0, keepdims=True), axis=1, keepdims=True)
    for number in range(reports_ref.shape[0]):
        square = square + reports_ref[number, :, WIDTH + half : WIDTH + half + 1]
    norm_ref[...] = jnp.broadcast_to(jnp.sqrt(square), (8, 128))


def owner_kernel(role_ref, pull_ref, heads_ref, class_ref, dq_ref, *refs):
    rows, out_ref = refs[:6], refs[6]
    chip, core = role_ref[0], role_ref[1]
    half = WIDTH // 2
    base = 3 * WIDTH

    def product(left, right):
        total = None
        for piece in rows:
            term = dot(left(piece), right(piece), TN)
            total = term if total is None else total + term
        return total

    @pl.when((chip >= 7) & (chip <= 14))
    def _():
        is_two = chip >= 11
        out_ref[...] = product(
            lambda piece: jnp.where(is_two, piece[:, :half], piece[:, half:WIDTH]),
            lambda piece: jnp.where(is_two, piece[:, 2 * WIDTH : base], piece[:, WIDTH : 2 * WIDTH]),
        )

    @pl.when(chip == 6)
    def _():
        lanes = pl.ds(pl.multiple_of(base + core * half, 128), half)
        out_ref[...] = product(lambda piece: piece[:, lanes], lambda piece: piece[:, base + WIDTH :])

    @pl.when(chip == 15)
    def _():
        lanes = pl.ds(pl.multiple_of(base + core * (PROJ // 2), 128), PROJ // 2)
        out_ref[: PROJ // 2] = product(
            lambda piece: piece[:, lanes],
            lambda piece: piece[:, base + PROJ : base + PROJ + WIDTH],
        )
        out_ref[PROJ // 2 :] = jnp.zeros((512 - PROJ // 2, WIDTH), F32)

    @pl.when(chip == 4)
    def _():
        out_ref[...] = dot(
            pull_ref[...], heads_ref[...].astype(F32), TN, precision=lax.Precision.HIGHEST
        )

    @pl.when(chip == 3)
    def _():
        out_ref[...] = dot(
            class_ref[...].astype(F32), jnp.concatenate([dq_ref[0:1], jnp.zeros((7, WIDTH), F32)]),
            TN, precision=lax.Precision.HIGHEST,
        )


def finish_kernel(
    role_ref, formed_ref, dq_ref, toward_ref, total_ref, first_ref, second_ref, aside_ref, third_ref,
    out_ref, top_ref, end_ref, report_ref,
):
    chip = role_ref[0]

    @pl.when(chip < 3)
    def _():
        out_ref[...] = total_ref[...] + first_ref[...].astype(F32) + second_ref[...].astype(F32)

    @pl.when(chip == 5)
    def _():
        out_ref[...] = (
            second_ref[...].astype(F32) + aside_ref[...].astype(F32) + third_ref[...].astype(F32)
        )

    @pl.when((chip >= 3) & (chip != 5))
    def _():
        out_ref[...] = formed_ref[...]

    edge = top_ref.shape[0]
    top_ref[...] = out_ref[:edge]
    end_ref[...] = out_ref[-edge:]
    grads = out_ref[...]
    square = jnp.sum(jnp.sum(grads * grads, axis=0, keepdims=True), axis=1, keepdims=True)
    report_ref[...] = jnp.concatenate(
        [dq_ref[...], toward_ref[...], jnp.broadcast_to(square, (1, 128))], axis=1
    )


def update_kernel(
    source_ref, scalar_ref, before_ref, grad_ref, behind_ref, w_ref, m_ref, v_ref,
    nw_ref, nm_ref, nv_ref,
):
    step = pl.program_id(0)
    slots = grad_ref.shape[0]
    factor, fix_one, fix_two = scalar_ref[0], scalar_ref[1], scalar_ref[2]
    for k in range(w_ref.shape[0]):
        at = source_ref[step * w_ref.shape[0] + k]
        inside = (at >= 0) & (at < slots)
        grad = jnp.where(
            inside,
            grad_ref[jnp.clip(at, 0, slots - 1)],
            jnp.where(
                at < 0,
                before_ref[jnp.clip(at + JITTER, 0, JITTER - 1)],
                behind_ref[jnp.clip(at - slots, 0, JITTER - 1)],
            ),
        )
        grad = grad * jnp.where(at >= -JITTER, factor, 0.0)
        weight = w_ref[k]
        first = BETA_ONE * m_ref[k] + (1.0 - BETA_ONE) * grad
        second = BETA_TWO * v_ref[k] + (1.0 - BETA_TWO) * grad * grad
        nm_ref[k] = first
        nv_ref[k] = second
        nw_ref[k] = weight - LEARN_RATE * (
            (first * fix_one) / (jnp.sqrt(second * fix_two) + ADAM_EPS) + DECAY_RATE * weight
        )


def update_call(source, scalars, before, grads, behind, masters, first, second):
    slots, part, width = masters.shape
    block = 16
    spec = pl.BlockSpec((block, part, width), lambda i: (i, 0, 0))
    return pl.pallas_call(
        update_kernel,
        grid=(slots // block,),
        in_specs=[smem(), smem(), vmem(), vmem(), vmem(), spec, spec, spec],
        out_specs=[spec] * 3,
        out_shape=[shape(masters.shape, F32)] * 3,
        compiler_params=pltpu.CompilerParams(vmem_limit_bytes=58 * 2**20),
        cost_estimate=pl.CostEstimate(
            flops=2 * 10**7, bytes_accessed=7 * masters.size * 4, transcendentals=0
        ),
        name="update",
    )(source, scalars, before, grads, behind, masters, first, second)


CHIPS = 16
CHIP = ("z", "y", "x")
ALL = ("z", "y", "x", "c")
PLANE = ("y", "x", "c")
FLIP_X = [(i, i ^ 1) for i in range(CHIPS)]
FLIP_Y = [(i, i ^ 2) for i in range(CHIPS)]
FLIP_CORE = [(0, 1), (1, 0)]


def hop(values, pairs):
    return lax.ppermute(values, CHIP, pairs)


def swap(values):
    return lax.ppermute(values, "c", FLIP_CORE)


def after(values, *others):
    return lax.optimization_barrier((values,) + others)[0]


def among(img, chips):
    hit = img == chips[0]
    for chip in chips[1:]:
        hit = hit | (img == chip)
    return hit


def choose(img, cases, otherwise):
    out = otherwise
    for chips, values in cases:
        out = jnp.where(among(img, chips), values, out)
    return out


def together(*values):
    return lax.optimization_barrier(values)


def plane_gather(block, diagonal_by_x):
    by_x, by_y, block_peer = hop(block, FLIP_X), hop(block, FLIP_Y), swap(block)
    proj_top = jnp.where(img == 15, corner[0], corner[1] + corner[2] + corner[3])
    diagonal = hop(by_y, FLIP_X) if diagonal_by_x else hop(by_x, FLIP_Y)
    return [block, by_x, by_y, diagonal]


def in_plane(values):
    return lax.all_to_all(values, PLANE, 0, 0, tiled=True)


def from_all(values):
    sent = jnp.broadcast_to(values[None], (2 * CHIPS,) + values.shape)
    return lax.all_to_all(sent, ALL, 0, 0, tiled=True)


def natural(values):
    lead = values.shape[:-2]
    units = values.shape[-1] // 16
    split = values.reshape(lead + (2, units, 16))
    return jnp.swapaxes(split, -3, -2).reshape(lead + (units * 32,))


def halves(values):
    lead = values.shape[:-1]
    units = values.shape[-1] // 32
    return jnp.swapaxes(values.reshape(lead + (units, 2, 16)), -3, -2).reshape(
        lead + (2, units * 16)
    )


def per_device_16(
    pixels, keep_mask, partner_index, partner_emb, masters, first_moment_slots,
    second_moment_slots, slot_unit_index, small_params, small_first, small_second, step_count,
):
    img, core = lax.axis_index(CHIP), lax.axis_index("c")
    col, plane = img % 4, img // 4
    images = pixels.shape[0]
    slots = masters.shape[0]
    is_one = core == 1
    where = jnp.stack([col, core]).astype(jnp.int32)
    shuffle = shuffle_matrix()
    rows = small_params
    class_state = small_params[0] + small_params[1]

    def mine_of(pair):
        return jnp.where(is_one, pair[1], pair[0])

    def theirs_of(pair):
        return jnp.where(is_one, pair[0], pair[1])

    near = slots_near(slot_unit_index, img, slots)
    held = low(masters)
    ids = img * slots + jnp.arange(slots, dtype=jnp.int32)
    matches = [near[s : s + slots] == ids for s in range(2 * JITTER + 1)]
    middle = pick(held[6:26], [m[8:24] for m in matches], 16).reshape(256, WIDTH)
    one_a = hop(middle, [(0, 4), (1, 5), (2, 6), (5, 7)])
    partners = from_all(after(partner_emb, middle))
    before, behind = halo(after(held, middle), CHIPS, CHIP)
    lower = pick(jnp.concatenate([before, held[:10]]), [m[:8] for m in matches], 8)
    upper = pick(jnp.concatenate([held[22:], behind]), [m[24:] for m in matches], 8)
    outer = jnp.concatenate([lower, upper]).reshape(256, WIDTH)
    own_w = jnp.concatenate([outer[:128], middle, outer[128:]])
    class_hidden = low(layer_norm(class_state, small_params[R_GAIN1], small_params[R_SHIFT1]))
    class_half = mine_of(halves(class_hidden))
    query = dot(class_half[None], own_w)
    query = query + swap(query)
    wo_quarter = hop(own_w[384:], [(6, 7)]) + hop(own_w[:128], [(6, 4)])
    wo_quarter = wo_quarter + hop(own_w[128:256], [(6, 5)])
    wo_quarter = jnp.where(img == 6, own_w[256:384], wo_quarter)
    down_one = hop(
        own_w,
        [(12, 8), (13, 9), (14, 10), (11, 7), (8, 4), (9, 5), (10, 6), (7, 3)],
    )
    one_a, outer, query = together(one_a, outer, query)
    query = hop(query, [(3, 4)])
    one_b = hop(outer, [(0, 4), (1, 5), (2, 6), (5, 7)])
    two_a = hop(one_a, [(4, 8), (5, 9), (6, 10), (7, 11)])
    pix = prep(after(pixels, one_a), shuffle).reshape(2, images * SLOT, PIX // 2)
    corner = after(own_w[: PROJ // 2], one_a)
    corner = [corner] + [hop(corner, [(15, 15 ^ flip)]) for flip in (1, 2, 3)]
    query = low((query + small_params[R_SHIFT1 + 1 : R_SHIFT1 + 2]) * SCALE)
    query_heads = jnp.where(head_mask(HEADS), query, jnp.zeros((), BF))
    pulled = jnp.pad(low(dot(query_heads, own_w, NT)), ((0, 0), (0, WIDTH // 2)))
    one_b, two_a, wo_quarter, pulled, down_one = together(
        one_b, two_a, wo_quarter, pulled, down_one
    )
    mid_b = jnp.concatenate([one_b, wo_quarter, pulled])
    two_b = hop(mid_b, [(4, 8), (5, 9), (6, 10), (7, 11)])
    three_a = hop(
        jnp.where(img == 7, one_a, two_a), [(8, 12), (9, 13), (10, 14), (11, 15), (7, 3)]
    )
    low_b = hop(mid_b[256:], [(4, 0), (5, 1), (6, 2)])
    two_b, three_a, low_b, pix, partners, *corner = together(
        two_b, three_a, low_b, pix, partners, *corner
    )
    block_a = jnp.where(img < 3, middle, one_a + two_a + three_a)
    x_a, y_a = hop(block_a, FLIP_X), hop(block_a, FLIP_Y)
    three_b = hop(
        jnp.where(img == 7, mid_b, two_b), [(8, 12), (9, 13), (10, 14), (11, 15), (7, 3)]
    )
    pix_own, pix_send = mine_of(pix), theirs_of(pix)
    x_a, y_a, three_b, pix_own, pix_send = together(x_a, y_a, three_b, pix_own, pix_send)
    spot = jnp.stack([img, plane]).astype(jnp.int32)
    block_b = second_block(spot, [outer, low_b, mid_b, two_b, three_b])
    x_b, y_b = hop(block_b, FLIP_X), hop(block_b, FLIP_Y)
    down_two = hop(
        after(down_one, three_b), [(8, 4), (9, 5), (10, 6), (7, 3), (4, 0), (5, 1), (6, 2)]
    )
    proj_top = jnp.where(img == 15, corner[0], corner[1] + corner[2] + corner[3])
    (partners,) = call(
        partner_kernel, "partners", [], [partners], [shape((2 * CHIPS * images, PROJ), BF)]
    )
    up_one = hop(
        after(own_w, three_b), [(8, 12), (9, 13), (10, 14), (7, 11), (11, 15)]
    )
    peers_a = [swap(block_a), swap(x_a), swap(y_a), swap(block_b)]
    x_b, y_b, up_one, down_two, *peers_a = together(x_b, y_b, up_one, down_two, *peers_a)
    up_two = hop(up_one, [(11, 15)])
    proj_one = hop(after(proj_top, x_b), [(12, 4), (13, 5), (14, 6), (15, 7)])
    d_a, d_b = hop(y_a, FLIP_X), hop(x_b, FLIP_Y)
    down_three = hop(after(down_two, y_b), [(4, 0), (5, 1), (6, 2)])
    x_peer, y_peer = swap(x_b), swap(y_b)
    d_a, d_b, x_peer, y_peer = together(d_a, d_b, x_peer, y_peer)
    segments = [(source, ((0, 128, 256),), -1) for source in range(4)]
    segments += [(source, ((0, 0, 128), (128, 384, 128)), 256) for source in range(4)]
    own_pieces = [block_a, x_a, y_a, d_a, block_b, x_b, y_b, d_b]
    peer_pieces = [*peers_a[:3], swap(d_a), peers_a[3], x_peer, y_peer, swap(d_b)]
    pix_peer = swap(pix_send)
    valid = jnp.concatenate(
        [
            keep_mask,
            jnp.ones((images, 1), jnp.int32),
            jnp.zeros((images, SLOT - TOKS), jnp.int32),
        ],
        axis=1,
    ).reshape(images * SLOT, 1)
    (
        hid, xhat, rstd, p, pooled, mass, wv, wo, qk, resid, hidden_sent,
    ) = forward_call(
        segments, images, where, pix, own_pieces, peer_pieces, rows, valid, shuffle
    )
    pooled_own = mine_of(pooled)
    pooled_peer = swap(theirs_of(pooled))

    hidden_all = in_plane(hidden_sent)
    hidden_all, pooled_peer = together(hidden_all, pooled_peer)
    ff_block = (col + 1) % 4
    bias_part = lax.dynamic_slice(
        small_params[R_SHIFT2 + 1 : R_C2].reshape(4, 32, 2, 16),
        (ff_block, 0, core, 0),
        (1, 32, 1, 16),
    ).reshape(1, 512)
    candidates = [own_w, up_one, up_two, down_one, down_two, down_three]
    pick_one = choose(
        img, [((15,), 2), ((12, 13, 14, 11), 1), ((4, 5, 6, 3), 3), ((0, 1, 2), 4)], 0
    )
    pick_two = choose(
        img, [((15,), 1), ((8, 9, 10, 7), 3), ((4, 5, 6, 3), 4), ((0, 1, 2), 5)], 0
    )
    picks = jnp.stack([pick_one, pick_two]).astype(jnp.int32)
    preact, active, part = ff_call(
        ff_kernel, "ff", picks, [hidden_all, bias_part], candidates,
        [shape((8 * images, 512), F32), shape((8 * images, 512), BF), shape((8, images, WIDTH), BF)],
    )
    proj_mid = hop(
        after(jnp.where(plane == 3, proj_top, proj_one), hidden_sent),
        [(12, 8), (13, 9), (14, 10), (15, 11), (4, 0), (5, 1), (6, 2), (7, 3)],
    )
    hidden_all = in_plane(hidden_sent)
    ff_block = (col + 1) % 4
    bias_part = lax.dynamic_slice(
        small_params[R_SHIFT2 + 1 : R_C2].reshape(4, 32, 2, 16),
        (ff_block, 0, core, 0),
        (1, 32, 1, 16),
    ).reshape(1, 512)
    candidates = [own_w, up_one, up_two, down_one, down_two, down_three]
    pick_one = choose(
        img, [((15,), 2), ((12, 13, 14, 11), 1), ((4, 5, 6, 3), 3), ((0, 1, 2), 4)], 0
    )
    pick_two = choose(
        img, [((15,), 1), ((8, 9, 10, 7), 3), ((4, 5, 6, 3), 4), ((0, 1, 2), 5)], 0
    )
    picks = jnp.stack([pick_one, pick_two]).astype(jnp.int32)
    preact, active, part = ff_call(
        ff_kernel, "ff", picks, [hidden_all, bias_part], candidates,
        [shape((8 * images, 512), F32), shape((8 * images, 512), BF), shape((8, images, WIDTH), BF)],
    )
    proj = choose(
        plane, [((3,), proj_top), ((1,), proj_one)], after(proj_mid, hidden_sent)
    )
    proj_peer = swap(proj)
    part = in_plane(part)
    proj = choose(plane, [((3,), proj_top), ((1,), proj_one)], after(proj_mid, part))
    proj_peer = swap(proj)
    d_state, d_state_sent, head_vec = call(
        head_kernel, "head", [where],
        [part, resid, proj, proj_peer, partners, partner_index[:, None], rows],
        [
            shape((images, WIDTH), F32), shape((8, images, 2 * WIDTH + PROJ), BF),
            shape((8, WIDTH), F32),
        ],
        [pltpu.VMEM((images, PROJ), BF)],
    )
    d_state_all = in_plane(d_state_sent)
    d_preact, d_preact_sum, part = ff_call(
        ff_back_kernel, "ff_back", picks, [d_state_all, preact], candidates,
        [shape((8 * images, 512), BF), shape((1, 512), F32), shape((8, images, WIDTH), BF)],
    )
    part = in_plane(part)

    d_embed, d_attended, d_resid, d_pos, d_vec, pull = backward_call(
        images, where,
        [part, d_state, resid, wo, wv, hid, xhat, rstd, p, mass, qk, rows, shuffle],
    )
    arrays = [
        pix_own, pix_peer, d_embed, swap(d_embed), pooled_own, pooled_peer, d_attended,
        swap(d_attended),
    ]
    far_x, far_y = embed_grad_call(
        images, "embed_grad_far", [(3, 0, 256, BF), (3, 256, 256, BF)], where, arrays
    )
    got_y, got_x = hop(far_x, FLIP_X), hop(far_y, FLIP_Y)
    own_part, x_low, x_high, y_low, y_high = embed_grad_call(
        images, "embed_grad_near",
        [(0, 0, 512, F32), (1, 0, 256, BF), (1, 256, 256, F32), (2, 0, 256, F32), (2, 256, 256, BF)],
        after(where, far_x), arrays,
    )
    d_resid = in_plane(after(d_resid, far_x))
    d_pos, d_vec, head_vec, d_preact_sum, pull, _ = together(
        d_pos, d_vec, head_vec, d_preact_sum, pull, far_x
    )
    (small_sent,) = call(
        collect_kernel, "collect", [where], [d_pos, d_vec, head_vec, d_preact_sum, pull, shuffle],
        [shape((32, 3, WIDTH), F32)], [pltpu.VMEM((96, WIDTH), F32)],
    )
    got_x, got_y, own_part, x_low, x_high, y_low, y_high, d_resid, small_sent = together(
        got_x, got_y, own_part, x_low, x_high, y_low, y_high, d_resid, small_sent
    )
    part_x, part_y = add_far([x_low, x_high, got_x, y_low, got_y, y_high])
    part_x, part_y = part_x.reshape(512, WIDTH), part_y.reshape(512, WIDTH)
    sum_x, sum_y = hop(part_x, FLIP_X), hop(part_y, FLIP_Y)
    shares = lax.all_to_all(small_sent, ALL, 0, 0, tiled=True)
    (ff_rows,) = call(
        rows_kernel, "rows", [where], [active, d_preact, hidden_all, d_state_all, d_resid],
        [shape((8 * images, 5 * WIDTH), BF)],
    )
    rise = [(i, i + 4) for i in range(12)]
    fall = [(12, 8), (13, 9), (14, 10), (15, 11), (10, 6), (11, 7)]
    up_one, down_one = hop(ff_rows, rise), hop(ff_rows, fall)
    sum_x, sum_y, shares = together(sum_x, sum_y, shares)
    total = own_part + sum_x.astype(F32) + sum_y.astype(F32)
    sent = low(total)
    first = hop(sent, [(12, 8), (13, 9), (14, 10), (15, 11), (4, 0), (5, 1), (6, 2)])
    aside = hop(sent, [(3, 1), (7, 5)])
    (small_sent,) = call(share_kernel, "share", [], [shares], [shape((32, 3, WIDTH), F32)])
    shares = lax.all_to_all(small_sent, ALL, 0, 0, tiled=True)
    up_two, down_two = hop(up_one, rise[4:]), hop(down_one, fall[4:])
    first, aside, up_two, down_two, total = together(first, aside, up_two, down_two, total)
    partial = low(total + first.astype(F32))
    second = hop(partial, [(8, 0), (9, 1), (10, 2), (11, 5)])
    third = hop(aside, [(1, 5)])
    up_three = hop(up_two, rise[8:])
    d_query, pull_half, small_total = call(
        query_back_kernel, "query_back", [core.reshape(1).astype(jnp.int32)],
        [shares, own_w, shuffle],
        [shape((8, WIDTH), F32), shape((HEADS, WIDTH // 2), F32), shape((96, WIDTH), F32)],
    )
    loss = small_total[R_SMALL + HEADS, 0]
    d_query = d_query[0:1]
    d_query = d_query + swap(d_query)
    d_query = hop(d_query, [(4, 3)])
    toward = dot(low(d_query), own_w, NT)

    every = [ff_rows, up_one, up_two, up_three, down_one, down_two]
    class_rows = jnp.concatenate([class_half[None], jnp.zeros((7, WIDTH // 2), BF)])
    role = jnp.stack([img, core]).astype(jnp.int32)
    (formed,) = call(
        owner_kernel, "owner", [role], [pull_half, query_heads, class_rows, d_query, *every],
        [shape((512, WIDTH), F32)],
    )
    edge = shape((JITTER * 16, WIDTH), F32)
    own_grad, top, end, report = call(
        finish_kernel, "finish", [role],
        [formed, d_query, toward, total, first, second, aside, third],
        [shape((512, WIDTH), F32), edge, edge, shape((1, WIDTH + 640), F32)],
    )
    reports = from_all(report)
    before = hop(end, [(i, i + 1) for i in range(CHIPS - 1)]).reshape(JITTER, 16, WIDTH)
    behind = hop(top, [(i + 1, i) for i in range(CHIPS - 1)]).reshape(JITTER, 16, WIDTH)
    small_grad, norm = call(
        complete_kernel, "complete", [], [small_total, reports, rows, shuffle],
        [shape((R_SMALL, WIDTH), F32), shape((8, 128), F32)],
    )
    grad_norm = norm[0, 0]
    factor = 1.0 / jnp.maximum(grad_norm, 1.0)
    own_grad = own_grad.reshape(slots, 16, WIDTH)
    here = near[JITTER : JITTER + slots]
    source = jnp.where(here < UNIT_COUNT, here - img * slots, -100)
    step_value = step_count.astype(F32)
    scalars = jnp.stack(
        [
            factor,
            1.0 / (1.0 - jnp.power(BETA_ONE, step_value)),
            1.0 / (1.0 - jnp.power(BETA_TWO, step_value)),
        ]
    )
    new_masters, new_first, new_second = update_call(
        source, scalars, before, own_grad, behind, masters, first_moment_slots,
        second_moment_slots,
    )
    new_small, new_small_first, new_small_second = adamw(
        small_params, small_grad * factor, small_first, small_second, step_value
    )
    return (
        new_masters, new_first, new_second, new_small, new_small_first, new_small_second,
        loss, grad_norm,
    )


def per_device_any(
    pixels, keep_mask, partner_index, partner_emb, masters, first_moment_slots,
    second_moment_slots, slot_unit_index, small_params, small_first, small_second, step_count,
):
    chips, seq = lax.axis_size("img"), lax.axis_size("seq")
    img = lax.axis_index("img")
    images = pixels.shape[0]
    slots, part = masters.shape[0], masters.shape[1]
    near = slots_near(slot_unit_index, img, slots)
    own_w = to_units(low(masters), near, img, chips)
    gathered = lax.all_gather(own_w, ("img", "seq"), axis=0, tiled=False)
    flat = gathered.reshape(chips, seq, slots, part, WIDTH).transpose(0, 2, 1, 3, 4)
    flat = flat.reshape(chips * slots * ROWS_PER_UNIT, WIDTH)
    bounds = [0, PIX, WIDTH, WIDTH, WIDTH, WIDTH, FF, FF, PROJ]
    parts, offset = [], 0
    for size in bounds[1:]:
        parts.append(flat[offset : offset + size])
        offset += size
    embed_w, query_w, key_w, value_w, output_w, fc_in_w, fc_out_w, proj_w = parts
    (
        class_row, pos_rows, patch_bias, gain_one, shift_one, query_bias, value_bias, out_bias,
        gain_two, shift_two, fc_in_bias, fc_out_bias, gain_end, shift_end,
    ) = small_parts(small_params)
    class_state = class_row + pos_rows[0]
    embedded = jnp.einsum("itp,pd->itd", pixels, embed_w, preferred_element_type=F32)
    tokens = jnp.concatenate(
        [
            jnp.broadcast_to(class_state, (images, 1, WIDTH)),
            embedded + patch_bias + pos_rows[1:],
        ],
        axis=1,
    )
    hidden = low(layer_norm(tokens, gain_one, shift_one))
    class_hidden = hidden[0, 0]
    mask16 = head_mask(HEADS)
    query = low((dot(class_hidden[None], query_w)[0] + query_bias) * SCALE)
    query_heads = jnp.where(mask16, query[None], jnp.zeros((), BF))
    qk = low(dot(query_heads, key_w, NT))
    scores = jnp.einsum("hd,itd->iht", qk, hidden, preferred_element_type=F32)
    keep = jnp.concatenate([jnp.ones((images, 1), jnp.int32), keep_mask], axis=1)
    scores = jnp.where(keep[:, None, :] > 0, scores, MASKED)
    weights = jax.nn.softmax(scores, axis=-1)
    weights_low = low(weights)
    pooled = low(jnp.einsum("iht,itd->ihd", weights_low, hidden, preferred_element_type=F32))
    mass = jnp.sum(weights_low.astype(F32), axis=-1)
    mixed = dot(pooled.reshape(-1, WIDTH), value_w).reshape(images, HEADS, WIDTH)
    mixed = mixed + mass[:, :, None] * value_bias
    attended = low(jnp.sum(jnp.where(mask16, mixed, 0.0), axis=1))
    resid = class_state + dot(attended, output_w) + out_bias
    hidden_two = low(layer_norm(resid, gain_two, shift_two))
    preact = dot(hidden_two, fc_in_w, NT) + fc_in_bias
    active = low(exact_gelu(preact))
    state = resid + dot(active, fc_out_w) + fc_out_bias
    final = low(layer_norm(state, gain_end, shift_end))
    projected = dot(final, proj_w, NT)
    unit = low(normalize(projected))
    partners = lax.all_gather(partner_emb, ("img", "seq"), axis=0, tiled=True)
    count = partners.shape[0]
    logits = dot(unit, partners, NT) / SOFTMAX_SCALE
    onehot = (jnp.arange(count, dtype=jnp.int32)[None] == partner_index[:, None]).astype(F32)
    total = jax.nn.logsumexp(logits, axis=-1)
    loss_part = jnp.sum(total - jnp.sum(logits * onehot, axis=-1)) / count
    d_logits = (jax.nn.softmax(logits, axis=-1) - onehot) / count
    d_unit = dot(low(d_logits / SOFTMAX_SCALE), partners)
    d_projected = low(jax.vjp(normalize, projected)[1](d_unit)[0])
    d_final = dot(d_projected, proj_w)
    d_state, d_gain_end, d_shift_end = jax.vjp(layer_norm, state, gain_end, shift_end)[1](d_final)
    d_state_low = low(d_state)
    d_active = dot(d_state_low, fc_out_w, NT)
    d_preact = low(jax.vjp(exact_gelu, preact)[1](d_active)[0])
    d_hidden_two = dot(d_preact, fc_in_w)
    d_norm, d_gain_two, d_shift_two = jax.vjp(layer_norm, resid, gain_two, shift_two)[1](
        d_hidden_two
    )
    d_resid = d_state + d_norm
    d_resid_low = low(d_resid)
    d_attended = low(dot(d_resid_low, output_w, NT))
    wide = jnp.where(mask16, d_attended[:, None, :], jnp.zeros((), BF))
    d_pooled = low(dot(wide.reshape(-1, WIDTH), value_w, NT)).reshape(images, HEADS, WIDTH)
    d_weights = jnp.einsum("ihd,itd->iht", d_pooled, hidden, preferred_element_type=F32)
    d_weights = d_weights + jnp.sum(wide.astype(F32) * value_bias, axis=-1)[:, :, None]
    d_scores = low(weights * (d_weights - jnp.sum(weights * d_weights, axis=-1, keepdims=True)))
    d_hidden = jnp.einsum("iht,ihd->itd", weights_low, d_pooled, preferred_element_type=F32)
    d_hidden = d_hidden + jnp.einsum("iht,hd->itd", d_scores, qk, preferred_element_type=F32)
    pull = jnp.einsum("iht,itd->hd", d_scores, hidden, preferred_element_type=F32)
    d_query = jnp.sum(jnp.where(mask16, dot(low(pull), key_w), 0.0), axis=0) * SCALE
    d_class_hidden = dot(low(d_query)[None], query_w, NT)
    d_tokens, d_gain_one, d_shift_one = jax.vjp(layer_norm, tokens, gain_one, shift_one)[1](
        d_hidden
    )
    d_class, d_gain_cls, d_shift_cls = jax.vjp(layer_norm, class_state[None], gain_one, shift_one)[
        1
    ](d_class_hidden)
    d_class = d_class[0] + jnp.sum(d_tokens[:, 0], axis=0) + jnp.sum(d_resid, axis=0)
    d_patch = d_tokens[:, 1:]
    d_embed_w = jnp.einsum("itp,itd->pd", pixels, low(d_patch), preferred_element_type=F32)
    d_value_w = dot(pooled.reshape(-1, WIDTH), wide.reshape(-1, WIDTH), TN)
    d_key_w = dot(pull, query_heads.astype(F32), TN, precision=lax.Precision.HIGHEST)
    small_local = jnp.concatenate(
        [
            d_class[None],
            d_class[None],
            jnp.sum(d_patch, axis=0),
            jnp.sum(d_patch, axis=(0, 1))[None],
            (d_gain_one + d_gain_cls)[None],
            (d_shift_one + d_shift_cls)[None],
            d_query[None],
            jnp.sum(wide.astype(F32) * mass[:, :, None], axis=(0, 1))[None],
            jnp.sum(d_resid, axis=0)[None],
            d_gain_two[None],
            d_shift_two[None],
            jnp.sum(d_preact.astype(F32), axis=0).reshape(FF // WIDTH, WIDTH),
            jnp.sum(d_state, axis=0)[None],
            d_gain_end[None],
            d_shift_end[None],
        ],
        axis=0,
    )
    grad_table = jnp.concatenate(
        [
            d_embed_w,
            class_hidden.astype(F32)[:, None] * d_query[None, :],
            d_key_w,
            d_value_w,
            dot(attended, d_resid_low, TN),
            dot(d_preact, hidden_two, TN),
            dot(active, d_state_low, TN),
            dot(d_projected, final, TN),
            jnp.zeros(((chips * slots - UNIT_COUNT) * ROWS_PER_UNIT, WIDTH), F32),
        ],
        axis=0,
    ).reshape(chips * slots, ROWS_PER_UNIT, WIDTH)
    small_grad, loss = lax.psum((small_local, loss_part), ("img", "seq"))
    core_half = lax.psum_scatter(low(grad_table), "seq", scatter_dimension=1, tiled=True)
    own_grad = lax.psum_scatter(core_half.astype(F32), "img", scatter_dimension=0, tiled=True)
    owner_total = lax.psum(jnp.sum(own_grad * own_grad), ("img", "seq"))
    grad_norm = jnp.sqrt(owner_total + jnp.sum(small_grad * small_grad))
    factor = 1.0 / jnp.maximum(grad_norm, 1.0)
    slot_grad = to_slots(own_grad, near, img, chips)
    step_value = step_count.astype(F32)
    new_masters, new_first, new_second = adamw(
        masters, slot_grad * factor, first_moment_slots, second_moment_slots, step_value
    )
    new_small, new_small_first, new_small_second = adamw(
        small_params, small_grad * factor, small_first, small_second, step_value
    )
    return (
        new_masters, new_first, new_second, new_small, new_small_first, new_small_second,
        loss, grad_norm,
    )


def solution(mesh):
    chip, devices = "img", ("img", "seq")
    core, body = "seq", per_device_any
    if mesh.shape["img"] == CHIPS and mesh.shape["seq"] == 2:
        mesh = jax.sharding.Mesh(mesh.devices.reshape(4, 2, 2, 2), ALL)
        chip, devices, core, body = CHIP, ALL, "c", per_device_16
    weights = P(chip, core, None)
    return jax.shard_map(
        body,
        mesh=mesh,
        in_specs=(
            P(devices, None, None),
            P(devices, None),
            P(devices),
            P(devices, None),
            weights,
            weights,
            weights,
            P(),
            P(),
            P(),
            P(),
            P(),
        ),
        out_specs=(weights, weights, weights, P(), P(), P(), P(), P()),
        check_vma=False,
    )
```

```python
import functools
import math

import jax
import jax.numpy as jnp
from jax import lax
from jax.experimental import pallas as pl
from jax.experimental.pallas import tpu as pltpu
from jax.sharding import PartitionSpec as P

WIDTH = 1024
HEADS = 16
HEAD_DIM = 64
FF = 4096
PIX = 3072
PROJ = 768
TOKS = 50
PATCHES = TOKS - 1
ROWS_PER_UNIT = 32
UNIT_COUNT = 504
JITTER = 2

EPS_NORM = 1e-06
SOFTMAX_SCALE = 0.07
LEARN_RATE = 0.03
BETA_ONE = 0.5
BETA_TWO = 0.5
DECAY_RATE = 0.05
ADAM_EPS = 1e-08
MASKED = -1000000000.0
SCALE = HEAD_DIM ** (-0.5)

F32 = jnp.float32
BF = jnp.bfloat16
ROW_BASE = 1 + TOKS
ROW_TAIL = ROW_BASE + 8 + FF // WIDTH
SLOT = 64


def low(values):
    return values.astype(BF)


def dot(a, b, dims=((1,), (0,)), precision=None):
    return lax.dot_general(a, b, (dims, ((), ())), precision=precision, preferred_element_type=F32)


NN = ((1,), (0,))
NT = ((1,), (1,))
TN = ((0,), (0,))


def layer_norm(values, gain, shift):
    center = values - jnp.mean(values, axis=-1, keepdims=True)
    spread = jnp.mean(center * center, axis=-1, keepdims=True)
    return center * lax.rsqrt(spread + EPS_NORM) * gain + shift


def normalize(values):
    return values * lax.rsqrt(jnp.sum(values * values, axis=-1, keepdims=True) + EPS_NORM)


def exact_gelu(values):
    return jax.nn.gelu(values, approximate=False)


def small_parts(small):
    base, tail = ROW_BASE, ROW_TAIL
    return (
        small[0],
        small[1:base],
        small[base],
        small[base + 1],
        small[base + 2],
        small[base + 3],
        small[base + 4],
        small[base + 5],
        small[base + 6],
        small[base + 7],
        small[base + 8 : tail].reshape(FF),
        small[tail],
        small[tail + 1],
        small[tail + 2],
    )


def adamw(weight, grad, first, second, step):
    first_new = BETA_ONE * first + (1.0 - BETA_ONE) * grad
    second_new = BETA_TWO * second + (1.0 - BETA_TWO) * grad * grad
    first_hat = first_new / (1.0 - jnp.power(BETA_ONE, step))
    second_hat = second_new / (1.0 - jnp.power(BETA_TWO, step))
    weight_new = weight - LEARN_RATE * (
        first_hat / (jnp.sqrt(second_hat) + ADAM_EPS) + DECAY_RATE * weight
    )
    return (weight_new, first_new, second_new)


def halo(values, chips, axes):
    before = lax.ppermute(values[-JITTER:], axes, [(i, i + 1) for i in range(chips - 1)])
    behind = lax.ppermute(values[:JITTER], axes, [(i + 1, i) for i in range(chips - 1)])
    return before, behind


def with_halo(values, chips, axes):
    before, behind = halo(values, chips, axes)
    return jnp.concatenate([before, values, behind], axis=0)


def slots_near(slot_unit_index, img, slots):
    padded = jnp.pad(slot_unit_index, (JITTER, JITTER), constant_values=-1)
    return lax.dynamic_slice(padded, (img * slots,), (slots + 2 * JITTER,))


def pick(ext, matches, slots):
    out = jnp.zeros((slots,) + ext.shape[1:], ext.dtype)
    for shift in range(2 * JITTER + 1):
        out = jnp.where(matches[shift][:, None, None], ext[shift : shift + slots], out)
    return out


def to_units(values, near, img, chips, axes="img"):
    slots = values.shape[0]
    ids = img * slots + jnp.arange(slots, dtype=jnp.int32)
    matches = [near[s : s + slots] == ids for s in range(2 * JITTER + 1)]
    return pick(with_halo(values, chips, axes), matches, slots)


def to_slots(values, near, img, chips, axes="img"):
    slots = values.shape[0]
    here = near[JITTER : JITTER + slots]
    ids = img * slots + jnp.arange(slots, dtype=jnp.int32)
    matches = [
        (here == ids + (s - JITTER)) & (here < UNIT_COUNT) for s in range(2 * JITTER + 1)
    ]
    return pick(with_halo(values, chips, axes), matches, slots)


def shuffle_matrix():
    source = lax.broadcasted_iota(jnp.int32, (256, 256), 0)
    target = lax.broadcasted_iota(jnp.int32, (256, 256), 1)
    moved = ((source // 16) % 2) * 128 + (source // 32) * 16 + source % 16
    return (moved == target).astype(F32).astype(BF)


def vmem():
    return pl.BlockSpec(memory_space=pltpu.VMEM)


def smem():
    return pl.BlockSpec(memory_space=pltpu.SMEM)


def shape(dims, dtype):
    return jax.ShapeDtypeStruct(dims, dtype)


def call(kernel, name, scalars, arrays, outs, scratch=(), mib=16, flops=10**9, far=()):
    moved = sum(a.size * a.dtype.itemsize for a in [*arrays, *outs, *far])
    return pl.pallas_call(
        kernel,
        in_specs=[smem()] * len(scalars)
        + [vmem()] * len(arrays)
        + [pl.BlockSpec(memory_space=pl.ANY)] * len(far),
        out_specs=[vmem()] * len(outs),
        out_shape=list(outs),
        scratch_shapes=list(scratch),
        compiler_params=pltpu.CompilerParams(vmem_limit_bytes=mib * 2**20),
        cost_estimate=pl.CostEstimate(flops=flops, bytes_accessed=moved, transcendentals=0),
        name=name,
    )(*scalars, *arrays, *far)


def prep_kernel(pix_ref, shuffle_ref, out_ref):
    shuffle = shuffle_ref[...]
    out_ref[...] = jnp.zeros_like(out_ref)
    for block in range(PIX // 256):
        moved = dot(pix_ref[0, :, 256 * block : 256 * block + 256], shuffle).astype(BF)
        out_ref[0, 0, :PATCHES, 128 * block : 128 * block + 128] = moved[:, :128]
        out_ref[1, 0, :PATCHES, 128 * block : 128 * block + 128] = moved[:, 128:]


def prep(pixels, shuffle):
    images = pixels.shape[0]
    return pl.pallas_call(
        prep_kernel,
        grid=(images,),
        in_specs=[
            pl.BlockSpec((1, PATCHES, PIX), lambda i: (i, 0, 0)),
            pl.BlockSpec((256, 256), lambda i: (0, 0)),
        ],
        out_specs=pl.BlockSpec((2, 1, SLOT, PIX // 2), lambda i: (0, i, 0, 0)),
        out_shape=jax.ShapeDtypeStruct((2, images, SLOT, PIX // 2), BF),
        compiler_params=pltpu.CompilerParams(vmem_limit_bytes=24 * 2**20),
        cost_estimate=pl.CostEstimate(flops=8 * 10**8, bytes_accessed=6 * 2**20, transcendentals=0),
        name="prep",
    )(pixels, shuffle)


def head_mask(rows):
    lane = lax.broadcasted_iota(jnp.int32, (rows, WIDTH), 1) // HEAD_DIM
    row = lax.broadcasted_iota(jnp.int32, (rows, WIDTH), 0) % HEADS
    return lane == row


def norm_parts(values):
    center = values - jnp.mean(values, axis=-1, keepdims=True)
    rstd = lax.rsqrt(jnp.mean(center * center, axis=-1, keepdims=True) + EPS_NORM)
    return center * rstd, rstd


def norm_back(grad, gain, xhat, rstd):
    gy = grad * gain
    return rstd * (
        gy - jnp.mean(gy, axis=-1, keepdims=True) - xhat * jnp.mean(gy * xhat, axis=-1, keepdims=True)
    )


def rowsum(values):
    return jnp.sum(values, axis=0, keepdims=True)


def to_halves(values, shuffle):
    first, second = [], []
    for block in range(values.shape[1] // 256):
        moved = low(dot(values[:, 256 * block : 256 * block + 256], shuffle))
        first.append(moved[:, :128])
        second.append(moved[:, 128:])
    return jnp.concatenate(first, axis=1), jnp.concatenate(second, axis=1)


def to_natural(first, second, shuffle):
    out = []
    for block in range(first.shape[1] // 128):
        lanes = slice(128 * block, 128 * block + 128)
        both = jnp.concatenate([first[:, lanes], second[:, lanes]], axis=1)
        out.append(low(dot(both, shuffle, NT)))
    return jnp.concatenate(out, axis=1)


R_PATCH, R_GAIN1, R_SHIFT1, R_VB, R_OB, R_GAIN2, R_SHIFT2 = 51, 52, 53, 55, 56, 57, 58
R_C2, R_GAINF, R_SHIFTF, R_SMALL = 63, 64, 65, 66
QUARTER = 128


def partner_kernel(raw_ref, out_ref):
    source = lax.broadcasted_iota(jnp.int32, (PROJ, PROJ), 0)
    target = lax.broadcasted_iota(jnp.int32, (PROJ, PROJ), 1)
    moved = ((source // 16) % 2) * (PROJ // 2) + (source // 32) * 16 + source % 16
    select = low((moved == target).astype(F32))
    out_ref[...] = low(dot(raw_ref[...].reshape(-1, PROJ), select))


def second_block_kernel(
    role_ref, outer_ref, low_ref, mid_ref, two_ref, three_ref, out_ref, held_ref, sems
):
    chip, plane = role_ref[0], role_ref[1]

    @pl.when(chip < 3)
    def _():
        head = pltpu.make_async_copy(outer_ref, held_ref.at[pl.ds(0, 256)], sems.at[0])
        tail = pltpu.make_async_copy(low_ref, held_ref.at[pl.ds(256, QUARTER + HEADS)], sems.at[1])
        head.start()
        tail.start()
        head.wait()
        tail.wait()

    for number, ref in ((1, mid_ref), (2, two_ref), (3, three_ref)):
        here = (plane == number) | (chip == 3) if number == 3 else plane == number

        @pl.when(here)
        def _():
            whole = pltpu.make_async_copy(ref, held_ref, sems.at[0])
            whole.start()
            whole.wait()

    out = pltpu.make_async_copy(held_ref, out_ref, sems.at[0])
    out.start()
    out.wait()


def second_block(role, pieces):
    any_place = pl.BlockSpec(memory_space=pl.ANY)
    return pl.pallas_call(
        second_block_kernel,
        in_specs=[smem()] + [any_place] * len(pieces),
        out_specs=pl.BlockSpec(memory_space=pltpu.HBM),
        out_shape=shape((256 + QUARTER + HEADS, WIDTH), BF),
        scratch_shapes=[
            pltpu.VMEM((256 + QUARTER + HEADS, WIDTH), BF),
            pltpu.SemaphoreType.DMA((2,)),
        ],
        compiler_params=pltpu.CompilerParams(vmem_limit_bytes=4 * 2**20),
        cost_estimate=pl.CostEstimate(flops=0, bytes_accessed=2 * 2**20, transcendentals=0),
        name="second_block",
    )(role, *pieces)


def forward_kernel(segments, images, where_ref, pix_ref, rows_ref, valid_ref, shuffle_ref, *refs):
    count = len(segments)
    own, peer = refs[:count], refs[count : 2 * count]
    (
        hid_ref, xhat_ref, rstd_ref, p_ref, pooled_ref, mass_ref, wv_ref, wo_ref, qk_ref,
        resid_ref, low_ref, acc_ref, pool_ref, half_ref, table_ref, sems,
    ) = refs[2 * count :]
    col, core = where_ref[0], where_ref[1]
    waits = ([], [])
    for flip, group in ((0, own), (1, peer)):
        half = core ^ flip
        for (source, parts, late), ref in zip(segments, group):
            block = col ^ source
            for row, lane, rows in parts:
                part = ref.at[pl.ds(row, rows)]
                line = pl.multiple_of(block * 512 + lane, 128)
                copy = pltpu.make_async_copy(part, table_ref.at[half, pl.ds(line, rows)], sems.at[flip])
                copy.start()
                waits[flip].append(copy)
            if late >= 0:
                part = ref.at[pl.ds(late, QUARTER)]
                line = pl.multiple_of(block * QUARTER, QUARTER)
                copy = pltpu.make_async_copy(part, wo_ref.at[half, pl.ds(line, QUARTER)], sems.at[2])
                copy.start()
                waits[1].append(copy)
                part = ref.at[pl.ds(late + QUARTER, HEADS)]
                copy = pltpu.make_async_copy(part, half_ref.at[half, block], sems.at[3])
                copy.start()
                waits[1].append(copy)
    patch = rows_ref[2 : 1 + TOKS] + rows_ref[R_PATCH : R_PATCH + 1]
    class_state = rows_ref[0:1] + rows_ref[1:2]
    for i in range(images):
        acc_ref[SLOT * i : SLOT * i + PATCHES] = patch
        acc_ref[SLOT * i + PATCHES : SLOT * i + TOKS] = class_state
        acc_ref[SLOT * i + TOKS : SLOT * (i + 1)] = jnp.zeros((SLOT - TOKS, WIDTH), F32)
    for copy in waits[0]:
        copy.wait()
    acc_ref[...] += dot(pix_ref[core], table_ref[core, :1536])
    for copy in waits[1]:
        copy.wait()
    acc_ref[...] += dot(pix_ref[1 - core], table_ref[1 - core, :1536])
    wv_ref[...] = table_ref[:, 1536:]
    shuffle = shuffle_ref[...]
    gain, shift, value_bias = (rows_ref[r : r + 1] for r in (R_GAIN1, R_SHIFT1, R_VB))
    half = WIDTH // 2
    qk = to_natural(half_ref[0, 0, :, :half], half_ref[1, 0, :, :half], shuffle)
    qk_ref[...] = qk
    valid = valid_ref[...] > 0
    for i in range(images):
        part = slice(SLOT * i, SLOT * (i + 1))
        xhat, rstd = norm_parts(acc_ref[part])
        hid = low(xhat * gain + shift)
        xhat_ref[part] = xhat
        rstd_ref[part] = jnp.broadcast_to(rstd, (SLOT, 128))
        hid_ref[part] = hid
        scores = jnp.where(valid[part], dot(hid, qk, NT), MASKED)
        e = jnp.exp(scores - jnp.max(scores, axis=0, keepdims=True))
        p = e / jnp.sum(e, axis=0, keepdims=True)
        p_ref[part] = p
        pb = low(p)
        pool_ref[HEADS * i : HEADS * (i + 1)] = low(dot(pb, hid, TN))
        mass_ref[HEADS * i : HEADS * (i + 1)] = dot(pb, jnp.ones((SLOT, 128), BF), TN)
    pooled_ref[0], pooled_ref[1] = to_halves(pool_ref[...], shuffle)
    rows = images * HEADS
    mixed = dot(pooled_ref[0], wv_ref[0]) + dot(pooled_ref[1], wv_ref[1])
    mixed = mixed + mass_ref[:, 0:1] * value_bias
    mixed = jnp.where(head_mask(rows), mixed, 0.0)
    joined = low(jnp.sum(mixed.reshape(images, HEADS, WIDTH), axis=1))
    first, second = to_halves(joined, shuffle)
    resid = class_state + dot(first, wo_ref[0]) + dot(second, wo_ref[1])
    resid = resid + rows_ref[R_OB : R_OB + 1]
    resid_ref[...] = resid
    xhat, _ = norm_parts(resid)
    hidden = low(xhat * rows_ref[R_GAIN2 : R_GAIN2 + 1] + rows_ref[R_SHIFT2 : R_SHIFT2 + 1])
    sent = jnp.concatenate([hidden, first, second], axis=1)
    low_ref[...] = jnp.broadcast_to(sent[None], low_ref.shape)


def forward_call(segments, images, where, pix, own, peer, rows, valid, shuffle):
    tokens = images * SLOT
    outs = [
        shape((tokens, WIDTH), BF),
        shape((tokens, WIDTH), F32),
        shape((tokens, 128), F32),
        shape((tokens, HEADS), F32),
        shape((2, images * HEADS, WIDTH // 2), BF),
        shape((images * HEADS, 128), F32),
        shape((2, WIDTH // 2, WIDTH), BF),
        shape((2, WIDTH // 2, WIDTH), BF),
        shape((HEADS, WIDTH), BF),
        shape((images, WIDTH), F32),
        shape((8, images, 2 * WIDTH), BF),
    ]
    scratch = [
        pltpu.VMEM((tokens, WIDTH), F32),
        pltpu.VMEM((images * HEADS, WIDTH), BF),
        pltpu.VMEM((2, 4, HEADS, WIDTH), BF),
        pltpu.VMEM((2, 2048, WIDTH), BF),
        pltpu.SemaphoreType.DMA((4,)),
    ]
    return call(
        functools.partial(forward_kernel, segments, images), "forward", [where],
        [pix, rows, valid, shuffle], outs, scratch, mib=52, flops=4 * 10**9,
        far=[*own, *peer],
    )


def fetch(pick_ref, slot, candidates, out_ref, sem):
    for number, candidate in enumerate(candidates):

        @pl.when(pick_ref[slot] == number)
        def _():
            pltpu.make_async_copy(candidate, out_ref, sem).start()


def arrived(candidate, out_ref, sem):
    pltpu.make_async_copy(candidate, out_ref, sem).wait()


def ff_kernel(pick_ref, hid_ref, bias_ref, *refs):
    candidates, (pre_ref, act_ref, part_ref, w1_ref, w2_ref, sems) = refs[:6], refs[6:]
    fetch(pick_ref, 0, candidates, w1_ref, sems.at[0])
    fetch(pick_ref, 1, candidates, w2_ref, sems.at[1])
    hidden = hid_ref[:, :, :WIDTH].reshape(-1, WIDTH)
    arrived(candidates[0], w1_ref, sems.at[0])
    pre = dot(hidden, w1_ref[...], NT) + bias_ref[...]
    pre_ref[...] = pre
    active = low(0.5 * pre * (1.0 + lax.erf(pre * (0.5**0.5))))
    act_ref[...] = active
    arrived(candidates[0], w2_ref, sems.at[1])
    part_ref[...] = low(dot(active, w2_ref[...])).reshape(part_ref.shape)


def ff_back_kernel(pick_ref, dst_ref, pre_ref, *refs):
    candidates, (dpre_ref, sum_ref, part_ref, w1_ref, w2_ref, sems) = refs[:6], refs[6:]
    fetch(pick_ref, 1, candidates, w2_ref, sems.at[1])
    fetch(pick_ref, 0, candidates, w1_ref, sems.at[0])
    d_state = dst_ref[:, :, :WIDTH].reshape(-1, WIDTH)
    pre = pre_ref[...]
    slope = 0.5 * (1.0 + lax.erf(pre * (0.5**0.5))) + pre * jnp.exp(-0.5 * pre * pre) * (
        1.0 / (2.0 * math.pi) ** 0.5
    )
    arrived(candidates[0], w2_ref, sems.at[1])
    d_pre = low(dot(d_state, w2_ref[...], NT) * slope)
    dpre_ref[...] = d_pre
    sum_ref[...] = rowsum(d_pre.astype(F32))
    arrived(candidates[0], w1_ref, sems.at[0])
    part_ref[...] = low(dot(d_pre, w1_ref[...])).reshape(part_ref.shape)


def ff_call(kernel, name, pick, arrays, candidates, outs):
    moved = sum(a.size * a.dtype.itemsize for a in list(arrays) + list(outs))
    return pl.pallas_call(
        kernel,
        in_specs=[smem()]
        + [vmem()] * len(arrays)
        + [pl.BlockSpec(memory_space=pl.ANY)] * len(candidates),
        out_specs=[vmem()] * len(outs),
        out_shape=list(outs),
        scratch_shapes=[
            pltpu.VMEM((512, WIDTH), BF),
            pltpu.VMEM((512, WIDTH), BF),
            pltpu.SemaphoreType.DMA((2,)),
        ],
        compiler_params=pltpu.CompilerParams(vmem_limit_bytes=24 * 2**20),
        cost_estimate=pl.CostEstimate(
            flops=2 * 10**8, bytes_accessed=moved + 2 * 2**20, transcendentals=0
        ),
        name=name,
    )(pick, *arrays, *candidates)


def head_kernel(
    where_ref, part_ref, resid_ref, pj_ref, pjp_ref, partners_ref, target_ref, rows_ref,
    state_ref, low_ref, vec_ref, dz_ref,
):
    images = resid_ref.shape[0]
    state = resid_ref[...] + jnp.sum(part_ref[...].astype(F32), axis=0) + rows_ref[R_C2 : R_C2 + 1]
    gain = rows_ref[R_GAINF : R_GAINF + 1]
    xhat, rstd = norm_parts(state)
    final = low(xhat * gain + rows_ref[R_SHIFTF : R_SHIFTF + 1])
    z_own, z_peer = dot(final, pj_ref[...], NT), dot(final, pjp_ref[...], NT)
    square = jnp.sum(z_own * z_own, axis=-1, keepdims=True) + jnp.sum(
        z_peer * z_peer, axis=-1, keepdims=True
    )
    inv = lax.rsqrt(square + EPS_NORM)
    core = where_ref[1]
    half = PROJ // 2
    own_lanes = pl.ds(pl.multiple_of(core * half, 128), half)
    peer_lanes = pl.ds(pl.multiple_of((1 - core) * half, 128), half)
    ptn_own, ptn_peer = partners_ref[:, own_lanes], partners_ref[:, peer_lanes]
    logits = dot(low(z_own * inv), ptn_own, NT) + dot(low(z_peer * inv), ptn_peer, NT)
    logits = logits / SOFTMAX_SCALE
    total = logits.shape[1]
    hit = lax.broadcasted_iota(jnp.int32, (images, total), 1) == target_ref[...]
    top = jnp.max(logits, axis=-1, keepdims=True)
    e = jnp.exp(logits - top)
    mass = jnp.sum(e, axis=-1, keepdims=True)
    aim = jnp.sum(jnp.where(hit, logits, 0.0), axis=-1, keepdims=True)
    losses = jnp.log(mass) + top - aim
    d_logits = (e / mass - jnp.where(hit, 1.0, 0.0)) / total
    g_logits = low(d_logits / SOFTMAX_SCALE)
    d_own, d_peer = dot(g_logits, ptn_own), dot(g_logits, ptn_peer)
    along = jnp.sum(d_own * z_own, axis=-1, keepdims=True) + jnp.sum(
        d_peer * z_peer, axis=-1, keepdims=True
    )
    shrink = along * inv * inv * inv
    dz_own, dz_peer = low(d_own * inv - z_own * shrink), low(d_peer * inv - z_peer * shrink)
    dz_ref[:, own_lanes] = dz_own
    dz_ref[:, peer_lanes] = dz_peer
    d_final = dot(dz_own, pj_ref[...]) + dot(dz_peer, pjp_ref[...])
    d_state = norm_back(d_final, gain, xhat, rstd)
    state_ref[...] = d_state
    sent = jnp.concatenate([low(d_state), dz_ref[...], final], axis=1)
    low_ref[...] = jnp.broadcast_to(sent[None], low_ref.shape)
    vec_ref[...] = jnp.zeros_like(vec_ref)
    vec_ref[0:1] = rowsum(d_state)
    vec_ref[1:2] = rowsum(d_final * xhat)
    vec_ref[2:3] = rowsum(d_final)
    vec_ref[3:4] = jnp.broadcast_to(rowsum(losses) / total, (1, WIDTH))


def backward_kernel(
    images, where_ref, part_ref, dstate_ref, resid_ref, wo_ref, wv_ref, hid_ref, xhat_ref,
    rstd_ref, p_ref, mass_ref, qk_ref, rows_ref, shuffle_ref,
    de_ref, do_ref, dres_ref, pos_ref, vec_ref, pull_ref, dom_ref, da_ref,
):
    rows = images * HEADS
    gain, value_bias = rows_ref[R_GAIN1 : R_GAIN1 + 1], rows_ref[R_VB : R_VB + 1]
    shuffle = shuffle_ref[...]
    vec_ref[...] = jnp.zeros_like(vec_ref)
    d_two = jnp.sum(part_ref[...].astype(F32), axis=0)
    xhat2, rstd2 = norm_parts(resid_ref[...])
    d_resid = dstate_ref[...] + norm_back(d_two, rows_ref[R_GAIN2 : R_GAIN2 + 1], xhat2, rstd2)
    vec_ref[3:4] = rowsum(d_resid)
    vec_ref[4:5] = rowsum(d_two * xhat2)
    vec_ref[5:6] = rowsum(d_two)
    d_low = low(d_resid)
    dres_ref[...] = jnp.broadcast_to(d_low[None], dres_ref.shape)
    d_att = to_natural(
        low(dot(d_low, wo_ref[0], NT)), low(dot(d_low, wo_ref[1], NT)), shuffle
    )
    do_ref[...] = d_att
    spread = jnp.broadcast_to(d_att.reshape(images, 1, WIDTH).astype(F32), (images, HEADS, WIDTH))
    wide = jnp.where(head_mask(rows), spread.reshape(rows, WIDTH), 0.0)
    dom_ref[...] = low(wide)
    vec_ref[2:3] = rowsum(wide * mass_ref[:, 0:1])
    da_ref[...] = to_natural(
        low(dot(dom_ref[...], wv_ref[0], NT)), low(dot(dom_ref[...], wv_ref[1], NT)), shuffle
    )
    qk = qk_ref[...]
    bias_rows = low(jnp.broadcast_to(value_bias, (8, WIDTH)))
    real = lax.broadcasted_iota(jnp.int32, (SLOT, WIDTH), 0) < PATCHES
    for i in range(images):
        part = slice(SLOT * i, SLOT * (i + 1))
        mine = slice(HEADS * i, HEADS * (i + 1))
        hid, p, da = hid_ref[part], p_ref[part], da_ref[mine]
        dp = dot(hid, da, NT) + dot(bias_rows, dom_ref[mine], NT)[0:1]
        ds = low(p * (dp - rowsum(p * dp)))
        dh = dot(low(p), da) + dot(ds, qk)
        pull = dot(ds, hid, TN)
        xhat, rstd = xhat_ref[part], rstd_ref[part, 0:1]
        dx = norm_back(dh, gain, xhat, rstd)
        de_ref[part] = low(jnp.where(real, dx, 0.0))
        vec_ref[0:1] += rowsum(dh * xhat)
        vec_ref[1:2] += rowsum(dh)
        if i == 0:
            pos_ref[...] = dx
            pull_ref[...] = pull
        else:
            pos_ref[...] += dx
            pull_ref[...] += pull


def backward_call(images, where, arrays):
    tokens = images * SLOT
    outs = [
        shape((tokens, WIDTH), BF),
        shape((images, WIDTH), BF),
        shape((8, images, WIDTH), BF),
        shape((SLOT, WIDTH), F32),
        shape((8, WIDTH), F32),
        shape((HEADS, WIDTH), F32),
    ]
    scratch = [pltpu.VMEM((images * HEADS, WIDTH), BF)] * 2
    return call(
        functools.partial(backward_kernel, images), "backward", [where], arrays, outs, scratch
    )


def rows_kernel(where_ref, act_ref, dpre_ref, hid_ref, dst_ref, dres_ref, out_ref):
    half = WIDTH // 2
    base = 3 * WIDTH
    out_ref[:, :half] = act_ref[...]
    out_ref[:, half:WIDTH] = dpre_ref[...]
    count = out_ref.shape[0]
    out_ref[:, WIDTH : 2 * WIDTH] = hid_ref[:, :, :WIDTH].reshape(count, WIDTH)
    out_ref[:, 2 * WIDTH : base] = dst_ref[:, :, :WIDTH].reshape(count, WIDTH)

    @pl.when(where_ref[0] == 2)
    def _():
        out_ref[:, base : base + WIDTH] = hid_ref[:, :, WIDTH:].reshape(count, WIDTH)
        out_ref[:, base + WIDTH :] = dres_ref[...].reshape(count, WIDTH)

    @pl.when(where_ref[0] != 2)
    def _():
        out_ref[:, base : base + WIDTH + PROJ] = dst_ref[:, :, WIDTH:].reshape(count, WIDTH + PROJ)
        out_ref[:, base + WIDTH + PROJ :] = jnp.zeros((count, WIDTH - PROJ), BF)


def embed_grad_kernel(
    images, plan, where_ref, pix_ref, pixp_ref, de_ref, dep_ref, pooled_ref, pooledp_ref,
    do_ref, dop_ref, *out_refs,
):
    col = where_ref[0]
    heads = images * HEADS
    for (source, first, rows, _), out_ref in zip(plan, out_refs):
        block = col ^ source

        @pl.when(block < 3)
        def _():
            lanes = pl.ds(pl.multiple_of(block * 512 + first, 128), rows)
            total = dot(pix_ref[:, lanes], de_ref[...], TN) + dot(pixp_ref[:, lanes], dep_ref[...], TN)
            out_ref[...] = total.astype(out_ref.dtype)

        @pl.when(block == 3)
        def _():
            total = None
            for pooled, do in ((pooled_ref, do_ref), (pooledp_ref, dop_ref)):
                spread = jnp.broadcast_to(
                    do[...].reshape(images, 1, WIDTH).astype(F32), (images, HEADS, WIDTH)
                )
                wide = low(jnp.where(head_mask(heads), spread.reshape(heads, WIDTH), 0.0))
                term = dot(pooled[:, first : first + rows], wide, TN)
                total = term if total is None else total + term
            out_ref[...] = total.astype(out_ref.dtype)


def embed_grad_call(images, name, plan, where, arrays):
    outs = [shape((rows, WIDTH), dtype) for _, _, rows, dtype in plan]
    return call(
        functools.partial(embed_grad_kernel, images, plan), name, [where], arrays, outs
    )


def add_far_kernel(x_low_ref, x_high_ref, got_x_ref, y_low_ref, got_y_ref, y_high_ref, x_ref, y_ref):
    x_ref[0] = x_low_ref[...]
    x_ref[1] = low(x_high_ref[...] + got_x_ref[...].astype(F32))
    y_ref[0] = low(y_low_ref[...] + got_y_ref[...].astype(F32))
    y_ref[1] = y_high_ref[...]


def add_far(pieces):
    rows = pieces[0].shape[0]
    step = rows // 4
    out = shape((2, rows, WIDTH), BF)
    return pl.pallas_call(
        add_far_kernel,
        grid=(4,),
        in_specs=[pl.BlockSpec((step, WIDTH), lambda i: (i, 0))] * 6,
        out_specs=[pl.BlockSpec((2, step, WIDTH), lambda i: (0, i, 0))] * 2,
        out_shape=[out, out],
        compiler_params=pltpu.CompilerParams(vmem_limit_bytes=58 * 2**20),
        cost_estimate=pl.CostEstimate(flops=10**6, bytes_accessed=6 * 2**20, transcendentals=0),
        name="add_far",
    )(*pieces)


def to_natural_exact(first, second, shuffle):
    wide = shuffle.astype(F32)
    out = []
    for block in range(first.shape[1] // 128):
        lanes = slice(128 * block, 128 * block + 128)
        both = jnp.concatenate([first[:, lanes], second[:, lanes]], axis=1)
        out.append(dot(both, wide, NT, precision=lax.Precision.HIGHEST))
    return jnp.concatenate(out, axis=1)


def collect_kernel(
    where_ref, pos_ref, vec_ref, head_ref, sum_ref, pull_ref, shuffle_ref, sent_ref, out_ref
):
    col, core = where_ref[0], where_ref[1]
    out_ref[...] = jnp.zeros_like(out_ref)
    top = pos_ref[PATCHES:TOKS] + vec_ref[3:4]
    out_ref[0:1] = top
    out_ref[1:2] = top
    patches = pos_ref[0:PATCHES]
    out_ref[2 : 1 + TOKS] = patches
    out_ref[R_PATCH : R_PATCH + 1] = rowsum(patches)
    out_ref[R_GAIN1 : R_SHIFT1 + 1] = vec_ref[0:2]
    out_ref[R_VB : R_VB + 1] = vec_ref[2:3]
    out_ref[R_OB : R_SHIFT2 + 1] = vec_ref[3:6]
    sums = jnp.broadcast_to(sum_ref[...], (8, WIDTH // 2))
    nothing = jnp.zeros_like(sums)
    row = to_natural_exact(
        jnp.where(core == 0, sums, nothing), jnp.where(core == 0, nothing, sums), shuffle_ref[...]
    )
    for block in range(4):
        mine = (col + 1) % 4 == block
        out_ref[R_SHIFT2 + 1 + block : R_SHIFT2 + 2 + block] = jnp.where(mine, row[0:1], 0.0)
    out_ref[R_C2 : R_SHIFTF + 1] = head_ref[0:3]
    out_ref[R_SMALL : R_SMALL + HEADS] = pull_ref[...]
    out_ref[R_SMALL + HEADS : R_SMALL + HEADS + 1] = head_ref[3:4]
    for number in range(sent_ref.shape[0]):
        sent_ref[number] = out_ref[3 * number : 3 * number + 3]


def share_kernel(got_ref, sent_ref):
    sent_ref[...] = jnp.broadcast_to(jnp.sum(got_ref[...], axis=0, keepdims=True), sent_ref.shape)


def query_back_kernel(core_ref, got_ref, w_ref, shuffle_ref, dq_ref, pull_ref, total_ref):
    for number in range(got_ref.shape[0]):
        total_ref[3 * number : 3 * number + 3] = got_ref[number]
    wide = shuffle_ref[...].astype(F32)
    pull = total_ref[R_SMALL : R_SMALL + HEADS]
    is_one = core_ref[0] == 1
    out = []
    for block in range(WIDTH // 256):
        moved = dot(pull[:, 256 * block : 256 * block + 256], wide, precision=lax.Precision.HIGHEST)
        out.append(jnp.where(is_one, moved[:, 128:], moved[:, :128]))
    half = jnp.concatenate(out, axis=1)
    pull_ref[...] = half
    d_query = jnp.where(head_mask(HEADS), dot(low(half), w_ref[...]), 0.0)
    dq_ref[...] = jnp.broadcast_to(rowsum(d_query) * SCALE, dq_ref.shape)


def complete_kernel(total_ref, reports_ref, rows_ref, shuffle_ref, out_ref, norm_ref):
    out_ref[...] = total_ref[0:R_SMALL]
    half = WIDTH // 2
    first = jnp.broadcast_to(reports_ref[6, :, WIDTH : WIDTH + half], (8, half))
    second = jnp.broadcast_to(reports_ref[7, :, WIDTH : WIDTH + half], (8, half))
    d_hidden = to_natural_exact(first, second, shuffle_ref[...])[0:1]
    xhat, rstd = norm_parts(rows_ref[0:1] + rows_ref[1:2])
    d_class = norm_back(d_hidden, rows_ref[R_GAIN1 : R_GAIN1 + 1], xhat, rstd)
    out_ref[0:1] += d_class
    out_ref[1:2] += d_class
    out_ref[R_GAIN1 : R_GAIN1 + 1] += d_hidden * xhat
    out_ref[R_SHIFT1 : R_SHIFT1 + 1] += d_hidden
    out_ref[R_SHIFT1 + 1 : R_SHIFT1 + 2] = reports_ref[6, :, :WIDTH]
    grads = out_ref[...]
    square = jnp.sum(jnp.sum(grads * grads, axis=0, keepdims=True), axis=1, keepdims=True)
    for number in range(reports_ref.shape[0]):
        square = square + reports_ref[number, :, WIDTH + half : WIDTH + half + 1]
    norm_ref[...] = jnp.broadcast_to(jnp.sqrt(square), (8, 128))


def owner_kernel(role_ref, pull_ref, heads_ref, class_ref, dq_ref, *refs):
    rows, out_ref = refs[:6], refs[6]
    chip, core = role_ref[0], role_ref[1]
    half = WIDTH // 2
    base = 3 * WIDTH

    def product(left, right):
        total = None
        for piece in rows:
            term = dot(left(piece), right(piece), TN)
            total = term if total is None else total + term
        return total

    @pl.when((chip >= 7) & (chip <= 14))
    def _():
        is_two = chip >= 11
        out_ref[...] = product(
            lambda piece: jnp.where(is_two, piece[:, :half], piece[:, half:WIDTH]),
            lambda piece: jnp.where(is_two, piece[:, 2 * WIDTH : base], piece[:, WIDTH : 2 * WIDTH]),
        )

    @pl.when(chip == 6)
    def _():
        lanes = pl.ds(pl.multiple_of(base + core * half, 128), half)
        out_ref[...] = product(lambda piece: piece[:, lanes], lambda piece: piece[:, base + WIDTH :])

    @pl.when(chip == 15)
    def _():
        lanes = pl.ds(pl.multiple_of(base + core * (PROJ // 2), 128), PROJ // 2)
        out_ref[: PROJ // 2] = product(
            lambda piece: piece[:, lanes],
            lambda piece: piece[:, base + PROJ : base + PROJ + WIDTH],
        )
        out_ref[PROJ // 2 :] = jnp.zeros((512 - PROJ // 2, WIDTH), F32)

    @pl.when(chip == 4)
    def _():
        out_ref[...] = dot(
            pull_ref[...], heads_ref[...].astype(F32), TN, precision=lax.Precision.HIGHEST
        )

    @pl.when(chip == 3)
    def _():
        out_ref[...] = dot(
            class_ref[...].astype(F32), jnp.concatenate([dq_ref[0:1], jnp.zeros((7, WIDTH), F32)]),
            TN, precision=lax.Precision.HIGHEST,
        )


def finish_kernel(
    role_ref, formed_ref, dq_ref, toward_ref, total_ref, first_ref, second_ref, aside_ref, third_ref,
    out_ref, top_ref, end_ref, report_ref,
):
    chip = role_ref[0]

    @pl.when(chip < 3)
    def _():
        out_ref[...] = total_ref[...] + first_ref[...].astype(F32) + second_ref[...].astype(F32)

    @pl.when(chip == 5)
    def _():
        out_ref[...] = (
            second_ref[...].astype(F32) + aside_ref[...].astype(F32) + third_ref[...].astype(F32)
        )

    @pl.when((chip >= 3) & (chip != 5))
    def _():
        out_ref[...] = formed_ref[...]

    edge = top_ref.shape[0]
    top_ref[...] = out_ref[:edge]
    end_ref[...] = out_ref[-edge:]
    grads = out_ref[...]
    square = jnp.sum(jnp.sum(grads * grads, axis=0, keepdims=True), axis=1, keepdims=True)
    report_ref[...] = jnp.concatenate(
        [dq_ref[...], toward_ref[...], jnp.broadcast_to(square, (1, 128))], axis=1
    )


def update_kernel(
    source_ref, scalar_ref, before_ref, grad_ref, behind_ref, w_ref, m_ref, v_ref,
    nw_ref, nm_ref, nv_ref,
):
    step = pl.program_id(0)
    slots = grad_ref.shape[0]
    factor, fix_one, fix_two = scalar_ref[0], scalar_ref[1], scalar_ref[2]
    for k in range(w_ref.shape[0]):
        at = source_ref[step * w_ref.shape[0] + k]
        inside = (at >= 0) & (at < slots)
        grad = jnp.where(
            inside,
            grad_ref[jnp.clip(at, 0, slots - 1)],
            jnp.where(
                at < 0,
                before_ref[jnp.clip(at + JITTER, 0, JITTER - 1)],
                behind_ref[jnp.clip(at - slots, 0, JITTER - 1)],
            ),
        )
        grad = grad * jnp.where(at >= -JITTER, factor, 0.0)
        weight = w_ref[k]
        first = BETA_ONE * m_ref[k] + (1.0 - BETA_ONE) * grad
        second = BETA_TWO * v_ref[k] + (1.0 - BETA_TWO) * grad * grad
        nm_ref[k] = first
        nv_ref[k] = second
        nw_ref[k] = weight - LEARN_RATE * (
            (first * fix_one) / (jnp.sqrt(second * fix_two) + ADAM_EPS) + DECAY_RATE * weight
        )


def update_call(source, scalars, before, grads, behind, masters, first, second):
    slots, part, width = masters.shape
    block = 16
    spec = pl.BlockSpec((block, part, width), lambda i: (i, 0, 0))
    return pl.pallas_call(
        update_kernel,
        grid=(slots // block,),
        in_specs=[smem(), smem(), vmem(), vmem(), vmem(), spec, spec, spec],
        out_specs=[spec] * 3,
        out_shape=[shape(masters.shape, F32)] * 3,
        compiler_params=pltpu.CompilerParams(vmem_limit_bytes=58 * 2**20),
        cost_estimate=pl.CostEstimate(
            flops=2 * 10**7, bytes_accessed=7 * masters.size * 4, transcendentals=0
        ),
        name="update",
    )(source, scalars, before, grads, behind, masters, first, second)


CHIPS = 16
CHIP = ("z", "y", "x")
ALL = ("z", "y", "x", "c")
PLANE = ("y", "x", "c")
FLIP_X = [(i, i ^ 1) for i in range(CHIPS)]
FLIP_Y = [(i, i ^ 2) for i in range(CHIPS)]
FLIP_CORE = [(0, 1), (1, 0)]


def hop(values, pairs):
    return lax.ppermute(values, CHIP, pairs)


def swap(values):
    return lax.ppermute(values, "c", FLIP_CORE)


def after(values, *others):
    return lax.optimization_barrier((values,) + others)[0]


def among(img, chips):
    hit = img == chips[0]
    for chip in chips[1:]:
        hit = hit | (img == chip)
    return hit


def choose(img, cases, otherwise):
    out = otherwise
    for chips, values in cases:
        out = jnp.where(among(img, chips), values, out)
    return out


def together(*values):
    return lax.optimization_barrier(values)


def plane_gather(block, diagonal_by_x):
    by_x, by_y, block_peer = hop(block, FLIP_X), hop(block, FLIP_Y), swap(block)
    proj_top = jnp.where(img == 15, corner[0], corner[1] + corner[2] + corner[3])
    diagonal = hop(by_y, FLIP_X) if diagonal_by_x else hop(by_x, FLIP_Y)
    return [block, by_x, by_y, diagonal]


def in_plane(values):
    return lax.all_to_all(values, PLANE, 0, 0, tiled=True)


def from_all(values):
    sent = jnp.broadcast_to(values[None], (2 * CHIPS,) + values.shape)
    return lax.all_to_all(sent, ALL, 0, 0, tiled=True)


def natural(values):
    lead = values.shape[:-2]
    units = values.shape[-1] // 16
    split = values.reshape(lead + (2, units, 16))
    return jnp.swapaxes(split, -3, -2).reshape(lead + (units * 32,))


def halves(values):
    lead = values.shape[:-1]
    units = values.shape[-1] // 32
    return jnp.swapaxes(values.reshape(lead + (units, 2, 16)), -3, -2).reshape(
        lead + (2, units * 16)
    )


def per_device_16(
    pixels, keep_mask, partner_index, partner_emb, masters, first_moment_slots,
    second_moment_slots, slot_unit_index, small_params, small_first, small_second, step_count,
):
    img, core = lax.axis_index(CHIP), lax.axis_index("c")
    col, plane = img % 4, img // 4
    images = pixels.shape[0]
    slots = masters.shape[0]
    is_one = core == 1
    where = jnp.stack([col, core]).astype(jnp.int32)
    shuffle = shuffle_matrix()
    rows = small_params
    class_state = small_params[0] + small_params[1]

    def mine_of(pair):
        return jnp.where(is_one, pair[1], pair[0])

    def theirs_of(pair):
        return jnp.where(is_one, pair[0], pair[1])

    near = slots_near(slot_unit_index, img, slots)
    held = low(masters)
    ids = img * slots + jnp.arange(slots, dtype=jnp.int32)
    matches = [near[s : s + slots] == ids for s in range(2 * JITTER + 1)]
    middle = pick(held[6:26], [m[8:24] for m in matches], 16).reshape(256, WIDTH)
    one_a = hop(middle, [(0, 4), (1, 5), (2, 6), (5, 7)])
    partners = from_all(after(partner_emb, middle))
    before, behind = halo(after(held, middle), CHIPS, CHIP)
    lower = pick(jnp.concatenate([before, held[:10]]), [m[:8] for m in matches], 8)
    upper = pick(jnp.concatenate([held[22:], behind]), [m[24:] for m in matches], 8)
    outer = jnp.concatenate([lower, upper]).reshape(256, WIDTH)
    own_w = jnp.concatenate([outer[:128], middle, outer[128:]])
    class_hidden = low(layer_norm(class_state, small_params[R_GAIN1], small_params[R_SHIFT1]))
    class_half = mine_of(halves(class_hidden))
    query = dot(class_half[None], own_w)
    query = query + swap(query)
    wo_quarter = hop(own_w[384:], [(6, 7)]) + hop(own_w[:128], [(6, 4)])
    wo_quarter = wo_quarter + hop(own_w[128:256], [(6, 5)])
    wo_quarter = jnp.where(img == 6, own_w[256:384], wo_quarter)
    down_one = hop(
        own_w,
        [(12, 8), (13, 9), (14, 10), (11, 7), (8, 4), (9, 5), (10, 6), (7, 3)],
    )
    one_a, outer, query = together(one_a, outer, query)
    query = hop(query, [(3, 4)])
    one_b = hop(outer, [(0, 4), (1, 5), (2, 6), (5, 7)])
    two_a = hop(one_a, [(4, 8), (5, 9), (6, 10), (7, 11)])
    pix = prep(after(pixels, one_a), shuffle).reshape(2, images * SLOT, PIX // 2)
    corner = after(own_w[: PROJ // 2], one_a)
    corner = [corner] + [hop(corner, [(15, 15 ^ flip)]) for flip in (1, 2, 3)]
    query = low((query + small_params[R_SHIFT1 + 1 : R_SHIFT1 + 2]) * SCALE)
    query_heads = jnp.where(head_mask(HEADS), query, jnp.zeros((), BF))
    pulled = jnp.pad(low(dot(query_heads, own_w, NT)), ((0, 0), (0, WIDTH // 2)))
    one_b, two_a, wo_quarter, pulled, down_one = together(
        one_b, two_a, wo_quarter, pulled, down_one
    )
    mid_b = jnp.concatenate([one_b, wo_quarter, pulled])
    two_b = hop(mid_b, [(4, 8), (5, 9), (6, 10), (7, 11)])
    three_a = hop(
        jnp.where(img == 7, one_a, two_a), [(8, 12), (9, 13), (10, 14), (11, 15), (7, 3)]
    )
    low_b = hop(mid_b[256:], [(4, 0), (5, 1), (6, 2)])
    two_b, three_a, low_b, pix, partners, *corner = together(
        two_b, three_a, low_b, pix, partners, *corner
    )
    block_a = jnp.where(img < 3, middle, one_a + two_a + three_a)
    x_a, y_a = hop(block_a, FLIP_X), hop(block_a, FLIP_Y)
    three_b = hop(
        jnp.where(img == 7, mid_b, two_b), [(8, 12), (9, 13), (10, 14), (11, 15), (7, 3)]
    )
    pix_own, pix_send = mine_of(pix), theirs_of(pix)
    x_a, y_a, three_b, pix_own, pix_send = together(x_a, y_a, three_b, pix_own, pix_send)
    spot = jnp.stack([img, plane]).astype(jnp.int32)
    block_b = second_block(spot, [outer, low_b, mid_b, two_b, three_b])
    x_b, y_b = hop(block_b, FLIP_X), hop(block_b, FLIP_Y)
    down_two = hop(
        after(down_one, three_b), [(8, 4), (9, 5), (10, 6), (7, 3), (4, 0), (5, 1), (6, 2)]
    )
    proj_top = jnp.where(img == 15, corner[0], corner[1] + corner[2] + corner[3])
    (partners,) = call(
        partner_kernel, "partners", [], [partners], [shape((2 * CHIPS * images, PROJ), BF)]
    )
    up_one = hop(
        after(own_w, three_b), [(8, 12), (9, 13), (10, 14), (7, 11), (11, 15)]
    )
    peers_a = [swap(block_a), swap(x_a), swap(y_a), swap(block_b)]
    x_b, y_b, up_one, down_two, *peers_a = together(x_b, y_b, up_one, down_two, *peers_a)
    up_two = hop(up_one, [(11, 15)])
    proj_one = hop(after(proj_top, x_b), [(12, 4), (13, 5), (14, 6), (15, 7)])
    d_a, d_b = hop(y_a, FLIP_X), hop(x_b, FLIP_Y)
    down_three = hop(after(down_two, y_b), [(4, 0), (5, 1), (6, 2)])
    x_peer, y_peer = swap(x_b), swap(y_b)
    d_a, d_b, x_peer, y_peer = together(d_a, d_b, x_peer, y_peer)
    segments = [(source, ((0, 128, 256),), -1) for source in range(4)]
    segments += [(source, ((0, 0, 128), (128, 384, 128)), 256) for source in range(4)]
    own_pieces = [block_a, x_a, y_a, d_a, block_b, x_b, y_b, d_b]
    peer_pieces = [*peers_a[:3], swap(d_a), peers_a[3], x_peer, y_peer, swap(d_b)]
    pix_peer = swap(pix_send)
    valid = jnp.concatenate(
        [
            keep_mask,
            jnp.ones((images, 1), jnp.int32),
            jnp.zeros((images, SLOT - TOKS), jnp.int32),
        ],
        axis=1,
    ).reshape(images * SLOT, 1)
    (
        hid, xhat, rstd, p, pooled, mass, wv, wo, qk, resid, hidden_sent,
    ) = forward_call(
        segments, images, where, pix, own_pieces, peer_pieces, rows, valid, shuffle
    )
    pooled_own = mine_of(pooled)
    pooled_peer = swap(theirs_of(pooled))

    hidden_all = in_plane(hidden_sent)
    hidden_all, pooled_peer = together(hidden_all, pooled_peer)
    ff_block = (col + 1) % 4
    bias_part = lax.dynamic_slice(
        small_params[R_SHIFT2 + 1 : R_C2].reshape(4, 32, 2, 16),
        (ff_block, 0, core, 0),
        (1, 32, 1, 16),
    ).reshape(1, 512)
    candidates = [own_w, up_one, up_two, down_one, down_two, down_three]
    pick_one = choose(
        img, [((15,), 2), ((12, 13, 14, 11), 1), ((4, 5, 6, 3), 3), ((0, 1, 2), 4)], 0
    )
    pick_two = choose(
        img, [((15,), 1), ((8, 9, 10, 7), 3), ((4, 5, 6, 3), 4), ((0, 1, 2), 5)], 0
    )
    picks = jnp.stack([pick_one, pick_two]).astype(jnp.int32)
    preact, active, part = ff_call(
        ff_kernel, "ff", picks, [hidden_all, bias_part], candidates,
        [shape((8 * images, 512), F32), shape((8 * images, 512), BF), shape((8, images, WIDTH), BF)],
    )
    proj_mid = hop(
        after(jnp.where(plane == 3, proj_top, proj_one), hidden_sent),
        [(12, 8), (13, 9), (14, 10), (15, 11), (4, 0), (5, 1), (6, 2), (7, 3)],
    )
    hidden_all = in_plane(hidden_sent)
    ff_block = (col + 1) % 4
    bias_part = lax.dynamic_slice(
        small_params[R_SHIFT2 + 1 : R_C2].reshape(4, 32, 2, 16),
        (ff_block, 0, core, 0),
        (1, 32, 1, 16),
    ).reshape(1, 512)
    candidates = [own_w, up_one, up_two, down_one, down_two, down_three]
    pick_one = choose(
        img, [((15,), 2), ((12, 13, 14, 11), 1), ((4, 5, 6, 3), 3), ((0, 1, 2), 4)], 0
    )
    pick_two = choose(
        img, [((15,), 1), ((8, 9, 10, 7), 3), ((4, 5, 6, 3), 4), ((0, 1, 2), 5)], 0
    )
    picks = jnp.stack([pick_one, pick_two]).astype(jnp.int32)
    preact, active, part = ff_call(
        ff_kernel, "ff", picks, [hidden_all, bias_part], candidates,
        [shape((8 * images, 512), F32), shape((8 * images, 512), BF), shape((8, images, WIDTH), BF)],
    )
    proj = choose(
        plane, [((3,), proj_top), ((1,), proj_one)], after(proj_mid, hidden_sent)
    )
    proj_peer = swap(proj)
    part = in_plane(part)
    proj = choose(plane, [((3,), proj_top), ((1,), proj_one)], after(proj_mid, part))
    proj_peer = swap(proj)
    d_state, d_state_sent, head_vec = call(
        head_kernel, "head", [where],
        [part, resid, proj, proj_peer, partners, partner_index[:, None], rows],
        [
            shape((images, WIDTH), F32), shape((8, images, 2 * WIDTH + PROJ), BF),
            shape((8, WIDTH), F32),
        ],
        [pltpu.VMEM((images, PROJ), BF)],
    )
    d_state_all = in_plane(d_state_sent)
    d_preact, d_preact_sum, part = ff_call(
        ff_back_kernel, "ff_back", picks, [d_state_all, preact], candidates,
        [shape((8 * images, 512), BF), shape((1, 512), F32), shape((8, images, WIDTH), BF)],
    )
    part = in_plane(part)

    d_embed, d_attended, d_resid, d_pos, d_vec, pull = backward_call(
        images, where,
        [part, d_state, resid, wo, wv, hid, xhat, rstd, p, mass, qk, rows, shuffle],
    )
    arrays = [
        pix_own, pix_peer, d_embed, swap(d_embed), pooled_own, pooled_peer, d_attended,
        swap(d_attended),
    ]
    far_x, far_y = embed_grad_call(
        images, "embed_grad_far", [(3, 0, 256, BF), (3, 256, 256, BF)], where, arrays
    )
    got_y, got_x = hop(far_x, FLIP_X), hop(far_y, FLIP_Y)
    own_part, x_low, x_high, y_low, y_high = embed_grad_call(
        images, "embed_grad_near",
        [(0, 0, 512, F32), (1, 0, 256, BF), (1, 256, 256, F32), (2, 0, 256, F32), (2, 256, 256, BF)],
        after(where, far_x), arrays,
    )
    d_resid = in_plane(after(d_resid, far_x))
    d_pos, d_vec, head_vec, d_preact_sum, pull, _ = together(
        d_pos, d_vec, head_vec, d_preact_sum, pull, far_x
    )
    (small_sent,) = call(
        collect_kernel, "collect", [where], [d_pos, d_vec, head_vec, d_preact_sum, pull, shuffle],
        [shape((32, 3, WIDTH), F32)], [pltpu.VMEM((96, WIDTH), F32)],
    )
    got_x, got_y, own_part, x_low, x_high, y_low, y_high, d_resid, small_sent = together(
        got_x, got_y, own_part, x_low, x_high, y_low, y_high, d_resid, small_sent
    )
    part_x, part_y = add_far([x_low, x_high, got_x, y_low, got_y, y_high])
    part_x, part_y = part_x.reshape(512, WIDTH), part_y.reshape(512, WIDTH)
    sum_x, sum_y = hop(part_x, FLIP_X), hop(part_y, FLIP_Y)
    shares = lax.all_to_all(small_sent, ALL, 0, 0, tiled=True)
    (ff_rows,) = call(
        rows_kernel, "rows", [where], [active, d_preact, hidden_all, d_state_all, d_resid],
        [shape((8 * images, 5 * WIDTH), BF)],
    )
    rise = [(i, i + 4) for i in range(12)]
    fall = [(12, 8), (13, 9), (14, 10), (15, 11), (10, 6), (11, 7)]
    up_one, down_one = hop(ff_rows, rise), hop(ff_rows, fall)
    sum_x, sum_y = together(sum_x, sum_y)
    total = own_part + sum_x.astype(F32) + sum_y.astype(F32)
    sent = low(total)
    first = hop(sent, [(12, 8), (13, 9), (14, 10), (15, 11), (4, 0), (5, 1), (6, 2)])
    aside = hop(sent, [(3, 1), (7, 5)])
    (small_sent,) = call(share_kernel, "share", [], [shares], [shape((32, 3, WIDTH), F32)])
    shares = lax.all_to_all(small_sent, ALL, 0, 0, tiled=True)
    up_two, down_two = hop(up_one, rise[4:]), hop(down_one, fall[4:])
    first, aside, up_two, down_two, total = together(first, aside, up_two, down_two, total)
    partial = low(total + first.astype(F32))
    second = hop(partial, [(8, 0), (9, 1), (10, 2), (11, 5)])
    third = hop(aside, [(1, 5)])
    up_three = hop(up_two, rise[8:])
    d_query, pull_half, small_total = call(
        query_back_kernel, "query_back", [core.reshape(1).astype(jnp.int32)],
        [shares, own_w, shuffle],
        [shape((8, WIDTH), F32), shape((HEADS, WIDTH // 2), F32), shape((96, WIDTH), F32)],
    )
    loss = small_total[R_SMALL + HEADS, 0]
    d_query = d_query[0:1]
    d_query = d_query + swap(d_query)
    d_query = hop(d_query, [(4, 3)])
    toward = dot(low(d_query), own_w, NT)

    every = [ff_rows, up_one, up_two, up_three, down_one, down_two]
    class_rows = jnp.concatenate([class_half[None], jnp.zeros((7, WIDTH // 2), BF)])
    role = jnp.stack([img, core]).astype(jnp.int32)
    (formed,) = call(
        owner_kernel, "owner", [role], [pull_half, query_heads, class_rows, d_query, *every],
        [shape((512, WIDTH), F32)],
    )
    edge = shape((JITTER * 16, WIDTH), F32)
    own_grad, top, end, report = call(
        finish_kernel, "finish", [role],
        [formed, d_query, toward, total, first, second, aside, third],
        [shape((512, WIDTH), F32), edge, edge, shape((1, WIDTH + 640), F32)],
    )
    reports = from_all(report)
    before = hop(end, [(i, i + 1) for i in range(CHIPS - 1)]).reshape(JITTER, 16, WIDTH)
    behind = hop(top, [(i + 1, i) for i in range(CHIPS - 1)]).reshape(JITTER, 16, WIDTH)
    small_grad, norm = call(
        complete_kernel, "complete", [], [small_total, reports, rows, shuffle],
        [shape((R_SMALL, WIDTH), F32), shape((8, 128), F32)],
    )
    grad_norm = norm[0, 0]
    factor = 1.0 / jnp.maximum(grad_norm, 1.0)
    own_grad = own_grad.reshape(slots, 16, WIDTH)
    here = near[JITTER : JITTER + slots]
    source = jnp.where(here < UNIT_COUNT, here - img * slots, -100)
    step_value = step_count.astype(F32)
    scalars = jnp.stack(
        [
            factor,
            1.0 / (1.0 - jnp.power(BETA_ONE, step_value)),
            1.0 / (1.0 - jnp.power(BETA_TWO, step_value)),
        ]
    )
    new_masters, new_first, new_second = update_call(
        source, scalars, before, own_grad, behind, masters, first_moment_slots,
        second_moment_slots,
    )
    new_small, new_small_first, new_small_second = adamw(
        small_params, small_grad * factor, small_first, small_second, step_value
    )
    return (
        new_masters, new_first, new_second, new_small, new_small_first, new_small_second,
        loss, grad_norm,
    )


def per_device_any(
    pixels, keep_mask, partner_index, partner_emb, masters, first_moment_slots,
    second_moment_slots, slot_unit_index, small_params, small_first, small_second, step_count,
):
    chips, seq = lax.axis_size("img"), lax.axis_size("seq")
    img = lax.axis_index("img")
    images = pixels.shape[0]
    slots, part = masters.shape[0], masters.shape[1]
    near = slots_near(slot_unit_index, img, slots)
    own_w = to_units(low(masters), near, img, chips)
    gathered = lax.all_gather(own_w, ("img", "seq"), axis=0, tiled=False)
    flat = gathered.reshape(chips, seq, slots, part, WIDTH).transpose(0, 2, 1, 3, 4)
    flat = flat.reshape(chips * slots * ROWS_PER_UNIT, WIDTH)
    bounds = [0, PIX, WIDTH, WIDTH, WIDTH, WIDTH, FF, FF, PROJ]
    parts, offset = [], 0
    for size in bounds[1:]:
        parts.append(flat[offset : offset + size])
        offset += size
    embed_w, query_w, key_w, value_w, output_w, fc_in_w, fc_out_w, proj_w = parts
    (
        class_row, pos_rows, patch_bias, gain_one, shift_one, query_bias, value_bias, out_bias,
        gain_two, shift_two, fc_in_bias, fc_out_bias, gain_end, shift_end,
    ) = small_parts(small_params)
    class_state = class_row + pos_rows[0]
    embedded = jnp.einsum("itp,pd->itd", pixels, embed_w, preferred_element_type=F32)
    tokens = jnp.concatenate(
        [
            jnp.broadcast_to(class_state, (images, 1, WIDTH)),
            embedded + patch_bias + pos_rows[1:],
        ],
        axis=1,
    )
    hidden = low(layer_norm(tokens, gain_one, shift_one))
    class_hidden = hidden[0, 0]
    mask16 = head_mask(HEADS)
    query = low((dot(class_hidden[None], query_w)[0] + query_bias) * SCALE)
    query_heads = jnp.where(mask16, query[None], jnp.zeros((), BF))
    qk = low(dot(query_heads, key_w, NT))
    scores = jnp.einsum("hd,itd->iht", qk, hidden, preferred_element_type=F32)
    keep = jnp.concatenate([jnp.ones((images, 1), jnp.int32), keep_mask], axis=1)
    scores = jnp.where(keep[:, None, :] > 0, scores, MASKED)
    weights = jax.nn.softmax(scores, axis=-1)
    weights_low = low(weights)
    pooled = low(jnp.einsum("iht,itd->ihd", weights_low, hidden, preferred_element_type=F32))
    mass = jnp.sum(weights_low.astype(F32), axis=-1)
    mixed = dot(pooled.reshape(-1, WIDTH), value_w).reshape(images, HEADS, WIDTH)
    mixed = mixed + mass[:, :, None] * value_bias
    attended = low(jnp.sum(jnp.where(mask16, mixed, 0.0), axis=1))
    resid = class_state + dot(attended, output_w) + out_bias
    hidden_two = low(layer_norm(resid, gain_two, shift_two))
    preact = dot(hidden_two, fc_in_w, NT) + fc_in_bias
    active = low(exact_gelu(preact))
    state = resid + dot(active, fc_out_w) + fc_out_bias
    final = low(layer_norm(state, gain_end, shift_end))
    projected = dot(final, proj_w, NT)
    unit = low(normalize(projected))
    partners = lax.all_gather(partner_emb, ("img", "seq"), axis=0, tiled=True)
    count = partners.shape[0]
    logits = dot(unit, partners, NT) / SOFTMAX_SCALE
    onehot = (jnp.arange(count, dtype=jnp.int32)[None] == partner_index[:, None]).astype(F32)
    total = jax.nn.logsumexp(logits, axis=-1)
    loss_part = jnp.sum(total - jnp.sum(logits * onehot, axis=-1)) / count
    d_logits = (jax.nn.softmax(logits, axis=-1) - onehot) / count
    d_unit = dot(low(d_logits / SOFTMAX_SCALE), partners)
    d_projected = low(jax.vjp(normalize, projected)[1](d_unit)[0])
    d_final = dot(d_projected, proj_w)
    d_state, d_gain_end, d_shift_end = jax.vjp(layer_norm, state, gain_end, shift_end)[1](d_final)
    d_state_low = low(d_state)
    d_active = dot(d_state_low, fc_out_w, NT)
    d_preact = low(jax.vjp(exact_gelu, preact)[1](d_active)[0])
    d_hidden_two = dot(d_preact, fc_in_w)
    d_norm, d_gain_two, d_shift_two = jax.vjp(layer_norm, resid, gain_two, shift_two)[1](
        d_hidden_two
    )
    d_resid = d_state + d_norm
    d_resid_low = low(d_resid)
    d_attended = low(dot(d_resid_low, output_w, NT))
    wide = jnp.where(mask16, d_attended[:, None, :], jnp.zeros((), BF))
    d_pooled = low(dot(wide.reshape(-1, WIDTH), value_w, NT)).reshape(images, HEADS, WIDTH)
    d_weights = jnp.einsum("ihd,itd->iht", d_pooled, hidden, preferred_element_type=F32)
    d_weights = d_weights + jnp.sum(wide.astype(F32) * value_bias, axis=-1)[:, :, None]
    d_scores = low(weights * (d_weights - jnp.sum(weights * d_weights, axis=-1, keepdims=True)))
    d_hidden = jnp.einsum("iht,ihd->itd", weights_low, d_pooled, preferred_element_type=F32)
    d_hidden = d_hidden + jnp.einsum("iht,hd->itd", d_scores, qk, preferred_element_type=F32)
    pull = jnp.einsum("iht,itd->hd", d_scores, hidden, preferred_element_type=F32)
    d_query = jnp.sum(jnp.where(mask16, dot(low(pull), key_w), 0.0), axis=0) * SCALE
    d_class_hidden = dot(low(d_query)[None], query_w, NT)
    d_tokens, d_gain_one, d_shift_one = jax.vjp(layer_norm, tokens, gain_one, shift_one)[1](
        d_hidden
    )
    d_class, d_gain_cls, d_shift_cls = jax.vjp(layer_norm, class_state[None], gain_one, shift_one)[
        1
    ](d_class_hidden)
    d_class = d_class[0] + jnp.sum(d_tokens[:, 0], axis=0) + jnp.sum(d_resid, axis=0)
    d_patch = d_tokens[:, 1:]
    d_embed_w = jnp.einsum("itp,itd->pd", pixels, low(d_patch), preferred_element_type=F32)
    d_value_w = dot(pooled.reshape(-1, WIDTH), wide.reshape(-1, WIDTH), TN)
    d_key_w = dot(pull, query_heads.astype(F32), TN, precision=lax.Precision.HIGHEST)
    small_local = jnp.concatenate(
        [
            d_class[None],
            d_class[None],
            jnp.sum(d_patch, axis=0),
            jnp.sum(d_patch, axis=(0, 1))[None],
            (d_gain_one + d_gain_cls)[None],
            (d_shift_one + d_shift_cls)[None],
            d_query[None],
            jnp.sum(wide.astype(F32) * mass[:, :, None], axis=(0, 1))[None],
            jnp.sum(d_resid, axis=0)[None],
            d_gain_two[None],
            d_shift_two[None],
            jnp.sum(d_preact.astype(F32), axis=0).reshape(FF // WIDTH, WIDTH),
            jnp.sum(d_state, axis=0)[None],
            d_gain_end[None],
            d_shift_end[None],
        ],
        axis=0,
    )
    grad_table = jnp.concatenate(
        [
            d_embed_w,
            class_hidden.astype(F32)[:, None] * d_query[None, :],
            d_key_w,
            d_value_w,
            dot(attended, d_resid_low, TN),
            dot(d_preact, hidden_two, TN),
            dot(active, d_state_low, TN),
            dot(d_projected, final, TN),
            jnp.zeros(((chips * slots - UNIT_COUNT) * ROWS_PER_UNIT, WIDTH), F32),
        ],
        axis=0,
    ).reshape(chips * slots, ROWS_PER_UNIT, WIDTH)
    small_grad, loss = lax.psum((small_local, loss_part), ("img", "seq"))
    core_half = lax.psum_scatter(low(grad_table), "seq", scatter_dimension=1, tiled=True)
    own_grad = lax.psum_scatter(core_half.astype(F32), "img", scatter_dimension=0, tiled=True)
    owner_total = lax.psum(jnp.sum(own_grad * own_grad), ("img", "seq"))
    grad_norm = jnp.sqrt(owner_total + jnp.sum(small_grad * small_grad))
    factor = 1.0 / jnp.maximum(grad_norm, 1.0)
    slot_grad = to_slots(own_grad, near, img, chips)
    step_value = step_count.astype(F32)
    new_masters, new_first, new_second = adamw(
        masters, slot_grad * factor, first_moment_slots, second_moment_slots, step_value
    )
    new_small, new_small_first, new_small_second = adamw(
        small_params, small_grad * factor, small_first, small_second, step_value
    )
    return (
        new_masters, new_first, new_second, new_small, new_small_first, new_small_second,
        loss, grad_norm,
    )


def solution(mesh):
    chip, devices = "img", ("img", "seq")
    core, body = "seq", per_device_any
    if mesh.shape["img"] == CHIPS and mesh.shape["seq"] == 2:
        mesh = jax.sharding.Mesh(mesh.devices.reshape(4, 2, 2, 2), ALL)
        chip, devices, core, body = CHIP, ALL, "c", per_device_16
    weights = P(chip, core, None)
    return jax.shard_map(
        body,
        mesh=mesh,
        in_specs=(
            P(devices, None, None),
            P(devices, None),
            P(devices),
            P(devices, None),
            weights,
            weights,
            weights,
            P(),
            P(),
            P(),
            P(),
            P(),
        ),
        out_specs=(weights, weights, weights, P(), P(), P(), P(), P()),
        check_vma=False,
    )
```

```python
import functools
import math

import jax
import jax.numpy as jnp
from jax import lax
from jax.experimental import pallas as pl
from jax.experimental.pallas import tpu as pltpu
from jax.sharding import PartitionSpec as P

WIDTH = 1024
HEADS = 16
HEAD_DIM = 64
FF = 4096
PIX = 3072
PROJ = 768
TOKS = 50
PATCHES = TOKS - 1
ROWS_PER_UNIT = 32
UNIT_COUNT = 504
JITTER = 2

EPS_NORM = 1e-06
SOFTMAX_SCALE = 0.07
LEARN_RATE = 0.03
BETA_ONE = 0.5
BETA_TWO = 0.5
DECAY_RATE = 0.05
ADAM_EPS = 1e-08
MASKED = -1000000000.0
SCALE = HEAD_DIM ** (-0.5)

F32 = jnp.float32
BF = jnp.bfloat16
ROW_BASE = 1 + TOKS
ROW_TAIL = ROW_BASE + 8 + FF // WIDTH
SLOT = 64


def low(values):
    return values.astype(BF)


def dot(a, b, dims=((1,), (0,)), precision=None):
    return lax.dot_general(a, b, (dims, ((), ())), precision=precision, preferred_element_type=F32)


NN = ((1,), (0,))
NT = ((1,), (1,))
TN = ((0,), (0,))


def layer_norm(values, gain, shift):
    center = values - jnp.mean(values, axis=-1, keepdims=True)
    spread = jnp.mean(center * center, axis=-1, keepdims=True)
    return center * lax.rsqrt(spread + EPS_NORM) * gain + shift


def normalize(values):
    return values * lax.rsqrt(jnp.sum(values * values, axis=-1, keepdims=True) + EPS_NORM)


def exact_gelu(values):
    return jax.nn.gelu(values, approximate=False)


def small_parts(small):
    base, tail = ROW_BASE, ROW_TAIL
    return (
        small[0],
        small[1:base],
        small[base],
        small[base + 1],
        small[base + 2],
        small[base + 3],
        small[base + 4],
        small[base + 5],
        small[base + 6],
        small[base + 7],
        small[base + 8 : tail].reshape(FF),
        small[tail],
        small[tail + 1],
        small[tail + 2],
    )


def adamw(weight, grad, first, second, step):
    first_new = BETA_ONE * first + (1.0 - BETA_ONE) * grad
    second_new = BETA_TWO * second + (1.0 - BETA_TWO) * grad * grad
    first_hat = first_new / (1.0 - jnp.power(BETA_ONE, step))
    second_hat = second_new / (1.0 - jnp.power(BETA_TWO, step))
    weight_new = weight - LEARN_RATE * (
        first_hat / (jnp.sqrt(second_hat) + ADAM_EPS) + DECAY_RATE * weight
    )
    return (weight_new, first_new, second_new)


def halo(values, chips, axes):
    before = lax.ppermute(values[-JITTER:], axes, [(i, i + 1) for i in range(chips - 1)])
    behind = lax.ppermute(values[:JITTER], axes, [(i + 1, i) for i in range(chips - 1)])
    return before, behind


def with_halo(values, chips, axes):
    before, behind = halo(values, chips, axes)
    return jnp.concatenate([before, values, behind], axis=0)


def slots_near(slot_unit_index, img, slots):
    padded = jnp.pad(slot_unit_index, (JITTER, JITTER), constant_values=-1)
    return lax.dynamic_slice(padded, (img * slots,), (slots + 2 * JITTER,))


def pick(ext, matches, slots):
    out = jnp.zeros((slots,) + ext.shape[1:], ext.dtype)
    for shift in range(2 * JITTER + 1):
        out = jnp.where(matches[shift][:, None, None], ext[shift : shift + slots], out)
    return out


def to_units(values, near, img, chips, axes="img"):
    slots = values.shape[0]
    ids = img * slots + jnp.arange(slots, dtype=jnp.int32)
    matches = [near[s : s + slots] == ids for s in range(2 * JITTER + 1)]
    return pick(with_halo(values, chips, axes), matches, slots)


def to_slots(values, near, img, chips, axes="img"):
    slots = values.shape[0]
    here = near[JITTER : JITTER + slots]
    ids = img * slots + jnp.arange(slots, dtype=jnp.int32)
    matches = [
        (here == ids + (s - JITTER)) & (here < UNIT_COUNT) for s in range(2 * JITTER + 1)
    ]
    return pick(with_halo(values, chips, axes), matches, slots)


def shuffle_matrix():
    source = lax.broadcasted_iota(jnp.int32, (256, 256), 0)
    target = lax.broadcasted_iota(jnp.int32, (256, 256), 1)
    moved = ((source // 16) % 2) * 128 + (source // 32) * 16 + source % 16
    return (moved == target).astype(F32).astype(BF)


def vmem():
    return pl.BlockSpec(memory_space=pltpu.VMEM)


def smem():
    return pl.BlockSpec(memory_space=pltpu.SMEM)


def shape(dims, dtype):
    return jax.ShapeDtypeStruct(dims, dtype)


def call(kernel, name, scalars, arrays, outs, scratch=(), mib=16, flops=10**9, far=()):
    moved = sum(a.size * a.dtype.itemsize for a in [*arrays, *outs, *far])
    return pl.pallas_call(
        kernel,
        in_specs=[smem()] * len(scalars)
        + [vmem()] * len(arrays)
        + [pl.BlockSpec(memory_space=pl.ANY)] * len(far),
        out_specs=[vmem()] * len(outs),
        out_shape=list(outs),
        scratch_shapes=list(scratch),
        compiler_params=pltpu.CompilerParams(vmem_limit_bytes=mib * 2**20),
        cost_estimate=pl.CostEstimate(flops=flops, bytes_accessed=moved, transcendentals=0),
        name=name,
    )(*scalars, *arrays, *far)


def prep_kernel(pix_ref, shuffle_ref, out_ref):
    shuffle = shuffle_ref[...]
    out_ref[...] = jnp.zeros_like(out_ref)
    for block in range(PIX // 256):
        moved = dot(pix_ref[0, :, 256 * block : 256 * block + 256], shuffle).astype(BF)
        out_ref[0, 0, :PATCHES, 128 * block : 128 * block + 128] = moved[:, :128]
        out_ref[1, 0, :PATCHES, 128 * block : 128 * block + 128] = moved[:, 128:]


def prep(pixels, shuffle):
    images = pixels.shape[0]
    return pl.pallas_call(
        prep_kernel,
        grid=(images,),
        in_specs=[
            pl.BlockSpec((1, PATCHES, PIX), lambda i: (i, 0, 0)),
            pl.BlockSpec((256, 256), lambda i: (0, 0)),
        ],
        out_specs=pl.BlockSpec((2, 1, SLOT, PIX // 2), lambda i: (0, i, 0, 0)),
        out_shape=jax.ShapeDtypeStruct((2, images, SLOT, PIX // 2), BF),
        compiler_params=pltpu.CompilerParams(vmem_limit_bytes=24 * 2**20),
        cost_estimate=pl.CostEstimate(flops=8 * 10**8, bytes_accessed=6 * 2**20, transcendentals=0),
        name="prep",
    )(pixels, shuffle)


def head_mask(rows):
    lane = lax.broadcasted_iota(jnp.int32, (rows, WIDTH), 1) // HEAD_DIM
    row = lax.broadcasted_iota(jnp.int32, (rows, WIDTH), 0) % HEADS
    return lane == row


def norm_parts(values):
    center = values - jnp.mean(values, axis=-1, keepdims=True)
    rstd = lax.rsqrt(jnp.mean(center * center, axis=-1, keepdims=True) + EPS_NORM)
    return center * rstd, rstd


def norm_back(grad, gain, xhat, rstd):
    gy = grad * gain
    return rstd * (
        gy - jnp.mean(gy, axis=-1, keepdims=True) - xhat * jnp.mean(gy * xhat, axis=-1, keepdims=True)
    )


def rowsum(values):
    return jnp.sum(values, axis=0, keepdims=True)


def to_halves(values, shuffle):
    first, second = [], []
    for block in range(values.shape[1] // 256):
        moved = low(dot(values[:, 256 * block : 256 * block + 256], shuffle))
        first.append(moved[:, :128])
        second.append(moved[:, 128:])
    return jnp.concatenate(first, axis=1), jnp.concatenate(second, axis=1)


def to_natural(first, second, shuffle):
    out = []
    for block in range(first.shape[1] // 128):
        lanes = slice(128 * block, 128 * block + 128)
        both = jnp.concatenate([first[:, lanes], second[:, lanes]], axis=1)
        out.append(low(dot(both, shuffle, NT)))
    return jnp.concatenate(out, axis=1)


R_PATCH, R_GAIN1, R_SHIFT1, R_VB, R_OB, R_GAIN2, R_SHIFT2 = 51, 52, 53, 55, 56, 57, 58
R_C2, R_GAINF, R_SHIFTF, R_SMALL = 63, 64, 65, 66
QUARTER = 128


def partner_kernel(raw_ref, out_ref):
    source = lax.broadcasted_iota(jnp.int32, (PROJ, PROJ), 0)
    target = lax.broadcasted_iota(jnp.int32, (PROJ, PROJ), 1)
    moved = ((source // 16) % 2) * (PROJ // 2) + (source // 32) * 16 + source % 16
    select = low((moved == target).astype(F32))
    out_ref[...] = low(dot(raw_ref[...].reshape(-1, PROJ), select))


def second_block_kernel(
    role_ref, outer_ref, low_ref, mid_ref, two_ref, three_ref, out_ref, held_ref, sems
):
    chip, plane = role_ref[0], role_ref[1]

    @pl.when(chip < 3)
    def _():
        head = pltpu.make_async_copy(outer_ref, held_ref.at[pl.ds(0, 256)], sems.at[0])
        tail = pltpu.make_async_copy(low_ref, held_ref.at[pl.ds(256, QUARTER + HEADS)], sems.at[1])
        head.start()
        tail.start()
        head.wait()
        tail.wait()

    for number, ref in ((1, mid_ref), (2, two_ref), (3, three_ref)):
        here = (plane == number) | (chip == 3) if number == 3 else plane == number

        @pl.when(here)
        def _():
            whole = pltpu.make_async_copy(ref, held_ref, sems.at[0])
            whole.start()
            whole.wait()

    out = pltpu.make_async_copy(held_ref, out_ref, sems.at[0])
    out.start()
    out.wait()


def second_block(role, pieces):
    any_place = pl.BlockSpec(memory_space=pl.ANY)
    return pl.pallas_call(
        second_block_kernel,
        in_specs=[smem()] + [any_place] * len(pieces),
        out_specs=pl.BlockSpec(memory_space=pltpu.HBM),
        out_shape=shape((256 + QUARTER + HEADS, WIDTH), BF),
        scratch_shapes=[
            pltpu.VMEM((256 + QUARTER + HEADS, WIDTH), BF),
            pltpu.SemaphoreType.DMA((2,)),
        ],
        compiler_params=pltpu.CompilerParams(vmem_limit_bytes=58 * 2**20),
        cost_estimate=pl.CostEstimate(flops=0, bytes_accessed=2 * 2**20, transcendentals=0),
        name="second_block",
    )(role, *pieces)


def forward_kernel(segments, images, where_ref, pix_ref, rows_ref, valid_ref, shuffle_ref, *refs):
    count = len(segments)
    own, peer = refs[:count], refs[count : 2 * count]
    (
        hid_ref, xhat_ref, rstd_ref, p_ref, pooled_ref, mass_ref, wv_ref, wo_ref, qk_ref,
        resid_ref, low_ref, acc_ref, pool_ref, half_ref, table_ref, sems,
    ) = refs[2 * count :]
    col, core = where_ref[0], where_ref[1]
    waits = ([], [])
    for flip, group in ((0, own), (1, peer)):
        half = core ^ flip
        for (source, parts, late), ref in zip(segments, group):
            block = col ^ source
            for row, lane, rows in parts:
                part = ref.at[pl.ds(row, rows)]
                line = pl.multiple_of(block * 512 + lane, 128)
                copy = pltpu.make_async_copy(part, table_ref.at[half, pl.ds(line, rows)], sems.at[flip])
                copy.start()
                waits[flip].append(copy)
            if late >= 0:
                part = ref.at[pl.ds(late, QUARTER)]
                line = pl.multiple_of(block * QUARTER, QUARTER)
                copy = pltpu.make_async_copy(part, wo_ref.at[half, pl.ds(line, QUARTER)], sems.at[2])
                copy.start()
                waits[1].append(copy)
                part = ref.at[pl.ds(late + QUARTER, HEADS)]
                copy = pltpu.make_async_copy(part, half_ref.at[half, block], sems.at[3])
                copy.start()
                waits[1].append(copy)
    patch = rows_ref[2 : 1 + TOKS] + rows_ref[R_PATCH : R_PATCH + 1]
    class_state = rows_ref[0:1] + rows_ref[1:2]
    for i in range(images):
        acc_ref[SLOT * i : SLOT * i + PATCHES] = patch
        acc_ref[SLOT * i + PATCHES : SLOT * i + TOKS] = class_state
        acc_ref[SLOT * i + TOKS : SLOT * (i + 1)] = jnp.zeros((SLOT - TOKS, WIDTH), F32)
    for copy in waits[0]:
        copy.wait()
    acc_ref[...] += dot(pix_ref[core], table_ref[core, :1536])
    for copy in waits[1]:
        copy.wait()
    acc_ref[...] += dot(pix_ref[1 - core], table_ref[1 - core, :1536])
    wv_ref[...] = table_ref[:, 1536:]
    shuffle = shuffle_ref[...]
    gain, shift, value_bias = (rows_ref[r : r + 1] for r in (R_GAIN1, R_SHIFT1, R_VB))
    half = WIDTH // 2
    qk = to_natural(half_ref[0, 0, :, :half], half_ref[1, 0, :, :half], shuffle)
    qk_ref[...] = qk
    valid = valid_ref[...] > 0
    for i in range(images):
        part = slice(SLOT * i, SLOT * (i + 1))
        xhat, rstd = norm_parts(acc_ref[part])
        hid = low(xhat * gain + shift)
        xhat_ref[part] = xhat
        rstd_ref[part] = jnp.broadcast_to(rstd, (SLOT, 128))
        hid_ref[part] = hid
        scores = jnp.where(valid[part], dot(hid, qk, NT), MASKED)
        e = jnp.exp(scores - jnp.max(scores, axis=0, keepdims=True))
        p = e / jnp.sum(e, axis=0, keepdims=True)
        p_ref[part] = p
        pb = low(p)
        pool_ref[HEADS * i : HEADS * (i + 1)] = low(dot(pb, hid, TN))
        mass_ref[HEADS * i : HEADS * (i + 1)] = dot(pb, jnp.ones((SLOT, 128), BF), TN)
    pooled_ref[0], pooled_ref[1] = to_halves(pool_ref[...], shuffle)
    rows = images * HEADS
    mixed = dot(pooled_ref[0], wv_ref[0]) + dot(pooled_ref[1], wv_ref[1])
    mixed = mixed + mass_ref[:, 0:1] * value_bias
    mixed = jnp.where(head_mask(rows), mixed, 0.0)
    joined = low(jnp.sum(mixed.reshape(images, HEADS, WIDTH), axis=1))
    first, second = to_halves(joined, shuffle)
    resid = class_state + dot(first, wo_ref[0]) + dot(second, wo_ref[1])
    resid = resid + rows_ref[R_OB : R_OB + 1]
    resid_ref[...] = resid
    xhat, _ = norm_parts(resid)
    hidden = low(xhat * rows_ref[R_GAIN2 : R_GAIN2 + 1] + rows_ref[R_SHIFT2 : R_SHIFT2 + 1])
    sent = jnp.concatenate([hidden, first, second], axis=1)
    low_ref[...] = jnp.broadcast_to(sent[None], low_ref.shape)


def forward_call(segments, images, where, pix, own, peer, rows, valid, shuffle):
    tokens = images * SLOT
    outs = [
        shape((tokens, WIDTH), BF),
        shape((tokens, WIDTH), F32),
        shape((tokens, 128), F32),
        shape((tokens, HEADS), F32),
        shape((2, images * HEADS, WIDTH // 2), BF),
        shape((images * HEADS, 128), F32),
        shape((2, WIDTH // 2, WIDTH), BF),
        shape((2, WIDTH // 2, WIDTH), BF),
        shape((HEADS, WIDTH), BF),
        shape((images, WIDTH), F32),
        shape((8, images, 2 * WIDTH), BF),
    ]
    scratch = [
        pltpu.VMEM((tokens, WIDTH), F32),
        pltpu.VMEM((images * HEADS, WIDTH), BF),
        pltpu.VMEM((2, 4, HEADS, WIDTH), BF),
        pltpu.VMEM((2, 2048, WIDTH), BF),
        pltpu.SemaphoreType.DMA((4,)),
    ]
    return call(
        functools.partial(forward_kernel, segments, images), "forward", [where],
        [pix, rows, valid, shuffle], outs, scratch, mib=52, flops=4 * 10**9,
        far=[*own, *peer],
    )


def fetch(pick_ref, slot, candidates, out_ref, sem):
    for number, candidate in enumerate(candidates):

        @pl.when(pick_ref[slot] == number)
        def _():
            pltpu.make_async_copy(candidate, out_ref, sem).start()


def arrived(candidate, out_ref, sem):
    pltpu.make_async_copy(candidate, out_ref, sem).wait()


def ff_kernel(pick_ref, hid_ref, bias_ref, *refs):
    candidates, (pre_ref, act_ref, part_ref, w1_ref, w2_ref, sems) = refs[:6], refs[6:]
    fetch(pick_ref, 0, candidates, w1_ref, sems.at[0])
    fetch(pick_ref, 1, candidates, w2_ref, sems.at[1])
    hidden = hid_ref[:, :, :WIDTH].reshape(-1, WIDTH)
    arrived(candidates[0], w1_ref, sems.at[0])
    pre = dot(hidden, w1_ref[...], NT) + bias_ref[...]
    pre_ref[...] = pre
    active = low(0.5 * pre * (1.0 + lax.erf(pre * (0.5**0.5))))
    act_ref[...] = active
    arrived(candidates[0], w2_ref, sems.at[1])
    part_ref[...] = low(dot(active, w2_ref[...])).reshape(part_ref.shape)


def ff_back_kernel(pick_ref, dst_ref, pre_ref, *refs):
    candidates, (dpre_ref, sum_ref, part_ref, w1_ref, w2_ref, sems) = refs[:6], refs[6:]
    fetch(pick_ref, 1, candidates, w2_ref, sems.at[1])
    fetch(pick_ref, 0, candidates, w1_ref, sems.at[0])
    d_state = dst_ref[:, :, :WIDTH].reshape(-1, WIDTH)
    pre = pre_ref[...]
    slope = 0.5 * (1.0 + lax.erf(pre * (0.5**0.5))) + pre * jnp.exp(-0.5 * pre * pre) * (
        1.0 / (2.0 * math.pi) ** 0.5
    )
    arrived(candidates[0], w2_ref, sems.at[1])
    d_pre = low(dot(d_state, w2_ref[...], NT) * slope)
    dpre_ref[...] = d_pre
    sum_ref[...] = rowsum(d_pre.astype(F32))
    arrived(candidates[0], w1_ref, sems.at[0])
    part_ref[...] = low(dot(d_pre, w1_ref[...])).reshape(part_ref.shape)


def ff_call(kernel, name, pick, arrays, candidates, outs):
    moved = sum(a.size * a.dtype.itemsize for a in list(arrays) + list(outs))
    return pl.pallas_call(
        kernel,
        in_specs=[smem()]
        + [vmem()] * len(arrays)
        + [pl.BlockSpec(memory_space=pl.ANY)] * len(candidates),
        out_specs=[vmem()] * len(outs),
        out_shape=list(outs),
        scratch_shapes=[
            pltpu.VMEM((512, WIDTH), BF),
            pltpu.VMEM((512, WIDTH), BF),
            pltpu.SemaphoreType.DMA((2,)),
        ],
        compiler_params=pltpu.CompilerParams(vmem_limit_bytes=24 * 2**20),
        cost_estimate=pl.CostEstimate(
            flops=2 * 10**8, bytes_accessed=moved + 2 * 2**20, transcendentals=0
        ),
        name=name,
    )(pick, *arrays, *candidates)


def head_kernel(
    where_ref, part_ref, resid_ref, pj_ref, pjp_ref, partners_ref, target_ref, rows_ref,
    state_ref, low_ref, vec_ref, dz_ref,
):
    images = resid_ref.shape[0]
    state = resid_ref[...] + jnp.sum(part_ref[...].astype(F32), axis=0) + rows_ref[R_C2 : R_C2 + 1]
    gain = rows_ref[R_GAINF : R_GAINF + 1]
    xhat, rstd = norm_parts(state)
    final = low(xhat * gain + rows_ref[R_SHIFTF : R_SHIFTF + 1])
    z_own, z_peer = dot(final, pj_ref[...], NT), dot(final, pjp_ref[...], NT)
    square = jnp.sum(z_own * z_own, axis=-1, keepdims=True) + jnp.sum(
        z_peer * z_peer, axis=-1, keepdims=True
    )
    inv = lax.rsqrt(square + EPS_NORM)
    core = where_ref[1]
    half = PROJ // 2
    own_lanes = pl.ds(pl.multiple_of(core * half, 128), half)
    peer_lanes = pl.ds(pl.multiple_of((1 - core) * half, 128), half)
    ptn_own, ptn_peer = partners_ref[:, own_lanes], partners_ref[:, peer_lanes]
    logits = dot(low(z_own * inv), ptn_own, NT) + dot(low(z_peer * inv), ptn_peer, NT)
    logits = logits / SOFTMAX_SCALE
    total = logits.shape[1]
    hit = lax.broadcasted_iota(jnp.int32, (images, total), 1) == target_ref[...]
    top = jnp.max(logits, axis=-1, keepdims=True)
    e = jnp.exp(logits - top)
    mass = jnp.sum(e, axis=-1, keepdims=True)
    aim = jnp.sum(jnp.where(hit, logits, 0.0), axis=-1, keepdims=True)
    losses = jnp.log(mass) + top - aim
    d_logits = (e / mass - jnp.where(hit, 1.0, 0.0)) / total
    g_logits = low(d_logits / SOFTMAX_SCALE)
    d_own, d_peer = dot(g_logits, ptn_own), dot(g_logits, ptn_peer)
    along = jnp.sum(d_own * z_own, axis=-1, keepdims=True) + jnp.sum(
        d_peer * z_peer, axis=-1, keepdims=True
    )
    shrink = along * inv * inv * inv
    dz_own, dz_peer = low(d_own * inv - z_own * shrink), low(d_peer * inv - z_peer * shrink)
    dz_ref[:, own_lanes] = dz_own
    dz_ref[:, peer_lanes] = dz_peer
    d_final = dot(dz_own, pj_ref[...]) + dot(dz_peer, pjp_ref[...])
    d_state = norm_back(d_final, gain, xhat, rstd)
    state_ref[...] = d_state
    sent = jnp.concatenate([low(d_state), dz_ref[...], final], axis=1)
    low_ref[...] = jnp.broadcast_to(sent[None], low_ref.shape)
    vec_ref[...] = jnp.zeros_like(vec_ref)
    vec_ref[0:1] = rowsum(d_state)
    vec_ref[1:2] = rowsum(d_final * xhat)
    vec_ref[2:3] = rowsum(d_final)
    vec_ref[3:4] = jnp.broadcast_to(rowsum(losses) / total, (1, WIDTH))


def backward_kernel(
    images, where_ref, part_ref, dstate_ref, resid_ref, wo_ref, wv_ref, hid_ref, xhat_ref,
    rstd_ref, p_ref, mass_ref, qk_ref, rows_ref, shuffle_ref,
    de_ref, do_ref, dres_ref, pos_ref, vec_ref, pull_ref, dom_ref, da_ref,
):
    rows = images * HEADS
    gain, value_bias = rows_ref[R_GAIN1 : R_GAIN1 + 1], rows_ref[R_VB : R_VB + 1]
    shuffle = shuffle_ref[...]
    vec_ref[...] = jnp.zeros_like(vec_ref)
    d_two = jnp.sum(part_ref[...].astype(F32), axis=0)
    xhat2, rstd2 = norm_parts(resid_ref[...])
    d_resid = dstate_ref[...] + norm_back(d_two, rows_ref[R_GAIN2 : R_GAIN2 + 1], xhat2, rstd2)
    vec_ref[3:4] = rowsum(d_resid)
    vec_ref[4:5] = rowsum(d_two * xhat2)
    vec_ref[5:6] = rowsum(d_two)
    d_low = low(d_resid)
    dres_ref[...] = jnp.broadcast_to(d_low[None], dres_ref.shape)
    d_att = to_natural(
        low(dot(d_low, wo_ref[0], NT)), low(dot(d_low, wo_ref[1], NT)), shuffle
    )
    do_ref[...] = d_att
    spread = jnp.broadcast_to(d_att.reshape(images, 1, WIDTH).astype(F32), (images, HEADS, WIDTH))
    wide = jnp.where(head_mask(rows), spread.reshape(rows, WIDTH), 0.0)
    dom_ref[...] = low(wide)
    vec_ref[2:3] = rowsum(wide * mass_ref[:, 0:1])
    da_ref[...] = to_natural(
        low(dot(dom_ref[...], wv_ref[0], NT)), low(dot(dom_ref[...], wv_ref[1], NT)), shuffle
    )
    qk = qk_ref[...]
    bias_rows = low(jnp.broadcast_to(value_bias, (8, WIDTH)))
    real = lax.broadcasted_iota(jnp.int32, (SLOT, WIDTH), 0) < PATCHES
    for i in range(images):
        part = slice(SLOT * i, SLOT * (i + 1))
        mine = slice(HEADS * i, HEADS * (i + 1))
        hid, p, da = hid_ref[part], p_ref[part], da_ref[mine]
        dp = dot(hid, da, NT) + dot(bias_rows, dom_ref[mine], NT)[0:1]
        ds = low(p * (dp - rowsum(p * dp)))
        dh = dot(low(p), da) + dot(ds, qk)
        pull = dot(ds, hid, TN)
        xhat, rstd = xhat_ref[part], rstd_ref[part, 0:1]
        dx = norm_back(dh, gain, xhat, rstd)
        de_ref[part] = low(jnp.where(real, dx, 0.0))
        vec_ref[0:1] += rowsum(dh * xhat)
        vec_ref[1:2] += rowsum(dh)
        if i == 0:
            pos_ref[...] = dx
            pull_ref[...] = pull
        else:
            pos_ref[...] += dx
            pull_ref[...] += pull


def backward_call(images, where, arrays):
    tokens = images * SLOT
    outs = [
        shape((tokens, WIDTH), BF),
        shape((images, WIDTH), BF),
        shape((8, images, WIDTH), BF),
        shape((SLOT, WIDTH), F32),
        shape((8, WIDTH), F32),
        shape((HEADS, WIDTH), F32),
    ]
    scratch = [pltpu.VMEM((images * HEADS, WIDTH), BF)] * 2
    return call(
        functools.partial(backward_kernel, images), "backward", [where], arrays, outs, scratch
    )


def rows_kernel(where_ref, act_ref, dpre_ref, hid_ref, dst_ref, dres_ref, out_ref):
    half = WIDTH // 2
    base = 3 * WIDTH
    out_ref[:, :half] = act_ref[...]
    out_ref[:, half:WIDTH] = dpre_ref[...]
    count = out_ref.shape[0]
    out_ref[:, WIDTH : 2 * WIDTH] = hid_ref[:, :, :WIDTH].reshape(count, WIDTH)
    out_ref[:, 2 * WIDTH : base] = dst_ref[:, :, :WIDTH].reshape(count, WIDTH)

    @pl.when(where_ref[0] == 2)
    def _():
        out_ref[:, base : base + WIDTH] = hid_ref[:, :, WIDTH:].reshape(count, WIDTH)
        out_ref[:, base + WIDTH :] = dres_ref[...].reshape(count, WIDTH)

    @pl.when(where_ref[0] != 2)
    def _():
        out_ref[:, base : base + WIDTH + PROJ] = dst_ref[:, :, WIDTH:].reshape(count, WIDTH + PROJ)
        out_ref[:, base + WIDTH + PROJ :] = jnp.zeros((count, WIDTH - PROJ), BF)


def embed_grad_kernel(
    images, plan, where_ref, pix_ref, pixp_ref, de_ref, dep_ref, pooled_ref, pooledp_ref,
    do_ref, dop_ref, *out_refs,
):
    col = where_ref[0]
    heads = images * HEADS
    for (source, first, rows, _), out_ref in zip(plan, out_refs):
        block = col ^ source

        @pl.when(block < 3)
        def _():
            lanes = pl.ds(pl.multiple_of(block * 512 + first, 128), rows)
            total = dot(pix_ref[:, lanes], de_ref[...], TN) + dot(pixp_ref[:, lanes], dep_ref[...], TN)
            out_ref[...] = total.astype(out_ref.dtype)

        @pl.when(block == 3)
        def _():
            total = None
            for pooled, do in ((pooled_ref, do_ref), (pooledp_ref, dop_ref)):
                spread = jnp.broadcast_to(
                    do[...].reshape(images, 1, WIDTH).astype(F32), (images, HEADS, WIDTH)
                )
                wide = low(jnp.where(head_mask(heads), spread.reshape(heads, WIDTH), 0.0))
                term = dot(pooled[:, first : first + rows], wide, TN)
                total = term if total is None else total + term
            out_ref[...] = total.astype(out_ref.dtype)


def embed_grad_call(images, name, plan, where, arrays):
    outs = [shape((rows, WIDTH), dtype) for _, _, rows, dtype in plan]
    return call(
        functools.partial(embed_grad_kernel, images, plan), name, [where], arrays, outs
    )


def add_far_kernel(x_low_ref, x_high_ref, got_x_ref, y_low_ref, got_y_ref, y_high_ref, x_ref, y_ref):
    x_ref[0] = x_low_ref[...]
    x_ref[1] = low(x_high_ref[...] + got_x_ref[...].astype(F32))
    y_ref[0] = low(y_low_ref[...] + got_y_ref[...].astype(F32))
    y_ref[1] = y_high_ref[...]


def add_far(pieces):
    rows = pieces[0].shape[0]
    step = rows // 4
    out = shape((2, rows, WIDTH), BF)
    return pl.pallas_call(
        add_far_kernel,
        grid=(4,),
        in_specs=[pl.BlockSpec((step, WIDTH), lambda i: (i, 0))] * 6,
        out_specs=[pl.BlockSpec((2, step, WIDTH), lambda i: (0, i, 0))] * 2,
        out_shape=[out, out],
        compiler_params=pltpu.CompilerParams(vmem_limit_bytes=58 * 2**20),
        cost_estimate=pl.CostEstimate(flops=10**6, bytes_accessed=6 * 2**20, transcendentals=0),
        name="add_far",
    )(*pieces)


def to_natural_exact(first, second, shuffle):
    wide = shuffle.astype(F32)
    out = []
    for block in range(first.shape[1] // 128):
        lanes = slice(128 * block, 128 * block + 128)
        both = jnp.concatenate([first[:, lanes], second[:, lanes]], axis=1)
        out.append(dot(both, wide, NT, precision=lax.Precision.HIGHEST))
    return jnp.concatenate(out, axis=1)


def collect_kernel(
    where_ref, pos_ref, vec_ref, head_ref, sum_ref, pull_ref, shuffle_ref, sent_ref, out_ref
):
    col, core = where_ref[0], where_ref[1]
    out_ref[...] = jnp.zeros_like(out_ref)
    top = pos_ref[PATCHES:TOKS] + vec_ref[3:4]
    out_ref[0:1] = top
    out_ref[1:2] = top
    patches = pos_ref[0:PATCHES]
    out_ref[2 : 1 + TOKS] = patches
    out_ref[R_PATCH : R_PATCH + 1] = rowsum(patches)
    out_ref[R_GAIN1 : R_SHIFT1 + 1] = vec_ref[0:2]
    out_ref[R_VB : R_VB + 1] = vec_ref[2:3]
    out_ref[R_OB : R_SHIFT2 + 1] = vec_ref[3:6]
    sums = jnp.broadcast_to(sum_ref[...], (8, WIDTH // 2))
    nothing = jnp.zeros_like(sums)
    row = to_natural_exact(
        jnp.where(core == 0, sums, nothing), jnp.where(core == 0, nothing, sums), shuffle_ref[...]
    )
    for block in range(4):
        mine = (col + 1) % 4 == block
        out_ref[R_SHIFT2 + 1 + block : R_SHIFT2 + 2 + block] = jnp.where(mine, row[0:1], 0.0)
    out_ref[R_C2 : R_SHIFTF + 1] = head_ref[0:3]
    out_ref[R_SMALL : R_SMALL + HEADS] = pull_ref[...]
    out_ref[R_SMALL + HEADS : R_SMALL + HEADS + 1] = head_ref[3:4]
    for number in range(sent_ref.shape[0]):
        sent_ref[number] = out_ref[3 * number : 3 * number + 3]


def share_kernel(got_ref, sent_ref):
    sent_ref[...] = jnp.broadcast_to(jnp.sum(got_ref[...], axis=0, keepdims=True), sent_ref.shape)


def query_back_kernel(core_ref, got_ref, w_ref, shuffle_ref, dq_ref, pull_ref, total_ref):
    for number in range(got_ref.shape[0]):
        total_ref[3 * number : 3 * number + 3] = got_ref[number]
    wide = shuffle_ref[...].astype(F32)
    pull = total_ref[R_SMALL : R_SMALL + HEADS]
    is_one = core_ref[0] == 1
    out = []
    for block in range(WIDTH // 256):
        moved = dot(pull[:, 256 * block : 256 * block + 256], wide, precision=lax.Precision.HIGHEST)
        out.append(jnp.where(is_one, moved[:, 128:], moved[:, :128]))
    half = jnp.concatenate(out, axis=1)
    pull_ref[...] = half
    d_query = jnp.where(head_mask(HEADS), dot(low(half), w_ref[...]), 0.0)
    dq_ref[...] = jnp.broadcast_to(rowsum(d_query) * SCALE, dq_ref.shape)


def complete_kernel(total_ref, reports_ref, rows_ref, shuffle_ref, out_ref, norm_ref):
    out_ref[...] = total_ref[0:R_SMALL]
    half = WIDTH // 2
    first = jnp.broadcast_to(reports_ref[6, :, WIDTH : WIDTH + half], (8, half))
    second = jnp.broadcast_to(reports_ref[7, :, WIDTH : WIDTH + half], (8, half))
    d_hidden = to_natural_exact(first, second, shuffle_ref[...])[0:1]
    xhat, rstd = norm_parts(rows_ref[0:1] + rows_ref[1:2])
    d_class = norm_back(d_hidden, rows_ref[R_GAIN1 : R_GAIN1 + 1], xhat, rstd)
    out_ref[0:1] += d_class
    out_ref[1:2] += d_class
    out_ref[R_GAIN1 : R_GAIN1 + 1] += d_hidden * xhat
    out_ref[R_SHIFT1 : R_SHIFT1 + 1] += d_hidden
    out_ref[R_SHIFT1 + 1 : R_SHIFT1 + 2] = reports_ref[6, :, :WIDTH]
    grads = out_ref[...]
    square = jnp.sum(jnp.sum(grads * grads, axis=0, keepdims=True), axis=1, keepdims=True)
    for number in range(reports_ref.shape[0]):
        square = square + reports_ref[number, :, WIDTH + half : WIDTH + half + 1]
    norm_ref[...] = jnp.broadcast_to(jnp.sqrt(square), (8, 128))


def owner_kernel(role_ref, pull_ref, heads_ref, class_ref, dq_ref, *refs):
    rows, out_ref = refs[:6], refs[6]
    chip, core = role_ref[0], role_ref[1]
    half = WIDTH // 2
    base = 3 * WIDTH

    def product(left, right):
        total = None
        for piece in rows:
            term = dot(left(piece), right(piece), TN)
            total = term if total is None else total + term
        return total

    @pl.when((chip >= 7) & (chip <= 14))
    def _():
        is_two = chip >= 11
        out_ref[...] = product(
            lambda piece: jnp.where(is_two, piece[:, :half], piece[:, half:WIDTH]),
            lambda piece: jnp.where(is_two, piece[:, 2 * WIDTH : base], piece[:, WIDTH : 2 * WIDTH]),
        )

    @pl.when(chip == 6)
    def _():
        lanes = pl.ds(pl.multiple_of(base + core * half, 128), half)
        out_ref[...] = product(lambda piece: piece[:, lanes], lambda piece: piece[:, base + WIDTH :])

    @pl.when(chip == 15)
    def _():
        lanes = pl.ds(pl.multiple_of(base + core * (PROJ // 2), 128), PROJ // 2)
        out_ref[: PROJ // 2] = product(
            lambda piece: piece[:, lanes],
            lambda piece: piece[:, base + PROJ : base + PROJ + WIDTH],
        )
        out_ref[PROJ // 2 :] = jnp.zeros((512 - PROJ // 2, WIDTH), F32)

    @pl.when(chip == 4)
    def _():
        out_ref[...] = dot(
            pull_ref[...], heads_ref[...].astype(F32), TN, precision=lax.Precision.HIGHEST
        )

    @pl.when(chip == 3)
    def _():
        out_ref[...] = dot(
            class_ref[...].astype(F32), jnp.concatenate([dq_ref[0:1], jnp.zeros((7, WIDTH), F32)]),
            TN, precision=lax.Precision.HIGHEST,
        )


def finish_kernel(
    role_ref, formed_ref, dq_ref, toward_ref, total_ref, first_ref, second_ref, aside_ref, third_ref,
    out_ref, top_ref, end_ref, report_ref,
):
    chip = role_ref[0]

    @pl.when(chip < 3)
    def _():
        out_ref[...] = total_ref[...] + first_ref[...].astype(F32) + second_ref[...].astype(F32)

    @pl.when(chip == 5)
    def _():
        out_ref[...] = (
            second_ref[...].astype(F32) + aside_ref[...].astype(F32) + third_ref[...].astype(F32)
        )

    @pl.when((chip >= 3) & (chip != 5))
    def _():
        out_ref[...] = formed_ref[...]

    edge = top_ref.shape[0]
    top_ref[...] = out_ref[:edge]
    end_ref[...] = out_ref[-edge:]
    grads = out_ref[...]
    square = jnp.sum(jnp.sum(grads * grads, axis=0, keepdims=True), axis=1, keepdims=True)
    report_ref[...] = jnp.concatenate(
        [dq_ref[...], toward_ref[...], jnp.broadcast_to(square, (1, 128))], axis=1
    )


def update_kernel(
    source_ref, scalar_ref, before_ref, grad_ref, behind_ref, w_ref, m_ref, v_ref,
    nw_ref, nm_ref, nv_ref,
):
    step = pl.program_id(0)
    slots = grad_ref.shape[0]
    factor, fix_one, fix_two = scalar_ref[0], scalar_ref[1], scalar_ref[2]
    for k in range(w_ref.shape[0]):
        at = source_ref[step * w_ref.shape[0] + k]
        inside = (at >= 0) & (at < slots)
        grad = jnp.where(
            inside,
            grad_ref[jnp.clip(at, 0, slots - 1)],
            jnp.where(
                at < 0,
                before_ref[jnp.clip(at + JITTER, 0, JITTER - 1)],
                behind_ref[jnp.clip(at - slots, 0, JITTER - 1)],
            ),
        )
        grad = grad * jnp.where(at >= -JITTER, factor, 0.0)
        weight = w_ref[k]
        first = BETA_ONE * m_ref[k] + (1.0 - BETA_ONE) * grad
        second = BETA_TWO * v_ref[k] + (1.0 - BETA_TWO) * grad * grad
        nm_ref[k] = first
        nv_ref[k] = second
        nw_ref[k] = weight - LEARN_RATE * (
            (first * fix_one) / (jnp.sqrt(second * fix_two) + ADAM_EPS) + DECAY_RATE * weight
        )


def update_call(source, scalars, before, grads, behind, masters, first, second):
    slots, part, width = masters.shape
    block = 16
    spec = pl.BlockSpec((block, part, width), lambda i: (i, 0, 0))
    return pl.pallas_call(
        update_kernel,
        grid=(slots // block,),
        in_specs=[smem(), smem(), vmem(), vmem(), vmem(), spec, spec, spec],
        out_specs=[spec] * 3,
        out_shape=[shape(masters.shape, F32)] * 3,
        compiler_params=pltpu.CompilerParams(vmem_limit_bytes=58 * 2**20),
        cost_estimate=pl.CostEstimate(
            flops=2 * 10**7, bytes_accessed=7 * masters.size * 4, transcendentals=0
        ),
        name="update",
    )(source, scalars, before, grads, behind, masters, first, second)


CHIPS = 16
CHIP = ("z", "y", "x")
ALL = ("z", "y", "x", "c")
PLANE = ("y", "x", "c")
FLIP_X = [(i, i ^ 1) for i in range(CHIPS)]
FLIP_Y = [(i, i ^ 2) for i in range(CHIPS)]
FLIP_CORE = [(0, 1), (1, 0)]


def hop(values, pairs):
    return lax.ppermute(values, CHIP, pairs)


def swap(values):
    return lax.ppermute(values, "c", FLIP_CORE)


def after(values, *others):
    return lax.optimization_barrier((values,) + others)[0]


def among(img, chips):
    hit = img == chips[0]
    for chip in chips[1:]:
        hit = hit | (img == chip)
    return hit


def choose(img, cases, otherwise):
    out = otherwise
    for chips, values in cases:
        out = jnp.where(among(img, chips), values, out)
    return out


def together(*values):
    return lax.optimization_barrier(values)


def plane_gather(block, diagonal_by_x):
    by_x, by_y, block_peer = hop(block, FLIP_X), hop(block, FLIP_Y), swap(block)
    proj_top = jnp.where(img == 15, corner[0], corner[1] + corner[2] + corner[3])
    diagonal = hop(by_y, FLIP_X) if diagonal_by_x else hop(by_x, FLIP_Y)
    return [block, by_x, by_y, diagonal]


def in_plane(values):
    return lax.all_to_all(values, PLANE, 0, 0, tiled=True)


def from_all(values):
    sent = jnp.broadcast_to(values[None], (2 * CHIPS,) + values.shape)
    return lax.all_to_all(sent, ALL, 0, 0, tiled=True)


def natural(values):
    lead = values.shape[:-2]
    units = values.shape[-1] // 16
    split = values.reshape(lead + (2, units, 16))
    return jnp.swapaxes(split, -3, -2).reshape(lead + (units * 32,))


def halves(values):
    lead = values.shape[:-1]
    units = values.shape[-1] // 32
    return jnp.swapaxes(values.reshape(lead + (units, 2, 16)), -3, -2).reshape(
        lead + (2, units * 16)
    )


def per_device_16(
    pixels, keep_mask, partner_index, partner_emb, masters, first_moment_slots,
    second_moment_slots, slot_unit_index, small_params, small_first, small_second, step_count,
):
    img, core = lax.axis_index(CHIP), lax.axis_index("c")
    col, plane = img % 4, img // 4
    images = pixels.shape[0]
    slots = masters.shape[0]
    is_one = core == 1
    where = jnp.stack([col, core]).astype(jnp.int32)
    shuffle = shuffle_matrix()
    rows = small_params
    class_state = small_params[0] + small_params[1]

    def mine_of(pair):
        return jnp.where(is_one, pair[1], pair[0])

    def theirs_of(pair):
        return jnp.where(is_one, pair[0], pair[1])

    near = slots_near(slot_unit_index, img, slots)
    held = low(masters)
    ids = img * slots + jnp.arange(slots, dtype=jnp.int32)
    matches = [near[s : s + slots] == ids for s in range(2 * JITTER + 1)]
    middle = pick(held[6:26], [m[8:24] for m in matches], 16).reshape(256, WIDTH)
    one_a = hop(middle, [(0, 4), (1, 5), (2, 6), (5, 7)])
    partners = from_all(after(partner_emb, middle))
    before, behind = halo(after(held, middle), CHIPS, CHIP)
    lower = pick(jnp.concatenate([before, held[:10]]), [m[:8] for m in matches], 8)
    upper = pick(jnp.concatenate([held[22:], behind]), [m[24:] for m in matches], 8)
    outer = jnp.concatenate([lower, upper]).reshape(256, WIDTH)
    own_w = jnp.concatenate([outer[:128], middle, outer[128:]])
    class_hidden = low(layer_norm(class_state, small_params[R_GAIN1], small_params[R_SHIFT1]))
    class_half = mine_of(halves(class_hidden))
    query = dot(class_half[None], own_w)
    query = query + swap(query)
    wo_quarter = hop(own_w[384:], [(6, 7)]) + hop(own_w[:128], [(6, 4)])
    wo_quarter = wo_quarter + hop(own_w[128:256], [(6, 5)])
    wo_quarter = jnp.where(img == 6, own_w[256:384], wo_quarter)
    down_one = hop(
        own_w,
        [(12, 8), (13, 9), (14, 10), (11, 7), (8, 4), (9, 5), (10, 6), (7, 3)],
    )
    one_a, outer, query = together(one_a, outer, query)
    query = hop(query, [(3, 4)])
    one_b = hop(outer, [(0, 4), (1, 5), (2, 6), (5, 7)])
    two_a = hop(one_a, [(4, 8), (5, 9), (6, 10), (7, 11)])
    pix = prep(after(pixels, one_a), shuffle).reshape(2, images * SLOT, PIX // 2)
    corner = after(own_w[: PROJ // 2], one_a)
    corner = [corner] + [hop(corner, [(15, 15 ^ flip)]) for flip in (1, 2, 3)]
    query = low((query + small_params[R_SHIFT1 + 1 : R_SHIFT1 + 2]) * SCALE)
    query_heads = jnp.where(head_mask(HEADS), query, jnp.zeros((), BF))
    pulled = jnp.pad(low(dot(query_heads, own_w, NT)), ((0, 0), (0, WIDTH // 2)))
    one_b, two_a, wo_quarter, pulled, down_one = together(
        one_b, two_a, wo_quarter, pulled, down_one
    )
    mid_b = jnp.concatenate([one_b, wo_quarter, pulled])
    two_b = hop(mid_b, [(4, 8), (5, 9), (6, 10), (7, 11)])
    three_a = hop(
        jnp.where(img == 7, one_a, two_a), [(8, 12), (9, 13), (10, 14), (11, 15), (7, 3)]
    )
    low_b = hop(mid_b[256:], [(4, 0), (5, 1), (6, 2)])
    two_b, three_a, low_b, pix, partners, *corner = together(
        two_b, three_a, low_b, pix, partners, *corner
    )
    block_a = jnp.where(img < 3, middle, one_a + two_a + three_a)
    x_a, y_a = hop(block_a, FLIP_X), hop(block_a, FLIP_Y)
    three_b = hop(
        jnp.where(img == 7, mid_b, two_b), [(8, 12), (9, 13), (10, 14), (11, 15), (7, 3)]
    )
    pix_own, pix_send = mine_of(pix), theirs_of(pix)
    x_a, y_a, three_b, pix_own, pix_send = together(x_a, y_a, three_b, pix_own, pix_send)
    spot = jnp.stack([img, plane]).astype(jnp.int32)
    block_b = second_block(spot, [outer, low_b, mid_b, two_b, three_b])
    x_b, y_b = hop(block_b, FLIP_X), hop(block_b, FLIP_Y)
    down_two = hop(
        after(down_one, three_b), [(8, 4), (9, 5), (10, 6), (7, 3), (4, 0), (5, 1), (6, 2)]
    )
    proj_top = jnp.where(img == 15, corner[0], corner[1] + corner[2] + corner[3])
    (partners,) = call(
        partner_kernel, "partners", [], [partners], [shape((2 * CHIPS * images, PROJ), BF)]
    )
    up_one = hop(
        after(own_w, three_b), [(8, 12), (9, 13), (10, 14), (7, 11), (11, 15)]
    )
    peers_a = [swap(block_a), swap(x_a), swap(y_a), swap(block_b)]
    x_b, y_b, up_one, down_two, *peers_a = together(x_b, y_b, up_one, down_two, *peers_a)
    up_two = hop(up_one, [(11, 15)])
    proj_one = hop(after(proj_top, x_b), [(12, 4), (13, 5), (14, 6), (15, 7)])
    d_a, d_b = hop(y_a, FLIP_X), hop(x_b, FLIP_Y)
    down_three = hop(after(down_two, y_b), [(4, 0), (5, 1), (6, 2)])
    x_peer, y_peer = swap(x_b), swap(y_b)
    d_a, d_b, x_peer, y_peer = together(d_a, d_b, x_peer, y_peer)
    segments = [(source, ((0, 128, 256),), -1) for source in range(4)]
    segments += [(source, ((0, 0, 128), (128, 384, 128)), 256) for source in range(4)]
    own_pieces = [block_a, x_a, y_a, d_a, block_b, x_b, y_b, d_b]
    peer_pieces = [*peers_a[:3], swap(d_a), peers_a[3], x_peer, y_peer, swap(d_b)]
    pix_peer = swap(pix_send)
    valid = jnp.concatenate(
        [
            keep_mask,
            jnp.ones((images, 1), jnp.int32),
            jnp.zeros((images, SLOT - TOKS), jnp.int32),
        ],
        axis=1,
    ).reshape(images * SLOT, 1)
    (
        hid, xhat, rstd, p, pooled, mass, wv, wo, qk, resid, hidden_sent,
    ) = forward_call(
        segments, images, where, pix, own_pieces, peer_pieces, rows, valid, shuffle
    )
    pooled_own = mine_of(pooled)
    pooled_peer = swap(theirs_of(pooled))

    hidden_all = in_plane(hidden_sent)
    hidden_all, pooled_peer = together(hidden_all, pooled_peer)
    ff_block = (col + 1) % 4
    bias_part = lax.dynamic_slice(
        small_params[R_SHIFT2 + 1 : R_C2].reshape(4, 32, 2, 16),
        (ff_block, 0, core, 0),
        (1, 32, 1, 16),
    ).reshape(1, 512)
    candidates = [own_w, up_one, up_two, down_one, down_two, down_three]
    pick_one = choose(
        img, [((15,), 2), ((12, 13, 14, 11), 1), ((4, 5, 6, 3), 3), ((0, 1, 2), 4)], 0
    )
    pick_two = choose(
        img, [((15,), 1), ((8, 9, 10, 7), 3), ((4, 5, 6, 3), 4), ((0, 1, 2), 5)], 0
    )
    picks = jnp.stack([pick_one, pick_two]).astype(jnp.int32)
    preact, active, part = ff_call(
        ff_kernel, "ff", picks, [hidden_all, bias_part], candidates,
        [shape((8 * images, 512), F32), shape((8 * images, 512), BF), shape((8, images, WIDTH), BF)],
    )
    proj_mid = hop(
        after(jnp.where(plane == 3, proj_top, proj_one), hidden_sent),
        [(12, 8), (13, 9), (14, 10), (15, 11), (4, 0), (5, 1), (6, 2), (7, 3)],
    )
    hidden_all = in_plane(hidden_sent)
    ff_block = (col + 1) % 4
    bias_part = lax.dynamic_slice(
        small_params[R_SHIFT2 + 1 : R_C2].reshape(4, 32, 2, 16),
        (ff_block, 0, core, 0),
        (1, 32, 1, 16),
    ).reshape(1, 512)
    candidates = [own_w, up_one, up_two, down_one, down_two, down_three]
    pick_one = choose(
        img, [((15,), 2), ((12, 13, 14, 11), 1), ((4, 5, 6, 3), 3), ((0, 1, 2), 4)], 0
    )
    pick_two = choose(
        img, [((15,), 1), ((8, 9, 10, 7), 3), ((4, 5, 6, 3), 4), ((0, 1, 2), 5)], 0
    )
    picks = jnp.stack([pick_one, pick_two]).astype(jnp.int32)
    preact, active, part = ff_call(
        ff_kernel, "ff", picks, [hidden_all, bias_part], candidates,
        [shape((8 * images, 512), F32), shape((8 * images, 512), BF), shape((8, images, WIDTH), BF)],
    )
    proj = choose(
        plane, [((3,), proj_top), ((1,), proj_one)], after(proj_mid, hidden_sent)
    )
    proj_peer = swap(proj)
    part = in_plane(part)
    proj = choose(plane, [((3,), proj_top), ((1,), proj_one)], after(proj_mid, part))
    proj_peer = swap(proj)
    d_state, d_state_sent, head_vec = call(
        head_kernel, "head", [where],
        [part, resid, proj, proj_peer, partners, partner_index[:, None], rows],
        [
            shape((images, WIDTH), F32), shape((8, images, 2 * WIDTH + PROJ), BF),
            shape((8, WIDTH), F32),
        ],
        [pltpu.VMEM((images, PROJ), BF)],
    )
    d_state_all = in_plane(d_state_sent)
    d_preact, d_preact_sum, part = ff_call(
        ff_back_kernel, "ff_back", picks, [d_state_all, preact], candidates,
        [shape((8 * images, 512), BF), shape((1, 512), F32), shape((8, images, WIDTH), BF)],
    )
    part = in_plane(part)

    d_embed, d_attended, d_resid, d_pos, d_vec, pull = backward_call(
        images, where,
        [part, d_state, resid, wo, wv, hid, xhat, rstd, p, mass, qk, rows, shuffle],
    )
    arrays = [
        pix_own, pix_peer, d_embed, swap(d_embed), pooled_own, pooled_peer, d_attended,
        swap(d_attended),
    ]
    far_x, far_y = embed_grad_call(
        images, "embed_grad_far", [(3, 0, 256, BF), (3, 256, 256, BF)], where, arrays
    )
    got_y, got_x = hop(far_x, FLIP_X), hop(far_y, FLIP_Y)
    own_part, x_low, x_high, y_low, y_high = embed_grad_call(
        images, "embed_grad_near",
        [(0, 0, 512, F32), (1, 0, 256, BF), (1, 256, 256, F32), (2, 0, 256, F32), (2, 256, 256, BF)],
        after(where, far_x), arrays,
    )
    d_resid = in_plane(after(d_resid, far_x))
    d_pos, d_vec, head_vec, d_preact_sum, pull, _ = together(
        d_pos, d_vec, head_vec, d_preact_sum, pull, far_x
    )
    (small_sent,) = call(
        collect_kernel, "collect", [where], [d_pos, d_vec, head_vec, d_preact_sum, pull, shuffle],
        [shape((32, 3, WIDTH), F32)], [pltpu.VMEM((96, WIDTH), F32)],
    )
    got_x, got_y, own_part, x_low, x_high, y_low, y_high, d_resid, small_sent = together(
        got_x, got_y, own_part, x_low, x_high, y_low, y_high, d_resid, small_sent
    )
    part_x, part_y = add_far([x_low, x_high, got_x, y_low, got_y, y_high])
    part_x, part_y = part_x.reshape(512, WIDTH), part_y.reshape(512, WIDTH)
    sum_x, sum_y = hop(part_x, FLIP_X), hop(part_y, FLIP_Y)
    shares = lax.all_to_all(small_sent, ALL, 0, 0, tiled=True)
    (ff_rows,) = call(
        rows_kernel, "rows", [where], [active, d_preact, hidden_all, d_state_all, d_resid],
        [shape((8 * images, 5 * WIDTH), BF)],
    )
    rise = [(i, i + 4) for i in range(12)]
    fall = [(12, 8), (13, 9), (14, 10), (15, 11), (10, 6), (11, 7)]
    up_one, down_one = hop(ff_rows, rise), hop(ff_rows, fall)
    sum_x, sum_y = together(sum_x, sum_y)
    total = own_part + sum_x.astype(F32) + sum_y.astype(F32)
    sent = low(total)
    first = hop(sent, [(12, 8), (13, 9), (14, 10), (15, 11), (4, 0), (5, 1), (6, 2)])
    aside = hop(sent, [(3, 1), (7, 5)])
    (small_sent,) = call(share_kernel, "share", [], [shares], [shape((32, 3, WIDTH), F32)])
    shares = lax.all_to_all(small_sent, ALL, 0, 0, tiled=True)
    up_two, down_two = hop(up_one, rise[4:]), hop(down_one, fall[4:])
    first, aside, up_two, down_two, total = together(first, aside, up_two, down_two, total)
    partial = low(total + first.astype(F32))
    second = hop(partial, [(8, 0), (9, 1), (10, 2), (11, 5)])
    third = hop(aside, [(1, 5)])
    up_three = hop(up_two, rise[8:])
    d_query, pull_half, small_total = call(
        query_back_kernel, "query_back", [core.reshape(1).astype(jnp.int32)],
        [shares, own_w, shuffle],
        [shape((8, WIDTH), F32), shape((HEADS, WIDTH // 2), F32), shape((96, WIDTH), F32)],
    )
    loss = small_total[R_SMALL + HEADS, 0]
    d_query = d_query[0:1]
    d_query = d_query + swap(d_query)
    d_query = hop(d_query, [(4, 3)])
    toward = dot(low(d_query), own_w, NT)

    every = [ff_rows, up_one, up_two, up_three, down_one, down_two]
    class_rows = jnp.concatenate([class_half[None], jnp.zeros((7, WIDTH // 2), BF)])
    role = jnp.stack([img, core]).astype(jnp.int32)
    (formed,) = call(
        owner_kernel, "owner", [role], [pull_half, query_heads, class_rows, d_query, *every],
        [shape((512, WIDTH), F32)],
    )
    edge = shape((JITTER * 16, WIDTH), F32)
    own_grad, top, end, report = call(
        finish_kernel, "finish", [role],
        [formed, d_query, toward, total, first, second, aside, third],
        [shape((512, WIDTH), F32), edge, edge, shape((1, WIDTH + 640), F32)],
    )
    reports = from_all(report)
    before = hop(end, [(i, i + 1) for i in range(CHIPS - 1)]).reshape(JITTER, 16, WIDTH)
    behind = hop(top, [(i + 1, i) for i in range(CHIPS - 1)]).reshape(JITTER, 16, WIDTH)
    small_grad, norm = call(
        complete_kernel, "complete", [], [small_total, reports, rows, shuffle],
        [shape((R_SMALL, WIDTH), F32), shape((8, 128), F32)],
    )
    grad_norm = norm[0, 0]
    factor = 1.0 / jnp.maximum(grad_norm, 1.0)
    own_grad = own_grad.reshape(slots, 16, WIDTH)
    here = near[JITTER : JITTER + slots]
    source = jnp.where(here < UNIT_COUNT, here - img * slots, -100)
    step_value = step_count.astype(F32)
    scalars = jnp.stack(
        [
            factor,
            1.0 / (1.0 - jnp.power(BETA_ONE, step_value)),
            1.0 / (1.0 - jnp.power(BETA_TWO, step_value)),
        ]
    )
    new_masters, new_first, new_second = update_call(
        source, scalars, before, own_grad, behind, masters, first_moment_slots,
        second_moment_slots,
    )
    new_small, new_small_first, new_small_second = adamw(
        small_params, small_grad * factor, small_first, small_second, step_value
    )
    return (
        new_masters, new_first, new_second, new_small, new_small_first, new_small_second,
        loss, grad_norm,
    )


def per_device_any(
    pixels, keep_mask, partner_index, partner_emb, masters, first_moment_slots,
    second_moment_slots, slot_unit_index, small_params, small_first, small_second, step_count,
):
    chips, seq = lax.axis_size("img"), lax.axis_size("seq")
    img = lax.axis_index("img")
    images = pixels.shape[0]
    slots, part = masters.shape[0], masters.shape[1]
    near = slots_near(slot_unit_index, img, slots)
    own_w = to_units(low(masters), near, img, chips)
    gathered = lax.all_gather(own_w, ("img", "seq"), axis=0, tiled=False)
    flat = gathered.reshape(chips, seq, slots, part, WIDTH).transpose(0, 2, 1, 3, 4)
    flat = flat.reshape(chips * slots * ROWS_PER_UNIT, WIDTH)
    bounds = [0, PIX, WIDTH, WIDTH, WIDTH, WIDTH, FF, FF, PROJ]
    parts, offset = [], 0
    for size in bounds[1:]:
        parts.append(flat[offset : offset + size])
        offset += size
    embed_w, query_w, key_w, value_w, output_w, fc_in_w, fc_out_w, proj_w = parts
    (
        class_row, pos_rows, patch_bias, gain_one, shift_one, query_bias, value_bias, out_bias,
        gain_two, shift_two, fc_in_bias, fc_out_bias, gain_end, shift_end,
    ) = small_parts(small_params)
    class_state = class_row + pos_rows[0]
    embedded = jnp.einsum("itp,pd->itd", pixels, embed_w, preferred_element_type=F32)
    tokens = jnp.concatenate(
        [
            jnp.broadcast_to(class_state, (images, 1, WIDTH)),
            embedded + patch_bias + pos_rows[1:],
        ],
        axis=1,
    )
    hidden = low(layer_norm(tokens, gain_one, shift_one))
    class_hidden = hidden[0, 0]
    mask16 = head_mask(HEADS)
    query = low((dot(class_hidden[None], query_w)[0] + query_bias) * SCALE)
    query_heads = jnp.where(mask16, query[None], jnp.zeros((), BF))
    qk = low(dot(query_heads, key_w, NT))
    scores = jnp.einsum("hd,itd->iht", qk, hidden, preferred_element_type=F32)
    keep = jnp.concatenate([jnp.ones((images, 1), jnp.int32), keep_mask], axis=1)
    scores = jnp.where(keep[:, None, :] > 0, scores, MASKED)
    weights = jax.nn.softmax(scores, axis=-1)
    weights_low = low(weights)
    pooled = low(jnp.einsum("iht,itd->ihd", weights_low, hidden, preferred_element_type=F32))
    mass = jnp.sum(weights_low.astype(F32), axis=-1)
    mixed = dot(pooled.reshape(-1, WIDTH), value_w).reshape(images, HEADS, WIDTH)
    mixed = mixed + mass[:, :, None] * value_bias
    attended = low(jnp.sum(jnp.where(mask16, mixed, 0.0), axis=1))
    resid = class_state + dot(attended, output_w) + out_bias
    hidden_two = low(layer_norm(resid, gain_two, shift_two))
    preact = dot(hidden_two, fc_in_w, NT) + fc_in_bias
    active = low(exact_gelu(preact))
    state = resid + dot(active, fc_out_w) + fc_out_bias
    final = low(layer_norm(state, gain_end, shift_end))
    projected = dot(final, proj_w, NT)
    unit = low(normalize(projected))
    partners = lax.all_gather(partner_emb, ("img", "seq"), axis=0, tiled=True)
    count = partners.shape[0]
    logits = dot(unit, partners, NT) / SOFTMAX_SCALE
    onehot = (jnp.arange(count, dtype=jnp.int32)[None] == partner_index[:, None]).astype(F32)
    total = jax.nn.logsumexp(logits, axis=-1)
    loss_part = jnp.sum(total - jnp.sum(logits * onehot, axis=-1)) / count
    d_logits = (jax.nn.softmax(logits, axis=-1) - onehot) / count
    d_unit = dot(low(d_logits / SOFTMAX_SCALE), partners)
    d_projected = low(jax.vjp(normalize, projected)[1](d_unit)[0])
    d_final = dot(d_projected, proj_w)
    d_state, d_gain_end, d_shift_end = jax.vjp(layer_norm, state, gain_end, shift_end)[1](d_final)
    d_state_low = low(d_state)
    d_active = dot(d_state_low, fc_out_w, NT)
    d_preact = low(jax.vjp(exact_gelu, preact)[1](d_active)[0])
    d_hidden_two = dot(d_preact, fc_in_w)
    d_norm, d_gain_two, d_shift_two = jax.vjp(layer_norm, resid, gain_two, shift_two)[1](
        d_hidden_two
    )
    d_resid = d_state + d_norm
    d_resid_low = low(d_resid)
    d_attended = low(dot(d_resid_low, output_w, NT))
    wide = jnp.where(mask16, d_attended[:, None, :], jnp.zeros((), BF))
    d_pooled = low(dot(wide.reshape(-1, WIDTH), value_w, NT)).reshape(images, HEADS, WIDTH)
    d_weights = jnp.einsum("ihd,itd->iht", d_pooled, hidden, preferred_element_type=F32)
    d_weights = d_weights + jnp.sum(wide.astype(F32) * value_bias, axis=-1)[:, :, None]
    d_scores = low(weights * (d_weights - jnp.sum(weights * d_weights, axis=-1, keepdims=True)))
    d_hidden = jnp.einsum("iht,ihd->itd", weights_low, d_pooled, preferred_element_type=F32)
    d_hidden = d_hidden + jnp.einsum("iht,hd->itd", d_scores, qk, preferred_element_type=F32)
    pull = jnp.einsum("iht,itd->hd", d_scores, hidden, preferred_element_type=F32)
    d_query = jnp.sum(jnp.where(mask16, dot(low(pull), key_w), 0.0), axis=0) * SCALE
    d_class_hidden = dot(low(d_query)[None], query_w, NT)
    d_tokens, d_gain_one, d_shift_one = jax.vjp(layer_norm, tokens, gain_one, shift_one)[1](
        d_hidden
    )
    d_class, d_gain_cls, d_shift_cls = jax.vjp(layer_norm, class_state[None], gain_one, shift_one)[
        1
    ](d_class_hidden)
    d_class = d_class[0] + jnp.sum(d_tokens[:, 0], axis=0) + jnp.sum(d_resid, axis=0)
    d_patch = d_tokens[:, 1:]
    d_embed_w = jnp.einsum("itp,itd->pd", pixels, low(d_patch), preferred_element_type=F32)
    d_value_w = dot(pooled.reshape(-1, WIDTH), wide.reshape(-1, WIDTH), TN)
    d_key_w = dot(pull, query_heads.astype(F32), TN, precision=lax.Precision.HIGHEST)
    small_local = jnp.concatenate(
        [
            d_class[None],
            d_class[None],
            jnp.sum(d_patch, axis=0),
            jnp.sum(d_patch, axis=(0, 1))[None],
            (d_gain_one + d_gain_cls)[None],
            (d_shift_one + d_shift_cls)[None],
            d_query[None],
            jnp.sum(wide.astype(F32) * mass[:, :, None], axis=(0, 1))[None],
            jnp.sum(d_resid, axis=0)[None],
            d_gain_two[None],
            d_shift_two[None],
            jnp.sum(d_preact.astype(F32), axis=0).reshape(FF // WIDTH, WIDTH),
            jnp.sum(d_state, axis=0)[None],
            d_gain_end[None],
            d_shift_end[None],
        ],
        axis=0,
    )
    grad_table = jnp.concatenate(
        [
            d_embed_w,
            class_hidden.astype(F32)[:, None] * d_query[None, :],
            d_key_w,
            d_value_w,
            dot(attended, d_resid_low, TN),
            dot(d_preact, hidden_two, TN),
            dot(active, d_state_low, TN),
            dot(d_projected, final, TN),
            jnp.zeros(((chips * slots - UNIT_COUNT) * ROWS_PER_UNIT, WIDTH), F32),
        ],
        axis=0,
    ).reshape(chips * slots, ROWS_PER_UNIT, WIDTH)
    small_grad, loss = lax.psum((small_local, loss_part), ("img", "seq"))
    core_half = lax.psum_scatter(low(grad_table), "seq", scatter_dimension=1, tiled=True)
    own_grad = lax.psum_scatter(core_half.astype(F32), "img", scatter_dimension=0, tiled=True)
    owner_total = lax.psum(jnp.sum(own_grad * own_grad), ("img", "seq"))
    grad_norm = jnp.sqrt(owner_total + jnp.sum(small_grad * small_grad))
    factor = 1.0 / jnp.maximum(grad_norm, 1.0)
    slot_grad = to_slots(own_grad, near, img, chips)
    step_value = step_count.astype(F32)
    new_masters, new_first, new_second = adamw(
        masters, slot_grad * factor, first_moment_slots, second_moment_slots, step_value
    )
    new_small, new_small_first, new_small_second = adamw(
        small_params, small_grad * factor, small_first, small_second, step_value
    )
    return (
        new_masters, new_first, new_second, new_small, new_small_first, new_small_second,
        loss, grad_norm,
    )


def solution(mesh):
    chip, devices = "img", ("img", "seq")
    core, body = "seq", per_device_any
    if mesh.shape["img"] == CHIPS and mesh.shape["seq"] == 2:
        mesh = jax.sharding.Mesh(mesh.devices.reshape(4, 2, 2, 2), ALL)
        chip, devices, core, body = CHIP, ALL, "c", per_device_16
    weights = P(chip, core, None)
    return jax.shard_map(
        body,
        mesh=mesh,
        in_specs=(
            P(devices, None, None),
            P(devices, None),
            P(devices),
            P(devices, None),
            weights,
            weights,
            weights,
            P(),
            P(),
            P(),
            P(),
            P(),
        ),
        out_specs=(weights, weights, weights, P(), P(), P(), P(), P()),
        check_vma=False,
    )
```
